32 devices in a mesh: seq: 8 (over z, x), grp: 4 (over y, core).
Axes of the slice: x: 2, y: 2, z: 4, core: 2. Of those that a mesh axis runs over, the one named last changes fastest.
Arguments:
- tokens: bfloat16 [8, 8, 256, 768], P('grp', 'seq'), may hold values from -6 to 6
- cotangent: bfloat16 [8, 8, 256, 768], P('grp', 'seq'), may hold values from -6 to 6
- col_count: int32 [8], P('grp'), may hold values from 64 to 256, as said below
- row_count: int32 [8], P('grp'), may hold values from 2 to 8, as said below
- attn_weight: float32 [8, 768, 768], P(None, 'seq'), as said below
- in_weight: float32 [768, 3072], P('seq'), as said below
- out_weight: float32 [3072, 768], P(None, 'seq'), may hold values from -0.109375 to 0.109375
- norm_param: float32 [6, 768], P(None, 'seq'), as said below
- attn_first: float32 [8, 768, 768], P(None, 'seq'), may hold values from -0.0048828125 to 0.0048828125
- attn_second: float32 [8, 768, 768], P(None, 'seq'), may hold values from 1.05963814e-07 to 4.2385525e-07
- in_first: float32 [768, 3072], P('seq'), may hold values from -0.0048828125 to 0.0048828125
- in_second: float32 [768, 3072], P('seq'), may hold values from 1.05963814e-07 to 4.2385525e-07
- out_first: float32 [3072, 768], P(None, 'seq'), may hold values from -0.0048828125 to 0.0048828125
- out_second: float32 [3072, 768], P(None, 'seq'), may hold values from 1.05963814e-07 to 4.2385525e-07
- norm_first: float32 [6, 768], P(None, 'seq'), may hold values from -0.01953125 to 0.01953125
- norm_second: float32 [6, 768], P(None, 'seq'), may hold values from 1.695421e-06 to 6.781684e-06
Outputs:
- block_out: bfloat16 [8, 8, 256, 768], P('grp', 'seq')
- grad_tokens: float32 [8, 8, 256, 768], P('grp', 'seq')
- grad_norm: float32 [], replicated
- attn_first_new: float32 [8, 768, 768], P(None, 'seq')
- attn_second_new: float32 [8, 768, 768], P(None, 'seq')
- attn_weight_new: float32 [8, 768, 768], P(None, 'seq')
- attn_copy: bfloat16 [8, 768, 768], P(None, 'seq')
- in_first_new: float32 [768, 3072], P('seq')
- in_second_new: float32 [768, 3072], P('seq')
- in_weight_new: float32 [768, 3072], P('seq')
- in_copy: bfloat16 [768, 3072], P('seq')
- out_first_new: float32 [3072, 768], P(None, 'seq')
- out_second_new: float32 [3072, 768], P(None, 'seq')
- out_weight_new: float32 [3072, 768], P(None, 'seq')
- out_copy: bfloat16 [3072, 768], P(None, 'seq')
- norm_first_new: float32 [6, 768], P(None, 'seq')
- norm_second_new: float32 [6, 768], P(None, 'seq')
- norm_new: float32 [6, 768], P(None, 'seq')
The draws below stay inside these ranges and needn't reach their ends.
Inputs may be any that keep to these rules, and one draw needn't show every extreme that they name: `col_count`: in each group of 2 consecutive proteins one, drawn from the seed, has 256 live columns and 8 live rows. `row_count`: the protein with 256 live columns in each group also has 8 live rows. `attn_weight`: entries scaled per matrix, of order 768 ** -0.5 in the query, key and value matrices. `in_weight`: entries of order 768 ** -0.5. `norm_param`: gains near one, shifts of both signs.
All inputs are finite; a program needn't handle non-finite values.
Results may differ from the reference program's by a relative error of at most 0.019.
Values may be sent and summed in bfloat16 or wider, within the bound.
No kernel may reach another device: no remote copies, remote signals or barrier semaphores. Data moves between devices by JAX's collectives and lax.ppermute only.
A program may use at most 256 MiB of HBM per device.

```python
import math
import jax
import jax.numpy as jnp
from jax import lax

D = 768
H = 12
DH = 64
FF = 3072
COLS = 256
PROT = 2
STEP = 5
ROWS = 8
PROTEINS = 8


def full_slots(key):
    key = jax.random.fold_in(key, 7)
    groups = PROTEINS // PROT
    picked = jax.random.randint(key, (groups,), 0, PROT)
    slots = jnp.arange(PROTEINS, dtype=jnp.int32)
    return slots % PROT == picked[slots // PROT]


def draw_col_count(key, part):
    full = full_slots(key)
    key = jax.random.fold_in(key, 11)
    spread = jax.random.randint(key, (PROTEINS,), COLS // 4, COLS + 1)
    return jnp.where(full, COLS, spread).astype(jnp.int32)


def draw_row_count(key, part):
    full = full_slots(key)
    key = jax.random.fold_in(key, 13)
    spread = jax.random.randint(key, (PROTEINS,), ROWS // 4, ROWS + 1)
    return jnp.where(full, ROWS, spread).astype(jnp.int32)


def draw_attn_weight(key, part):
    key = jax.random.fold_in(key, 17)
    base = jnp.clip(jax.random.normal(key, (8, D, D), jnp.float32), -6.0, 6.0)
    shared_key = jax.random.fold_in(key, 23)
    shared = jnp.clip(jax.random.normal(shared_key, (8, 1, D), jnp.float32), -4.0, 4.0)
    reads_norm = jnp.array([1.0, 1.0, 1.0, 0.0, 1.0, 1.0, 1.0, 0.0], jnp.float32)
    base = base + 0.4 * reads_norm[:, None, None] * shared
    row_gain = math.sqrt(max(COLS / 4.0, 1.0))
    col_gain = math.sqrt(max(ROWS / 4.0, 1.0))
    slot_scale = jnp.array([1.0, 1.0, 1.0, row_gain, 1.0, 1.0, 1.0, col_gain], jnp.float32) / math.sqrt(D)
    return base * slot_scale[:, None, None]


def draw_in_weight(key, part):
    key = jax.random.fold_in(key, 29)
    base = jnp.clip(jax.random.normal(key, (D, FF), jnp.float32), -6.0, 6.0)
    shared_key = jax.random.fold_in(key, 31)
    shared = jnp.clip(jax.random.normal(shared_key, (1, FF), jnp.float32), -4.0, 4.0)
    return (base + 0.4 * shared) / math.sqrt(D)


def draw_norm_param(key, part):
    key = jax.random.fold_in(key, 19)
    noise = jnp.clip(jax.random.normal(key, (6, D), jnp.float32), -4.0, 4.0)
    rising = 0.75 + 0.6 * jnp.arange(D, dtype=jnp.float32) / D
    gains = rising[None, :] * (1.0 + 0.1 * noise)
    shifts = 0.3 * noise
    is_gain = (jnp.arange(6) % 2 == 0)[:, None]
    return jnp.where(is_gain, gains, shifts)


def block_scale(own_key, extent, pieces, least, largest):
    loudness = 1.0
    for position, shards_of in pieces:
        heights = jax.random.uniform(jax.random.fold_in(jax.random.fold_in(own_key, 6), position), (shards_of,), jnp.float32, least / len(pieces), largest / len(pieces))
        loudness = loudness * jnp.repeat(jnp.exp(heights), extent[position] // shards_of).reshape((-1,) + (1,) * (len(extent) - 1 - position))
    return loudness


def normal_values(own_key, shape, deviation, bound, split=(), kind=jnp.bfloat16):
    level = block_scale(own_key, shape, split, -0.22, 0.18) if split else 1.0
    entries = jax.random.normal(own_key, shape, jnp.float32) * deviation * level
    return jnp.minimum(jnp.maximum(entries, -bound), bound).astype(kind)


def setup_inputs(seed: int = 0) -> dict:
    key_of = jax.random.split(jax.random.key(seed), 17)
    tokens = normal_values(key_of[0], (PROTEINS, ROWS, COLS, D), 1.0, 6.0, ((0, 4), (1, 8)))
    cotangent = normal_values(key_of[1], (PROTEINS, ROWS, COLS, D), 1.0, 6.0, ((0, 4), (1, 8)))
    col_count = draw_col_count(jax.random.fold_in(key_of[16], 71), 0)
    row_count = draw_row_count(jax.random.fold_in(key_of[16], 71), 0)
    attn_weight = draw_attn_weight(jax.random.fold_in(key_of[16], 71), 0)
    in_weight = draw_in_weight(jax.random.fold_in(key_of[16], 71), 0)
    out_weight = normal_values(key_of[6], (FF, D), FF ** -0.5, 0.109375, ((1, 8),), jnp.float32)
    norm_param = draw_norm_param(jax.random.fold_in(key_of[16], 71), 0)
    attn_first = normal_values(key_of[8], (8, D, D), ((8 * D * D + 2 * D * FF) ** -0.5), 0.0048828125, ((1, 8),), jnp.float32)
    attn_second = jnp.clip(jnp.exp(math.log(4.238552548940788e-07) - 1.3862944 * jax.random.uniform(key_of[9], (8, D, D), jnp.float32) ** block_scale(key_of[9], (8, D, D), ((1, 8),), -0.2, 0.2)), 1.059638137235197e-07, 4.238552548940788e-07)
    in_first = normal_values(key_of[10], (D, FF), ((8 * D * D + 2 * D * FF) ** -0.5), 0.0048828125, ((0, 8),), jnp.float32)
    in_second = jnp.clip(jnp.exp(math.log(4.238552548940788e-07) - 1.3862944 * jax.random.uniform(key_of[11], (D, FF), jnp.float32) ** block_scale(key_of[11], (D, FF), ((0, 8),), -0.2, 0.2)), 1.059638137235197e-07, 4.238552548940788e-07)
    out_first = normal_values(key_of[12], (FF, D), ((8 * D * D + 2 * D * FF) ** -0.5), 0.0048828125, ((1, 8),), jnp.float32)
    out_second = jnp.clip(jnp.exp(math.log(4.238552548940788e-07) - 1.3862944 * jax.random.uniform(key_of[13], (FF, D), jnp.float32) ** block_scale(key_of[13], (FF, D), ((1, 8),), -0.2, 0.2)), 1.059638137235197e-07, 4.238552548940788e-07)
    norm_first = normal_values(key_of[14], (6, D), (4 * (8 * D * D + 2 * D * FF) ** -0.5), 0.01953125, ((1, 8),), jnp.float32)
    norm_second = jnp.clip(jnp.exp(math.log(6.781684078305261e-06) - 1.3862944 * jax.random.uniform(key_of[15], (6, D), jnp.float32) ** block_scale(key_of[15], (6, D), ((1, 8),), -0.2, 0.2)), 1.6954210195763153e-06, 6.781684078305261e-06)
    return {"tokens": tokens, "cotangent": cotangent, "col_count": col_count, "row_count": row_count, "attn_weight": attn_weight, "in_weight": in_weight, "out_weight": out_weight, "norm_param": norm_param, "attn_first": attn_first, "attn_second": attn_second, "in_first": in_first, "in_second": in_second, "out_first": out_first, "out_second": out_second, "norm_first": norm_first, "norm_second": norm_second}


@jax.custom_vjp
def low(v):
    return lax.optimization_barrier(v.astype(jnp.bfloat16)).astype(jnp.float32)

@jax.custom_vjp
def low_back(v):
    return v

def low_keep(v):
    return (low(v), None)

def low_pass(kept, grad):
    return (grad,)

def back_keep(v):
    return (v, None)

def back_low(kept, grad):
    return (low(grad),)
low.defvjp(low_keep, low_pass)
low_back.defvjp(back_keep, back_low)
precise = lax.Precision.HIGHEST
eps_norm = 1e-05
masked_score = -1000000000.0
clip_bound = 1.0
beta_one = 0.5
beta_two = 0.5
matrix_rate = 0.06
norm_rate = 0.3
decay_rate = 0.01
adam_eps = 1e-08

def layer_norm(value, gain, shift):
    mean = lax.optimization_barrier(jnp.mean(value, axis=-1, keepdims=True))
    centred = value - mean
    spread = lax.optimization_barrier(jnp.mean(centred * centred, axis=-1, keepdims=True))
    return centred * lax.rsqrt(spread + eps_norm) * gain + shift

def project(value, weight):
    return jnp.einsum('rcd,de->rce', value, weight, precision=precise)

def split_heads(value):
    return value.reshape(value.shape[:-1] + (H, DH))

def rounded_heads(value, weight):
    return split_heads(low_back(low(project(value, weight))))

def protein_forward(masters, tokens_in, col_live, row_live, tie_scale):
    attn = low(masters[0])
    w_in = low(masters[1])
    w_out = low(masters[2])
    norms = low(masters[3])
    head_scale = 1.0 / math.sqrt(DH)
    normed_one = low(layer_norm(tokens_in, norms[0], norms[1]))
    query_one = rounded_heads(normed_one, attn[0])
    key_one = rounded_heads(normed_one, attn[1])
    value_one = rounded_heads(normed_one, attn[2])
    scores_one = jnp.einsum('rihe,rjhe->hij', query_one * row_live[:, None, None, None], key_one, precision=precise) * tie_scale
    scores_one = low_back(jnp.where(col_live[None, None, :] > 0, scores_one, masked_score))
    probs_one = low(jax.nn.softmax(scores_one, axis=-1))
    mixed_one = low_back(low(jnp.einsum('hij,rjhe->rihe', probs_one, value_one, precision=precise)))
    mixed_one = mixed_one.reshape(tokens_in.shape)
    stream_one = low(low_back(tokens_in + project(mixed_one, attn[3])))
    normed_two = low(layer_norm(stream_one, norms[2], norms[3]))
    query_two = rounded_heads(normed_two, attn[4])
    key_two = rounded_heads(normed_two, attn[5])
    value_two = rounded_heads(normed_two, attn[6])
    scores_two = jnp.einsum('rche,sche->chrs', query_two, key_two, precision=precise) * head_scale
    scores_two = low_back(jnp.where(row_live[None, None, None, :] > 0, scores_two, masked_score))
    probs_two = low(jax.nn.softmax(scores_two, axis=-1))
    mixed_two = low_back(low(jnp.einsum('chrs,sche->rche', probs_two, value_two, precision=precise)))
    mixed_two = mixed_two.reshape(tokens_in.shape)
    stream_two = stream_one + low_back(project(mixed_two, attn[7]))
    normed_three = low(layer_norm(stream_two, norms[4], norms[5]))
    inner = low_back(jnp.einsum('rcd,df->rcf', normed_three, w_in, precision=precise))
    activ = low(jax.nn.gelu(inner, approximate=True))
    return low(stream_two + jnp.einsum('rcf,fd->rcd', activ, w_out, precision=precise))

def adam_update(weight, first, second, grad, rate):
    first_new = beta_one * first + (1.0 - beta_one) * grad
    second_new = beta_two * second + (1.0 - beta_two) * grad * grad
    first_hat = first_new / (1.0 - beta_one ** STEP)
    second_hat = second_new / (1.0 - beta_two ** STEP)
    weight_new = weight - rate * (first_hat / (jnp.sqrt(second_hat) + adam_eps) + decay_rate * weight)
    return (first_new, second_new, weight_new)

def reference(tokens, cotangent, col_count, row_count, attn_weight, in_weight, out_weight, norm_param, attn_first, attn_second, in_first, in_second, out_first, out_second, norm_first, norm_second):
    masters = (attn_weight, in_weight, out_weight, norm_param)

    def per_protein(totals, inputs):
        tokens_p, cot_p, col_limit, row_limit = inputs
        col_live = (jnp.arange(COLS, dtype=jnp.int32) < col_limit).astype(jnp.float32)
        row_live = (jnp.arange(ROWS, dtype=jnp.int32) < row_limit).astype(jnp.float32)
        tie_scale = 1.0 / (jnp.sqrt(row_limit.astype(jnp.float32)) * math.sqrt(DH))

        def forward(weights, tokens_in):
            return protein_forward(weights, tokens_in, col_live, row_live, tie_scale)
        result, backward = jax.vjp(forward, masters, tokens_p.astype(jnp.float32))
        live = row_live[:, None, None] * col_live[None, :, None]
        grads, grad_in = backward(cot_p.astype(jnp.float32) * live)
        totals = jax.tree.map(jnp.add, totals, grads)
        return (totals, (result.astype(jnp.bfloat16), grad_in))
    zeros = jax.tree.map(jnp.zeros_like, masters)
    totals, (block_out, grad_tokens) = lax.scan(per_protein, zeros, (tokens, cotangent, col_count, row_count))
    attn_grad, in_grad, out_grad, norm_grad = totals
    squares = jnp.sum(attn_grad * attn_grad) + jnp.sum(in_grad * in_grad) + jnp.sum(out_grad * out_grad) + jnp.sum(norm_grad * norm_grad)
    grad_norm = jnp.sqrt(squares)
    factor = clip_bound / jnp.maximum(grad_norm, clip_bound)
    attn_first_new, attn_second_new, attn_weight_new = adam_update(attn_weight, attn_first, attn_second, attn_grad * factor, matrix_rate)
    in_first_new, in_second_new, in_weight_new = adam_update(in_weight, in_first, in_second, in_grad * factor, matrix_rate)
    out_first_new, out_second_new, out_weight_new = adam_update(out_weight, out_first, out_second, out_grad * factor, matrix_rate)
    norm_first_new, norm_second_new, norm_new = adam_update(norm_param, norm_first, norm_second, norm_grad * factor, norm_rate)
    return (block_out, grad_tokens, grad_norm, attn_first_new, attn_second_new, attn_weight_new, attn_weight_new.astype(jnp.bfloat16), in_first_new, in_second_new, in_weight_new, in_weight_new.astype(jnp.bfloat16), out_first_new, out_second_new, out_weight_new, out_weight_new.astype(jnp.bfloat16), norm_first_new, norm_second_new, norm_new)
```

```python
from functools import partial
import math

import jax
import jax.numpy as jnp
from jax import lax
from jax.experimental import pallas as pl
from jax.experimental.pallas import tpu as pltpu
from jax.sharding import Mesh
from jax.sharding import PartitionSpec as P

H = 12
DH = 64
STEP = 5


eps_norm = 1e-05
masked_score = -1000000000.0
clip_bound = 1.0
beta_one = 0.5
beta_two = 0.5
matrix_rate = 0.06
norm_rate = 0.3
decay_rate = 0.01
adam_eps = 1e-08


def in_blocks(x, dim, length):
    lengths = x.shape
    pieces = x.reshape(*lengths[:dim], length, lengths[dim] // length, *lengths[dim + 1 :])
    return jnp.moveaxis(pieces, dim, 0)


def sent_and_summed(x, axis, dim):
    length = lax.axis_size(axis)
    pieces = lax.all_to_all(in_blocks(x, dim, length), axis, 0, 0, tiled=True)
    return jnp.sum(pieces.astype(jnp.float32), axis=0)


def layer_norm(value, gain, shift):
    mean = jnp.mean(value, axis=-1, keepdims=True)
    centred = value - mean
    spread = jnp.mean(centred * centred, axis=-1, keepdims=True)
    return centred * lax.rsqrt(spread + eps_norm) * gain + shift


def softmax_rows(scores, keep):
    scores = jnp.where(keep, scores, masked_score)
    top = jnp.max(scores, axis=-1, keepdims=True)
    expo = jnp.exp(scores - top)
    return expo / jnp.sum(expo, axis=-1, keepdims=True)


def softmax_back(probs, grads):
    return probs * (grads - jnp.sum(probs * grads, axis=-1, keepdims=True))


def adam_update(weight, first, second, grad, rate):
    first_new = beta_one * first + (1.0 - beta_one) * grad
    second_new = beta_two * second + (1.0 - beta_two) * grad * grad
    first_hat = first_new / (1.0 - beta_one**STEP)
    second_hat = second_new / (1.0 - beta_two**STEP)
    weight_new = weight - rate * (
        first_hat / (jnp.sqrt(second_hat) + adam_eps) + decay_rate * weight
    )
    return (first_new, second_new, weight_new)


def attn_pair(normed, grad_proj, mixed, grad_branch):
    width = normed.shape[-1]
    qkv_terms = jnp.einsum("prcd,kprce->dke", normed, grad_proj, preferred_element_type=jnp.float32)
    output_terms = jnp.einsum(
        "prcd,prce->de", mixed, grad_branch, preferred_element_type=jnp.float32
    )
    return jnp.concatenate([qkv_terms, output_terms[:, None, :]], axis=1).reshape(width, 4 * width)


def general_body(
    tokens,
    cotangent,
    col_count,
    row_count,
    attn_weight,
    in_weight,
    out_weight,
    norm_param,
    attn_first,
    attn_second,
    in_first,
    in_second,
    out_first,
    out_second,
    norm_first,
    norm_second,
):
    f32 = jnp.float32
    bf16 = jnp.bfloat16
    prot, rows_dev, cols, width = tokens.shape
    hidden = in_weight.shape[1]
    head_scale = 1.0 / math.sqrt(DH)
    attn_full, in_full, out_full, norm_full = (
        lax.all_gather(attn_weight.astype(bf16), "seq", axis=1, tiled=True),
        lax.all_gather(in_weight.astype(bf16), "seq", axis=0, tiled=True),
        lax.all_gather(out_weight.astype(bf16), "seq", axis=1, tiled=True),
        lax.all_gather(norm_param.astype(bf16), "seq", axis=1, tiled=True),
    )
    norm_gain = norm_full.astype(f32)
    row_ids = lax.axis_index("seq") * rows_dev + jnp.arange(rows_dev, dtype=jnp.int32)
    row_live = (row_ids[None, :] < row_count[:, None]).astype(f32)
    col_live = jnp.arange(cols, dtype=jnp.int32)[None, :] < col_count[:, None]
    tie_scale = lax.rsqrt(row_count.astype(f32)) * head_scale
    live = row_live[:, :, None] * col_live.astype(f32)[:, None, :]
    grad_out = (cotangent.astype(f32) * live[..., None]).astype(bf16)
    resid_one = tokens.astype(f32)
    normed_one = layer_norm(resid_one, norm_gain[0], norm_gain[1]).astype(bf16)
    proj_one = jnp.einsum(
        "prcd,kde->kprce", normed_one, attn_full[0:3], preferred_element_type=f32
    ).astype(bf16)
    proj_one = proj_one.reshape(3, prot, rows_dev, cols, H, DH)
    query_one, key_one, value_one = (proj_one[0], proj_one[1], proj_one[2])
    masked_query = query_one * row_live[:, :, None, None, None].astype(bf16)
    partial_scores = (
        jnp.einsum("prihe,prjhe->phij", masked_query, key_one, preferred_element_type=f32)
        * tie_scale[:, None, None, None]
    )
    keep_cols = col_live[:, None, None, :]
    score_part = lax.psum_scatter(partial_scores, "seq", scatter_dimension=2, tiled=True)
    probs_one = softmax_rows(score_part, keep_cols)
    probs_low = lax.all_gather(probs_one.astype(bf16), "seq", axis=2, tiled=True)
    mixed_one = jnp.einsum(
        "phij,prjhe->prihe", probs_low, value_one, preferred_element_type=f32
    ).astype(bf16)
    mixed_one = mixed_one.reshape(prot, rows_dev, cols, width)
    branch_one = jnp.einsum("prcd,de->prce", mixed_one, attn_full[3], preferred_element_type=f32)
    stream_one = (resid_one + branch_one).astype(bf16)
    stream_cols, up_grad = (
        lax.all_to_all(stream_one, "seq", split_axis=2, concat_axis=1, tiled=True),
        lax.all_to_all(grad_out, "seq", split_axis=2, concat_axis=1, tiled=True),
    )
    rows = stream_cols.shape[1]
    cols_dev = stream_cols.shape[2]
    row_live_all = jnp.arange(rows, dtype=jnp.int32)[None, :] < row_count[:, None]
    resid_two = stream_cols.astype(f32)
    normed_two = layer_norm(resid_two, norm_gain[2], norm_gain[3]).astype(bf16)
    proj_two = jnp.einsum(
        "prcd,kde->kprce", normed_two, attn_full[4:7], preferred_element_type=f32
    ).astype(bf16)
    proj_two = proj_two.reshape(3, prot, rows, cols_dev, H, DH)
    query_two, key_two, value_two = (proj_two[0], proj_two[1], proj_two[2])
    scores_two = (
        jnp.einsum("prche,psche->pchrs", query_two, key_two, preferred_element_type=f32)
        * head_scale
    )
    probs_two = softmax_rows(scores_two, row_live_all[:, None, None, None, :])
    probs_two_low = probs_two.astype(bf16)
    mixed_two = jnp.einsum(
        "pchrs,psche->prche", probs_two_low, value_two, preferred_element_type=f32
    ).astype(bf16)
    mixed_two = mixed_two.reshape(prot, rows, cols_dev, width)
    resid_three = resid_two + jnp.einsum(
        "prcd,de->prce", mixed_two, attn_full[7], preferred_element_type=f32
    )
    normed_three = layer_norm(resid_three, norm_gain[4], norm_gain[5]).astype(bf16)
    inner = jnp.einsum("prcd,df->prcf", normed_three, in_full, preferred_element_type=f32)
    activ = jax.nn.gelu(inner, approximate=True).astype(bf16)
    result = (
        resid_three + jnp.einsum("prcf,fd->prcd", activ, out_full, preferred_element_type=f32)
    ).astype(bf16)
    block_out = lax.all_to_all(result, "seq", split_axis=1, concat_axis=2, tiled=True)
    grad_act = jnp.einsum("prcd,fd->prcf", up_grad, out_full, preferred_element_type=f32)
    _, gelu_back = jax.vjp(partial(jax.nn.gelu, approximate=True), inner)
    grad_inner = gelu_back(grad_act)[0].astype(bf16)
    grad_normed_three = jnp.einsum("prcf,df->prcd", grad_inner, in_full, preferred_element_type=f32)
    _, norm_back_three = jax.vjp(layer_norm, resid_three, norm_gain[4], norm_gain[5])
    part_three, gain_grad_three, shift_grad_three = norm_back_three(grad_normed_three)
    grad_three = up_grad.astype(f32) + part_three
    grad_branch_two = grad_three.astype(bf16)
    grad_mixed_two = jnp.einsum(
        "prce,de->prcd", grad_branch_two, attn_full[7], preferred_element_type=f32
    ).astype(bf16)
    grad_mixed_two = grad_mixed_two.reshape(prot, rows, cols_dev, H, DH)
    grad_probs_two = jnp.einsum(
        "prche,psche->pchrs", grad_mixed_two, value_two, preferred_element_type=f32
    )
    grad_value_two = jnp.einsum(
        "pchrs,prche->psche", probs_two_low, grad_mixed_two, preferred_element_type=f32
    )
    grad_scores_two = softmax_back(probs_two, grad_probs_two).astype(bf16)
    grad_query_two = (
        jnp.einsum("pchrs,psche->prche", grad_scores_two, key_two, preferred_element_type=f32)
        * head_scale
    )
    grad_key_two = (
        jnp.einsum("pchrs,prche->psche", grad_scores_two, query_two, preferred_element_type=f32)
        * head_scale
    )
    grad_proj_two = jnp.stack([grad_query_two, grad_key_two, grad_value_two]).astype(bf16)
    grad_proj_two = grad_proj_two.reshape(3, prot, rows, cols_dev, width)
    grad_normed_two = jnp.einsum(
        "kprce,kde->prcd", grad_proj_two, attn_full[4:7], preferred_element_type=f32
    )
    _, norm_back_two = jax.vjp(layer_norm, resid_two, norm_gain[2], norm_gain[3])
    part_two, gain_grad_two, shift_grad_two = norm_back_two(grad_normed_two)
    grad_stream = (grad_three + part_two).astype(bf16)
    col_attn_terms = attn_pair(normed_two, grad_proj_two, mixed_two, grad_branch_two)
    in_terms = jnp.einsum("prcd,prcf->df", normed_three, grad_inner, preferred_element_type=f32)
    out_terms = jnp.einsum("prcf,prcd->df", activ, up_grad, preferred_element_type=f32)
    grad_rows = lax.all_to_all(grad_stream, "seq", split_axis=1, concat_axis=2, tiled=True)
    grad_mixed_one = jnp.einsum(
        "prce,de->prcd", grad_rows, attn_full[3], preferred_element_type=f32
    ).astype(bf16)
    grad_mixed_one = grad_mixed_one.reshape(prot, rows_dev, cols, H, DH)
    partial_grads = jnp.einsum(
        "prihe,prjhe->phij", grad_mixed_one, value_one, preferred_element_type=f32
    )
    grad_value_one = jnp.einsum(
        "phij,prihe->prjhe", probs_low, grad_mixed_one, preferred_element_type=f32
    )
    grad_part = sent_and_summed(partial_grads.astype(jnp.bfloat16), "seq", 2)
    grad_scores_one = lax.all_gather(
        softmax_back(probs_one, grad_part).astype(bf16), "seq", axis=2, tiled=True
    )
    tie_rows = row_live[:, :, None, None, None] * tie_scale[:, None, None, None, None]
    grad_query_one = (
        jnp.einsum("phij,prjhe->prihe", grad_scores_one, key_one, preferred_element_type=f32)
        * tie_rows
    )
    grad_key_one = (
        jnp.einsum("phij,prihe->prjhe", grad_scores_one, masked_query, preferred_element_type=f32)
        * tie_scale[:, None, None, None, None]
    )
    grad_proj_one = jnp.stack([grad_query_one, grad_key_one, grad_value_one]).astype(bf16)
    grad_proj_one = grad_proj_one.reshape(3, prot, rows_dev, cols, width)
    grad_normed_one = jnp.einsum(
        "kprce,kde->prcd", grad_proj_one, attn_full[0:3], preferred_element_type=f32
    )
    _, norm_back_one = jax.vjp(layer_norm, resid_one, norm_gain[0], norm_gain[1])
    part_one, gain_grad_one, shift_grad_one = norm_back_one(grad_normed_one)
    grad_tokens = grad_rows.astype(f32) + part_one
    norm_stack = jnp.stack(
        [
            gain_grad_one,
            shift_grad_one,
            gain_grad_two,
            shift_grad_two,
            gain_grad_three,
            shift_grad_three,
        ]
    )
    row_attn_terms = attn_pair(normed_one, grad_proj_one, mixed_one, grad_rows)
    owned = lax.psum_scatter(
        jnp.concatenate(
            [row_attn_terms, col_attn_terms, in_terms, out_terms, norm_stack.T], axis=1
        ),
        "seq",
        scatter_dimension=0,
        tiled=True,
    )
    width_dev = owned.shape[0]
    row_part = owned[:, : 4 * width].reshape(width_dev, 4, width)
    col_part = owned[:, 4 * width : 8 * width].reshape(width_dev, 4, width)
    in_part = owned[:, 8 * width : 8 * width + hidden]
    out_part = owned[:, 8 * width + hidden : 8 * width + 2 * hidden].T
    norm_part = owned[:, 8 * width + 2 * hidden :].T
    attn_part = jnp.concatenate([row_part, col_part], axis=1).transpose(1, 0, 2)
    attn_grad, in_grad, out_grad, norm_grad = (
        lax.psum(attn_part.astype(jnp.bfloat16), "grp").astype(jnp.float32),
        lax.psum(in_part.astype(jnp.bfloat16), "grp").astype(jnp.float32),
        lax.psum(out_part.astype(jnp.bfloat16), "grp").astype(jnp.float32),
        lax.psum(norm_part.astype(jnp.bfloat16), "grp").astype(jnp.float32),
    )
    squares = (
        jnp.sum(attn_grad * attn_grad)
        + jnp.sum(in_grad * in_grad)
        + jnp.sum(out_grad * out_grad)
        + jnp.sum(norm_grad * norm_grad)
    )
    grad_norm = jnp.sqrt(lax.psum(squares, "seq"))
    factor = clip_bound / jnp.maximum(grad_norm, clip_bound)
    attn_first_new, attn_second_new, attn_weight_new = adam_update(
        attn_weight, attn_first, attn_second, attn_grad * factor, matrix_rate
    )
    in_first_new, in_second_new, in_weight_new = adam_update(
        in_weight, in_first, in_second, in_grad * factor, matrix_rate
    )
    out_first_new, out_second_new, out_weight_new = adam_update(
        out_weight, out_first, out_second, out_grad * factor, matrix_rate
    )
    norm_first_new, norm_second_new, norm_new = adam_update(
        norm_param, norm_first, norm_second, norm_grad * factor, norm_rate
    )
    return (
        block_out,
        grad_tokens,
        grad_norm,
        attn_first_new,
        attn_second_new,
        attn_weight_new,
        attn_weight_new.astype(bf16),
        in_first_new,
        in_second_new,
        in_weight_new,
        in_weight_new.astype(bf16),
        out_first_new,
        out_second_new,
        out_weight_new,
        out_weight_new.astype(bf16),
        norm_first_new,
        norm_second_new,
        norm_new,
    )


PAIR = [(0, 1), (1, 0)]
TILE = 128


def swap(value, axis):
    return lax.ppermute(value, axis, PAIR)


def pick(value, index, axis):
    return lax.dynamic_index_in_dim(value, index, axis, keepdims=False)


def merge(own, other, place, axis):
    return jnp.where(
        place == 0,
        jnp.stack([own, other], axis=axis),
        jnp.stack([other, own], axis=axis),
    )


def to_columns(value, c):
    prot, _, cols, width = value.shape
    part = cols // 4
    split = value.reshape(prot, 2, 2, part, width)
    got = swap(pick(split, 1 - c, 2), "c")
    both = merge(pick(split, c, 2), got, c, 0)
    both = both.reshape(8, part, width)
    return lax.all_to_all(both, ("z", "x"), 0, 0, tiled=True)


def to_rows(value, c):
    rows, part, width = value.shape
    got = lax.all_to_all(value, ("z", "x"), 0, 0, tiled=True)
    got = got.reshape(2, 2, 2, part, width)
    other = swap(pick(got, 1 - c, 0), "c")
    both = merge(pick(got, c, 0), other, c, 2)
    return both.reshape(2, 1, 4 * part, width)


def gather_pieces(own):
    over_z = [own]
    for i in (1, 2, 3):
        over_z.append(lax.ppermute(own, "z", [(k, k ^ i) for k in range(4)]))
    return over_z, [swap(piece, "x") for piece in over_z]


def place_kernel(plan, outs_at, place_ref, *refs):
    pieces = refs[: len(plan)]
    outs = refs[len(plan) : -1]
    sem = refs[-1]
    copies = []
    for ref, (i, j, k) in zip(pieces, plan):
        z = lax.bitwise_xor(place_ref[0], i)
        x = lax.bitwise_xor(place_ref[1], j)
        c = lax.bitwise_xor(place_ref[2], k)
        shard = z * 2 + x
        for source, target in outs_at(ref, outs, shard, c):
            copies.append(pltpu.make_async_copy(source, target, sem.at[len(copies)]))
    for copy in copies:
        copy.start()
    for copy in copies:
        copy.wait()


def placed_pieces(pieces, plan, outs_at, outs, place, count):
    anywhere = pl.BlockSpec(memory_space=pl.ANY)
    return pl.pallas_call(
        partial(place_kernel, plan, outs_at),
        in_specs=[pl.BlockSpec(memory_space=pltpu.SMEM)] + [anywhere] * len(pieces),
        out_specs=[anywhere] * len(outs),
        out_shape=[jax.ShapeDtypeStruct(shape, jnp.bfloat16) for shape in outs],
        scratch_shapes=[pltpu.SemaphoreType.DMA((count,))],
        cost_estimate=pl.CostEstimate(
            flops=0, transcendentals=0, bytes_accessed=sum(4 * math.prod(s) for s in outs)
        ),
    )(place, *pieces)


def row_attn_at(ref, outs, shard, c):
    depth = outs[0].shape[0] // 8
    at = pl.multiple_of(shard * depth, depth)
    return [
        (ref.at[pl.ds(0, depth)], outs[0].at[pl.ds(at, depth)]),
        (ref.at[pl.ds(depth, 16)], outs[1].at[shard]),
    ]


def halves_at(ref, outs, shard, c):
    depth, half = ref.shape[1], ref.shape[2]
    at = pl.multiple_of(shard * depth, depth)
    moves = []
    slots = [(o, n) for o, out in enumerate(outs) for n in range(out.shape[1] // (2 * half))]
    for k, (o, n) in enumerate(slots):
        lane = pl.multiple_of(c * half + n * 2 * half, TILE)
        moves.append((ref.at[k], outs[o].at[pl.ds(at, depth), pl.ds(lane, half)]))
    return moves


def all_halves(own_half, other_half, place, outs):
    over_z, over_x = gather_pieces(own_half)
    mine = over_z + over_x
    plan = [(i, j, 0) for j in (0, 1) for i in range(4)]
    theirs = [other_half] + [swap(piece, "c") for piece in mine[1:]]
    plan = plan + [(i, j, 1) for (i, j, _) in plan]
    pieces = mine + theirs
    return placed_pieces(
        pieces, plan, halves_at, outs, place, len(pieces) * own_half.shape[0]
    )


def contract(a, b, dims):
    return lax.dot_general(a, b, (dims, ((), ())), preferred_element_type=jnp.float32)


LAST = ((1,), (1,))
FIRST = ((0,), (0,))
PLAIN = ((1,), (0,))


def softmax_of(scores, keep):
    scores = jnp.where(keep, scores, masked_score)
    expo = jnp.exp(scores - jnp.max(scores, axis=-1, keepdims=True))
    return expo / jnp.sum(expo, axis=-1, keepdims=True)


def head_lanes(lanes):
    side = lax.broadcasted_iota(jnp.int32, (1, lanes), 1) % TILE < DH
    return (side, jnp.logical_not(side))


def only(keep, value):
    return jnp.where(keep, value, jnp.zeros_like(value))


def column_keep(info_ref, own_cols, near, part):
    key = lax.broadcasted_iota(jnp.int32, (1, 2 * near), 1)
    far = key >= near
    inner = key % near
    x = jnp.where(far, 1 - info_ref[1], info_ref[1])
    c = jnp.where(inner >= part, 1 - info_ref[2], info_ref[2])
    column = x * near + c * part + inner % part
    return column < info_ref[3]


def row_pair(ref, row):
    blocks, _, part, lanes = ref.shape
    return jnp.concatenate(
        [ref[:, row + n].reshape(blocks * part, lanes) for n in (0, 1)], axis=1
    )


def live_pair(value, row, info_ref):
    lane = lax.broadcasted_iota(jnp.int32, (1, value.shape[1]), 1) // TILE + row
    return only(lane < info_ref[4], value)


def row_fwd_kernel(info_ref, tie_ref, q_ref, k_ref, v_ref, kf_ref, vf_ref, o_ref):
    blocks, rows, part, lanes = q_ref.shape
    near = blocks * part
    sides = head_lanes(2 * lanes)
    keep = column_keep(info_ref, near, near, part)
    tie = tie_ref[0]
    scores = [jnp.zeros((near, 2 * near), jnp.float32) for _ in sides]
    for row in range(0, rows, 2):
        query = live_pair(row_pair(q_ref, row), row, info_ref)
        key = jnp.concatenate([row_pair(k_ref, row), row_pair(kf_ref, row)], axis=0)
        for n, side in enumerate(sides):
            scores[n] = scores[n] + contract(only(side, query), key, LAST)
    probs = [softmax_of(s * tie, keep).astype(jnp.bfloat16) for s in scores]
    for row in range(0, rows, 2):
        value = jnp.concatenate([row_pair(v_ref, row), row_pair(vf_ref, row)], axis=0)
        mixed = jnp.where(
            sides[0], contract(probs[0], value, PLAIN), contract(probs[1], value, PLAIN)
        ).astype(jnp.bfloat16)
        for n in (0, 1):
            o_ref[:, row + n] = mixed[:, n * lanes : (n + 1) * lanes].reshape(blocks, part, lanes)


def row_bwd_kernel(
    info_ref, tie_ref, q_ref, k_ref, v_ref, kf_ref, vf_ref, do_ref,
    dq_ref, dk_ref, dv_ref, dkf_ref, dvf_ref,
):
    bf16 = jnp.bfloat16
    blocks, rows, part, lanes = q_ref.shape
    near = blocks * part
    sides = head_lanes(2 * lanes)
    keep = column_keep(info_ref, near, near, part)
    tie = tie_ref[0]
    scores = [jnp.zeros((near, 2 * near), jnp.float32) for _ in sides]
    grads = [jnp.zeros((near, 2 * near), jnp.float32) for _ in sides]
    for row in range(0, rows, 2):
        query = live_pair(row_pair(q_ref, row), row, info_ref)
        key = jnp.concatenate([row_pair(k_ref, row), row_pair(kf_ref, row)], axis=0)
        value = jnp.concatenate([row_pair(v_ref, row), row_pair(vf_ref, row)], axis=0)
        out = row_pair(do_ref, row)
        for n, side in enumerate(sides):
            scores[n] = scores[n] + contract(only(side, query), key, LAST)
            grads[n] = grads[n] + contract(only(side, out), value, LAST)
    probs = [softmax_of(s * tie, keep) for s in scores]
    lows = [p.astype(bf16) for p in probs]
    deltas = [softmax_back(p, g).astype(bf16) for p, g in zip(probs, grads)]
    for row in range(0, rows, 2):
        query = live_pair(row_pair(q_ref, row), row, info_ref)
        key = jnp.concatenate([row_pair(k_ref, row), row_pair(kf_ref, row)], axis=0)
        out = row_pair(do_ref, row)
        dq = [contract(d, key, PLAIN) for d in deltas]
        dk = [contract(d, query, FIRST) for d in deltas]
        dv = [contract(p, out, FIRST) for p in lows]
        dq = live_pair(jnp.where(sides[0], dq[0], dq[1]) * tie, row, info_ref).astype(bf16)
        dk = (jnp.where(sides[0], dk[0], dk[1]) * tie).astype(bf16)
        dv = jnp.where(sides[0], dv[0], dv[1]).astype(bf16)
        for n in (0, 1):
            at = slice(n * lanes, (n + 1) * lanes)
            dq_ref[:, row + n] = dq[:, at].reshape(blocks, part, lanes)
            dk_ref[:, row + n] = dk[:near, at].reshape(blocks, part, lanes)
            dv_ref[:, row + n] = dv[:near, at].reshape(blocks, part, lanes)
            dkf_ref[:, row + n] = dk[near:, at].reshape(blocks, part, lanes)
            dvf_ref[:, row + n] = dv[near:, at].reshape(blocks, part, lanes)


def lane_block(shape, first):
    blocks, rows, part, _ = shape
    return pl.BlockSpec((blocks, rows, part, TILE), lambda t: (0, 0, 0, first + t))


def row_attention(info, tie, near, far):
    blocks, rows, part, lanes = near.shape
    tiles = lanes // 3 // TILE
    shape = near.shape
    small = pl.BlockSpec(memory_space=pltpu.SMEM)
    return pl.pallas_call(
        row_fwd_kernel,
        grid=(tiles,),
        in_specs=[small, small]
        + [lane_block(shape, n * tiles) for n in range(3)]
        + [lane_block(shape, n * tiles) for n in range(2)],
        out_specs=lane_block(shape, 0),
        out_shape=jax.ShapeDtypeStruct((blocks, rows, part, lanes // 3), jnp.bfloat16),
        compiler_params=pltpu.CompilerParams(vmem_limit_bytes=32 * 2**20),
    )(info, tie, near, near, near, far, far)


def row_attention_back(info, tie, near, far, grad):
    blocks, rows, part, lanes = near.shape
    tiles = lanes // 3 // TILE
    shape = near.shape
    small = pl.BlockSpec(memory_space=pltpu.SMEM)
    result = jax.ShapeDtypeStruct((blocks, rows, part, lanes // 3), jnp.bfloat16)
    return pl.pallas_call(
        row_bwd_kernel,
        grid=(tiles,),
        in_specs=[small, small]
        + [lane_block(shape, n * tiles) for n in range(3)]
        + [lane_block(shape, n * tiles) for n in range(2)]
        + [lane_block(shape, 0)],
        out_specs=[lane_block(shape, 0)] * 5,
        out_shape=[result] * 5,
        compiler_params=pltpu.CompilerParams(vmem_limit_bytes=32 * 2**20),
    )(info, tie, near, near, near, far, far, grad)


def column_masks(info_ref, rows, part):
    tokens = rows * part
    first = lax.broadcasted_iota(jnp.int32, (tokens, tokens), 0)
    second = lax.broadcasted_iota(jnp.int32, (tokens, tokens), 1)
    same = first % part == second % part
    return jnp.logical_and(same, second // part < info_ref[4])


def col_fwd_kernel(info_ref, qkv_ref, o_ref):
    rows, part, lanes = qkv_ref.shape
    width = lanes // 3
    qkv = qkv_ref[...].reshape(rows * part, lanes)
    keep = column_masks(info_ref, rows, part)
    sides = head_lanes(TILE)
    scale = 1.0 / math.sqrt(DH)
    for at in range(0, width, TILE):
        query = qkv[:, at : at + TILE]
        key = qkv[:, width + at : width + at + TILE]
        value = qkv[:, 2 * width + at : 2 * width + at + TILE]
        mixed = []
        for side in sides:
            probs = softmax_of(contract(only(side, query), key, LAST) * scale, keep)
            mixed.append(contract(probs.astype(jnp.bfloat16), value, PLAIN))
        mixed = jnp.where(sides[0], mixed[0], mixed[1]).astype(jnp.bfloat16)
        o_ref[:, :, at : at + TILE] = mixed.reshape(rows, part, TILE)


def col_bwd_kernel(info_ref, qkv_ref, do_ref, d_ref):
    bf16 = jnp.bfloat16
    rows, part, lanes = qkv_ref.shape
    width = lanes // 3
    qkv = qkv_ref[...].reshape(rows * part, lanes)
    out_grad = do_ref[...].reshape(rows * part, width)
    keep = column_masks(info_ref, rows, part)
    sides = head_lanes(TILE)
    scale = 1.0 / math.sqrt(DH)
    for at in range(0, width, TILE):
        query = qkv[:, at : at + TILE]
        key = qkv[:, width + at : width + at + TILE]
        value = qkv[:, 2 * width + at : 2 * width + at + TILE]
        out = out_grad[:, at : at + TILE]
        found = []
        for side in sides:
            probs = softmax_of(contract(only(side, query), key, LAST) * scale, keep)
            grads = contract(only(side, out), value, LAST)
            delta = softmax_back(probs, grads).astype(bf16)
            found.append(
                (
                    contract(delta, key, PLAIN) * scale,
                    contract(delta, query, FIRST) * scale,
                    contract(probs.astype(bf16), out, FIRST),
                )
            )
        for n in range(3):
            both = jnp.where(sides[0], found[0][n], found[1][n]).astype(bf16)
            first = n * width + at
            d_ref[:, :, first : first + TILE] = both.reshape(rows, part, TILE)


def column_block(rows, part, lanes):
    return pl.BlockSpec((rows, part, lanes), lambda b: (0, b, 0))


def column_attention(info, qkv, part=16):
    rows, cols, lanes = qkv.shape
    return pl.pallas_call(
        col_fwd_kernel,
        grid=(cols // part,),
        in_specs=[pl.BlockSpec(memory_space=pltpu.SMEM), column_block(rows, part, lanes)],
        out_specs=column_block(rows, part, lanes // 3),
        out_shape=jax.ShapeDtypeStruct((rows, cols, lanes // 3), jnp.bfloat16),
        compiler_params=pltpu.CompilerParams(vmem_limit_bytes=32 * 2**20),
    )(info, qkv)


def column_attention_back(info, qkv, grad, part=16):
    rows, cols, lanes = qkv.shape
    return pl.pallas_call(
        col_bwd_kernel,
        grid=(cols // part,),
        in_specs=[
            pl.BlockSpec(memory_space=pltpu.SMEM),
            column_block(rows, part, lanes),
            column_block(rows, part, lanes // 3),
        ],
        out_specs=column_block(rows, part, lanes),
        out_shape=jax.ShapeDtypeStruct((rows, cols, lanes), jnp.bfloat16),
        compiler_params=pltpu.CompilerParams(vmem_limit_bytes=32 * 2**20),
    )(info, qkv, grad)


def summed_to_owner(terms, x):
    bf16 = jnp.bfloat16
    f32 = jnp.float32
    depth = terms.shape[0] // 8
    blocks = terms.reshape(4, 2, depth, *terms.shape[1:])
    got = swap(pick(blocks, 1 - x, 1), "x")
    column = (pick(blocks, x, 1).astype(f32) + got.astype(f32)).astype(bf16)
    parts = lax.all_to_all(column, "z", 0, 0, tiled=True)
    shard = jnp.sum(parts.astype(f32), axis=0).astype(bf16)
    return (shard.astype(f32) + swap(shard, "y").astype(f32)).astype(bf16)


def paired_body(
    tokens,
    cotangent,
    col_count,
    row_count,
    attn_weight,
    in_weight,
    out_weight,
    norm_param,
    attn_first,
    attn_second,
    in_first,
    in_second,
    out_first,
    out_second,
    norm_first,
    norm_second,
):
    f32 = jnp.float32
    bf16 = jnp.bfloat16
    z, x, c = (lax.axis_index(name) for name in ("z", "x", "c"))
    width = tokens.shape[-1]
    hidden = in_weight.shape[1]
    depth = in_weight.shape[0]
    half = width // 2
    hidden_half = hidden // 2

    counts = jnp.stack([col_count, row_count])
    other_counts = swap(counts, "c")
    mine = jnp.where(z // 2 == c, counts, other_counts)
    mine = pick(mine, z % 2, 1)
    cols_live, rows_live = mine[0], mine[1]
    place = jnp.stack([z, x, c]).astype(jnp.int32)
    info = jnp.concatenate([place, mine])
    tie = (lax.rsqrt(rows_live.astype(f32)) * (1.0 / math.sqrt(DH))).reshape(1)

    attn_low = attn_weight.astype(bf16)
    halves = attn_low.reshape(8, depth, 2, half)
    qkv_half = jnp.moveaxis(pick(halves[:3], c, 2), 0, 1).reshape(depth, 3 * half)
    norm_row = jnp.pad(
        norm_param.astype(bf16).reshape(1, 6 * depth), ((0, 15), (0, 3 * half - 6 * depth))
    )
    over_z, over_x = gather_pieces(jnp.concatenate([qkv_half, norm_row]))
    plan = [(i, j, 0) for j in (0, 1) for i in range(4)]
    w_row, norm_rows = placed_pieces(
        over_z + over_x,
        plan,
        row_attn_at,
        [(width, 3 * half), (8, 16, 3 * half)],
        place,
        16,
    )
    norm_gain = norm_rows[:, 0, : 6 * depth].reshape(8, 6, depth)
    norm_gain = jnp.moveaxis(norm_gain, 0, 1).reshape(6, width).astype(f32)
    w_three, w_col, w_seven = all_halves(
        pick(halves[3:], c, 2),
        pick(halves[3:], 1 - c, 2),
        place,
        [(width, width), (width, 3 * width), (width, width)],
    )
    ffn_low = jnp.stack([in_weight.astype(bf16), out_weight.astype(bf16).T])
    ffn_halves = ffn_low.reshape(2, depth, 2, hidden_half)
    w_in, w_out = all_halves(
        pick(ffn_halves, c, 2),
        pick(ffn_halves, 1 - c, 2),
        place,
        [(width, hidden), (width, hidden)],
    )

    stream_zero = to_columns(tokens, c)
    rows, part, _ = stream_zero.shape
    count = rows * part
    resid_one = stream_zero.reshape(count, width).astype(f32)
    normed_one = layer_norm(resid_one, norm_gain[0], norm_gain[1]).astype(bf16)
    near_normed = jnp.concatenate([normed_one, swap(normed_one, "c")])
    far_first = swap(normed_one, "x")
    far_normed = jnp.concatenate([far_first, swap(far_first, "c")])
    near = contract(near_normed, w_row, PLAIN).astype(bf16).reshape(2, rows, part, 3 * half)
    far = contract(far_normed, w_row[:, half:], PLAIN).astype(bf16)
    far = far.reshape(2, rows, part, 2 * half)
    mixed_heads = row_attention(info, tie, near, far)
    mixed_one = merge(mixed_heads[0], swap(mixed_heads[1], "c"), c, 2).reshape(count, width)
    stream_one = (resid_one + contract(mixed_one, w_three, PLAIN)).astype(bf16)

    resid_two = stream_one.astype(f32)
    normed_two = layer_norm(resid_two, norm_gain[2], norm_gain[3]).astype(bf16)
    qkv_two = contract(normed_two, w_col, PLAIN).astype(bf16).reshape(rows, part, 3 * width)
    mixed_two = column_attention(info, qkv_two).reshape(count, width)
    resid_three = resid_two + contract(mixed_two, w_seven, PLAIN)

    normed_three = layer_norm(resid_three, norm_gain[4], norm_gain[5]).astype(bf16)
    inner = contract(normed_three, w_in, PLAIN)
    activ = jax.nn.gelu(inner, approximate=True).astype(bf16)
    result = (resid_three + contract(activ, w_out, LAST)).astype(bf16)
    block_out = to_rows(result.reshape(rows, part, width), c)

    up = to_columns(cotangent, c)
    column = x * (2 * part) + c * part + jnp.arange(part, dtype=jnp.int32)
    live = jnp.logical_and(
        (jnp.arange(rows, dtype=jnp.int32) < rows_live)[:, None], (column < cols_live)[None, :]
    )
    up = jnp.where(live[..., None], up, jnp.zeros_like(up)).reshape(count, width)
    grad_act = contract(up, w_out, PLAIN)
    _, gelu_back = jax.vjp(partial(jax.nn.gelu, approximate=True), inner)
    grad_inner = gelu_back(grad_act)[0].astype(bf16)

    def lanes_of(value, which, groups):
        split = value.reshape(value.shape[0], groups, 2, value.shape[1] // (2 * groups))
        return pick(split, which, 2).reshape(value.shape[0], value.shape[1] // 2)

    def over_cores(sides):
        sent = [contract(a, lanes_of(b, 1 - c, g), FIRST).astype(bf16) for a, b, g in sides]
        got = [swap(value, "c") for value in sent]
        kept = [contract(a, lanes_of(b, c, g), FIRST) for a, b, g in sides]
        return [(k + v.astype(f32)).astype(bf16) for k, v in zip(kept, got)]

    ffn_terms = over_cores([(normed_three, grad_inner, 1), (up, activ, 1)])
    ffn_grad = summed_to_owner(jnp.stack(ffn_terms, axis=1), x)
    grad_normed_three = contract(grad_inner, w_in, LAST)
    _, norm_back_three = jax.vjp(layer_norm, resid_three, norm_gain[4], norm_gain[5])
    part_three, gain_grad_three, shift_grad_three = norm_back_three(grad_normed_three)
    grad_three = up.astype(f32) + part_three

    grad_branch_two = grad_three.astype(bf16)
    grad_mixed_two = contract(grad_branch_two, w_seven, LAST).astype(bf16)
    grad_qkv_two = column_attention_back(
        info, qkv_two, grad_mixed_two.reshape(rows, part, width)
    ).reshape(count, 3 * width)
    grad_normed_two = contract(grad_qkv_two, w_col, LAST)
    _, norm_back_two = jax.vjp(layer_norm, resid_two, norm_gain[2], norm_gain[3])
    part_two, gain_grad_two, shift_grad_two = norm_back_two(grad_normed_two)
    grad_stream = (grad_three + part_two).astype(bf16)

    grad_mixed_one = contract(grad_stream, w_three, LAST).astype(bf16)
    split = grad_mixed_one.reshape(rows, part, 2, half)
    grad_heads = jnp.stack([pick(split, c, 2), swap(pick(split, 1 - c, 2), "c")])
    dq, dk, dv, dk_far, dv_far = row_attention_back(info, tie, near, far, grad_heads)
    grad_near = jnp.concatenate([dq, dk, dv], axis=-1).reshape(2 * count, 3 * half)
    grad_far = jnp.concatenate([dk_far, dv_far], axis=-1).reshape(2 * count, 2 * half)
    far_part = contract(grad_far, w_row[:, half:], LAST).reshape(2, count, width)
    far_sum = far_part[0] + swap(far_part[1].astype(bf16), "c").astype(f32)
    far_got = swap(far_sum.astype(bf16), "x")
    near_part = contract(grad_near, w_row, LAST).reshape(2, count, width)
    near_got = swap(near_part[1].astype(bf16), "c")
    grad_normed_one = near_part[0] + near_got.astype(f32) + far_got.astype(f32)
    _, norm_back_one = jax.vjp(layer_norm, resid_one, norm_gain[0], norm_gain[1])
    part_one, gain_grad_one, shift_grad_one = norm_back_one(grad_normed_one)
    grad_input = (grad_stream.astype(f32) + part_one).astype(bf16)
    grad_tokens = to_rows(grad_input.reshape(rows, part, width), c).astype(f32)

    attn_terms = over_cores(
        [
            (mixed_one, grad_stream, 1),
            (normed_two, grad_qkv_two, 3),
            (mixed_two, grad_branch_two, 1),
        ]
    )
    attn_grad_b = summed_to_owner(jnp.concatenate(attn_terms, axis=1), x)
    row_terms = contract(near_normed, grad_near, FIRST)
    far_terms = contract(far_normed, grad_far, FIRST)
    row_terms = jnp.concatenate([row_terms[:, :half], row_terms[:, half:] + far_terms], axis=1)
    norm_stack = jnp.stack(
        [
            gain_grad_one,
            shift_grad_one,
            gain_grad_two,
            shift_grad_two,
            gain_grad_three,
            shift_grad_three,
        ]
    )
    norm_terms = jnp.moveaxis(norm_stack.reshape(6, 8, depth), 0, 1).reshape(8, 1, 6 * depth)
    norm_terms = jnp.pad(norm_terms, ((0, 0), (0, 15), (0, 3 * half - 6 * depth)))
    row_terms = jnp.concatenate(
        [row_terms.reshape(8, depth, 3 * half), norm_terms], axis=1
    ).astype(bf16)
    row_grad = summed_to_owner(row_terms.reshape(8 * (depth + 16), 3 * half), x)

    row_other = swap(row_grad, "c")
    attn_other = swap(attn_grad_b, "c")
    ffn_other = swap(ffn_grad, "c")
    norm_grad = row_grad[depth, : 6 * depth].astype(f32) + row_other[depth, : 6 * depth].astype(f32)
    norm_grad = norm_grad.reshape(6, depth)
    row_parts = [
        merge(a.reshape(depth, 3, half), b.reshape(depth, 3, half), c, 2)
        for a, b in [(row_grad[:depth], row_other[:depth])]
    ][0].reshape(depth, 3, width)
    col_parts = merge(
        attn_grad_b.reshape(depth, 5, half), attn_other.reshape(depth, 5, half), c, 2
    ).reshape(depth, 5, width)
    attn_grad = jnp.moveaxis(jnp.concatenate([row_parts, col_parts], axis=1), 1, 0).astype(f32)
    ffn_parts = merge(ffn_grad, ffn_other, c, 2).reshape(depth, 2, hidden).astype(f32)
    in_grad = ffn_parts[:, 0]
    out_grad = ffn_parts[:, 1].T

    squares = (
        jnp.sum(attn_grad * attn_grad)
        + jnp.sum(in_grad * in_grad)
        + jnp.sum(out_grad * out_grad)
        + jnp.sum(norm_grad * norm_grad)
    )
    grad_norm = jnp.sqrt(lax.psum(squares, ("z", "x")))
    factor = clip_bound / jnp.maximum(grad_norm, clip_bound)
    attn_first_new, attn_second_new, attn_weight_new = adam_update(
        attn_weight, attn_first, attn_second, attn_grad * factor, matrix_rate
    )
    in_first_new, in_second_new, in_weight_new = adam_update(
        in_weight, in_first, in_second, in_grad * factor, matrix_rate
    )
    out_first_new, out_second_new, out_weight_new = adam_update(
        out_weight, out_first, out_second, out_grad * factor, matrix_rate
    )
    norm_first_new, norm_second_new, norm_new = adam_update(
        norm_param, norm_first, norm_second, norm_grad * factor, norm_rate
    )
    return (
        block_out,
        grad_tokens,
        grad_norm,
        attn_first_new,
        attn_second_new,
        attn_weight_new,
        attn_weight_new.astype(bf16),
        in_first_new,
        in_second_new,
        in_weight_new,
        in_weight_new.astype(bf16),
        out_first_new,
        out_second_new,
        out_weight_new,
        out_weight_new.astype(bf16),
        norm_first_new,
        norm_second_new,
        norm_new,
    )


def paired_layout(mesh):
    return dict(mesh.shape) == {"seq": 8, "grp": 4}


def mapped(run, mesh, seq, grp):
    placed = (
        P(grp, seq, None, None),
        P(grp, seq, None, None),
        P(grp),
        P(grp),
        P(None, seq, None),
        P(seq, None),
        P(None, seq),
        P(None, seq),
        P(None, seq, None),
        P(None, seq, None),
        P(seq, None),
        P(seq, None),
        P(None, seq),
        P(None, seq),
        P(None, seq),
        P(None, seq),
    )
    return jax.shard_map(
        run,
        mesh=mesh,
        in_specs=placed,
        out_specs=(
            P(grp, seq, None, None),
            P(grp, seq, None, None),
            P(),
            P(None, seq, None),
            P(None, seq, None),
            P(None, seq, None),
            P(None, seq, None),
            P(seq, None),
            P(seq, None),
            P(seq, None),
            P(seq, None),
            P(None, seq),
            P(None, seq),
            P(None, seq),
            P(None, seq),
            P(None, seq),
            P(None, seq),
            P(None, seq),
        ),
        check_vma=False,
    )


def solution(mesh):
    if not paired_layout(mesh):
        return mapped(general_body, mesh, "seq", "grp")
    fine = Mesh(mesh.devices.reshape(4, 2, 2, 2), ("z", "x", "y", "c"))
    return mapped(paired_body, fine, ("z", "x"), ("y", "c"))
```

```python
from functools import partial
import math

import jax
import jax.numpy as jnp
from jax import lax
from jax.experimental import pallas as pl
from jax.experimental.pallas import tpu as pltpu
from jax.sharding import Mesh
from jax.sharding import PartitionSpec as P

H = 12
DH = 64
STEP = 5


eps_norm = 1e-05
masked_score = -1000000000.0
clip_bound = 1.0
beta_one = 0.5
beta_two = 0.5
matrix_rate = 0.06
norm_rate = 0.3
decay_rate = 0.01
adam_eps = 1e-08


def in_blocks(x, dim, length):
    lengths = x.shape
    pieces = x.reshape(*lengths[:dim], length, lengths[dim] // length, *lengths[dim + 1 :])
    return jnp.moveaxis(pieces, dim, 0)


def sent_and_summed(x, axis, dim):
    length = lax.axis_size(axis)
    pieces = lax.all_to_all(in_blocks(x, dim, length), axis, 0, 0, tiled=True)
    return jnp.sum(pieces.astype(jnp.float32), axis=0)


def layer_norm(value, gain, shift):
    mean = jnp.mean(value, axis=-1, keepdims=True)
    centred = value - mean
    spread = jnp.mean(centred * centred, axis=-1, keepdims=True)
    return centred * lax.rsqrt(spread + eps_norm) * gain + shift


def softmax_rows(scores, keep):
    scores = jnp.where(keep, scores, masked_score)
    top = jnp.max(scores, axis=-1, keepdims=True)
    expo = jnp.exp(scores - top)
    return expo / jnp.sum(expo, axis=-1, keepdims=True)


def softmax_back(probs, grads):
    return probs * (grads - jnp.sum(probs * grads, axis=-1, keepdims=True))


def adam_update(weight, first, second, grad, rate):
    first_new = beta_one * first + (1.0 - beta_one) * grad
    second_new = beta_two * second + (1.0 - beta_two) * grad * grad
    first_hat = first_new / (1.0 - beta_one**STEP)
    second_hat = second_new / (1.0 - beta_two**STEP)
    weight_new = weight - rate * (
        first_hat / (jnp.sqrt(second_hat) + adam_eps) + decay_rate * weight
    )
    return (first_new, second_new, weight_new)


def attn_pair(normed, grad_proj, mixed, grad_branch):
    width = normed.shape[-1]
    qkv_terms = jnp.einsum("prcd,kprce->dke", normed, grad_proj, preferred_element_type=jnp.float32)
    output_terms = jnp.einsum(
        "prcd,prce->de", mixed, grad_branch, preferred_element_type=jnp.float32
    )
    return jnp.concatenate([qkv_terms, output_terms[:, None, :]], axis=1).reshape(width, 4 * width)


def general_body(
    tokens,
    cotangent,
    col_count,
    row_count,
    attn_weight,
    in_weight,
    out_weight,
    norm_param,
    attn_first,
    attn_second,
    in_first,
    in_second,
    out_first,
    out_second,
    norm_first,
    norm_second,
):
    f32 = jnp.float32
    bf16 = jnp.bfloat16
    prot, rows_dev, cols, width = tokens.shape
    hidden = in_weight.shape[1]
    head_scale = 1.0 / math.sqrt(DH)
    attn_full, in_full, out_full, norm_full = (
        lax.all_gather(attn_weight.astype(bf16), "seq", axis=1, tiled=True),
        lax.all_gather(in_weight.astype(bf16), "seq", axis=0, tiled=True),
        lax.all_gather(out_weight.astype(bf16), "seq", axis=1, tiled=True),
        lax.all_gather(norm_param.astype(bf16), "seq", axis=1, tiled=True),
    )
    norm_gain = norm_full.astype(f32)
    row_ids = lax.axis_index("seq") * rows_dev + jnp.arange(rows_dev, dtype=jnp.int32)
    row_live = (row_ids[None, :] < row_count[:, None]).astype(f32)
    col_live = jnp.arange(cols, dtype=jnp.int32)[None, :] < col_count[:, None]
    tie_scale = lax.rsqrt(row_count.astype(f32)) * head_scale
    live = row_live[:, :, None] * col_live.astype(f32)[:, None, :]
    grad_out = (cotangent.astype(f32) * live[..., None]).astype(bf16)
    resid_one = tokens.astype(f32)
    normed_one = layer_norm(resid_one, norm_gain[0], norm_gain[1]).astype(bf16)
    proj_one = jnp.einsum(
        "prcd,kde->kprce", normed_one, attn_full[0:3], preferred_element_type=f32
    ).astype(bf16)
    proj_one = proj_one.reshape(3, prot, rows_dev, cols, H, DH)
    query_one, key_one, value_one = (proj_one[0], proj_one[1], proj_one[2])
    masked_query = query_one * row_live[:, :, None, None, None].astype(bf16)
    partial_scores = (
        jnp.einsum("prihe,prjhe->phij", masked_query, key_one, preferred_element_type=f32)
        * tie_scale[:, None, None, None]
    )
    keep_cols = col_live[:, None, None, :]
    score_part = lax.psum_scatter(partial_scores, "seq", scatter_dimension=2, tiled=True)
    probs_one = softmax_rows(score_part, keep_cols)
    probs_low = lax.all_gather(probs_one.astype(bf16), "seq", axis=2, tiled=True)
    mixed_one = jnp.einsum(
        "phij,prjhe->prihe", probs_low, value_one, preferred_element_type=f32
    ).astype(bf16)
    mixed_one = mixed_one.reshape(prot, rows_dev, cols, width)
    branch_one = jnp.einsum("prcd,de->prce", mixed_one, attn_full[3], preferred_element_type=f32)
    stream_one = (resid_one + branch_one).astype(bf16)
    stream_cols, up_grad = (
        lax.all_to_all(stream_one, "seq", split_axis=2, concat_axis=1, tiled=True),
        lax.all_to_all(grad_out, "seq", split_axis=2, concat_axis=1, tiled=True),
    )
    rows = stream_cols.shape[1]
    cols_dev = stream_cols.shape[2]
    row_live_all = jnp.arange(rows, dtype=jnp.int32)[None, :] < row_count[:, None]
    resid_two = stream_cols.astype(f32)
    normed_two = layer_norm(resid_two, norm_gain[2], norm_gain[3]).astype(bf16)
    proj_two = jnp.einsum(
        "prcd,kde->kprce", normed_two, attn_full[4:7], preferred_element_type=f32
    ).astype(bf16)
    proj_two = proj_two.reshape(3, prot, rows, cols_dev, H, DH)
    query_two, key_two, value_two = (proj_two[0], proj_two[1], proj_two[2])
    scores_two = (
        jnp.einsum("prche,psche->pchrs", query_two, key_two, preferred_element_type=f32)
        * head_scale
    )
    probs_two = softmax_rows(scores_two, row_live_all[:, None, None, None, :])
    probs_two_low = probs_two.astype(bf16)
    mixed_two = jnp.einsum(
        "pchrs,psche->prche", probs_two_low, value_two, preferred_element_type=f32
    ).astype(bf16)
    mixed_two = mixed_two.reshape(prot, rows, cols_dev, width)
    resid_three = resid_two + jnp.einsum(
        "prcd,de->prce", mixed_two, attn_full[7], preferred_element_type=f32
    )
    normed_three = layer_norm(resid_three, norm_gain[4], norm_gain[5]).astype(bf16)
    inner = jnp.einsum("prcd,df->prcf", normed_three, in_full, preferred_element_type=f32)
    activ = jax.nn.gelu(inner, approximate=True).astype(bf16)
    result = (
        resid_three + jnp.einsum("prcf,fd->prcd", activ, out_full, preferred_element_type=f32)
    ).astype(bf16)
    block_out = lax.all_to_all(result, "seq", split_axis=1, concat_axis=2, tiled=True)
    grad_act = jnp.einsum("prcd,fd->prcf", up_grad, out_full, preferred_element_type=f32)
    _, gelu_back = jax.vjp(partial(jax.nn.gelu, approximate=True), inner)
    grad_inner = gelu_back(grad_act)[0].astype(bf16)
    grad_normed_three = jnp.einsum("prcf,df->prcd", grad_inner, in_full, preferred_element_type=f32)
    _, norm_back_three = jax.vjp(layer_norm, resid_three, norm_gain[4], norm_gain[5])
    part_three, gain_grad_three, shift_grad_three = norm_back_three(grad_normed_three)
    grad_three = up_grad.astype(f32) + part_three
    grad_branch_two = grad_three.astype(bf16)
    grad_mixed_two = jnp.einsum(
        "prce,de->prcd", grad_branch_two, attn_full[7], preferred_element_type=f32
    ).astype(bf16)
    grad_mixed_two = grad_mixed_two.reshape(prot, rows, cols_dev, H, DH)
    grad_probs_two = jnp.einsum(
        "prche,psche->pchrs", grad_mixed_two, value_two, preferred_element_type=f32
    )
    grad_value_two = jnp.einsum(
        "pchrs,prche->psche", probs_two_low, grad_mixed_two, preferred_element_type=f32
    )
    grad_scores_two = softmax_back(probs_two, grad_probs_two).astype(bf16)
    grad_query_two = (
        jnp.einsum("pchrs,psche->prche", grad_scores_two, key_two, preferred_element_type=f32)
        * head_scale
    )
    grad_key_two = (
        jnp.einsum("pchrs,prche->psche", grad_scores_two, query_two, preferred_element_type=f32)
        * head_scale
    )
    grad_proj_two = jnp.stack([grad_query_two, grad_key_two, grad_value_two]).astype(bf16)
    grad_proj_two = grad_proj_two.reshape(3, prot, rows, cols_dev, width)
    grad_normed_two = jnp.einsum(
        "kprce,kde->prcd", grad_proj_two, attn_full[4:7], preferred_element_type=f32
    )
    _, norm_back_two = jax.vjp(layer_norm, resid_two, norm_gain[2], norm_gain[3])
    part_two, gain_grad_two, shift_grad_two = norm_back_two(grad_normed_two)
    grad_stream = (grad_three + part_two).astype(bf16)
    col_attn_terms = attn_pair(normed_two, grad_proj_two, mixed_two, grad_branch_two)
    in_terms = jnp.einsum("prcd,prcf->df", normed_three, grad_inner, preferred_element_type=f32)
    out_terms = jnp.einsum("prcf,prcd->df", activ, up_grad, preferred_element_type=f32)
    grad_rows = lax.all_to_all(grad_stream, "seq", split_axis=1, concat_axis=2, tiled=True)
    grad_mixed_one = jnp.einsum(
        "prce,de->prcd", grad_rows, attn_full[3], preferred_element_type=f32
    ).astype(bf16)
    grad_mixed_one = grad_mixed_one.reshape(prot, rows_dev, cols, H, DH)
    partial_grads = jnp.einsum(
        "prihe,prjhe->phij", grad_mixed_one, value_one, preferred_element_type=f32
    )
    grad_value_one = jnp.einsum(
        "phij,prihe->prjhe", probs_low, grad_mixed_one, preferred_element_type=f32
    )
    grad_part = sent_and_summed(partial_grads.astype(jnp.bfloat16), "seq", 2)
    grad_scores_one = lax.all_gather(
        softmax_back(probs_one, grad_part).astype(bf16), "seq", axis=2, tiled=True
    )
    tie_rows = row_live[:, :, None, None, None] * tie_scale[:, None, None, None, None]
    grad_query_one = (
        jnp.einsum("phij,prjhe->prihe", grad_scores_one, key_one, preferred_element_type=f32)
        * tie_rows
    )
    grad_key_one = (
        jnp.einsum("phij,prihe->prjhe", grad_scores_one, masked_query, preferred_element_type=f32)
        * tie_scale[:, None, None, None, None]
    )
    grad_proj_one = jnp.stack([grad_query_one, grad_key_one, grad_value_one]).astype(bf16)
    grad_proj_one = grad_proj_one.reshape(3, prot, rows_dev, cols, width)
    grad_normed_one = jnp.einsum(
        "kprce,kde->prcd", grad_proj_one, attn_full[0:3], preferred_element_type=f32
    )
    _, norm_back_one = jax.vjp(layer_norm, resid_one, norm_gain[0], norm_gain[1])
    part_one, gain_grad_one, shift_grad_one = norm_back_one(grad_normed_one)
    grad_tokens = grad_rows.astype(f32) + part_one
    norm_stack = jnp.stack(
        [
            gain_grad_one,
            shift_grad_one,
            gain_grad_two,
            shift_grad_two,
            gain_grad_three,
            shift_grad_three,
        ]
    )
    row_attn_terms = attn_pair(normed_one, grad_proj_one, mixed_one, grad_rows)
    owned = lax.psum_scatter(
        jnp.concatenate(
            [row_attn_terms, col_attn_terms, in_terms, out_terms, norm_stack.T], axis=1
        ),
        "seq",
        scatter_dimension=0,
        tiled=True,
    )
    width_dev = owned.shape[0]
    row_part = owned[:, : 4 * width].reshape(width_dev, 4, width)
    col_part = owned[:, 4 * width : 8 * width].reshape(width_dev, 4, width)
    in_part = owned[:, 8 * width : 8 * width + hidden]
    out_part = owned[:, 8 * width + hidden : 8 * width + 2 * hidden].T
    norm_part = owned[:, 8 * width + 2 * hidden :].T
    attn_part = jnp.concatenate([row_part, col_part], axis=1).transpose(1, 0, 2)
    attn_grad, in_grad, out_grad, norm_grad = (
        lax.psum(attn_part.astype(jnp.bfloat16), "grp").astype(jnp.float32),
        lax.psum(in_part.astype(jnp.bfloat16), "grp").astype(jnp.float32),
        lax.psum(out_part.astype(jnp.bfloat16), "grp").astype(jnp.float32),
        lax.psum(norm_part.astype(jnp.bfloat16), "grp").astype(jnp.float32),
    )
    squares = (
        jnp.sum(attn_grad * attn_grad)
        + jnp.sum(in_grad * in_grad)
        + jnp.sum(out_grad * out_grad)
        + jnp.sum(norm_grad * norm_grad)
    )
    grad_norm = jnp.sqrt(lax.psum(squares, "seq"))
    factor = clip_bound / jnp.maximum(grad_norm, clip_bound)
    attn_first_new, attn_second_new, attn_weight_new = adam_update(
        attn_weight, attn_first, attn_second, attn_grad * factor, matrix_rate
    )
    in_first_new, in_second_new, in_weight_new = adam_update(
        in_weight, in_first, in_second, in_grad * factor, matrix_rate
    )
    out_first_new, out_second_new, out_weight_new = adam_update(
        out_weight, out_first, out_second, out_grad * factor, matrix_rate
    )
    norm_first_new, norm_second_new, norm_new = adam_update(
        norm_param, norm_first, norm_second, norm_grad * factor, norm_rate
    )
    return (
        block_out,
        grad_tokens,
        grad_norm,
        attn_first_new,
        attn_second_new,
        attn_weight_new,
        attn_weight_new.astype(bf16),
        in_first_new,
        in_second_new,
        in_weight_new,
        in_weight_new.astype(bf16),
        out_first_new,
        out_second_new,
        out_weight_new,
        out_weight_new.astype(bf16),
        norm_first_new,
        norm_second_new,
        norm_new,
    )


PAIR = [(0, 1), (1, 0)]
TILE = 128


def swap(value, axis):
    return lax.ppermute(value, axis, PAIR)


def pick(value, index, axis):
    return lax.dynamic_index_in_dim(value, index, axis, keepdims=False)


def joined(own, other, place, axis):
    return jnp.where(
        place == 0,
        jnp.concatenate([own, other], axis=axis),
        jnp.concatenate([other, own], axis=axis),
    )


def merge(own, other, place, axis):
    return jnp.where(
        place == 0,
        jnp.stack([own, other], axis=axis),
        jnp.stack([other, own], axis=axis),
    )


def to_columns(value, c):
    prot, _, cols, width = value.shape
    part = cols // 4
    split = value.reshape(prot, 2, 2, part, width)
    got = swap(pick(split, 1 - c, 2), "c")
    both = merge(pick(split, c, 2), got, c, 0)
    both = both.reshape(8, part, width)
    return lax.all_to_all(both, ("z", "x"), 0, 0, tiled=True)


def to_rows(value, c):
    rows, part, width = value.shape
    got = lax.all_to_all(value, ("z", "x"), 0, 0, tiled=True)
    got = got.reshape(2, 2, 2, part, width)
    other = swap(pick(got, 1 - c, 0), "c")
    both = merge(pick(got, c, 0), other, c, 2)
    return both.reshape(2, 1, 4 * part, width)


def gather_pieces(own):
    over_z = [own]
    for i in (1, 2, 3):
        over_z.append(lax.ppermute(own, "z", [(k, k ^ i) for k in range(4)]))
    return over_z, [swap(piece, "x") for piece in over_z]


def place_kernel(plan, outs_at, place_ref, *refs):
    pieces = refs[: len(plan)]
    outs = refs[len(plan) : -1]
    sem = refs[-1]
    copies = []
    for ref, (i, j, k) in zip(pieces, plan):
        z = lax.bitwise_xor(place_ref[0], i)
        x = lax.bitwise_xor(place_ref[1], j)
        c = lax.bitwise_xor(place_ref[2], k)
        shard = z * 2 + x
        for source, target in outs_at(ref, outs, shard, c):
            copies.append(pltpu.make_async_copy(source, target, sem.at[len(copies)]))
    for copy in copies:
        copy.start()
    for copy in copies:
        copy.wait()


def placed_pieces(pieces, plan, outs_at, outs, place, count):
    anywhere = pl.BlockSpec(memory_space=pl.ANY)
    return pl.pallas_call(
        partial(place_kernel, plan, outs_at),
        in_specs=[pl.BlockSpec(memory_space=pltpu.SMEM)] + [anywhere] * len(pieces),
        out_specs=[pl.BlockSpec(memory_space=pltpu.VMEM)] * len(outs),
        out_shape=[jax.ShapeDtypeStruct(shape, jnp.bfloat16) for shape in outs],
        scratch_shapes=[pltpu.SemaphoreType.DMA((count,))],
        compiler_params=pltpu.CompilerParams(
            vmem_limit_bytes=sum(2 * math.prod(s) for s in outs) + 2 * 2**20
        ),
        cost_estimate=pl.CostEstimate(
            flops=0, transcendentals=0, bytes_accessed=sum(4 * math.prod(s) for s in outs)
        ),
    )(place, *pieces)


def row_attn_at(ref, outs, shard, c):
    depth = outs[0].shape[0] // 8
    at = pl.multiple_of(shard * depth, depth)
    return [
        (ref.at[pl.ds(0, depth)], outs[0].at[pl.ds(at, depth)]),
        (ref.at[pl.ds(depth, 16)], outs[1].at[shard]),
    ]


def halves_at(ref, outs, shard, c):
    depth, half = ref.shape[1], ref.shape[2]
    at = pl.multiple_of(shard * depth, depth)
    moves = []
    slots = [(o, n) for o, out in enumerate(outs) for n in range(out.shape[1] // (2 * half))]
    for k, (o, n) in enumerate(slots):
        lane = pl.multiple_of(c * half + n * 2 * half, TILE)
        moves.append((ref.at[k], outs[o].at[pl.ds(at, depth), pl.ds(lane, half)]))
    return moves


def all_halves(own_half, other_half, place, outs):
    over_z, over_x = gather_pieces(own_half)
    mine = over_z + over_x
    plan = [(i, j, 0) for j in (0, 1) for i in range(4)]
    theirs = [other_half] + [swap(piece, "c") for piece in mine[1:]]
    plan = plan + [(i, j, 1) for (i, j, _) in plan]
    pieces = mine + theirs
    return placed_pieces(
        pieces, plan, halves_at, outs, place, len(pieces) * own_half.shape[0]
    )


def contract(a, b, dims):
    return lax.dot_general(a, b, (dims, ((), ())), preferred_element_type=jnp.float32)


LAST = ((1,), (1,))
FIRST = ((0,), (0,))
PLAIN = ((1,), (0,))


def softmax_of(scores, keep):
    scores = jnp.where(keep, scores, masked_score)
    expo = jnp.exp(scores - jnp.max(scores, axis=-1, keepdims=True))
    return expo / jnp.sum(expo, axis=-1, keepdims=True)


def head_lanes(lanes):
    side = lax.broadcasted_iota(jnp.int32, (1, lanes), 1) % TILE < DH
    return (side, jnp.logical_not(side))


def only(keep, value):
    return jnp.where(keep, value, jnp.zeros_like(value))


def column_keep(info_ref, own_cols, near, part):
    key = lax.broadcasted_iota(jnp.int32, (1, 2 * near), 1)
    far = key >= near
    inner = key % near
    x = jnp.where(far, 1 - info_ref[1], info_ref[1])
    c = jnp.where(inner >= part, 1 - info_ref[2], info_ref[2])
    column = x * near + c * part + inner % part
    return column < info_ref[3]


def row_pair(ref, row):
    blocks, _, part, lanes = ref.shape
    return jnp.concatenate(
        [ref[:, row + n].reshape(blocks * part, lanes) for n in (0, 1)], axis=1
    )


def live_pair(value, row, info_ref):
    lane = lax.broadcasted_iota(jnp.int32, (1, value.shape[1]), 1) // TILE + row
    return only(lane < info_ref[4], value)


def row_fwd_kernel(info_ref, tie_ref, q_ref, k_ref, v_ref, kf_ref, vf_ref, o_ref):
    blocks, rows, part, lanes = q_ref.shape
    near = blocks * part
    sides = head_lanes(2 * lanes)
    keep = column_keep(info_ref, near, near, part)
    tie = tie_ref[0]
    scores = [jnp.zeros((near, 2 * near), jnp.float32) for _ in sides]
    for row in range(0, rows, 2):
        query = live_pair(row_pair(q_ref, row), row, info_ref)
        key = jnp.concatenate([row_pair(k_ref, row), row_pair(kf_ref, row)], axis=0)
        for n, side in enumerate(sides):
            scores[n] = scores[n] + contract(only(side, query), key, LAST)
    probs = [softmax_of(s * tie, keep).astype(jnp.bfloat16) for s in scores]
    for row in range(0, rows, 2):
        value = jnp.concatenate([row_pair(v_ref, row), row_pair(vf_ref, row)], axis=0)
        mixed = jnp.where(
            sides[0], contract(probs[0], value, PLAIN), contract(probs[1], value, PLAIN)
        ).astype(jnp.bfloat16)
        for n in (0, 1):
            o_ref[:, row + n] = mixed[:, n * lanes : (n + 1) * lanes].reshape(blocks, part, lanes)


def row_bwd_kernel(
    info_ref, tie_ref, q_ref, k_ref, v_ref, kf_ref, vf_ref, do_ref,
    dq_ref, dk_ref, dv_ref, dkf_ref, dvf_ref,
):
    bf16 = jnp.bfloat16
    blocks, rows, part, lanes = q_ref.shape
    near = blocks * part
    sides = head_lanes(2 * lanes)
    keep = column_keep(info_ref, near, near, part)
    tie = tie_ref[0]
    scores = [jnp.zeros((near, 2 * near), jnp.float32) for _ in sides]
    grads = [jnp.zeros((near, 2 * near), jnp.float32) for _ in sides]
    for row in range(0, rows, 2):
        query = live_pair(row_pair(q_ref, row), row, info_ref)
        key = jnp.concatenate([row_pair(k_ref, row), row_pair(kf_ref, row)], axis=0)
        value = jnp.concatenate([row_pair(v_ref, row), row_pair(vf_ref, row)], axis=0)
        out = row_pair(do_ref, row)
        for n, side in enumerate(sides):
            scores[n] = scores[n] + contract(only(side, query), key, LAST)
            grads[n] = grads[n] + contract(only(side, out), value, LAST)
    probs = [softmax_of(s * tie, keep) for s in scores]
    lows = [p.astype(bf16) for p in probs]
    deltas = [softmax_back(p, g).astype(bf16) for p, g in zip(probs, grads)]
    for row in range(0, rows, 2):
        query = live_pair(row_pair(q_ref, row), row, info_ref)
        key = jnp.concatenate([row_pair(k_ref, row), row_pair(kf_ref, row)], axis=0)
        out = row_pair(do_ref, row)
        dq = [contract(d, key, PLAIN) for d in deltas]
        dk = [contract(d, query, FIRST) for d in deltas]
        dv = [contract(p, out, FIRST) for p in lows]
        dq = live_pair(jnp.where(sides[0], dq[0], dq[1]) * tie, row, info_ref).astype(bf16)
        dk = (jnp.where(sides[0], dk[0], dk[1]) * tie).astype(bf16)
        dv = jnp.where(sides[0], dv[0], dv[1]).astype(bf16)
        for n in (0, 1):
            at = slice(n * lanes, (n + 1) * lanes)
            dq_ref[:, row + n] = dq[:, at].reshape(blocks, part, lanes)
            dk_ref[:, row + n] = dk[:near, at].reshape(blocks, part, lanes)
            dv_ref[:, row + n] = dv[:near, at].reshape(blocks, part, lanes)
            dkf_ref[:, row + n] = dk[near:, at].reshape(blocks, part, lanes)
            dvf_ref[:, row + n] = dv[near:, at].reshape(blocks, part, lanes)


def lane_block(shape, first):
    blocks, rows, part, _ = shape
    return pl.BlockSpec((blocks, rows, part, TILE), lambda t: (0, 0, 0, first + t))


def row_attention(info, tie, near, far):
    blocks, rows, part, lanes = near.shape
    tiles = lanes // 3 // TILE
    shape = near.shape
    small = pl.BlockSpec(memory_space=pltpu.SMEM)
    return pl.pallas_call(
        row_fwd_kernel,
        grid=(tiles,),
        in_specs=[small, small]
        + [lane_block(shape, n * tiles) for n in range(3)]
        + [lane_block(shape, n * tiles) for n in range(2)],
        out_specs=lane_block(shape, 0),
        out_shape=jax.ShapeDtypeStruct((blocks, rows, part, lanes // 3), jnp.bfloat16),
        compiler_params=pltpu.CompilerParams(vmem_limit_bytes=32 * 2**20),
    )(info, tie, near, near, near, far, far)


def row_attention_back(info, tie, near, far, grad):
    blocks, rows, part, lanes = near.shape
    tiles = lanes // 3 // TILE
    shape = near.shape
    small = pl.BlockSpec(memory_space=pltpu.SMEM)
    result = jax.ShapeDtypeStruct((blocks, rows, part, lanes // 3), jnp.bfloat16)
    return pl.pallas_call(
        row_bwd_kernel,
        grid=(tiles,),
        in_specs=[small, small]
        + [lane_block(shape, n * tiles) for n in range(3)]
        + [lane_block(shape, n * tiles) for n in range(2)]
        + [lane_block(shape, 0)],
        out_specs=[lane_block(shape, 0)] * 5,
        out_shape=[result] * 5,
        compiler_params=pltpu.CompilerParams(vmem_limit_bytes=32 * 2**20),
    )(info, tie, near, near, near, far, far, grad)


def column_masks(info_ref, rows, part):
    tokens = rows * part
    first = lax.broadcasted_iota(jnp.int32, (tokens, tokens), 0)
    second = lax.broadcasted_iota(jnp.int32, (tokens, tokens), 1)
    same = first % part == second % part
    return jnp.logical_and(same, second // part < info_ref[4])


def col_fwd_kernel(info_ref, qkv_ref, o_ref):
    rows, part, lanes = qkv_ref.shape
    width = lanes // 3
    qkv = qkv_ref[...].reshape(rows * part, lanes)
    keep = column_masks(info_ref, rows, part)
    sides = head_lanes(TILE)
    scale = 1.0 / math.sqrt(DH)
    for at in range(0, width, TILE):
        query = qkv[:, at : at + TILE]
        key = qkv[:, width + at : width + at + TILE]
        value = qkv[:, 2 * width + at : 2 * width + at + TILE]
        mixed = []
        for side in sides:
            probs = softmax_of(contract(only(side, query), key, LAST) * scale, keep)
            mixed.append(contract(probs.astype(jnp.bfloat16), value, PLAIN))
        mixed = jnp.where(sides[0], mixed[0], mixed[1]).astype(jnp.bfloat16)
        o_ref[:, :, at : at + TILE] = mixed.reshape(rows, part, TILE)


def col_bwd_kernel(info_ref, qkv_ref, do_ref, d_ref):
    bf16 = jnp.bfloat16
    rows, part, lanes = qkv_ref.shape
    width = lanes // 3
    qkv = qkv_ref[...].reshape(rows * part, lanes)
    out_grad = do_ref[...].reshape(rows * part, width)
    keep = column_masks(info_ref, rows, part)
    sides = head_lanes(TILE)
    scale = 1.0 / math.sqrt(DH)
    for at in range(0, width, TILE):
        query = qkv[:, at : at + TILE]
        key = qkv[:, width + at : width + at + TILE]
        value = qkv[:, 2 * width + at : 2 * width + at + TILE]
        out = out_grad[:, at : at + TILE]
        found = []
        for side in sides:
            probs = softmax_of(contract(only(side, query), key, LAST) * scale, keep)
            grads = contract(only(side, out), value, LAST)
            delta = softmax_back(probs, grads).astype(bf16)
            found.append(
                (
                    contract(delta, key, PLAIN) * scale,
                    contract(delta, query, FIRST) * scale,
                    contract(probs.astype(bf16), out, FIRST),
                )
            )
        for n in range(3):
            both = jnp.where(sides[0], found[0][n], found[1][n]).astype(bf16)
            first = n * width + at
            d_ref[:, :, first : first + TILE] = both.reshape(rows, part, TILE)


def column_block(rows, part, lanes):
    return pl.BlockSpec((rows, part, lanes), lambda b: (0, b, 0))


def column_attention(info, qkv, part=16):
    rows, cols, lanes = qkv.shape
    return pl.pallas_call(
        col_fwd_kernel,
        grid=(cols // part,),
        in_specs=[pl.BlockSpec(memory_space=pltpu.SMEM), column_block(rows, part, lanes)],
        out_specs=column_block(rows, part, lanes // 3),
        out_shape=jax.ShapeDtypeStruct((rows, cols, lanes // 3), jnp.bfloat16),
        compiler_params=pltpu.CompilerParams(vmem_limit_bytes=32 * 2**20),
    )(info, qkv)


def column_attention_back(info, qkv, grad, part=16):
    rows, cols, lanes = qkv.shape
    return pl.pallas_call(
        col_bwd_kernel,
        grid=(cols // part,),
        in_specs=[
            pl.BlockSpec(memory_space=pltpu.SMEM),
            column_block(rows, part, lanes),
            column_block(rows, part, lanes // 3),
        ],
        out_specs=column_block(rows, part, lanes),
        out_shape=jax.ShapeDtypeStruct((rows, cols, lanes), jnp.bfloat16),
        compiler_params=pltpu.CompilerParams(vmem_limit_bytes=32 * 2**20),
    )(info, qkv, grad)


def summed_to_owner(terms, x):
    bf16 = jnp.bfloat16
    f32 = jnp.float32
    depth = terms.shape[0] // 8
    blocks = terms.reshape(4, 2, depth, *terms.shape[1:])
    got = swap(pick(blocks, 1 - x, 1), "x")
    column = (pick(blocks, x, 1).astype(f32) + got.astype(f32)).astype(bf16)
    parts = lax.all_to_all(column, "z", 0, 0, tiled=True)
    shard = jnp.sum(parts.astype(f32), axis=0).astype(bf16)
    return (shard.astype(f32) + swap(shard, "y").astype(f32)).astype(bf16)


def paired_body(
    tokens,
    cotangent,
    col_count,
    row_count,
    attn_weight,
    in_weight,
    out_weight,
    norm_param,
    attn_first,
    attn_second,
    in_first,
    in_second,
    out_first,
    out_second,
    norm_first,
    norm_second,
):
    f32 = jnp.float32
    bf16 = jnp.bfloat16
    z, x, c = (lax.axis_index(name) for name in ("z", "x", "c"))
    width = tokens.shape[-1]
    hidden = in_weight.shape[1]
    depth = in_weight.shape[0]
    half = width // 2
    hidden_half = hidden // 2

    counts = jnp.stack([col_count, row_count])
    other_counts = swap(counts, "c")
    mine = jnp.where(z // 2 == c, counts, other_counts)
    mine = pick(mine, z % 2, 1)
    cols_live, rows_live = mine[0], mine[1]
    place = jnp.stack([z, x, c]).astype(jnp.int32)
    info = jnp.concatenate([place, mine])
    tie = (lax.rsqrt(rows_live.astype(f32)) * (1.0 / math.sqrt(DH))).reshape(1)

    attn_low = attn_weight.astype(bf16)
    halves = attn_low.reshape(8, depth, 2, half)
    qkv_half = jnp.moveaxis(pick(halves[:3], c, 2), 0, 1).reshape(depth, 3 * half)
    norm_row = jnp.pad(
        norm_param.astype(bf16).reshape(1, 6 * depth), ((0, 15), (0, 3 * half - 6 * depth))
    )
    over_z, over_x = gather_pieces(jnp.concatenate([qkv_half, norm_row]))
    plan = [(i, j, 0) for j in (0, 1) for i in range(4)]
    w_row, norm_rows = placed_pieces(
        over_z + over_x,
        plan,
        row_attn_at,
        [(width, 3 * half), (8, 16, 3 * half)],
        place,
        16,
    )
    norm_gain = norm_rows[:, 0, : 6 * depth].reshape(8, 6, depth)
    norm_gain = jnp.moveaxis(norm_gain, 0, 1).reshape(6, width).astype(f32)
    w_three, w_col, w_seven = all_halves(
        pick(halves[3:], c, 2),
        pick(halves[3:], 1 - c, 2),
        place,
        [(width, width), (width, 3 * width), (width, width)],
    )
    ffn_low = jnp.stack([in_weight.astype(bf16), out_weight.astype(bf16).T])
    ffn_halves = ffn_low.reshape(2, depth, 2, hidden_half)
    w_in, w_out = all_halves(
        pick(ffn_halves, c, 2),
        pick(ffn_halves, 1 - c, 2),
        place,
        [(width, hidden), (width, hidden)],
    )

    stream_zero = to_columns(tokens, c)
    rows, part, _ = stream_zero.shape
    count = rows * part
    resid_one = stream_zero.reshape(count, width).astype(f32)
    normed_one = layer_norm(resid_one, norm_gain[0], norm_gain[1]).astype(bf16)
    near_normed = jnp.concatenate([normed_one, swap(normed_one, "c")])
    far_first = swap(normed_one, "x")
    far_normed = jnp.concatenate([far_first, swap(far_first, "c")])
    near = contract(near_normed, w_row, PLAIN).astype(bf16).reshape(2, rows, part, 3 * half)
    far = contract(far_normed, w_row[:, half:], PLAIN).astype(bf16)
    far = far.reshape(2, rows, part, 2 * half)
    mixed_heads = row_attention(info, tie, near, far)
    mixed_one = joined(
        mixed_heads[0].reshape(count, half), swap(mixed_heads[1].reshape(count, half), "c"), c, 1
    )
    stream_one = (resid_one + contract(mixed_one, w_three, PLAIN)).astype(bf16)

    resid_two = stream_one.astype(f32)
    normed_two = layer_norm(resid_two, norm_gain[2], norm_gain[3]).astype(bf16)
    qkv_two = contract(normed_two, w_col, PLAIN).astype(bf16).reshape(rows, part, 3 * width)
    mixed_two = column_attention(info, qkv_two).reshape(count, width)
    resid_three = resid_two + contract(mixed_two, w_seven, PLAIN)

    normed_three = layer_norm(resid_three, norm_gain[4], norm_gain[5]).astype(bf16)
    inner = contract(normed_three, w_in, PLAIN)
    activ = jax.nn.gelu(inner, approximate=True).astype(bf16)
    result = (resid_three + contract(activ, w_out, LAST)).astype(bf16)
    block_out = to_rows(result.reshape(rows, part, width), c)

    up = to_columns(cotangent, c)
    column = x * (2 * part) + c * part + jnp.arange(part, dtype=jnp.int32)
    live = jnp.logical_and(
        (jnp.arange(rows, dtype=jnp.int32) < rows_live)[:, None], (column < cols_live)[None, :]
    )
    up = jnp.where(live[..., None], up, jnp.zeros_like(up)).reshape(count, width)
    grad_act = contract(up, w_out, PLAIN)
    _, gelu_back = jax.vjp(partial(jax.nn.gelu, approximate=True), inner)
    grad_inner = gelu_back(grad_act)[0].astype(bf16)

    def lanes_of(value, which, groups):
        size = value.shape[1] // (2 * groups)
        first, second = (
            [value[:, (2 * n + k) * size : (2 * n + k + 1) * size] for n in range(groups)]
            for k in (0, 1)
        )
        chosen = [jnp.where(which == 0, a, b) for a, b in zip(first, second)]
        return chosen[0] if groups == 1 else jnp.concatenate(chosen, axis=1)

    def over_cores(sides):
        sent = [contract(a, lanes_of(b, 1 - c, g), FIRST).astype(bf16) for a, b, g in sides]
        got = [swap(value, "c") for value in sent]
        kept = [contract(a, lanes_of(b, c, g), FIRST) for a, b, g in sides]
        return [(k + v.astype(f32)).astype(bf16) for k, v in zip(kept, got)]

    ffn_terms = over_cores([(normed_three, grad_inner, 1), (up, activ, 1)])
    ffn_grad = summed_to_owner(jnp.concatenate(ffn_terms, axis=1), x)
    grad_normed_three = contract(grad_inner, w_in, LAST)
    _, norm_back_three = jax.vjp(layer_norm, resid_three, norm_gain[4], norm_gain[5])
    part_three, gain_grad_three, shift_grad_three = norm_back_three(grad_normed_three)
    grad_three = up.astype(f32) + part_three

    grad_branch_two = grad_three.astype(bf16)
    grad_mixed_two = contract(grad_branch_two, w_seven, LAST).astype(bf16)
    grad_qkv_two = column_attention_back(
        info, qkv_two, grad_mixed_two.reshape(rows, part, width)
    ).reshape(count, 3 * width)
    grad_normed_two = contract(grad_qkv_two, w_col, LAST)
    _, norm_back_two = jax.vjp(layer_norm, resid_two, norm_gain[2], norm_gain[3])
    part_two, gain_grad_two, shift_grad_two = norm_back_two(grad_normed_two)
    grad_stream = (grad_three + part_two).astype(bf16)

    grad_mixed_one = contract(grad_stream, w_three, LAST).astype(bf16)
    grad_heads = jnp.stack(
        [lanes_of(grad_mixed_one, c, 1), swap(lanes_of(grad_mixed_one, 1 - c, 1), "c")]
    ).reshape(2, rows, part, half)
    dq, dk, dv, dk_far, dv_far = row_attention_back(info, tie, near, far, grad_heads)
    grad_near = jnp.concatenate([dq, dk, dv], axis=-1).reshape(2 * count, 3 * half)
    grad_far = jnp.concatenate([dk_far, dv_far], axis=-1).reshape(2 * count, 2 * half)
    far_part = contract(grad_far, w_row[:, half:], LAST).reshape(2, count, width)
    far_sum = far_part[0] + swap(far_part[1].astype(bf16), "c").astype(f32)
    far_got = swap(far_sum.astype(bf16), "x")
    near_part = contract(grad_near, w_row, LAST).reshape(2, count, width)
    near_got = swap(near_part[1].astype(bf16), "c")
    grad_normed_one = near_part[0] + near_got.astype(f32) + far_got.astype(f32)
    _, norm_back_one = jax.vjp(layer_norm, resid_one, norm_gain[0], norm_gain[1])
    part_one, gain_grad_one, shift_grad_one = norm_back_one(grad_normed_one)
    grad_input = (grad_stream.astype(f32) + part_one).astype(bf16)
    grad_tokens = to_rows(grad_input.reshape(rows, part, width), c).astype(f32)

    attn_terms = over_cores(
        [
            (mixed_one, grad_stream, 1),
            (normed_two, grad_qkv_two, 3),
            (mixed_two, grad_branch_two, 1),
        ]
    )
    attn_grad_b = summed_to_owner(jnp.concatenate(attn_terms, axis=1), x)
    row_terms = contract(near_normed, grad_near, FIRST)
    far_terms = contract(far_normed, grad_far, FIRST)
    row_terms = jnp.concatenate([row_terms[:, :half], row_terms[:, half:] + far_terms], axis=1)
    norm_stack = jnp.stack(
        [
            gain_grad_one,
            shift_grad_one,
            gain_grad_two,
            shift_grad_two,
            gain_grad_three,
            shift_grad_three,
        ]
    )
    norm_terms = jnp.moveaxis(norm_stack.reshape(6, 8, depth), 0, 1).reshape(8, 1, 6 * depth)
    norm_terms = jnp.pad(norm_terms, ((0, 0), (0, 15), (0, 3 * half - 6 * depth)))
    row_terms = jnp.concatenate(
        [row_terms.reshape(8, depth, 3 * half), norm_terms], axis=1
    ).astype(bf16)
    row_grad = summed_to_owner(row_terms.reshape(8 * (depth + 16), 3 * half), x)

    row_other = swap(row_grad, "c")
    attn_other = swap(attn_grad_b, "c")
    ffn_other = swap(ffn_grad, "c")
    norm_grad = row_grad[depth, : 6 * depth].astype(f32) + row_other[depth, : 6 * depth].astype(f32)
    norm_grad = norm_grad.reshape(6, depth)
    def whole(own, other, groups):
        size = own.shape[1] // groups
        return [
            joined(own[:depth, n * size : (n + 1) * size], other[:depth, n * size : (n + 1) * size], c, 1)
            for n in range(groups)
        ]

    attn_grad = jnp.stack(whole(row_grad, row_other, 3) + whole(attn_grad_b, attn_other, 5))
    attn_grad = attn_grad.astype(f32)
    in_grad, out_grad = whole(ffn_grad, ffn_other, 2)
    in_grad = in_grad.astype(f32)
    out_grad = out_grad.astype(f32).T

    squares = (
        jnp.sum(attn_grad * attn_grad)
        + jnp.sum(in_grad * in_grad)
        + jnp.sum(out_grad * out_grad)
        + jnp.sum(norm_grad * norm_grad)
    )
    grad_norm = jnp.sqrt(lax.psum(squares, ("z", "x")))
    factor = clip_bound / jnp.maximum(grad_norm, clip_bound)
    attn_first_new, attn_second_new, attn_weight_new = adam_update(
        attn_weight, attn_first, attn_second, attn_grad * factor, matrix_rate
    )
    in_first_new, in_second_new, in_weight_new = adam_update(
        in_weight, in_first, in_second, in_grad * factor, matrix_rate
    )
    out_first_new, out_second_new, out_weight_new = adam_update(
        out_weight, out_first, out_second, out_grad * factor, matrix_rate
    )
    norm_first_new, norm_second_new, norm_new = adam_update(
        norm_param, norm_first, norm_second, norm_grad * factor, norm_rate
    )
    return (
        block_out,
        grad_tokens,
        grad_norm,
        attn_first_new,
        attn_second_new,
        attn_weight_new,
        attn_weight_new.astype(bf16),
        in_first_new,
        in_second_new,
        in_weight_new,
        in_weight_new.astype(bf16),
        out_first_new,
        out_second_new,
        out_weight_new,
        out_weight_new.astype(bf16),
        norm_first_new,
        norm_second_new,
        norm_new,
    )


def paired_layout(mesh):
    return dict(mesh.shape) == {"seq": 8, "grp": 4}


def mapped(run, mesh, seq, grp):
    placed = (
        P(grp, seq, None, None),
        P(grp, seq, None, None),
        P(grp),
        P(grp),
        P(None, seq, None),
        P(seq, None),
        P(None, seq),
        P(None, seq),
        P(None, seq, None),
        P(None, seq, None),
        P(seq, None),
        P(seq, None),
        P(None, seq),
        P(None, seq),
        P(None, seq),
        P(None, seq),
    )
    return jax.shard_map(
        run,
        mesh=mesh,
        in_specs=placed,
        out_specs=(
            P(grp, seq, None, None),
            P(grp, seq, None, None),
            P(),
            P(None, seq, None),
            P(None, seq, None),
            P(None, seq, None),
            P(None, seq, None),
            P(seq, None),
            P(seq, None),
            P(seq, None),
            P(seq, None),
            P(None, seq),
            P(None, seq),
            P(None, seq),
            P(None, seq),
            P(None, seq),
            P(None, seq),
            P(None, seq),
        ),
        check_vma=False,
    )


def solution(mesh):
    if not paired_layout(mesh):
        return mapped(general_body, mesh, "seq", "grp")
    fine = Mesh(mesh.devices.reshape(4, 2, 2, 2), ("z", "x", "y", "c"))
    return mapped(paired_body, fine, ("z", "x"), ("y", "c"))
```

```python
from functools import partial
import math

import jax
import jax.numpy as jnp
from jax import lax
from jax.experimental import pallas as pl
from jax.experimental.pallas import tpu as pltpu
from jax.sharding import Mesh
from jax.sharding import PartitionSpec as P

H = 12
DH = 64
STEP = 5


eps_norm = 1e-05
masked_score = -1000000000.0
clip_bound = 1.0
beta_one = 0.5
beta_two = 0.5
matrix_rate = 0.06
norm_rate = 0.3
decay_rate = 0.01
adam_eps = 1e-08


def in_blocks(x, dim, length):
    lengths = x.shape
    pieces = x.reshape(*lengths[:dim], length, lengths[dim] // length, *lengths[dim + 1 :])
    return jnp.moveaxis(pieces, dim, 0)


def sent_and_summed(x, axis, dim):
    length = lax.axis_size(axis)
    pieces = lax.all_to_all(in_blocks(x, dim, length), axis, 0, 0, tiled=True)
    return jnp.sum(pieces.astype(jnp.float32), axis=0)


def layer_norm(value, gain, shift):
    mean = jnp.mean(value, axis=-1, keepdims=True)
    centred = value - mean
    spread = jnp.mean(centred * centred, axis=-1, keepdims=True)
    return centred * lax.rsqrt(spread + eps_norm) * gain + shift


def softmax_rows(scores, keep):
    scores = jnp.where(keep, scores, masked_score)
    top = jnp.max(scores, axis=-1, keepdims=True)
    expo = jnp.exp(scores - top)
    return expo / jnp.sum(expo, axis=-1, keepdims=True)


def softmax_back(probs, grads):
    return probs * (grads - jnp.sum(probs * grads, axis=-1, keepdims=True))


def adam_update(weight, first, second, grad, rate):
    first_new = beta_one * first + (1.0 - beta_one) * grad
    second_new = beta_two * second + (1.0 - beta_two) * grad * grad
    first_hat = first_new / (1.0 - beta_one**STEP)
    second_hat = second_new / (1.0 - beta_two**STEP)
    weight_new = weight - rate * (
        first_hat / (jnp.sqrt(second_hat) + adam_eps) + decay_rate * weight
    )
    return (first_new, second_new, weight_new)


def attn_pair(normed, grad_proj, mixed, grad_branch):
    width = normed.shape[-1]
    qkv_terms = jnp.einsum("prcd,kprce->dke", normed, grad_proj, preferred_element_type=jnp.float32)
    output_terms = jnp.einsum(
        "prcd,prce->de", mixed, grad_branch, preferred_element_type=jnp.float32
    )
    return jnp.concatenate([qkv_terms, output_terms[:, None, :]], axis=1).reshape(width, 4 * width)


def general_body(
    tokens,
    cotangent,
    col_count,
    row_count,
    attn_weight,
    in_weight,
    out_weight,
    norm_param,
    attn_first,
    attn_second,
    in_first,
    in_second,
    out_first,
    out_second,
    norm_first,
    norm_second,
):
    f32 = jnp.float32
    bf16 = jnp.bfloat16
    prot, rows_dev, cols, width = tokens.shape
    hidden = in_weight.shape[1]
    head_scale = 1.0 / math.sqrt(DH)
    attn_full, in_full, out_full, norm_full = (
        lax.all_gather(attn_weight.astype(bf16), "seq", axis=1, tiled=True),
        lax.all_gather(in_weight.astype(bf16), "seq", axis=0, tiled=True),
        lax.all_gather(out_weight.astype(bf16), "seq", axis=1, tiled=True),
        lax.all_gather(norm_param.astype(bf16), "seq", axis=1, tiled=True),
    )
    norm_gain = norm_full.astype(f32)
    row_ids = lax.axis_index("seq") * rows_dev + jnp.arange(rows_dev, dtype=jnp.int32)
    row_live = (row_ids[None, :] < row_count[:, None]).astype(f32)
    col_live = jnp.arange(cols, dtype=jnp.int32)[None, :] < col_count[:, None]
    tie_scale = lax.rsqrt(row_count.astype(f32)) * head_scale
    live = row_live[:, :, None] * col_live.astype(f32)[:, None, :]
    grad_out = (cotangent.astype(f32) * live[..., None]).astype(bf16)
    resid_one = tokens.astype(f32)
    normed_one = layer_norm(resid_one, norm_gain[0], norm_gain[1]).astype(bf16)
    proj_one = jnp.einsum(
        "prcd,kde->kprce", normed_one, attn_full[0:3], preferred_element_type=f32
    ).astype(bf16)
    proj_one = proj_one.reshape(3, prot, rows_dev, cols, H, DH)
    query_one, key_one, value_one = (proj_one[0], proj_one[1], proj_one[2])
    masked_query = query_one * row_live[:, :, None, None, None].astype(bf16)
    partial_scores = (
        jnp.einsum("prihe,prjhe->phij", masked_query, key_one, preferred_element_type=f32)
        * tie_scale[:, None, None, None]
    )
    keep_cols = col_live[:, None, None, :]
    score_part = lax.psum_scatter(partial_scores, "seq", scatter_dimension=2, tiled=True)
    probs_one = softmax_rows(score_part, keep_cols)
    probs_low = lax.all_gather(probs_one.astype(bf16), "seq", axis=2, tiled=True)
    mixed_one = jnp.einsum(
        "phij,prjhe->prihe", probs_low, value_one, preferred_element_type=f32
    ).astype(bf16)
    mixed_one = mixed_one.reshape(prot, rows_dev, cols, width)
    branch_one = jnp.einsum("prcd,de->prce", mixed_one, attn_full[3], preferred_element_type=f32)
    stream_one = (resid_one + branch_one).astype(bf16)
    stream_cols, up_grad = (
        lax.all_to_all(stream_one, "seq", split_axis=2, concat_axis=1, tiled=True),
        lax.all_to_all(grad_out, "seq", split_axis=2, concat_axis=1, tiled=True),
    )
    rows = stream_cols.shape[1]
    cols_dev = stream_cols.shape[2]
    row_live_all = jnp.arange(rows, dtype=jnp.int32)[None, :] < row_count[:, None]
    resid_two = stream_cols.astype(f32)
    normed_two = layer_norm(resid_two, norm_gain[2], norm_gain[3]).astype(bf16)
    proj_two = jnp.einsum(
        "prcd,kde->kprce", normed_two, attn_full[4:7], preferred_element_type=f32
    ).astype(bf16)
    proj_two = proj_two.reshape(3, prot, rows, cols_dev, H, DH)
    query_two, key_two, value_two = (proj_two[0], proj_two[1], proj_two[2])
    scores_two = (
        jnp.einsum("prche,psche->pchrs", query_two, key_two, preferred_element_type=f32)
        * head_scale
    )
    probs_two = softmax_rows(scores_two, row_live_all[:, None, None, None, :])
    probs_two_low = probs_two.astype(bf16)
    mixed_two = jnp.einsum(
        "pchrs,psche->prche", probs_two_low, value_two, preferred_element_type=f32
    ).astype(bf16)
    mixed_two = mixed_two.reshape(prot, rows, cols_dev, width)
    resid_three = resid_two + jnp.einsum(
        "prcd,de->prce", mixed_two, attn_full[7], preferred_element_type=f32
    )
    normed_three = layer_norm(resid_three, norm_gain[4], norm_gain[5]).astype(bf16)
    inner = jnp.einsum("prcd,df->prcf", normed_three, in_full, preferred_element_type=f32)
    activ = jax.nn.gelu(inner, approximate=True).astype(bf16)
    result = (
        resid_three + jnp.einsum("prcf,fd->prcd", activ, out_full, preferred_element_type=f32)
    ).astype(bf16)
    block_out = lax.all_to_all(result, "seq", split_axis=1, concat_axis=2, tiled=True)
    grad_act = jnp.einsum("prcd,fd->prcf", up_grad, out_full, preferred_element_type=f32)
    _, gelu_back = jax.vjp(partial(jax.nn.gelu, approximate=True), inner)
    grad_inner = gelu_back(grad_act)[0].astype(bf16)
    grad_normed_three = jnp.einsum("prcf,df->prcd", grad_inner, in_full, preferred_element_type=f32)
    _, norm_back_three = jax.vjp(layer_norm, resid_three, norm_gain[4], norm_gain[5])
    part_three, gain_grad_three, shift_grad_three = norm_back_three(grad_normed_three)
    grad_three = up_grad.astype(f32) + part_three
    grad_branch_two = grad_three.astype(bf16)
    grad_mixed_two = jnp.einsum(
        "prce,de->prcd", grad_branch_two, attn_full[7], preferred_element_type=f32
    ).astype(bf16)
    grad_mixed_two = grad_mixed_two.reshape(prot, rows, cols_dev, H, DH)
    grad_probs_two = jnp.einsum(
        "prche,psche->pchrs", grad_mixed_two, value_two, preferred_element_type=f32
    )
    grad_value_two = jnp.einsum(
        "pchrs,prche->psche", probs_two_low, grad_mixed_two, preferred_element_type=f32
    )
    grad_scores_two = softmax_back(probs_two, grad_probs_two).astype(bf16)
    grad_query_two = (
        jnp.einsum("pchrs,psche->prche", grad_scores_two, key_two, preferred_element_type=f32)
        * head_scale
    )
    grad_key_two = (
        jnp.einsum("pchrs,prche->psche", grad_scores_two, query_two, preferred_element_type=f32)
        * head_scale
    )
    grad_proj_two = jnp.stack([grad_query_two, grad_key_two, grad_value_two]).astype(bf16)
    grad_proj_two = grad_proj_two.reshape(3, prot, rows, cols_dev, width)
    grad_normed_two = jnp.einsum(
        "kprce,kde->prcd", grad_proj_two, attn_full[4:7], preferred_element_type=f32
    )
    _, norm_back_two = jax.vjp(layer_norm, resid_two, norm_gain[2], norm_gain[3])
    part_two, gain_grad_two, shift_grad_two = norm_back_two(grad_normed_two)
    grad_stream = (grad_three + part_two).astype(bf16)
    col_attn_terms = attn_pair(normed_two, grad_proj_two, mixed_two, grad_branch_two)
    in_terms = jnp.einsum("prcd,prcf->df", normed_three, grad_inner, preferred_element_type=f32)
    out_terms = jnp.einsum("prcf,prcd->df", activ, up_grad, preferred_element_type=f32)
    grad_rows = lax.all_to_all(grad_stream, "seq", split_axis=1, concat_axis=2, tiled=True)
    grad_mixed_one = jnp.einsum(
        "prce,de->prcd", grad_rows, attn_full[3], preferred_element_type=f32
    ).astype(bf16)
    grad_mixed_one = grad_mixed_one.reshape(prot, rows_dev, cols, H, DH)
    partial_grads = jnp.einsum(
        "prihe,prjhe->phij", grad_mixed_one, value_one, preferred_element_type=f32
    )
    grad_value_one = jnp.einsum(
        "phij,prihe->prjhe", probs_low, grad_mixed_one, preferred_element_type=f32
    )
    grad_part = sent_and_summed(partial_grads.astype(jnp.bfloat16), "seq", 2)
    grad_scores_one = lax.all_gather(
        softmax_back(probs_one, grad_part).astype(bf16), "seq", axis=2, tiled=True
    )
    tie_rows = row_live[:, :, None, None, None] * tie_scale[:, None, None, None, None]
    grad_query_one = (
        jnp.einsum("phij,prjhe->prihe", grad_scores_one, key_one, preferred_element_type=f32)
        * tie_rows
    )
    grad_key_one = (
        jnp.einsum("phij,prihe->prjhe", grad_scores_one, masked_query, preferred_element_type=f32)
        * tie_scale[:, None, None, None, None]
    )
    grad_proj_one = jnp.stack([grad_query_one, grad_key_one, grad_value_one]).astype(bf16)
    grad_proj_one = grad_proj_one.reshape(3, prot, rows_dev, cols, width)
    grad_normed_one = jnp.einsum(
        "kprce,kde->prcd", grad_proj_one, attn_full[0:3], preferred_element_type=f32
    )
    _, norm_back_one = jax.vjp(layer_norm, resid_one, norm_gain[0], norm_gain[1])
    part_one, gain_grad_one, shift_grad_one = norm_back_one(grad_normed_one)
    grad_tokens = grad_rows.astype(f32) + part_one
    norm_stack = jnp.stack(
        [
            gain_grad_one,
            shift_grad_one,
            gain_grad_two,
            shift_grad_two,
            gain_grad_three,
            shift_grad_three,
        ]
    )
    row_attn_terms = attn_pair(normed_one, grad_proj_one, mixed_one, grad_rows)
    owned = lax.psum_scatter(
        jnp.concatenate(
            [row_attn_terms, col_attn_terms, in_terms, out_terms, norm_stack.T], axis=1
        ),
        "seq",
        scatter_dimension=0,
        tiled=True,
    )
    width_dev = owned.shape[0]
    row_part = owned[:, : 4 * width].reshape(width_dev, 4, width)
    col_part = owned[:, 4 * width : 8 * width].reshape(width_dev, 4, width)
    in_part = owned[:, 8 * width : 8 * width + hidden]
    out_part = owned[:, 8 * width + hidden : 8 * width + 2 * hidden].T
    norm_part = owned[:, 8 * width + 2 * hidden :].T
    attn_part = jnp.concatenate([row_part, col_part], axis=1).transpose(1, 0, 2)
    attn_grad, in_grad, out_grad, norm_grad = (
        lax.psum(attn_part.astype(jnp.bfloat16), "grp").astype(jnp.float32),
        lax.psum(in_part.astype(jnp.bfloat16), "grp").astype(jnp.float32),
        lax.psum(out_part.astype(jnp.bfloat16), "grp").astype(jnp.float32),
        lax.psum(norm_part.astype(jnp.bfloat16), "grp").astype(jnp.float32),
    )
    squares = (
        jnp.sum(attn_grad * attn_grad)
        + jnp.sum(in_grad * in_grad)
        + jnp.sum(out_grad * out_grad)
        + jnp.sum(norm_grad * norm_grad)
    )
    grad_norm = jnp.sqrt(lax.psum(squares, "seq"))
    factor = clip_bound / jnp.maximum(grad_norm, clip_bound)
    attn_first_new, attn_second_new, attn_weight_new = adam_update(
        attn_weight, attn_first, attn_second, attn_grad * factor, matrix_rate
    )
    in_first_new, in_second_new, in_weight_new = adam_update(
        in_weight, in_first, in_second, in_grad * factor, matrix_rate
    )
    out_first_new, out_second_new, out_weight_new = adam_update(
        out_weight, out_first, out_second, out_grad * factor, matrix_rate
    )
    norm_first_new, norm_second_new, norm_new = adam_update(
        norm_param, norm_first, norm_second, norm_grad * factor, norm_rate
    )
    return (
        block_out,
        grad_tokens,
        grad_norm,
        attn_first_new,
        attn_second_new,
        attn_weight_new,
        attn_weight_new.astype(bf16),
        in_first_new,
        in_second_new,
        in_weight_new,
        in_weight_new.astype(bf16),
        out_first_new,
        out_second_new,
        out_weight_new,
        out_weight_new.astype(bf16),
        norm_first_new,
        norm_second_new,
        norm_new,
    )


PAIR = [(0, 1), (1, 0)]
TILE = 128


def swap(value, axis):
    return lax.ppermute(value, axis, PAIR)


def pick(value, index, axis):
    return lax.dynamic_index_in_dim(value, index, axis, keepdims=False)


def joined(own, other, place, axis):
    return jnp.where(
        place == 0,
        jnp.concatenate([own, other], axis=axis),
        jnp.concatenate([other, own], axis=axis),
    )


def merge(own, other, place, axis):
    return jnp.where(
        place == 0,
        jnp.stack([own, other], axis=axis),
        jnp.stack([other, own], axis=axis),
    )


def to_columns(value, c):
    prot, _, cols, width = value.shape
    part = cols // 4
    split = value.reshape(prot, 2, 2, part, width)
    got = swap(pick(split, 1 - c, 2), "c")
    both = merge(pick(split, c, 2), got, c, 0)
    both = both.reshape(8, part, width)
    return lax.all_to_all(both, ("z", "x"), 0, 0, tiled=True)


def to_rows(value, c):
    rows, part, width = value.shape
    got = lax.all_to_all(value, ("z", "x"), 0, 0, tiled=True)
    got = got.reshape(2, 2, 2, part, width)
    other = swap(pick(got, 1 - c, 0), "c")
    both = merge(pick(got, c, 0), other, c, 2)
    return both.reshape(2, 1, 4 * part, width)


def after(value, *earlier):
    return lax.optimization_barrier((value, *earlier))[0]


def gather_z(own):
    others = [lax.ppermute(own, "z", [(k, k ^ i) for k in range(4)]) for i in (1, 2, 3)]
    return jnp.stack([own] + others)


def spread(over_z):
    over_x = swap(over_z, "x")
    quarter = [((0, 0, 0), over_z), ((1, 0, 0), over_x)]
    return quarter + [((j, 1, 0), swap(value, "y")) for (j, _, _), value in quarter]


def both_cores(half):
    return half + [((j, m, 1), swap(value, "c")) for (j, m, _), value in half]


def placing(plan, outs_at, place_ref, stacks, outs, sem):
    copies = []
    for stack, (j, m, k) in zip(stacks, plan):
        x, y, c = (lax.bitwise_xor(place_ref[n], step) for n, step in ((1, j), (3, m), (2, k)))
        for i in range(4):
            shard = lax.bitwise_xor(place_ref[0], i) * 2 + x
            for source, target in outs_at(stack.at[i], outs, shard, y, c):
                copies.append(pltpu.make_async_copy(source, target, sem.at[len(copies)]))
    return copies


def place_kernel(plan, outs_at, place_ref, *refs):
    stacks = refs[: len(plan)]
    copies = placing(plan, outs_at, place_ref, stacks, refs[len(plan) : -1], refs[-1])
    for copy in copies:
        copy.start()
    for copy in copies:
        copy.wait()


def placed_pieces(pieces, outs_at, outs, place, count):
    anywhere = pl.BlockSpec(memory_space=pl.ANY)
    return pl.pallas_call(
        partial(place_kernel, [step for step, _ in pieces], outs_at),
        in_specs=[pl.BlockSpec(memory_space=pltpu.SMEM)] + [anywhere] * len(pieces),
        out_specs=[pl.BlockSpec(memory_space=pltpu.VMEM)] * len(outs),
        out_shape=[jax.ShapeDtypeStruct(shape, jnp.bfloat16) for shape in outs],
        scratch_shapes=[pltpu.SemaphoreType.DMA((count,))],
        compiler_params=pltpu.CompilerParams(
            vmem_limit_bytes=sum(2 * math.prod(s) for s in outs) + 2 * 2**20
        ),
    )(place, *[value for _, value in pieces])


def row_attn_at(ref, outs, shard, y, c):
    depth = outs[0].shape[0] // 8
    at = pl.multiple_of(shard * depth, depth)
    return [
        (ref.at[pl.ds(0, depth)], outs[0].at[pl.ds(at, depth)]),
        (ref.at[pl.ds(depth, 16)], outs[1].at[shard]),
    ]


def ffn_at(ref, outs, shard, y, c):
    depth = ref.shape[0]
    at = pl.multiple_of((y * 8 + shard) * depth, depth)
    return [(ref, outs[0].at[pl.ds(at, depth)])]


def col_attn_at(ref, outs, shard, y, c):
    depth, half = ref.shape[1], ref.shape[2]
    at = pl.multiple_of((shard * 2 + y) * depth, depth)
    moves = []
    slots = [(o, n) for o, out in enumerate(outs) for n in range(out.shape[1] // (2 * half))]
    for k, (o, n) in enumerate(slots):
        lane = pl.multiple_of(c * half + n * 2 * half, TILE)
        moves.append((ref.at[k], outs[o].at[pl.ds(at, depth), pl.ds(lane, half)]))
    return moves


def contract(a, b, dims):
    return lax.dot_general(a, b, (dims, ((), ())), preferred_element_type=jnp.float32)


LAST = ((1,), (1,))
FIRST = ((0,), (0,))
PLAIN = ((1,), (0,))


def softmax_of(scores, keep):
    scores = jnp.where(keep, scores, masked_score)
    expo = jnp.exp(scores - jnp.max(scores, axis=-1, keepdims=True))
    return expo / jnp.sum(expo, axis=-1, keepdims=True)


def head_lanes(lanes):
    side = lax.broadcasted_iota(jnp.int32, (1, lanes), 1) % TILE < DH
    return (side, jnp.logical_not(side))


def only(keep, value):
    return jnp.where(keep, value, jnp.zeros_like(value))


def column_keep(info_ref, own_cols, near, part):
    key = lax.broadcasted_iota(jnp.int32, (1, 2 * near), 1)
    far = key >= near
    inner = key % near
    x = jnp.where(far, 1 - info_ref[1], info_ref[1])
    c = jnp.where(inner >= part, 1 - info_ref[2], info_ref[2])
    column = x * near + c * part + inner % part
    return column < info_ref[3]


def row_pair(ref, row):
    blocks, _, part, lanes = ref.shape
    return jnp.concatenate(
        [ref[:, row + n].reshape(blocks * part, lanes) for n in (0, 1)], axis=1
    )


def live_pair(value, row, info_ref):
    lane = lax.broadcasted_iota(jnp.int32, (1, value.shape[1]), 1) // TILE + row
    return only(lane < info_ref[4], value)


def row_fwd_kernel(info_ref, tie_ref, q_ref, k_ref, v_ref, kf_ref, vf_ref, o_ref):
    blocks, rows, part, lanes = q_ref.shape
    near = blocks * part
    sides = head_lanes(2 * lanes)
    keep = column_keep(info_ref, near, near, part)
    tie = tie_ref[0]
    scores = [jnp.zeros((near, 2 * near), jnp.float32) for _ in sides]
    for row in range(0, rows, 2):
        query = live_pair(row_pair(q_ref, row), row, info_ref)
        key = jnp.concatenate([row_pair(k_ref, row), row_pair(kf_ref, row)], axis=0)
        for n, side in enumerate(sides):
            scores[n] = scores[n] + contract(only(side, query), key, LAST)
    probs = [softmax_of(s * tie, keep).astype(jnp.bfloat16) for s in scores]
    for row in range(0, rows, 2):
        value = jnp.concatenate([row_pair(v_ref, row), row_pair(vf_ref, row)], axis=0)
        mixed = jnp.where(
            sides[0], contract(probs[0], value, PLAIN), contract(probs[1], value, PLAIN)
        ).astype(jnp.bfloat16)
        for n in (0, 1):
            o_ref[:, row + n] = mixed[:, n * lanes : (n + 1) * lanes].reshape(blocks, part, lanes)


def row_bwd_kernel(
    info_ref, tie_ref, q_ref, k_ref, v_ref, kf_ref, vf_ref, do_ref,
    dq_ref, dk_ref, dv_ref, dkf_ref, dvf_ref,
):
    bf16 = jnp.bfloat16
    blocks, rows, part, lanes = q_ref.shape
    near = blocks * part
    sides = head_lanes(2 * lanes)
    keep = column_keep(info_ref, near, near, part)
    tie = tie_ref[0]
    scores = [jnp.zeros((near, 2 * near), jnp.float32) for _ in sides]
    grads = [jnp.zeros((near, 2 * near), jnp.float32) for _ in sides]
    for row in range(0, rows, 2):
        query = live_pair(row_pair(q_ref, row), row, info_ref)
        key = jnp.concatenate([row_pair(k_ref, row), row_pair(kf_ref, row)], axis=0)
        value = jnp.concatenate([row_pair(v_ref, row), row_pair(vf_ref, row)], axis=0)
        out = row_pair(do_ref, row)
        for n, side in enumerate(sides):
            scores[n] = scores[n] + contract(only(side, query), key, LAST)
            grads[n] = grads[n] + contract(only(side, out), value, LAST)
    probs = [softmax_of(s * tie, keep) for s in scores]
    lows = [p.astype(bf16) for p in probs]
    deltas = [softmax_back(p, g).astype(bf16) for p, g in zip(probs, grads)]
    for row in range(0, rows, 2):
        query = live_pair(row_pair(q_ref, row), row, info_ref)
        key = jnp.concatenate([row_pair(k_ref, row), row_pair(kf_ref, row)], axis=0)
        out = row_pair(do_ref, row)
        dq = [contract(d, key, PLAIN) for d in deltas]
        dk = [contract(d, query, FIRST) for d in deltas]
        dv = [contract(p, out, FIRST) for p in lows]
        dq = live_pair(jnp.where(sides[0], dq[0], dq[1]) * tie, row, info_ref).astype(bf16)
        dk = (jnp.where(sides[0], dk[0], dk[1]) * tie).astype(bf16)
        dv = jnp.where(sides[0], dv[0], dv[1]).astype(bf16)
        for n in (0, 1):
            at = slice(n * lanes, (n + 1) * lanes)
            dq_ref[:, row + n] = dq[:, at].reshape(blocks, part, lanes)
            dk_ref[:, row + n] = dk[:near, at].reshape(blocks, part, lanes)
            dv_ref[:, row + n] = dv[:near, at].reshape(blocks, part, lanes)
            dkf_ref[:, row + n] = dk[near:, at].reshape(blocks, part, lanes)
            dvf_ref[:, row + n] = dv[near:, at].reshape(blocks, part, lanes)


def lane_block(shape, first):
    blocks, rows, part, _ = shape
    return pl.BlockSpec((blocks, rows, part, TILE), lambda t: (0, 0, 0, first + t))


def row_attention(info, tie, near, far):
    blocks, rows, part, lanes = near.shape
    tiles = lanes // 3 // TILE
    shape = near.shape
    small = pl.BlockSpec(memory_space=pltpu.SMEM)
    return pl.pallas_call(
        row_fwd_kernel,
        grid=(tiles,),
        in_specs=[small, small]
        + [lane_block(shape, n * tiles) for n in range(3)]
        + [lane_block(shape, n * tiles) for n in range(2)],
        out_specs=lane_block(shape, 0),
        out_shape=jax.ShapeDtypeStruct((blocks, rows, part, lanes // 3), jnp.bfloat16),
        compiler_params=pltpu.CompilerParams(vmem_limit_bytes=32 * 2**20),
    )(info, tie, near, near, near, far, far)


def row_attention_back(info, tie, near, far, grad):
    blocks, rows, part, lanes = near.shape
    tiles = lanes // 3 // TILE
    shape = near.shape
    small = pl.BlockSpec(memory_space=pltpu.SMEM)
    result = jax.ShapeDtypeStruct((blocks, rows, part, lanes // 3), jnp.bfloat16)
    return pl.pallas_call(
        row_bwd_kernel,
        grid=(tiles,),
        in_specs=[small, small]
        + [lane_block(shape, n * tiles) for n in range(3)]
        + [lane_block(shape, n * tiles) for n in range(2)]
        + [lane_block(shape, 0)],
        out_specs=[lane_block(shape, 0)] * 5,
        out_shape=[result] * 5,
        compiler_params=pltpu.CompilerParams(vmem_limit_bytes=32 * 2**20),
    )(info, tie, near, near, near, far, far, grad)


def normed(value, gain, shift):
    centred = value - jnp.mean(value, axis=-1, keepdims=True)
    scale = lax.rsqrt(jnp.mean(centred * centred, axis=-1, keepdims=True) + eps_norm)
    unit = centred * scale
    return unit * gain + shift, unit, scale


def normed_back(grad, unit, scale, gain):
    inner = grad * gain
    mean = jnp.mean(inner, axis=-1, keepdims=True)
    along = jnp.mean(inner * unit, axis=-1, keepdims=True)
    return scale * (inner - mean - unit * along)


def column_masks(info_ref, rows, part):
    tokens = rows * part
    key = lax.broadcasted_iota(jnp.int32, (tokens, tokens), 0)
    query = lax.broadcasted_iota(jnp.int32, (tokens, tokens), 1)
    same = key % part == query % part
    return jnp.logical_and(same, key // part < info_ref[4])


def stacked(value, sides):
    return jnp.concatenate([only(side, value) for side in sides], axis=0)


def column_probs(query, key, keep, sides):
    scores = contract(stacked(key, sides), query, LAST) * (1.0 / math.sqrt(DH))
    tokens = query.shape[0]
    probs = []
    for n in (0, 1):
        part = jnp.where(keep, scores[n * tokens : (n + 1) * tokens], masked_score)
        expo = jnp.exp(part - jnp.max(part, axis=0, keepdims=True))
        probs.append(expo / jnp.sum(expo, axis=0, keepdims=True))
    return probs


def col_fwd_kernel(
    info_ref, x_ref, own_ref, other_ref, three_ref, col_ref, seven_ref, gain_ref,
    mixed_one_ref, one_ref, normed_two_ref, qkv_ref, mixed_ref, resid_ref, normed_three_ref,
):
    bf16 = jnp.bfloat16
    rows, cols, lanes = qkv_ref.shape
    width = lanes // 3
    part = 16
    own, other = own_ref[...], other_ref[...]
    flip = info_ref[2] == 0
    mixed_one = jnp.concatenate(
        [jnp.where(flip, own, other), jnp.where(flip, other, own)], axis=1
    )
    mixed_one_ref[...] = mixed_one
    stream = (x_ref[...].astype(jnp.float32) + contract(mixed_one, three_ref[...], PLAIN)).astype(bf16)
    one_ref[...] = stream
    normed_two = normed(stream.astype(jnp.float32), gain_ref[2:3], gain_ref[3:4])[0].astype(bf16)
    normed_two_ref[...] = normed_two
    for n in range(3):
        at = slice(n * width, (n + 1) * width)
        found = contract(normed_two, col_ref[:, at], PLAIN).astype(bf16)
        qkv_ref[:, :, at] = found.reshape(rows, cols, width)
    keep = column_masks(info_ref, rows, part)
    sides = head_lanes(TILE)

    def attend(b, carry):
        at = pl.ds(pl.multiple_of(b * part, part), part)
        def tile(n, t):
            lane = n * width + t * TILE
            return qkv_ref[:, at, lane : lane + TILE].reshape(rows * part, TILE)
        tiles = range(width // TILE)
        probs = [column_probs(tile(0, t), tile(1, t), keep, sides) for t in tiles]
        for t in tiles:
            low = jnp.concatenate(probs[t], axis=0).astype(bf16)
            mixed = contract(low, stacked(tile(2, t), sides), FIRST).astype(bf16)
            mixed_ref[:, at, t * TILE : (t + 1) * TILE] = mixed.reshape(rows, part, TILE)
        return carry

    lax.fori_loop(0, cols // part, attend, 0)
    mixed = mixed_ref[...].reshape(rows * cols, width)
    resid = one_ref[...].astype(jnp.float32) + contract(mixed, seven_ref[...], PLAIN)
    resid_ref[...] = resid
    normed_three_ref[...] = normed(resid, gain_ref[4:5], gain_ref[5:6])[0].astype(bf16)


def col_bwd_kernel(
    info_ref, up_ref, da_ref, da_got_ref, resid_ref, one_ref, qkv_ref, three_ref, col_ref, seven_ref,
    gain_ref, branch_ref, dqkv_ref, stream_ref, own_ref, other_ref, norms_ref, do_ref,
):
    bf16 = jnp.bfloat16
    f32 = jnp.float32
    rows, cols, lanes = qkv_ref.shape
    width = lanes // 3
    part = 16
    da = da_ref[...] + da_got_ref[...].astype(f32)
    gain = gain_ref[4:5]
    _, unit, scale = normed(resid_ref[...], gain, 0.0)
    grad_three = up_ref[...].astype(f32) + normed_back(da, unit, scale, gain)
    norms_ref[2:3] = jnp.sum(da * unit, axis=0, keepdims=True)
    norms_ref[3:4] = jnp.sum(da, axis=0, keepdims=True)
    branch = grad_three.astype(bf16)
    branch_ref[...] = branch
    do_ref[...] = contract(branch, seven_ref[...], LAST).astype(bf16).reshape(rows, cols, width)
    keep = column_masks(info_ref, rows, part)
    sides = head_lanes(TILE)
    ratio = 1.0 / math.sqrt(DH)

    def attend(b, carry):
        at = pl.ds(pl.multiple_of(b * part, part), part)
        tokens = rows * part

        def tile(n, t):
            lane = n * width + t * TILE
            return qkv_ref[:, at, lane : lane + TILE].reshape(tokens, TILE)

        def out_tile(t):
            return do_ref[:, at, t * TILE : (t + 1) * TILE].reshape(tokens, TILE)

        def put(n, t, value):
            lane = n * width + t * TILE
            dqkv_ref[:, at, lane : lane + TILE] = value.astype(bf16).reshape(rows, part, TILE)

        for t in range(width // TILE):
            query, key, out = tile(0, t), tile(1, t), out_tile(t)
            keys = stacked(key, sides)
            probs = column_probs(query, key, keep, sides)
            grads = contract(stacked(tile(2, t), sides), out, LAST)
            deltas = []
            for n, p in enumerate(probs):
                g = grads[n * tokens : (n + 1) * tokens]
                deltas.append((p * (g - jnp.sum(p * g, axis=0, keepdims=True))).astype(bf16))
            put(0, t, contract(jnp.concatenate(deltas, axis=0), keys, FIRST) * ratio)
            wide = jnp.concatenate(deltas, axis=1)
            put(1, t, contract(wide, stacked(query, sides), PLAIN) * ratio)
            wide = jnp.concatenate([p.astype(bf16) for p in probs], axis=1)
            put(2, t, contract(wide, stacked(out, sides), PLAIN))
        return carry

    lax.fori_loop(0, cols // part, attend, 0)
    grad_normed = contract(dqkv_ref[...].reshape(rows * cols, lanes), col_ref[...], LAST)
    gain = gain_ref[2:3]
    _, unit, scale = normed(one_ref[...].astype(f32), gain, 0.0)
    norms_ref[0:1] = jnp.sum(grad_normed * unit, axis=0, keepdims=True)
    norms_ref[1:2] = jnp.sum(grad_normed, axis=0, keepdims=True)
    stream = (grad_three + normed_back(grad_normed, unit, scale, gain)).astype(bf16)
    stream_ref[...] = stream
    mixed = contract(stream, three_ref[...], LAST).astype(bf16)
    half = width // 2
    flip = info_ref[2] == 0
    own_ref[...] = jnp.where(flip, mixed[:, :half], mixed[:, half:])
    other_ref[...] = jnp.where(flip, mixed[:, half:], mixed[:, :half])


def whole_call(kernel, info, args, outs, scratch=()):
    inside = pl.BlockSpec(memory_space=pltpu.VMEM)
    return pl.pallas_call(
        kernel,
        in_specs=[pl.BlockSpec(memory_space=pltpu.SMEM)] + [inside] * len(args),
        out_specs=[inside] * len(outs),
        out_shape=[jax.ShapeDtypeStruct(shape, kind) for shape, kind in outs],
        scratch_shapes=list(scratch),
        compiler_params=pltpu.CompilerParams(vmem_limit_bytes=56 * 2**20),
    )(info, *args)


def gelu_pair(u):
    ratio = math.sqrt(2.0 / math.pi)
    square = u * u
    tanh = jnp.tanh(ratio * u * (1.0 + 0.044715 * square))
    rise = 0.5 * (1.0 + tanh)
    slope = (0.5 * ratio) * (1.0 - tanh * tanh) * (1.0 + (3.0 * 0.044715) * square)
    return u * rise, rise + u * slope


def ffn_kernel(
    plan, place_ref, a_ref, a_got_ref, up_ref, up_got_ref, *refs
):
    bf16 = jnp.bfloat16
    stacks, refs = refs[: len(plan)], refs[len(plan) :]
    out_ref, out_other_ref, da_ref, da_other_ref, sent_ref, kept_ref = refs[:6]
    w_ref, tokens_ref, turned_ref, out_sum, da_sum, sem = refs[6:]
    step = pl.program_id(0)
    count, width = a_ref.shape
    chunk = sent_ref.shape[1]

    @pl.when(step == 0)
    def _():
        copies = placing(plan, ffn_at, place_ref, stacks, [w_ref], sem)
        for copy in copies:
            copy.start()
        for n, ref in enumerate((a_ref, a_got_ref, up_ref, up_got_ref)):
            k, at = n // 2, slice((n % 2) * count, (n % 2 + 1) * count)
            tokens_ref[k, at] = ref[...]
            turned_ref[k, :, at] = ref[...].T
        out_sum[...] = jnp.zeros_like(out_sum)
        da_sum[...] = jnp.zeros_like(da_sum)
        for copy in copies:
            copy.wait()

    lane = pl.ds(pl.multiple_of(step * chunk, chunk), chunk)
    w_in = w_ref[:width, lane]
    w_out = w_ref[width:, lane]
    activs, grads = [], []
    for n in (0, 1):
        at = slice(n * count, (n + 1) * count)
        activ, slope = gelu_pair(contract(tokens_ref[0, at], w_in, PLAIN))
        activ = activ.astype(bf16)
        grad = (contract(tokens_ref[1, at], w_out, PLAIN) * slope).astype(bf16)
        out_sum[at] += contract(activ, w_out, LAST)
        da_sum[at] += contract(grad, w_in, LAST)
        activs.append(activ)
        grads.append(grad)
    in_terms = contract(turned_ref[0], jnp.concatenate(grads, axis=0), PLAIN).astype(bf16)
    out_terms = contract(turned_ref[1], jnp.concatenate(activs, axis=0), PLAIN).astype(bf16)
    first = place_ref[3] == 0
    kept_ref[...] = jnp.where(first, in_terms, out_terms)
    sent_ref[...] = jnp.where(first, out_terms, in_terms)

    @pl.when(step == pl.num_programs(0) - 1)
    def _():
        out_ref[...] = out_sum[:count]
        out_other_ref[...] = out_sum[count:].astype(bf16)
        da_ref[...] = da_sum[:count]
        da_other_ref[...] = da_sum[count:].astype(bf16)


def feed_forward(place, normed_own, normed_got, up_own, up_got, pieces, chunk=512):
    count, width = normed_own.shape
    half = pieces[0][1].shape[-1]
    anywhere = pl.BlockSpec(memory_space=pl.ANY)
    inside = pl.BlockSpec(memory_space=pltpu.VMEM)
    lanes = pl.BlockSpec((width, chunk), lambda n: (0, n))
    f32, bf16 = jnp.float32, jnp.bfloat16
    shapes = [((count, width), kind) for kind in (f32, bf16, f32, bf16)] + [((width, half), bf16)] * 2
    return pl.pallas_call(
        partial(ffn_kernel, [step for step, _ in pieces]),
        grid=(half // chunk,),
        in_specs=[pl.BlockSpec(memory_space=pltpu.SMEM)] + [inside] * 4 + [anywhere] * len(pieces),
        out_specs=[inside] * 4 + [lanes] * 2,
        out_shape=[jax.ShapeDtypeStruct(shape, kind) for shape, kind in shapes],
        scratch_shapes=[
            pltpu.VMEM((2 * width, half), bf16),
            pltpu.VMEM((2, 2 * count, width), bf16),
            pltpu.VMEM((2, width, 2 * count), bf16),
            pltpu.VMEM((2 * count, width), f32),
            pltpu.VMEM((2 * count, width), f32),
            pltpu.SemaphoreType.DMA((16,)),
        ],
        compiler_params=pltpu.CompilerParams(vmem_limit_bytes=56 * 2**20),
    )(place, normed_own, normed_got, up_own, up_got, *[value for _, value in pieces])


def added(a, b):
    return (a.astype(jnp.float32) + b.astype(jnp.float32)).astype(jnp.bfloat16)


def x_summed(blocks, x):
    return added(pick(blocks, x, 1), swap(pick(blocks, 1 - x, 1), "x"))


def z_summed(column, z):
    shard = pick(column, z, 0).astype(jnp.float32)
    for i in (1, 2, 3):
        other = pick(column, lax.bitwise_xor(z, i), 0)
        got = lax.ppermute(other, "z", [(k, k ^ i) for k in range(4)])
        shard = shard + got.astype(jnp.float32)
    return shard.astype(jnp.bfloat16)


def paired_body(
    tokens,
    cotangent,
    col_count,
    row_count,
    attn_weight,
    in_weight,
    out_weight,
    norm_param,
    attn_first,
    attn_second,
    in_first,
    in_second,
    out_first,
    out_second,
    norm_first,
    norm_second,
):
    f32 = jnp.float32
    bf16 = jnp.bfloat16
    z, x, y, c = (lax.axis_index(name) for name in ("z", "x", "y", "c"))
    width = tokens.shape[-1]
    hidden = in_weight.shape[1]
    depth = in_weight.shape[0]
    half = width // 2
    hidden_half = hidden // 2

    counts = jnp.stack([col_count, row_count])
    other_counts = swap(counts, "c")
    mine = jnp.where(z // 2 == c, counts, other_counts)
    mine = pick(mine, z % 2, 1)
    cols_live, rows_live = mine[0], mine[1]
    place = jnp.stack([z, x, c, y]).astype(jnp.int32)
    info = jnp.concatenate([place[:3], mine])
    tie = (lax.rsqrt(rows_live.astype(f32)) * (1.0 / math.sqrt(DH))).reshape(1)

    attn_low = attn_weight.astype(bf16)
    halves = attn_low.reshape(8, depth, 2, half)
    qkv_half = jnp.moveaxis(pick(halves[:3], c, 2), 0, 1).reshape(depth, 3 * half)
    norm_row = jnp.pad(
        norm_param.astype(bf16).reshape(1, 6 * depth), ((0, 15), (0, 3 * half - 6 * depth))
    )
    row_z = gather_z(jnp.concatenate([qkv_half, norm_row]))
    w_row, norm_rows = placed_pieces(
        [((0, 0, 0), row_z), ((1, 0, 0), swap(row_z, "x"))],
        row_attn_at,
        [(width, 3 * half), (8, 16, 3 * half)],
        place,
        16,
    )
    norm_gain = norm_rows[:, 0, : 6 * depth].reshape(8, 6, depth)
    norm_gain = jnp.moveaxis(norm_gain, 0, 1).reshape(6, width).astype(f32)
    col_quarter = pick(pick(halves[3:], c, 2).reshape(5, 2, depth // 2, half), y, 1)
    col_z = gather_z(after(col_quarter, row_z))

    ffn_low = [in_weight.astype(bf16), out_weight.astype(bf16).T]
    ffn_low = [
        jnp.where(c == 0, low[:, :hidden_half], low[:, hidden_half:]) for low in ffn_low
    ]
    ffn_z = gather_z(after(jnp.where(y == 0, *ffn_low), col_z))

    stream_zero = to_columns(tokens, c)
    rows, part, _ = stream_zero.shape
    count = rows * part
    resid_one = stream_zero.reshape(count, width).astype(f32)
    normed_one = layer_norm(resid_one, norm_gain[0], norm_gain[1]).astype(bf16)
    col_z = after(col_z, normed_one)
    w_three, w_col, w_seven = placed_pieces(
        both_cores(spread(col_z)),
        col_attn_at,
        [(width, width), (width, 3 * width), (width, width)],
        place,
        8 * 4 * 5,
    )
    near_normed = after(jnp.concatenate([normed_one, swap(normed_one, "c")]), col_z)
    far_first = swap(normed_one, "x")
    far_normed = jnp.concatenate([far_first, swap(far_first, "c")])
    near = contract(near_normed, w_row, PLAIN).astype(bf16).reshape(2, rows, part, 3 * half)
    far = contract(far_normed, w_row[:, half:], PLAIN).astype(bf16)
    far = far.reshape(2, rows, part, 2 * half)
    ffn_pieces = spread(ffn_z)
    mixed_heads = row_attention(info, tie, after(near, ffn_z), far).reshape(2, count, half)

    whole_shape, wide_shape = ((count, width), bf16), ((rows, part, 3 * width), bf16)
    stream_zero = stream_zero.reshape(count, width)
    mixed_one, stream_one, normed_two, qkv_two, mixed_two, resid_three, normed_three = whole_call(
        col_fwd_kernel,
        info,
        [
            stream_zero,
            mixed_heads[0],
            swap(mixed_heads[1], "c"),
            w_three,
            w_col,
            w_seven,
            norm_gain,
        ],
        [whole_shape] * 3
        + [wide_shape, ((rows, part, width), bf16), ((count, width), f32), whole_shape],
    )
    mixed_two = mixed_two.reshape(count, width)

    up = to_columns(after(cotangent, mixed_heads), c)
    column = x * (2 * part) + c * part + jnp.arange(part, dtype=jnp.int32)
    live = jnp.logical_and(
        (jnp.arange(rows, dtype=jnp.int32) < rows_live)[:, None], (column < cols_live)[None, :]
    )
    up = jnp.where(live[..., None], up, jnp.zeros_like(up)).reshape(count, width)
    out_own, out_other, da_own, da_other, ffn_sent, ffn_kept = feed_forward(
        place, normed_three, swap(normed_three, "c"), up, swap(up, "c"), ffn_pieces
    )
    da_got = swap(da_other, "c")
    result = (resid_three + out_own + swap(out_other, "c").astype(f32)).astype(bf16)
    block_out = to_rows(result.reshape(rows, part, width), c)
    ffn_pair = added(ffn_kept, swap(ffn_sent, "y"))

    branch_shape = ((count, width), bf16)
    grad_branch_two, grad_qkv_two, grad_stream, grad_own, grad_other, col_norms = whole_call(
        col_bwd_kernel,
        info,
        [
            up,
            da_own,
            da_got,
            resid_three,
            stream_one,
            qkv_two,
            w_three,
            w_col,
            w_seven,
            norm_gain,
        ],
        [branch_shape, wide_shape, branch_shape]
        + [((count, half), bf16)] * 2
        + [((4, width), f32)],
        [pltpu.VMEM((rows, part, width), bf16)],
    )
    grad_qkv_two = grad_qkv_two.reshape(count, 3 * width)

    def lanes_of(value, which, groups):
        size = value.shape[1] // (2 * groups)
        first, second = (
            [value[:, (2 * n + k) * size : (2 * n + k + 1) * size] for n in range(groups)]
            for k in (0, 1)
        )
        chosen = [jnp.where(which == 0, a, b) for a, b in zip(first, second)]
        return chosen[0] if groups == 1 else jnp.concatenate(chosen, axis=1)

    def over_cores(sides):
        sent = [contract(a, lanes_of(b, 1 - c, g), FIRST).astype(bf16) for a, b, g in sides]
        got = [swap(value, "c") for value in sent]
        kept = [contract(a, lanes_of(b, c, g), FIRST) for a, b, g in sides]
        return [(k + v.astype(f32)).astype(bf16) for k, v in zip(kept, got)]

    attn_terms = over_cores(
        [
            (mixed_one, grad_stream, 1),
            (normed_two, grad_qkv_two, 3),
            (mixed_two, grad_branch_two, 1),
        ]
    )
    attn_terms = jnp.concatenate(attn_terms, axis=1).reshape(8, 2, depth // 2, 5 * half)
    attn_pair_terms = added(pick(attn_terms, y, 1), swap(pick(attn_terms, 1 - y, 1), "y"))

    grad_heads = jnp.stack([grad_own, swap(grad_other, "c")]).reshape(2, rows, part, half)
    ffn_column = x_summed(ffn_pair.reshape(4, 2, depth, hidden_half), x)
    dq, dk, dv, dk_far, dv_far = row_attention_back(
        info, tie, near, far, after(grad_heads, ffn_pair)
    )
    grad_near = jnp.concatenate([dq, dk, dv], axis=-1).reshape(2 * count, 3 * half)
    grad_far = jnp.concatenate([dk_far, dv_far], axis=-1).reshape(2 * count, 2 * half)
    row_terms = contract(near_normed, grad_near, FIRST)
    far_terms = contract(far_normed, grad_far, FIRST)
    row_terms = jnp.concatenate([row_terms[:, :half], row_terms[:, half:] + far_terms], axis=1)
    row_column = x_summed(row_terms.astype(bf16).reshape(4, 2, depth, 3 * half), x)
    far_part = contract(grad_far, w_row[:, half:], LAST).reshape(2, count, width)
    far_sum = far_part[0] + swap(far_part[1].astype(bf16), "c").astype(f32)
    far_got = swap(far_sum.astype(bf16), "x")
    near_part = contract(grad_near, w_row, LAST).reshape(2, count, width)
    near_got = swap(near_part[1].astype(bf16), "c")
    grad_normed_one = near_part[0] + near_got.astype(f32) + far_got.astype(f32)
    _, norm_back_one = jax.vjp(layer_norm, resid_one, norm_gain[0], norm_gain[1])
    part_one, gain_grad_one, shift_grad_one = norm_back_one(grad_normed_one)
    grad_input = (grad_stream.astype(f32) + part_one).astype(bf16)
    grad_tokens = to_rows(grad_input.reshape(rows, part, width), c).astype(f32)

    norm_stack = jnp.concatenate([jnp.stack([gain_grad_one, shift_grad_one]), col_norms])
    norm_terms = jnp.moveaxis(norm_stack.reshape(6, 4, 2, depth), 0, 2).reshape(4, 2, 1, 6 * depth)
    norm_terms = jnp.pad(norm_terms, ((0, 0), (0, 0), (0, 15), (0, 3 * half - 6 * depth)))
    norm_column = x_summed(norm_terms.astype(bf16), x)
    attn_column = x_summed(attn_pair_terms.reshape(4, 2, depth // 2, 5 * half), x)

    ffn_own = z_summed(ffn_column, z)
    attn_own = z_summed(attn_column, z)
    row_own = z_summed(jnp.concatenate([row_column, norm_column], axis=1), z)
    row_grad = added(row_own, swap(row_own, "y"))
    ffn_grads = [ffn_own, swap(ffn_own, "y")]
    attn_grad_b = joined(attn_own, swap(attn_own, "y"), y, 0)

    row_other = swap(row_grad, "c")
    attn_other = swap(attn_grad_b, "c")
    ffn_whole = [joined(piece, swap(piece, "c"), c, 1) for piece in ffn_grads]
    norm_grad = row_grad[depth, : 6 * depth].astype(f32) + row_other[depth, : 6 * depth].astype(f32)
    norm_grad = norm_grad.reshape(6, depth)

    def whole(own, other, groups):
        size = own.shape[1] // groups
        return [
            joined(
                own[:depth, n * size : (n + 1) * size], other[:depth, n * size : (n + 1) * size], c, 1
            )
            for n in range(groups)
        ]

    attn_grad = jnp.stack(whole(row_grad, row_other, 3) + whole(attn_grad_b, attn_other, 5))
    attn_grad = attn_grad.astype(f32)
    in_grad = jnp.where(y == 0, *ffn_whole).astype(f32)
    out_grad = jnp.where(y == 0, *ffn_whole[::-1]).astype(f32).T

    squares = sum(
        jnp.sum(jnp.square(g.astype(f32))) for g in (row_grad[:depth], attn_grad_b, *ffn_grads)
    )
    squares = squares + swap(squares, "c") + jnp.sum(norm_grad * norm_grad)
    squares = squares + swap(squares, "x")
    squares = squares + lax.ppermute(squares, "z", [(k, k ^ 1) for k in range(4)])
    squares = squares + lax.ppermute(squares, "z", [(k, k ^ 2) for k in range(4)])
    grad_norm = jnp.sqrt(squares)
    factor = clip_bound / jnp.maximum(grad_norm, clip_bound)
    attn_first_new, attn_second_new, attn_weight_new = adam_update(
        attn_weight, attn_first, attn_second, attn_grad * factor, matrix_rate
    )
    in_first_new, in_second_new, in_weight_new = adam_update(
        in_weight, in_first, in_second, in_grad * factor, matrix_rate
    )
    out_first_new, out_second_new, out_weight_new = adam_update(
        out_weight, out_first, out_second, out_grad * factor, matrix_rate
    )
    norm_first_new, norm_second_new, norm_new = adam_update(
        norm_param, norm_first, norm_second, norm_grad * factor, norm_rate
    )
    return (
        block_out,
        grad_tokens,
        grad_norm,
        attn_first_new,
        attn_second_new,
        attn_weight_new,
        attn_weight_new.astype(bf16),
        in_first_new,
        in_second_new,
        in_weight_new,
        in_weight_new.astype(bf16),
        out_first_new,
        out_second_new,
        out_weight_new,
        out_weight_new.astype(bf16),
        norm_first_new,
        norm_second_new,
        norm_new,
    )


def paired_layout(mesh):
    return dict(mesh.shape) == {"seq": 8, "grp": 4}


def mapped(run, mesh, seq, grp):
    placed = (
        P(grp, seq, None, None),
        P(grp, seq, None, None),
        P(grp),
        P(grp),
        P(None, seq, None),
        P(seq, None),
        P(None, seq),
        P(None, seq),
        P(None, seq, None),
        P(None, seq, None),
        P(seq, None),
        P(seq, None),
        P(None, seq),
        P(None, seq),
        P(None, seq),
        P(None, seq),
    )
    return jax.shard_map(
        run,
        mesh=mesh,
        in_specs=placed,
        out_specs=(
            P(grp, seq, None, None),
            P(grp, seq, None, None),
            P(),
            P(None, seq, None),
            P(None, seq, None),
            P(None, seq, None),
            P(None, seq, None),
            P(seq, None),
            P(seq, None),
            P(seq, None),
            P(seq, None),
            P(None, seq),
            P(None, seq),
            P(None, seq),
            P(None, seq),
            P(None, seq),
            P(None, seq),
            P(None, seq),
        ),
        check_vma=False,
    )


def solution(mesh):
    if not paired_layout(mesh):
        return mapped(general_body, mesh, "seq", "grp")
    fine = Mesh(mesh.devices.reshape(4, 2, 2, 2), ("z", "x", "y", "c"))
    return mapped(paired_body, fine, ("z", "x"), ("y", "c"))
```

```python
from functools import partial
import math

import jax
import jax.numpy as jnp
from jax import lax
from jax.experimental import pallas as pl
from jax.experimental.pallas import tpu as pltpu
from jax.sharding import Mesh
from jax.sharding import PartitionSpec as P

H = 12
DH = 64
STEP = 5


eps_norm = 1e-05
masked_score = -1000000000.0
clip_bound = 1.0
beta_one = 0.5
beta_two = 0.5
matrix_rate = 0.06
norm_rate = 0.3
decay_rate = 0.01
adam_eps = 1e-08


def in_blocks(x, dim, length):
    lengths = x.shape
    pieces = x.reshape(*lengths[:dim], length, lengths[dim] // length, *lengths[dim + 1 :])
    return jnp.moveaxis(pieces, dim, 0)


def sent_and_summed(x, axis, dim):
    length = lax.axis_size(axis)
    pieces = lax.all_to_all(in_blocks(x, dim, length), axis, 0, 0, tiled=True)
    return jnp.sum(pieces.astype(jnp.float32), axis=0)


def layer_norm(value, gain, shift):
    mean = jnp.mean(value, axis=-1, keepdims=True)
    centred = value - mean
    spread = jnp.mean(centred * centred, axis=-1, keepdims=True)
    return centred * lax.rsqrt(spread + eps_norm) * gain + shift


def softmax_rows(scores, keep):
    scores = jnp.where(keep, scores, masked_score)
    top = jnp.max(scores, axis=-1, keepdims=True)
    expo = jnp.exp(scores - top)
    return expo / jnp.sum(expo, axis=-1, keepdims=True)


def softmax_back(probs, grads):
    return probs * (grads - jnp.sum(probs * grads, axis=-1, keepdims=True))


def adam_update(weight, first, second, grad, rate):
    first_new = beta_one * first + (1.0 - beta_one) * grad
    second_new = beta_two * second + (1.0 - beta_two) * grad * grad
    first_hat = first_new / (1.0 - beta_one**STEP)
    second_hat = second_new / (1.0 - beta_two**STEP)
    weight_new = weight - rate * (
        first_hat / (jnp.sqrt(second_hat) + adam_eps) + decay_rate * weight
    )
    return (first_new, second_new, weight_new)


def attn_pair(normed, grad_proj, mixed, grad_branch):
    width = normed.shape[-1]
    qkv_terms = jnp.einsum("prcd,kprce->dke", normed, grad_proj, preferred_element_type=jnp.float32)
    output_terms = jnp.einsum(
        "prcd,prce->de", mixed, grad_branch, preferred_element_type=jnp.float32
    )
    return jnp.concatenate([qkv_terms, output_terms[:, None, :]], axis=1).reshape(width, 4 * width)


def general_body(
    tokens,
    cotangent,
    col_count,
    row_count,
    attn_weight,
    in_weight,
    out_weight,
    norm_param,
    attn_first,
    attn_second,
    in_first,
    in_second,
    out_first,
    out_second,
    norm_first,
    norm_second,
):
    f32 = jnp.float32
    bf16 = jnp.bfloat16
    prot, rows_dev, cols, width = tokens.shape
    hidden = in_weight.shape[1]
    head_scale = 1.0 / math.sqrt(DH)
    attn_full, in_full, out_full, norm_full = (
        lax.all_gather(attn_weight.astype(bf16), "seq", axis=1, tiled=True),
        lax.all_gather(in_weight.astype(bf16), "seq", axis=0, tiled=True),
        lax.all_gather(out_weight.astype(bf16), "seq", axis=1, tiled=True),
        lax.all_gather(norm_param.astype(bf16), "seq", axis=1, tiled=True),
    )
    norm_gain = norm_full.astype(f32)
    row_ids = lax.axis_index("seq") * rows_dev + jnp.arange(rows_dev, dtype=jnp.int32)
    row_live = (row_ids[None, :] < row_count[:, None]).astype(f32)
    col_live = jnp.arange(cols, dtype=jnp.int32)[None, :] < col_count[:, None]
    tie_scale = lax.rsqrt(row_count.astype(f32)) * head_scale
    live = row_live[:, :, None] * col_live.astype(f32)[:, None, :]
    grad_out = (cotangent.astype(f32) * live[..., None]).astype(bf16)
    resid_one = tokens.astype(f32)
    normed_one = layer_norm(resid_one, norm_gain[0], norm_gain[1]).astype(bf16)
    proj_one = jnp.einsum(
        "prcd,kde->kprce", normed_one, attn_full[0:3], preferred_element_type=f32
    ).astype(bf16)
    proj_one = proj_one.reshape(3, prot, rows_dev, cols, H, DH)
    query_one, key_one, value_one = (proj_one[0], proj_one[1], proj_one[2])
    masked_query = query_one * row_live[:, :, None, None, None].astype(bf16)
    partial_scores = (
        jnp.einsum("prihe,prjhe->phij", masked_query, key_one, preferred_element_type=f32)
        * tie_scale[:, None, None, None]
    )
    keep_cols = col_live[:, None, None, :]
    score_part = lax.psum_scatter(partial_scores, "seq", scatter_dimension=2, tiled=True)
    probs_one = softmax_rows(score_part, keep_cols)
    probs_low = lax.all_gather(probs_one.astype(bf16), "seq", axis=2, tiled=True)
    mixed_one = jnp.einsum(
        "phij,prjhe->prihe", probs_low, value_one, preferred_element_type=f32
    ).astype(bf16)
    mixed_one = mixed_one.reshape(prot, rows_dev, cols, width)
    branch_one = jnp.einsum("prcd,de->prce", mixed_one, attn_full[3], preferred_element_type=f32)
    stream_one = (resid_one + branch_one).astype(bf16)
    stream_cols, up_grad = (
        lax.all_to_all(stream_one, "seq", split_axis=2, concat_axis=1, tiled=True),
        lax.all_to_all(grad_out, "seq", split_axis=2, concat_axis=1, tiled=True),
    )
    rows = stream_cols.shape[1]
    cols_dev = stream_cols.shape[2]
    row_live_all = jnp.arange(rows, dtype=jnp.int32)[None, :] < row_count[:, None]
    resid_two = stream_cols.astype(f32)
    normed_two = layer_norm(resid_two, norm_gain[2], norm_gain[3]).astype(bf16)
    proj_two = jnp.einsum(
        "prcd,kde->kprce", normed_two, attn_full[4:7], preferred_element_type=f32
    ).astype(bf16)
    proj_two = proj_two.reshape(3, prot, rows, cols_dev, H, DH)
    query_two, key_two, value_two = (proj_two[0], proj_two[1], proj_two[2])
    scores_two = (
        jnp.einsum("prche,psche->pchrs", query_two, key_two, preferred_element_type=f32)
        * head_scale
    )
    probs_two = softmax_rows(scores_two, row_live_all[:, None, None, None, :])
    probs_two_low = probs_two.astype(bf16)
    mixed_two = jnp.einsum(
        "pchrs,psche->prche", probs_two_low, value_two, preferred_element_type=f32
    ).astype(bf16)
    mixed_two = mixed_two.reshape(prot, rows, cols_dev, width)
    resid_three = resid_two + jnp.einsum(
        "prcd,de->prce", mixed_two, attn_full[7], preferred_element_type=f32
    )
    normed_three = layer_norm(resid_three, norm_gain[4], norm_gain[5]).astype(bf16)
    inner = jnp.einsum("prcd,df->prcf", normed_three, in_full, preferred_element_type=f32)
    activ = jax.nn.gelu(inner, approximate=True).astype(bf16)
    result = (
        resid_three + jnp.einsum("prcf,fd->prcd", activ, out_full, preferred_element_type=f32)
    ).astype(bf16)
    block_out = lax.all_to_all(result, "seq", split_axis=1, concat_axis=2, tiled=True)
    grad_act = jnp.einsum("prcd,fd->prcf", up_grad, out_full, preferred_element_type=f32)
    _, gelu_back = jax.vjp(partial(jax.nn.gelu, approximate=True), inner)
    grad_inner = gelu_back(grad_act)[0].astype(bf16)
    grad_normed_three = jnp.einsum("prcf,df->prcd", grad_inner, in_full, preferred_element_type=f32)
    _, norm_back_three = jax.vjp(layer_norm, resid_three, norm_gain[4], norm_gain[5])
    part_three, gain_grad_three, shift_grad_three = norm_back_three(grad_normed_three)
    grad_three = up_grad.astype(f32) + part_three
    grad_branch_two = grad_three.astype(bf16)
    grad_mixed_two = jnp.einsum(
        "prce,de->prcd", grad_branch_two, attn_full[7], preferred_element_type=f32
    ).astype(bf16)
    grad_mixed_two = grad_mixed_two.reshape(prot, rows, cols_dev, H, DH)
    grad_probs_two = jnp.einsum(
        "prche,psche->pchrs", grad_mixed_two, value_two, preferred_element_type=f32
    )
    grad_value_two = jnp.einsum(
        "pchrs,prche->psche", probs_two_low, grad_mixed_two, preferred_element_type=f32
    )
    grad_scores_two = softmax_back(probs_two, grad_probs_two).astype(bf16)
    grad_query_two = (
        jnp.einsum("pchrs,psche->prche", grad_scores_two, key_two, preferred_element_type=f32)
        * head_scale
    )
    grad_key_two = (
        jnp.einsum("pchrs,prche->psche", grad_scores_two, query_two, preferred_element_type=f32)
        * head_scale
    )
    grad_proj_two = jnp.stack([grad_query_two, grad_key_two, grad_value_two]).astype(bf16)
    grad_proj_two = grad_proj_two.reshape(3, prot, rows, cols_dev, width)
    grad_normed_two = jnp.einsum(
        "kprce,kde->prcd", grad_proj_two, attn_full[4:7], preferred_element_type=f32
    )
    _, norm_back_two = jax.vjp(layer_norm, resid_two, norm_gain[2], norm_gain[3])
    part_two, gain_grad_two, shift_grad_two = norm_back_two(grad_normed_two)
    grad_stream = (grad_three + part_two).astype(bf16)
    col_attn_terms = attn_pair(normed_two, grad_proj_two, mixed_two, grad_branch_two)
    in_terms = jnp.einsum("prcd,prcf->df", normed_three, grad_inner, preferred_element_type=f32)
    out_terms = jnp.einsum("prcf,prcd->df", activ, up_grad, preferred_element_type=f32)
    grad_rows = lax.all_to_all(grad_stream, "seq", split_axis=1, concat_axis=2, tiled=True)
    grad_mixed_one = jnp.einsum(
        "prce,de->prcd", grad_rows, attn_full[3], preferred_element_type=f32
    ).astype(bf16)
    grad_mixed_one = grad_mixed_one.reshape(prot, rows_dev, cols, H, DH)
    partial_grads = jnp.einsum(
        "prihe,prjhe->phij", grad_mixed_one, value_one, preferred_element_type=f32
    )
    grad_value_one = jnp.einsum(
        "phij,prihe->prjhe", probs_low, grad_mixed_one, preferred_element_type=f32
    )
    grad_part = sent_and_summed(partial_grads.astype(jnp.bfloat16), "seq", 2)
    grad_scores_one = lax.all_gather(
        softmax_back(probs_one, grad_part).astype(bf16), "seq", axis=2, tiled=True
    )
    tie_rows = row_live[:, :, None, None, None] * tie_scale[:, None, None, None, None]
    grad_query_one = (
        jnp.einsum("phij,prjhe->prihe", grad_scores_one, key_one, preferred_element_type=f32)
        * tie_rows
    )
    grad_key_one = (
        jnp.einsum("phij,prihe->prjhe", grad_scores_one, masked_query, preferred_element_type=f32)
        * tie_scale[:, None, None, None, None]
    )
    grad_proj_one = jnp.stack([grad_query_one, grad_key_one, grad_value_one]).astype(bf16)
    grad_proj_one = grad_proj_one.reshape(3, prot, rows_dev, cols, width)
    grad_normed_one = jnp.einsum(
        "kprce,kde->prcd", grad_proj_one, attn_full[0:3], preferred_element_type=f32
    )
    _, norm_back_one = jax.vjp(layer_norm, resid_one, norm_gain[0], norm_gain[1])
    part_one, gain_grad_one, shift_grad_one = norm_back_one(grad_normed_one)
    grad_tokens = grad_rows.astype(f32) + part_one
    norm_stack = jnp.stack(
        [
            gain_grad_one,
            shift_grad_one,
            gain_grad_two,
            shift_grad_two,
            gain_grad_three,
            shift_grad_three,
        ]
    )
    row_attn_terms = attn_pair(normed_one, grad_proj_one, mixed_one, grad_rows)
    owned = lax.psum_scatter(
        jnp.concatenate(
            [row_attn_terms, col_attn_terms, in_terms, out_terms, norm_stack.T], axis=1
        ),
        "seq",
        scatter_dimension=0,
        tiled=True,
    )
    width_dev = owned.shape[0]
    row_part = owned[:, : 4 * width].reshape(width_dev, 4, width)
    col_part = owned[:, 4 * width : 8 * width].reshape(width_dev, 4, width)
    in_part = owned[:, 8 * width : 8 * width + hidden]
    out_part = owned[:, 8 * width + hidden : 8 * width + 2 * hidden].T
    norm_part = owned[:, 8 * width + 2 * hidden :].T
    attn_part = jnp.concatenate([row_part, col_part], axis=1).transpose(1, 0, 2)
    attn_grad, in_grad, out_grad, norm_grad = (
        lax.psum(attn_part.astype(jnp.bfloat16), "grp").astype(jnp.float32),
        lax.psum(in_part.astype(jnp.bfloat16), "grp").astype(jnp.float32),
        lax.psum(out_part.astype(jnp.bfloat16), "grp").astype(jnp.float32),
        lax.psum(norm_part.astype(jnp.bfloat16), "grp").astype(jnp.float32),
    )
    squares = (
        jnp.sum(attn_grad * attn_grad)
        + jnp.sum(in_grad * in_grad)
        + jnp.sum(out_grad * out_grad)
        + jnp.sum(norm_grad * norm_grad)
    )
    grad_norm = jnp.sqrt(lax.psum(squares, "seq"))
    factor = clip_bound / jnp.maximum(grad_norm, clip_bound)
    attn_first_new, attn_second_new, attn_weight_new = adam_update(
        attn_weight, attn_first, attn_second, attn_grad * factor, matrix_rate
    )
    in_first_new, in_second_new, in_weight_new = adam_update(
        in_weight, in_first, in_second, in_grad * factor, matrix_rate
    )
    out_first_new, out_second_new, out_weight_new = adam_update(
        out_weight, out_first, out_second, out_grad * factor, matrix_rate
    )
    norm_first_new, norm_second_new, norm_new = adam_update(
        norm_param, norm_first, norm_second, norm_grad * factor, norm_rate
    )
    return (
        block_out,
        grad_tokens,
        grad_norm,
        attn_first_new,
        attn_second_new,
        attn_weight_new,
        attn_weight_new.astype(bf16),
        in_first_new,
        in_second_new,
        in_weight_new,
        in_weight_new.astype(bf16),
        out_first_new,
        out_second_new,
        out_weight_new,
        out_weight_new.astype(bf16),
        norm_first_new,
        norm_second_new,
        norm_new,
    )


PAIR = [(0, 1), (1, 0)]
TILE = 128


def swap(value, axis):
    return lax.ppermute(value, axis, PAIR)


def pick(value, index, axis):
    return lax.dynamic_index_in_dim(value, index, axis, keepdims=False)


def joined(own, other, place, axis):
    return jnp.where(
        place == 0,
        jnp.concatenate([own, other], axis=axis),
        jnp.concatenate([other, own], axis=axis),
    )


def merge(own, other, place, axis):
    return jnp.where(
        place == 0,
        jnp.stack([own, other], axis=axis),
        jnp.stack([other, own], axis=axis),
    )


def merge_cores(value, c):
    prot, _, cols, width = value.shape
    part = cols // 4
    split = value.reshape(prot, 2, 2, part, width)
    got = swap(pick(split, 1 - c, 2), "c")
    both = merge(pick(split, c, 2), got, c, 0)
    return both.reshape(8, part, width)


def to_rows(value, c):
    rows, part, width = value.shape
    got = lax.all_to_all(value, ("z", "x"), 0, 0, tiled=True)
    got = got.reshape(2, 2, 2, part, width)
    other = swap(pick(got, 1 - c, 0), "c")
    both = merge(pick(got, c, 0), other, c, 2)
    return both.reshape(2, 1, 4 * part, width)


def together(*values):
    return lax.optimization_barrier(values)


def gather_z(own):
    return [own] + [lax.ppermute(own, "z", [(k, k ^ i) for k in range(4)]) for i in (1, 2, 3)]


def spread(over_z):
    over_x = swap(over_z, "x")
    quarter = [((0, 0, 0), over_z), ((1, 0, 0), over_x)]
    return quarter + [((j, 1, 0), swap(value, "y")) for (j, _, _), value in quarter]


def both_cores(half):
    return half + [((j, m, 1), swap(value, "c")) for (j, m, _), value in half]


def placing(plan, outs_at, place_ref, stacks, outs, sem):
    copies = []
    for stack, (j, m, k) in zip(stacks, plan):
        x, y, c = (lax.bitwise_xor(place_ref[n], step) for n, step in ((1, j), (3, m), (2, k)))
        for i in range(4):
            shard = lax.bitwise_xor(place_ref[0], i) * 2 + x
            for source, target in outs_at(stack.at[i], outs, shard, y, c):
                copies.append(pltpu.make_async_copy(source, target, sem.at[len(copies)]))
    return copies


def place_kernel(plan, outs_at, place_ref, *refs):
    stacks = refs[: len(plan)]
    copies = placing(plan, outs_at, place_ref, stacks, refs[len(plan) : -1], refs[-1])
    for copy in copies:
        copy.start()
    for copy in copies:
        copy.wait()


def placed_pieces(pieces, outs_at, outs, place, count):
    anywhere = pl.BlockSpec(memory_space=pl.ANY)
    return pl.pallas_call(
        partial(place_kernel, [step for step, _ in pieces], outs_at),
        in_specs=[pl.BlockSpec(memory_space=pltpu.SMEM)] + [anywhere] * len(pieces),
        out_specs=[pl.BlockSpec(memory_space=pltpu.VMEM)] * len(outs),
        out_shape=[jax.ShapeDtypeStruct(shape, jnp.bfloat16) for shape in outs],
        scratch_shapes=[pltpu.SemaphoreType.DMA((count,))],
        compiler_params=pltpu.CompilerParams(
            vmem_limit_bytes=sum(2 * math.prod(s) for s in outs) + 2 * 2**20
        ),
    )(place, *[value for _, value in pieces])


def row_attn_at(ref, outs, shard, y, c):
    depth = outs[0].shape[0] // 16
    at = pl.multiple_of((shard * 2 + y) * depth, depth)
    return [
        (ref.at[pl.ds(0, depth)], outs[0].at[pl.ds(at, depth)]),
        (ref.at[pl.ds(depth, 16)], outs[1].at[shard * 2 + y]),
    ]


def ffn_at(ref, outs, shard, y, c):
    depth = ref.shape[0]
    at = pl.multiple_of((y * 8 + shard) * depth, depth)
    return [(ref, outs[0].at[pl.ds(at, depth)])]


def col_attn_at(ref, outs, shard, y, c):
    depth, half = ref.shape[1], ref.shape[2]
    at = pl.multiple_of((shard * 2 + y) * depth, depth)
    moves = []
    slots = [(o, n) for o, out in enumerate(outs) for n in range(out.shape[1] // (2 * half))]
    for k, (o, n) in enumerate(slots):
        lane = pl.multiple_of(c * half + n * 2 * half, TILE)
        moves.append((ref.at[k], outs[o].at[pl.ds(at, depth), pl.ds(lane, half)]))
    return moves


def contract(a, b, dims):
    return lax.dot_general(a, b, (dims, ((), ())), preferred_element_type=jnp.float32)


LAST = ((1,), (1,))
FIRST = ((0,), (0,))
PLAIN = ((1,), (0,))


def softmax_of(scores, keep):
    scores = jnp.where(keep, scores, masked_score)
    expo = jnp.exp(scores - jnp.max(scores, axis=-1, keepdims=True))
    return expo / jnp.sum(expo, axis=-1, keepdims=True)


def head_lanes(lanes):
    side = lax.broadcasted_iota(jnp.int32, (1, lanes), 1) % TILE < DH
    return (side, jnp.logical_not(side))


def only(keep, value):
    return jnp.where(keep, value, jnp.zeros_like(value))


def column_keep(info_ref, own_cols, near, part):
    key = lax.broadcasted_iota(jnp.int32, (1, 2 * near), 1)
    far = key >= near
    inner = key % near
    x = jnp.where(far, 1 - info_ref[1], info_ref[1])
    c = jnp.where(inner >= part, 1 - info_ref[2], info_ref[2])
    column = x * near + c * part + inner % part
    return column < info_ref[3]


def row_pair(ref, row):
    blocks, _, part, lanes = ref.shape
    return jnp.concatenate(
        [ref[:, row + n].reshape(blocks * part, lanes) for n in (0, 1)], axis=1
    )


def live_pair(value, row, info_ref):
    lane = lax.broadcasted_iota(jnp.int32, (1, value.shape[1]), 1) // TILE + row
    return only(lane < info_ref[4], value)


def row_fwd_kernel(info_ref, tie_ref, q_ref, k_ref, v_ref, kf_ref, vf_ref, o_ref):
    blocks, rows, part, lanes = q_ref.shape
    near = blocks * part
    sides = head_lanes(2 * lanes)
    keep = column_keep(info_ref, near, near, part)
    tie = tie_ref[0]
    scores = [jnp.zeros((near, 2 * near), jnp.float32) for _ in sides]
    for row in range(0, rows, 2):
        query = live_pair(row_pair(q_ref, row), row, info_ref)
        key = jnp.concatenate([row_pair(k_ref, row), row_pair(kf_ref, row)], axis=0)
        for n, side in enumerate(sides):
            scores[n] = scores[n] + contract(only(side, query), key, LAST)
    probs = [softmax_of(s * tie, keep).astype(jnp.bfloat16) for s in scores]
    for row in range(0, rows, 2):
        value = jnp.concatenate([row_pair(v_ref, row), row_pair(vf_ref, row)], axis=0)
        mixed = jnp.where(
            sides[0], contract(probs[0], value, PLAIN), contract(probs[1], value, PLAIN)
        ).astype(jnp.bfloat16)
        for n in (0, 1):
            o_ref[:, row + n] = mixed[:, n * lanes : (n + 1) * lanes].reshape(blocks, part, lanes)


def row_bwd_kernel(
    info_ref, tie_ref, near_ref, far_ref, own_ref, got_ref, w_ref, near_tokens_ref, far_tokens_ref,
    near_part_ref, near_theirs_ref, far_part_ref, far_theirs_ref, sent_ref, kept_ref,
    do_ref, d_near_ref, d_far_ref,
):
    bf16 = jnp.bfloat16
    blocks, rows, part, lanes = near_ref.shape
    half = lanes // 3
    near = blocks * part
    sides = head_lanes(2 * TILE)
    keep = column_keep(info_ref, near, near, part)
    tie = tie_ref[0]
    do_ref[0] = own_ref[...].reshape(rows, part, half)
    do_ref[1] = got_ref[...].reshape(rows, part, half)

    for lane in range(0, half, TILE):

        def pair(ref, row, first):
            at = slice(first + lane, first + lane + TILE)
            found = [ref[:, row + n, :, at].reshape(near, TILE) for n in (0, 1)]
            return jnp.concatenate(found, axis=1)

        def both(row, first):
            return jnp.concatenate(
                [pair(near_ref, row, first), pair(far_ref, row, first - half)], axis=0
            )

        scores = [jnp.zeros((near, 2 * near), jnp.float32) for _ in sides]
        grads = [jnp.zeros((near, 2 * near), jnp.float32) for _ in sides]
        for row in range(0, rows, 2):
            query = live_pair(pair(near_ref, row, 0), row, info_ref)
            key, value = both(row, half), both(row, 2 * half)
            out = pair(do_ref, row, 0)
            for n, side in enumerate(sides):
                scores[n] = scores[n] + contract(only(side, query), key, LAST)
                grads[n] = grads[n] + contract(only(side, out), value, LAST)
        probs = [softmax_of(s * tie, keep) for s in scores]
        lows = [p.astype(bf16) for p in probs]
        deltas = [softmax_back(p, g).astype(bf16) for p, g in zip(probs, grads)]
        low_turned = [p.T for p in lows]
        delta_turned = [d.T for d in deltas]
        for row in range(0, rows, 2):
            query = live_pair(pair(near_ref, row, 0), row, info_ref)
            key, out = both(row, half), pair(do_ref, row, 0)
            dq = [contract(d, key, PLAIN) for d in deltas]
            dk = [contract(d, query, PLAIN) for d in delta_turned]
            dv = [contract(p, out, PLAIN) for p in low_turned]
            dq = live_pair(jnp.where(sides[0], dq[0], dq[1]) * tie, row, info_ref).astype(bf16)
            dk = (jnp.where(sides[0], dk[0], dk[1]) * tie).astype(bf16)
            dv = jnp.where(sides[0], dv[0], dv[1]).astype(bf16)

            def put(ref, first, value):
                for n in (0, 1):
                    piece = value[:, n * TILE : (n + 1) * TILE].reshape(blocks, part, TILE)
                    ref[:, row + n, :, first + lane : first + lane + TILE] = piece

            put(d_near_ref, 0, dq)
            put(d_near_ref, half, dk[:near])
            put(d_near_ref, 2 * half, dv[:near])
            put(d_far_ref, 0, dk[near:])
            put(d_far_ref, half, dv[near:])

    count = rows * part
    d_far = d_far_ref[...].reshape(blocks * count, 2 * half)
    far_weights = w_ref[:, half:]
    far_part_ref[...] = contract(d_far[:count], far_weights, LAST)
    far_theirs_ref[...] = contract(d_far[count:], far_weights, LAST).astype(bf16)
    d_near = d_near_ref[...].reshape(blocks * count, lanes)
    near_part_ref[...] = contract(d_near[:count], w_ref[...], LAST)
    near_theirs_ref[...] = contract(d_near[count:], w_ref[...], LAST).astype(bf16)
    near_turned = near_tokens_ref[...].T
    far_turned = far_tokens_ref[...].T
    zs, depth = kept_ref.shape[0], kept_ref.shape[1]
    first = info_ref[1] == 0
    for n in range(3):
        at = slice(n * half, (n + 1) * half)
        terms = contract(near_turned, d_near[:, at], PLAIN)
        if n > 0:
            terms = terms + contract(far_turned, d_far[:, (n - 1) * half : n * half], PLAIN)
        terms = terms.astype(bf16).reshape(zs, 2, depth, half)
        kept_ref[:, :, at] = jnp.where(first, terms[:, 0], terms[:, 1])
        sent_ref[:, :, at] = jnp.where(first, terms[:, 1], terms[:, 0])


def lane_block(shape, first):
    blocks, rows, part, _ = shape
    return pl.BlockSpec((blocks, rows, part, TILE), lambda t: (0, 0, 0, first + t))


def row_attention(info, tie, near, far):
    blocks, rows, part, lanes = near.shape
    tiles = lanes // 3 // TILE
    shape = near.shape
    small = pl.BlockSpec(memory_space=pltpu.SMEM)
    return pl.pallas_call(
        row_fwd_kernel,
        grid=(tiles,),
        in_specs=[small, small]
        + [lane_block(shape, n * tiles) for n in range(3)]
        + [lane_block(shape, n * tiles) for n in range(2)],
        out_specs=lane_block(shape, 0),
        out_shape=jax.ShapeDtypeStruct((blocks, rows, part, lanes // 3), jnp.bfloat16),
        compiler_params=pltpu.CompilerParams(vmem_limit_bytes=32 * 2**20),
    )(info, tie, near, near, near, far, far)


def row_attention_back(info, tie, near, far, own, got, weights, near_tokens, far_tokens):
    blocks, rows, part, lanes = near.shape
    count, width = rows * part, weights.shape[0]
    half = lanes // 3
    f32, bf16 = jnp.float32, jnp.bfloat16
    small = pl.BlockSpec(memory_space=pltpu.SMEM)
    inside = pl.BlockSpec(memory_space=pltpu.VMEM)
    shapes = [((count, width), kind) for kind in (f32, bf16) * 2]
    shapes = shapes + [((4, width // 8, lanes), bf16)] * 2
    return pl.pallas_call(
        row_bwd_kernel,
        in_specs=[small, small] + [inside] * 7,
        out_specs=[inside] * 6,
        out_shape=[jax.ShapeDtypeStruct(shape, kind) for shape, kind in shapes],
        scratch_shapes=[
            pltpu.VMEM((blocks, rows, part, half), bf16),
            pltpu.VMEM((blocks, rows, part, lanes), bf16),
            pltpu.VMEM((blocks, rows, part, 2 * half), bf16),
        ],
        compiler_params=pltpu.CompilerParams(vmem_limit_bytes=56 * 2**20),
    )(info, tie, near, far, own, got, weights, near_tokens, far_tokens)


def normed(value, gain, shift):
    centred = value - jnp.mean(value, axis=-1, keepdims=True)
    scale = lax.rsqrt(jnp.mean(centred * centred, axis=-1, keepdims=True) + eps_norm)
    unit = centred * scale
    return unit * gain + shift, unit, scale


def normed_back(grad, unit, scale, gain):
    inner = grad * gain
    mean = jnp.mean(inner, axis=-1, keepdims=True)
    along = jnp.mean(inner * unit, axis=-1, keepdims=True)
    return scale * (inner - mean - unit * along)


def column_masks(info_ref, rows, part):
    tokens = rows * part
    key = lax.broadcasted_iota(jnp.int32, (tokens, tokens), 0)
    query = lax.broadcasted_iota(jnp.int32, (tokens, tokens), 1)
    same = key % part == query % part
    return jnp.logical_and(same, key // part < info_ref[4])


def stacked(value, sides):
    return jnp.concatenate([only(side, value) for side in sides], axis=0)


def column_probs(query, key, keep, sides):
    scores = contract(stacked(key, sides), query, LAST) * (1.0 / math.sqrt(DH))
    tokens = query.shape[0]
    probs = []
    for n in (0, 1):
        part = jnp.where(keep, scores[n * tokens : (n + 1) * tokens], masked_score)
        expo = jnp.exp(part - jnp.max(part, axis=0, keepdims=True))
        probs.append(expo / jnp.sum(expo, axis=0, keepdims=True))
    return probs


def col_fwd_kernel(
    info_ref, x_ref, own_ref, other_ref, three_ref, col_ref, seven_ref, gain_ref,
    acts_ref, one_ref, qkv_ref, resid_ref, normed_three_ref, mixed_ref,
):
    bf16 = jnp.bfloat16
    rows, cols, lanes = qkv_ref.shape
    width = lanes // 3
    part = 16
    own, other = own_ref[...], other_ref[...]
    flip = info_ref[2] == 0
    mixed_one = jnp.concatenate(
        [jnp.where(flip, own, other), jnp.where(flip, other, own)], axis=1
    )
    acts_ref[:, :width] = mixed_one
    stream = (x_ref[...].astype(jnp.float32) + contract(mixed_one, three_ref[...], PLAIN)).astype(bf16)
    one_ref[...] = stream
    normed_two = normed(stream.astype(jnp.float32), gain_ref[2:3], gain_ref[3:4])[0].astype(bf16)
    acts_ref[:, width : 2 * width] = normed_two
    for n in range(3):
        at = slice(n * width, (n + 1) * width)
        found = contract(normed_two, col_ref[:, at], PLAIN).astype(bf16)
        qkv_ref[:, :, at] = found.reshape(rows, cols, width)
    keep = column_masks(info_ref, rows, part)
    sides = head_lanes(TILE)

    def attend(b, carry):
        at = pl.ds(pl.multiple_of(b * part, part), part)
        def tile(n, t):
            lane = n * width + t * TILE
            return qkv_ref[:, at, lane : lane + TILE].reshape(rows * part, TILE)
        tiles = range(width // TILE)
        probs = [column_probs(tile(0, t), tile(1, t), keep, sides) for t in tiles]
        for t in tiles:
            low = jnp.concatenate(probs[t], axis=0).astype(bf16)
            mixed = contract(low, stacked(tile(2, t), sides), FIRST).astype(bf16)
            mixed_ref[:, at, t * TILE : (t + 1) * TILE] = mixed.reshape(rows, part, TILE)
        return carry

    lax.fori_loop(0, cols // part, attend, 0)
    mixed = mixed_ref[...].reshape(rows * cols, width)
    acts_ref[:, 2 * width :] = mixed
    resid = one_ref[...].astype(jnp.float32) + contract(mixed, seven_ref[...], PLAIN)
    resid_ref[...] = resid
    normed_three_ref[...] = normed(resid, gain_ref[4:5], gain_ref[5:6])[0].astype(bf16)


def col_bwd_kernel(
    info_ref, up_ref, da_ref, da_got_ref, resid_ref, one_ref, qkv_ref, three_ref, col_ref, seven_ref,
    gain_ref, stream_ref, own_ref, other_ref, mine_ref, theirs_ref, norms_ref, dqkv_ref, do_ref,
):
    bf16 = jnp.bfloat16
    f32 = jnp.float32
    rows, cols, lanes = qkv_ref.shape
    width = lanes // 3
    part = 16
    da = da_ref[...] + da_got_ref[...].astype(f32)
    gain = gain_ref[4:5]
    _, unit, scale = normed(resid_ref[...], gain, 0.0)
    grad_three = up_ref[...].astype(f32) + normed_back(da, unit, scale, gain)
    norms_ref[2:3] = jnp.sum(da * unit, axis=0, keepdims=True)
    norms_ref[3:4] = jnp.sum(da, axis=0, keepdims=True)
    branch = grad_three.astype(bf16)
    half = width // 2
    flip = info_ref[2] == 0

    def put_halves(first, value):
        at = slice(first, first + half)
        mine_ref[:, at] = jnp.where(flip, value[:, :half], value[:, half:])
        theirs_ref[:, at] = jnp.where(flip, value[:, half:], value[:, :half])

    put_halves(4 * half, branch)
    do_ref[...] = contract(branch, seven_ref[...], LAST).astype(bf16).reshape(rows, cols, width)
    keep = column_masks(info_ref, rows, part)
    sides = head_lanes(TILE)
    ratio = 1.0 / math.sqrt(DH)

    def attend(b, carry):
        at = pl.ds(pl.multiple_of(b * part, part), part)
        tokens = rows * part

        def tile(n, t):
            lane = n * width + t * TILE
            return qkv_ref[:, at, lane : lane + TILE].reshape(tokens, TILE)

        def out_tile(t):
            return do_ref[:, at, t * TILE : (t + 1) * TILE].reshape(tokens, TILE)

        def put(n, t, value):
            lane = n * width + t * TILE
            dqkv_ref[:, at, lane : lane + TILE] = value.astype(bf16).reshape(rows, part, TILE)

        for t in range(width // TILE):
            query, key, out = tile(0, t), tile(1, t), out_tile(t)
            keys = stacked(key, sides)
            probs = column_probs(query, key, keep, sides)
            grads = contract(stacked(tile(2, t), sides), out, LAST)
            deltas = []
            for n, p in enumerate(probs):
                g = grads[n * tokens : (n + 1) * tokens]
                deltas.append((p * (g - jnp.sum(p * g, axis=0, keepdims=True))).astype(bf16))
            put(0, t, contract(jnp.concatenate(deltas, axis=0), keys, FIRST) * ratio)
            wide = jnp.concatenate(deltas, axis=1)
            put(1, t, contract(wide, stacked(query, sides), PLAIN) * ratio)
            wide = jnp.concatenate([p.astype(bf16) for p in probs], axis=1)
            put(2, t, contract(wide, stacked(out, sides), PLAIN))
        return carry

    lax.fori_loop(0, cols // part, attend, 0)
    dqkv = dqkv_ref[...].reshape(rows * cols, lanes)
    for n in range(3):
        put_halves((n + 1) * half, dqkv[:, n * width : (n + 1) * width])
    grad_normed = contract(dqkv, col_ref[...], LAST)
    gain = gain_ref[2:3]
    _, unit, scale = normed(one_ref[...].astype(f32), gain, 0.0)
    norms_ref[0:1] = jnp.sum(grad_normed * unit, axis=0, keepdims=True)
    norms_ref[1:2] = jnp.sum(grad_normed, axis=0, keepdims=True)
    stream = (grad_three + normed_back(grad_normed, unit, scale, gain)).astype(bf16)
    stream_ref[...] = stream
    put_halves(0, stream)
    mixed = contract(stream, three_ref[...], LAST).astype(bf16)
    own_ref[...] = jnp.where(flip, mixed[:, :half], mixed[:, half:])
    other_ref[...] = jnp.where(flip, mixed[:, half:], mixed[:, :half])


def attn_terms_kernel(place_ref, acts_ref, got_ref, mine_ref, theirs_ref, sent_ref, kept_ref):
    width = acts_ref.shape[1] // 3
    half = width // 2
    depth = sent_ref.shape[1]
    turned = [
        jnp.concatenate([ref[:, n * width : (n + 1) * width].T for ref in (acts_ref, got_ref)], axis=1)
        for n in range(3)
    ]
    first = place_ref[3] == 0
    for n, m in enumerate((0, 1, 1, 1, 2)):
        at = slice(n * half, (n + 1) * half)
        grads = jnp.concatenate([mine_ref[:, at], theirs_ref[:, at]], axis=0)
        terms = contract(turned[m], grads, PLAIN).astype(jnp.bfloat16)
        terms = terms.reshape(sent_ref.shape[0], 2, depth, half)
        kept_ref[:, :, at] = jnp.where(first, terms[:, 0], terms[:, 1])
        sent_ref[:, :, at] = jnp.where(first, terms[:, 1], terms[:, 0])


def whole_call(kernel, info, args, outs, scratch=()):
    inside = pl.BlockSpec(memory_space=pltpu.VMEM)
    return pl.pallas_call(
        kernel,
        in_specs=[pl.BlockSpec(memory_space=pltpu.SMEM)] + [inside] * len(args),
        out_specs=[inside] * len(outs),
        out_shape=[jax.ShapeDtypeStruct(shape, kind) for shape, kind in outs],
        scratch_shapes=list(scratch),
        compiler_params=pltpu.CompilerParams(vmem_limit_bytes=56 * 2**20),
    )(info, *args)


def gelu_pair(u):
    ratio = math.sqrt(2.0 / math.pi)
    square = u * u
    tanh = jnp.tanh(ratio * u * (1.0 + 0.044715 * square))
    rise = 0.5 * (1.0 + tanh)
    slope = (0.5 * ratio) * (1.0 - tanh * tanh) * (1.0 + (3.0 * 0.044715) * square)
    return u * rise, rise + u * slope


def ffn_kernel(
    plan, place_ref, a_ref, a_got_ref, up_ref, up_got_ref, *refs
):
    bf16 = jnp.bfloat16
    stacks, refs = refs[: len(plan)], refs[len(plan) :]
    out_ref, out_other_ref, da_ref, da_other_ref, sent_ref, kept_ref = refs[:6]
    w_ref, tokens_ref, turned_ref, out_sum, da_sum, sem = refs[6:]
    step = pl.program_id(0)
    count, width = a_ref.shape
    chunk = sent_ref.shape[1]

    @pl.when(step == 0)
    def _():
        copies = placing(plan, ffn_at, place_ref, stacks, [w_ref], sem)
        for copy in copies:
            copy.start()
        for n, ref in enumerate((a_ref, a_got_ref, up_ref, up_got_ref)):
            k, at = n // 2, slice((n % 2) * count, (n % 2 + 1) * count)
            tokens_ref[k, at] = ref[...]
            turned_ref[k, :, at] = ref[...].T
        out_sum[...] = jnp.zeros_like(out_sum)
        da_sum[...] = jnp.zeros_like(da_sum)
        for copy in copies:
            copy.wait()

    lane = pl.ds(pl.multiple_of(step * chunk, chunk), chunk)
    w_in = w_ref[:width, lane]
    w_out = w_ref[width:, lane]
    activs, grads = [], []
    for n in (0, 1):
        at = slice(n * count, (n + 1) * count)
        activ, slope = gelu_pair(contract(tokens_ref[0, at], w_in, PLAIN))
        activ = activ.astype(bf16)
        grad = (contract(tokens_ref[1, at], w_out, PLAIN) * slope).astype(bf16)
        out_sum[at] += contract(activ, w_out, LAST)
        da_sum[at] += contract(grad, w_in, LAST)
        activs.append(activ)
        grads.append(grad)
    in_terms = contract(turned_ref[0], jnp.concatenate(grads, axis=0), PLAIN).astype(bf16)
    out_terms = contract(turned_ref[1], jnp.concatenate(activs, axis=0), PLAIN).astype(bf16)
    first = place_ref[3] == 0
    kept_ref[...] = jnp.where(first, in_terms, out_terms)
    sent_ref[...] = jnp.where(first, out_terms, in_terms)

    @pl.when(step == pl.num_programs(0) - 1)
    def _():
        out_ref[...] = out_sum[:count]
        out_other_ref[...] = out_sum[count:].astype(bf16)
        da_ref[...] = da_sum[:count]
        da_other_ref[...] = da_sum[count:].astype(bf16)


def feed_forward(place, normed_own, normed_got, up_own, up_got, pieces, chunk=512):
    count, width = normed_own.shape
    half = pieces[0][1].shape[-1]
    anywhere = pl.BlockSpec(memory_space=pl.ANY)
    inside = pl.BlockSpec(memory_space=pltpu.VMEM)
    lanes = pl.BlockSpec((width, chunk), lambda n: (0, n))
    f32, bf16 = jnp.float32, jnp.bfloat16
    shapes = [((count, width), kind) for kind in (f32, bf16, f32, bf16)] + [((width, half), bf16)] * 2
    return pl.pallas_call(
        partial(ffn_kernel, [step for step, _ in pieces]),
        grid=(half // chunk,),
        in_specs=[pl.BlockSpec(memory_space=pltpu.SMEM)] + [inside] * 4 + [anywhere] * len(pieces),
        out_specs=[inside] * 4 + [lanes] * 2,
        out_shape=[jax.ShapeDtypeStruct(shape, kind) for shape, kind in shapes],
        scratch_shapes=[
            pltpu.VMEM((2 * width, half), bf16),
            pltpu.VMEM((2, 2 * count, width), bf16),
            pltpu.VMEM((2, width, 2 * count), bf16),
            pltpu.VMEM((2 * count, width), f32),
            pltpu.VMEM((2 * count, width), f32),
            pltpu.SemaphoreType.DMA((16,)),
        ],
        compiler_params=pltpu.CompilerParams(vmem_limit_bytes=56 * 2**20),
    )(place, normed_own, normed_got, up_own, up_got, *[value for _, value in pieces])


def added(a, b):
    return (a.astype(jnp.float32) + b.astype(jnp.float32)).astype(jnp.bfloat16)


def z_summed(column, z):
    shard = pick(column, z, 0).astype(jnp.float32)
    for i in (1, 2, 3):
        other = pick(column, lax.bitwise_xor(z, i), 0)
        got = lax.ppermute(other, "z", [(k, k ^ i) for k in range(4)])
        shard = shard + got.astype(jnp.float32)
    return shard.astype(jnp.bfloat16)


def paired_body(
    tokens,
    cotangent,
    col_count,
    row_count,
    attn_weight,
    in_weight,
    out_weight,
    norm_param,
    attn_first,
    attn_second,
    in_first,
    in_second,
    out_first,
    out_second,
    norm_first,
    norm_second,
):
    f32 = jnp.float32
    bf16 = jnp.bfloat16
    z, x, y, c = (lax.axis_index(name) for name in ("z", "x", "y", "c"))
    width = tokens.shape[-1]
    hidden = in_weight.shape[1]
    depth = in_weight.shape[0]
    half = width // 2
    hidden_half = hidden // 2

    counts = jnp.stack([col_count, row_count])
    other_counts = swap(counts, "c")
    mine = jnp.where(z // 2 == c, counts, other_counts)
    mine = pick(mine, z % 2, 1)
    cols_live, rows_live = mine[0], mine[1]
    place = jnp.stack([z, x, c, y]).astype(jnp.int32)
    info = jnp.concatenate([place[:3], mine])
    tie = (lax.rsqrt(rows_live.astype(f32)) * (1.0 / math.sqrt(DH))).reshape(1)

    tokens_here = merge_cores(tokens, c)

    attn_low = attn_weight.astype(bf16)
    halves = attn_low.reshape(8, depth, 2, half)
    row_half = jnp.moveaxis(pick(halves[:3], c, 2), 0, 1).reshape(2, depth // 2, 3 * half)
    norm_row = jnp.pad(
        norm_param.astype(bf16).reshape(1, 6 * depth), ((0, 15), (0, 3 * half - 6 * depth))
    )
    row_quarter = jnp.concatenate([pick(row_half, y, 0), norm_row])
    col_quarter = pick(pick(halves[3:], c, 2).reshape(5, 2, depth // 2, half), y, 1)
    ffn_low = [in_weight.astype(bf16), out_weight.astype(bf16).T]
    ffn_low = [
        jnp.where(c == 0, low[:, :hidden_half], low[:, hidden_half:]) for low in ffn_low
    ]
    ffn_quarter = jnp.where(y == 0, *ffn_low)
    tokens_here, row_quarter, col_quarter, ffn_quarter = together(
        tokens_here, row_quarter, col_quarter, ffn_quarter
    )

    stream_zero = lax.all_to_all(tokens_here, ("z", "x"), 0, 0, tiled=True)
    *row_z, col_quarter = together(*gather_z(row_quarter), col_quarter)
    w_row, norm_rows = placed_pieces(
        spread(jnp.stack(row_z)),
        row_attn_at,
        [(width, 3 * half), (16, 16, 3 * half)],
        place,
        32,
    )
    norm_gain = norm_rows.reshape(8, 2, 16, 3 * half)[:, 0, 0, : 6 * depth].reshape(8, 6, depth)
    norm_gain = jnp.moveaxis(norm_gain, 0, 1).reshape(6, width).astype(f32)
    rows, part, _ = stream_zero.shape
    count = rows * part
    stream_zero = stream_zero.reshape(count, width)
    resid_one = stream_zero.astype(f32)
    normed_one = layer_norm(resid_one, norm_gain[0], norm_gain[1]).astype(bf16)
    *col_z, normed_one, ffn_quarter = together(*gather_z(col_quarter), normed_one, ffn_quarter)
    near_normed = jnp.concatenate([normed_one, swap(normed_one, "c")])
    far_first = swap(normed_one, "x")
    col_pieces = spread(jnp.stack(col_z))
    near = contract(near_normed, w_row, PLAIN).astype(bf16).reshape(2, rows, part, 3 * half)
    ffn_z = gather_z(ffn_quarter)
    far_normed = jnp.concatenate([far_first, swap(far_first, "c")])
    far = contract(far_normed, w_row[:, half:], PLAIN).astype(bf16)
    far, *early = together(far.reshape(2, rows, part, 2 * half), *[v for _, v in col_pieces[:3]])
    col_pieces = [(step, v) for (step, _), v in zip(col_pieces[:3], early)] + col_pieces[3:]
    mixed_heads = row_attention(info, tie, near, far).reshape(2, count, half)
    mixed_heads, cotangent, *ffn_z = together(mixed_heads, cotangent, *ffn_z)
    ffn_pieces = spread(jnp.stack(ffn_z))
    w_three, w_col, w_seven = placed_pieces(
        both_cores(col_pieces),
        col_attn_at,
        [(width, width), (width, 3 * width), (width, width)],
        place,
        8 * 4 * 5,
    )

    whole_shape, wide_shape = ((count, width), bf16), ((rows, part, 3 * width), bf16)
    acts, stream_one, qkv_two, resid_three, normed_three = whole_call(
        col_fwd_kernel,
        info,
        [
            stream_zero,
            mixed_heads[0],
            swap(mixed_heads[1], "c"),
            w_three,
            w_col,
            w_seven,
            norm_gain,
        ],
        [((count, 3 * width), bf16), whole_shape, wide_shape, ((count, width), f32), whole_shape],
        [pltpu.VMEM((rows, part, width), bf16)],
    )

    up = lax.all_to_all(merge_cores(cotangent, c), ("z", "x"), 0, 0, tiled=True)
    column = x * (2 * part) + c * part + jnp.arange(part, dtype=jnp.int32)
    live = jnp.logical_and(
        (jnp.arange(rows, dtype=jnp.int32) < rows_live)[:, None], (column < cols_live)[None, :]
    )
    up = jnp.where(live[..., None], up, jnp.zeros_like(up)).reshape(count, width)
    out_own, out_other, da_own, da_other, ffn_sent, ffn_kept = feed_forward(
        place, normed_three, swap(normed_three, "c"), up, swap(up, "c"), ffn_pieces
    )
    da_got = swap(da_other, "c")
    result = (resid_three + out_own + swap(out_other, "c").astype(f32)).astype(bf16)
    ffn_got = swap(ffn_sent, "y")

    acts_got = swap(acts, "c")
    grad_stream, grad_own, grad_other, attn_mine, attn_theirs, col_norms = whole_call(
        col_bwd_kernel,
        info,
        [
            up,
            da_own,
            da_got,
            resid_three,
            stream_one,
            qkv_two,
            w_three,
            w_col,
            w_seven,
            norm_gain,
        ],
        [whole_shape]
        + [((count, half), bf16)] * 2
        + [((count, 5 * half), bf16)] * 2
        + [((4, width), f32)],
        [pltpu.VMEM((rows, part, 3 * width), bf16), pltpu.VMEM((rows, part, width), bf16)],
    )
    attn_sent, attn_kept = whole_call(
        attn_terms_kernel,
        place,
        [acts, acts_got, attn_mine, swap(attn_theirs, "c")],
        [((8, depth // 2, 5 * half), bf16)] * 2,
    )
    ffn_pair = added(ffn_kept, ffn_got).reshape(4, 2, depth, hidden_half)

    ffn_pair, attn_sent, attn_kept, grad_own = together(ffn_pair, attn_sent, attn_kept, grad_own)
    attn_got = swap(attn_sent, "y")
    ffn_column = added(pick(ffn_pair, x, 1), swap(pick(ffn_pair, 1 - x, 1), "x"))
    near_part, near_theirs, far_part, far_theirs, row_sent, row_kept = row_attention_back(
        info, tie, near, far, grad_own, swap(grad_other, "c"), w_row, near_normed, far_normed
    )
    ffn_column, row_sent, far_theirs, near_theirs = together(
        ffn_column, row_sent, far_theirs, near_theirs
    )
    row_column = added(row_kept, swap(row_sent, "x"))
    far_sum = added(far_part, swap(far_theirs, "c"))
    far_got = swap(far_sum, "x")
    near_got = swap(near_theirs, "c")
    attn_pair_terms = added(attn_kept, attn_got).reshape(4, 2, depth // 2, 5 * half)
    ffn_own = z_summed(ffn_column, z)
    row_column, attn_pair_terms, far_got, ffn_own = together(
        row_column, attn_pair_terms, far_got, ffn_own
    )
    row_own = z_summed(row_column, z)
    grad_normed_one = near_part + near_got.astype(f32) + far_got.astype(f32)
    _, norm_back_one = jax.vjp(layer_norm, resid_one, norm_gain[0], norm_gain[1])
    part_one, gain_grad_one, shift_grad_one = norm_back_one(grad_normed_one)
    grad_input = (grad_stream.astype(f32) + part_one).astype(bf16)
    both_out = jnp.concatenate([result, grad_input], axis=1).reshape(rows, part, 2 * width)
    both_out = to_rows(both_out, c)
    block_out, grad_tokens = both_out[..., :width], both_out[..., width:].astype(f32)

    norm_stack = jnp.concatenate([jnp.stack([gain_grad_one, shift_grad_one]), col_norms])
    norm_terms = jnp.moveaxis(norm_stack.reshape(6, 4, 2, depth), 0, 2).reshape(4, 2, 1, 6 * depth)
    norm_terms = jnp.pad(norm_terms, ((0, 0), (0, 0), (0, 15), (0, 5 * half - 6 * depth)))
    attn_blocks = jnp.concatenate([attn_pair_terms, norm_terms.astype(bf16)], axis=2)
    attn_column = added(pick(attn_blocks, x, 1), swap(pick(attn_blocks, 1 - x, 1), "x"))
    attn_column, row_own = together(attn_column, row_own)
    attn_own = z_summed(attn_column, z)
    row_grad = added(row_own, swap(row_own, "y"))
    attn_y = swap(attn_own, "y")
    attn_grad_b = joined(attn_own[: depth // 2], attn_y[: depth // 2], y, 0)
    norm_grad = added(attn_own[depth // 2 :], attn_y[depth // 2 :])
    ffn_grads = [ffn_own, swap(ffn_own, "y")]

    row_other = swap(row_grad, "c")
    attn_other = swap(jnp.concatenate([attn_grad_b, norm_grad]), "c")
    norm_grad = norm_grad[0, : 6 * depth].astype(f32) + attn_other[depth, : 6 * depth].astype(f32)
    norm_grad = norm_grad.reshape(6, depth)
    ffn_whole = [joined(piece, swap(piece, "c"), c, 1) for piece in ffn_grads]

    def whole(own, other, groups):
        size = own.shape[1] // groups
        return [
            joined(
                own[:depth, n * size : (n + 1) * size], other[:depth, n * size : (n + 1) * size], c, 1
            )
            for n in range(groups)
        ]

    attn_grad = jnp.stack(whole(row_grad, row_other, 3) + whole(attn_grad_b, attn_other, 5))
    attn_grad = attn_grad.astype(f32)
    in_grad = jnp.where(y == 0, *ffn_whole).astype(f32)
    out_grad = jnp.where(y == 0, *ffn_whole[::-1]).astype(f32).T

    squares = sum(
        jnp.sum(jnp.square(g.astype(f32))) for g in (row_grad, attn_grad_b, *ffn_grads)
    )
    squares = squares + swap(squares, "c") + jnp.sum(norm_grad * norm_grad)
    squares = squares + swap(squares, "x")
    squares = gather_z(squares)
    grad_norm = jnp.sqrt((squares[0] + squares[1]) + (squares[2] + squares[3]))
    factor = clip_bound / jnp.maximum(grad_norm, clip_bound)
    attn_first_new, attn_second_new, attn_weight_new = adam_update(
        attn_weight, attn_first, attn_second, attn_grad * factor, matrix_rate
    )
    in_first_new, in_second_new, in_weight_new = adam_update(
        in_weight, in_first, in_second, in_grad * factor, matrix_rate
    )
    out_first_new, out_second_new, out_weight_new = adam_update(
        out_weight, out_first, out_second, out_grad * factor, matrix_rate
    )
    norm_first_new, norm_second_new, norm_new = adam_update(
        norm_param, norm_first, norm_second, norm_grad * factor, norm_rate
    )
    return (
        block_out,
        grad_tokens,
        grad_norm,
        attn_first_new,
        attn_second_new,
        attn_weight_new,
        attn_weight_new.astype(bf16),
        in_first_new,
        in_second_new,
        in_weight_new,
        in_weight_new.astype(bf16),
        out_first_new,
        out_second_new,
        out_weight_new,
        out_weight_new.astype(bf16),
        norm_first_new,
        norm_second_new,
        norm_new,
    )


def paired_layout(mesh):
    return dict(mesh.shape) == {"seq": 8, "grp": 4}


def mapped(run, mesh, seq, grp):
    placed = (
        P(grp, seq, None, None),
        P(grp, seq, None, None),
        P(grp),
        P(grp),
        P(None, seq, None),
        P(seq, None),
        P(None, seq),
        P(None, seq),
        P(None, seq, None),
        P(None, seq, None),
        P(seq, None),
        P(seq, None),
        P(None, seq),
        P(None, seq),
        P(None, seq),
        P(None, seq),
    )
    return jax.shard_map(
        run,
        mesh=mesh,
        in_specs=placed,
        out_specs=(
            P(grp, seq, None, None),
            P(grp, seq, None, None),
            P(),
            P(None, seq, None),
            P(None, seq, None),
            P(None, seq, None),
            P(None, seq, None),
            P(seq, None),
            P(seq, None),
            P(seq, None),
            P(seq, None),
            P(None, seq),
            P(None, seq),
            P(None, seq),
            P(None, seq),
            P(None, seq),
            P(None, seq),
            P(None, seq),
        ),
        check_vma=False,
    )


def solution(mesh):
    if not paired_layout(mesh):
        return mapped(general_body, mesh, "seq", "grp")
    fine = Mesh(mesh.devices.reshape(4, 2, 2, 2), ("z", "x", "y", "c"))
    return mapped(paired_body, fine, ("z", "x"), ("y", "c"))
```

```python
from functools import partial
import math

import jax
import jax.numpy as jnp
from jax import lax
from jax.experimental import pallas as pl
from jax.experimental.pallas import tpu as pltpu
from jax.sharding import Mesh
from jax.sharding import PartitionSpec as P

H = 12
DH = 64
STEP = 5


eps_norm = 1e-05
masked_score = -1000000000.0
clip_bound = 1.0
beta_one = 0.5
beta_two = 0.5
matrix_rate = 0.06
norm_rate = 0.3
decay_rate = 0.01
adam_eps = 1e-08


def in_blocks(x, dim, length):
    lengths = x.shape
    pieces = x.reshape(*lengths[:dim], length, lengths[dim] // length, *lengths[dim + 1 :])
    return jnp.moveaxis(pieces, dim, 0)


def sent_and_summed(x, axis, dim):
    length = lax.axis_size(axis)
    pieces = lax.all_to_all(in_blocks(x, dim, length), axis, 0, 0, tiled=True)
    return jnp.sum(pieces.astype(jnp.float32), axis=0)


def layer_norm(value, gain, shift):
    mean = jnp.mean(value, axis=-1, keepdims=True)
    centred = value - mean
    spread = jnp.mean(centred * centred, axis=-1, keepdims=True)
    return centred * lax.rsqrt(spread + eps_norm) * gain + shift


def softmax_rows(scores, keep):
    scores = jnp.where(keep, scores, masked_score)
    top = jnp.max(scores, axis=-1, keepdims=True)
    expo = jnp.exp(scores - top)
    return expo / jnp.sum(expo, axis=-1, keepdims=True)


def softmax_back(probs, grads):
    return probs * (grads - jnp.sum(probs * grads, axis=-1, keepdims=True))


def adam_update(weight, first, second, grad, rate):
    first_new = beta_one * first + (1.0 - beta_one) * grad
    second_new = beta_two * second + (1.0 - beta_two) * grad * grad
    first_hat = first_new / (1.0 - beta_one**STEP)
    second_hat = second_new / (1.0 - beta_two**STEP)
    weight_new = weight - rate * (
        first_hat / (jnp.sqrt(second_hat) + adam_eps) + decay_rate * weight
    )
    return (first_new, second_new, weight_new)


def attn_pair(normed, grad_proj, mixed, grad_branch):
    width = normed.shape[-1]
    qkv_terms = jnp.einsum("prcd,kprce->dke", normed, grad_proj, preferred_element_type=jnp.float32)
    output_terms = jnp.einsum(
        "prcd,prce->de", mixed, grad_branch, preferred_element_type=jnp.float32
    )
    return jnp.concatenate([qkv_terms, output_terms[:, None, :]], axis=1).reshape(width, 4 * width)


def general_body(
    tokens,
    cotangent,
    col_count,
    row_count,
    attn_weight,
    in_weight,
    out_weight,
    norm_param,
    attn_first,
    attn_second,
    in_first,
    in_second,
    out_first,
    out_second,
    norm_first,
    norm_second,
):
    f32 = jnp.float32
    bf16 = jnp.bfloat16
    prot, rows_dev, cols, width = tokens.shape
    hidden = in_weight.shape[1]
    head_scale = 1.0 / math.sqrt(DH)
    attn_full, in_full, out_full, norm_full = (
        lax.all_gather(attn_weight.astype(bf16), "seq", axis=1, tiled=True),
        lax.all_gather(in_weight.astype(bf16), "seq", axis=0, tiled=True),
        lax.all_gather(out_weight.astype(bf16), "seq", axis=1, tiled=True),
        lax.all_gather(norm_param.astype(bf16), "seq", axis=1, tiled=True),
    )
    norm_gain = norm_full.astype(f32)
    row_ids = lax.axis_index("seq") * rows_dev + jnp.arange(rows_dev, dtype=jnp.int32)
    row_live = (row_ids[None, :] < row_count[:, None]).astype(f32)
    col_live = jnp.arange(cols, dtype=jnp.int32)[None, :] < col_count[:, None]
    tie_scale = lax.rsqrt(row_count.astype(f32)) * head_scale
    live = row_live[:, :, None] * col_live.astype(f32)[:, None, :]
    grad_out = (cotangent.astype(f32) * live[..., None]).astype(bf16)
    resid_one = tokens.astype(f32)
    normed_one = layer_norm(resid_one, norm_gain[0], norm_gain[1]).astype(bf16)
    proj_one = jnp.einsum(
        "prcd,kde->kprce", normed_one, attn_full[0:3], preferred_element_type=f32
    ).astype(bf16)
    proj_one = proj_one.reshape(3, prot, rows_dev, cols, H, DH)
    query_one, key_one, value_one = (proj_one[0], proj_one[1], proj_one[2])
    masked_query = query_one * row_live[:, :, None, None, None].astype(bf16)
    partial_scores = (
        jnp.einsum("prihe,prjhe->phij", masked_query, key_one, preferred_element_type=f32)
        * tie_scale[:, None, None, None]
    )
    keep_cols = col_live[:, None, None, :]
    score_part = lax.psum_scatter(partial_scores, "seq", scatter_dimension=2, tiled=True)
    probs_one = softmax_rows(score_part, keep_cols)
    probs_low = lax.all_gather(probs_one.astype(bf16), "seq", axis=2, tiled=True)
    mixed_one = jnp.einsum(
        "phij,prjhe->prihe", probs_low, value_one, preferred_element_type=f32
    ).astype(bf16)
    mixed_one = mixed_one.reshape(prot, rows_dev, cols, width)
    branch_one = jnp.einsum("prcd,de->prce", mixed_one, attn_full[3], preferred_element_type=f32)
    stream_one = (resid_one + branch_one).astype(bf16)
    stream_cols, up_grad = (
        lax.all_to_all(stream_one, "seq", split_axis=2, concat_axis=1, tiled=True),
        lax.all_to_all(grad_out, "seq", split_axis=2, concat_axis=1, tiled=True),
    )
    rows = stream_cols.shape[1]
    cols_dev = stream_cols.shape[2]
    row_live_all = jnp.arange(rows, dtype=jnp.int32)[None, :] < row_count[:, None]
    resid_two = stream_cols.astype(f32)
    normed_two = layer_norm(resid_two, norm_gain[2], norm_gain[3]).astype(bf16)
    proj_two = jnp.einsum(
        "prcd,kde->kprce", normed_two, attn_full[4:7], preferred_element_type=f32
    ).astype(bf16)
    proj_two = proj_two.reshape(3, prot, rows, cols_dev, H, DH)
    query_two, key_two, value_two = (proj_two[0], proj_two[1], proj_two[2])
    scores_two = (
        jnp.einsum("prche,psche->pchrs", query_two, key_two, preferred_element_type=f32)
        * head_scale
    )
    probs_two = softmax_rows(scores_two, row_live_all[:, None, None, None, :])
    probs_two_low = probs_two.astype(bf16)
    mixed_two = jnp.einsum(
        "pchrs,psche->prche", probs_two_low, value_two, preferred_element_type=f32
    ).astype(bf16)
    mixed_two = mixed_two.reshape(prot, rows, cols_dev, width)
    resid_three = resid_two + jnp.einsum(
        "prcd,de->prce", mixed_two, attn_full[7], preferred_element_type=f32
    )
    normed_three = layer_norm(resid_three, norm_gain[4], norm_gain[5]).astype(bf16)
    inner = jnp.einsum("prcd,df->prcf", normed_three, in_full, preferred_element_type=f32)
    activ = jax.nn.gelu(inner, approximate=True).astype(bf16)
    result = (
        resid_three + jnp.einsum("prcf,fd->prcd", activ, out_full, preferred_element_type=f32)
    ).astype(bf16)
    block_out = lax.all_to_all(result, "seq", split_axis=1, concat_axis=2, tiled=True)
    grad_act = jnp.einsum("prcd,fd->prcf", up_grad, out_full, preferred_element_type=f32)
    _, gelu_back = jax.vjp(partial(jax.nn.gelu, approximate=True), inner)
    grad_inner = gelu_back(grad_act)[0].astype(bf16)
    grad_normed_three = jnp.einsum("prcf,df->prcd", grad_inner, in_full, preferred_element_type=f32)
    _, norm_back_three = jax.vjp(layer_norm, resid_three, norm_gain[4], norm_gain[5])
    part_three, gain_grad_three, shift_grad_three = norm_back_three(grad_normed_three)
    grad_three = up_grad.astype(f32) + part_three
    grad_branch_two = grad_three.astype(bf16)
    grad_mixed_two = jnp.einsum(
        "prce,de->prcd", grad_branch_two, attn_full[7], preferred_element_type=f32
    ).astype(bf16)
    grad_mixed_two = grad_mixed_two.reshape(prot, rows, cols_dev, H, DH)
    grad_probs_two = jnp.einsum(
        "prche,psche->pchrs", grad_mixed_two, value_two, preferred_element_type=f32
    )
    grad_value_two = jnp.einsum(
        "pchrs,prche->psche", probs_two_low, grad_mixed_two, preferred_element_type=f32
    )
    grad_scores_two = softmax_back(probs_two, grad_probs_two).astype(bf16)
    grad_query_two = (
        jnp.einsum("pchrs,psche->prche", grad_scores_two, key_two, preferred_element_type=f32)
        * head_scale
    )
    grad_key_two = (
        jnp.einsum("pchrs,prche->psche", grad_scores_two, query_two, preferred_element_type=f32)
        * head_scale
    )
    grad_proj_two = jnp.stack([grad_query_two, grad_key_two, grad_value_two]).astype(bf16)
    grad_proj_two = grad_proj_two.reshape(3, prot, rows, cols_dev, width)
    grad_normed_two = jnp.einsum(
        "kprce,kde->prcd", grad_proj_two, attn_full[4:7], preferred_element_type=f32
    )
    _, norm_back_two = jax.vjp(layer_norm, resid_two, norm_gain[2], norm_gain[3])
    part_two, gain_grad_two, shift_grad_two = norm_back_two(grad_normed_two)
    grad_stream = (grad_three + part_two).astype(bf16)
    col_attn_terms = attn_pair(normed_two, grad_proj_two, mixed_two, grad_branch_two)
    in_terms = jnp.einsum("prcd,prcf->df", normed_three, grad_inner, preferred_element_type=f32)
    out_terms = jnp.einsum("prcf,prcd->df", activ, up_grad, preferred_element_type=f32)
    grad_rows = lax.all_to_all(grad_stream, "seq", split_axis=1, concat_axis=2, tiled=True)
    grad_mixed_one = jnp.einsum(
        "prce,de->prcd", grad_rows, attn_full[3], preferred_element_type=f32
    ).astype(bf16)
    grad_mixed_one = grad_mixed_one.reshape(prot, rows_dev, cols, H, DH)
    partial_grads = jnp.einsum(
        "prihe,prjhe->phij", grad_mixed_one, value_one, preferred_element_type=f32
    )
    grad_value_one = jnp.einsum(
        "phij,prihe->prjhe", probs_low, grad_mixed_one, preferred_element_type=f32
    )
    grad_part = sent_and_summed(partial_grads.astype(jnp.bfloat16), "seq", 2)
    grad_scores_one = lax.all_gather(
        softmax_back(probs_one, grad_part).astype(bf16), "seq", axis=2, tiled=True
    )
    tie_rows = row_live[:, :, None, None, None] * tie_scale[:, None, None, None, None]
    grad_query_one = (
        jnp.einsum("phij,prjhe->prihe", grad_scores_one, key_one, preferred_element_type=f32)
        * tie_rows
    )
    grad_key_one = (
        jnp.einsum("phij,prihe->prjhe", grad_scores_one, masked_query, preferred_element_type=f32)
        * tie_scale[:, None, None, None, None]
    )
    grad_proj_one = jnp.stack([grad_query_one, grad_key_one, grad_value_one]).astype(bf16)
    grad_proj_one = grad_proj_one.reshape(3, prot, rows_dev, cols, width)
    grad_normed_one = jnp.einsum(
        "kprce,kde->prcd", grad_proj_one, attn_full[0:3], preferred_element_type=f32
    )
    _, norm_back_one = jax.vjp(layer_norm, resid_one, norm_gain[0], norm_gain[1])
    part_one, gain_grad_one, shift_grad_one = norm_back_one(grad_normed_one)
    grad_tokens = grad_rows.astype(f32) + part_one
    norm_stack = jnp.stack(
        [
            gain_grad_one,
            shift_grad_one,
            gain_grad_two,
            shift_grad_two,
            gain_grad_three,
            shift_grad_three,
        ]
    )
    row_attn_terms = attn_pair(normed_one, grad_proj_one, mixed_one, grad_rows)
    owned = lax.psum_scatter(
        jnp.concatenate(
            [row_attn_terms, col_attn_terms, in_terms, out_terms, norm_stack.T], axis=1
        ),
        "seq",
        scatter_dimension=0,
        tiled=True,
    )
    width_dev = owned.shape[0]
    row_part = owned[:, : 4 * width].reshape(width_dev, 4, width)
    col_part = owned[:, 4 * width : 8 * width].reshape(width_dev, 4, width)
    in_part = owned[:, 8 * width : 8 * width + hidden]
    out_part = owned[:, 8 * width + hidden : 8 * width + 2 * hidden].T
    norm_part = owned[:, 8 * width + 2 * hidden :].T
    attn_part = jnp.concatenate([row_part, col_part], axis=1).transpose(1, 0, 2)
    attn_grad, in_grad, out_grad, norm_grad = (
        lax.psum(attn_part.astype(jnp.bfloat16), "grp").astype(jnp.float32),
        lax.psum(in_part.astype(jnp.bfloat16), "grp").astype(jnp.float32),
        lax.psum(out_part.astype(jnp.bfloat16), "grp").astype(jnp.float32),
        lax.psum(norm_part.astype(jnp.bfloat16), "grp").astype(jnp.float32),
    )
    squares = (
        jnp.sum(attn_grad * attn_grad)
        + jnp.sum(in_grad * in_grad)
        + jnp.sum(out_grad * out_grad)
        + jnp.sum(norm_grad * norm_grad)
    )
    grad_norm = jnp.sqrt(lax.psum(squares, "seq"))
    factor = clip_bound / jnp.maximum(grad_norm, clip_bound)
    attn_first_new, attn_second_new, attn_weight_new = adam_update(
        attn_weight, attn_first, attn_second, attn_grad * factor, matrix_rate
    )
    in_first_new, in_second_new, in_weight_new = adam_update(
        in_weight, in_first, in_second, in_grad * factor, matrix_rate
    )
    out_first_new, out_second_new, out_weight_new = adam_update(
        out_weight, out_first, out_second, out_grad * factor, matrix_rate
    )
    norm_first_new, norm_second_new, norm_new = adam_update(
        norm_param, norm_first, norm_second, norm_grad * factor, norm_rate
    )
    return (
        block_out,
        grad_tokens,
        grad_norm,
        attn_first_new,
        attn_second_new,
        attn_weight_new,
        attn_weight_new.astype(bf16),
        in_first_new,
        in_second_new,
        in_weight_new,
        in_weight_new.astype(bf16),
        out_first_new,
        out_second_new,
        out_weight_new,
        out_weight_new.astype(bf16),
        norm_first_new,
        norm_second_new,
        norm_new,
    )


PAIR = [(0, 1), (1, 0)]
TILE = 128


def swap(value, axis):
    return lax.ppermute(value, axis, PAIR)


def pick(value, index, axis):
    return lax.dynamic_index_in_dim(value, index, axis, keepdims=False)


def joined(own, other, place, axis):
    return jnp.where(
        place == 0,
        jnp.concatenate([own, other], axis=axis),
        jnp.concatenate([other, own], axis=axis),
    )


def merge(own, other, place, axis):
    return jnp.where(
        place == 0,
        jnp.stack([own, other], axis=axis),
        jnp.stack([other, own], axis=axis),
    )


def merge_cores(value, c):
    prot, _, cols, width = value.shape
    part = cols // 4
    split = value.reshape(prot, 2, 2, part, width)
    got = swap(pick(split, 1 - c, 2), "c")
    both = merge(pick(split, c, 2), got, c, 0)
    return both.reshape(8, part, width)


def to_blocks(value):
    return lax.all_to_all(value, ("z", "x"), 0, 0, tiled=True)


def to_rows(got, c):
    _, part, width = got.shape
    got = got.reshape(2, 2, 2, part, width)
    other = swap(pick(got, 1 - c, 0), "c")
    both = merge(pick(got, c, 0), other, c, 2)
    return both.reshape(2, 1, 4 * part, width)


def together(*values):
    return lax.optimization_barrier(values)


def gather_z(own):
    return [own] + [lax.ppermute(own, "z", [(k, k ^ i) for k in range(4)]) for i in (1, 2, 3)]


def spread(over_z):
    over_x = swap(over_z, "x")
    quarter = [((0, 0, 0), over_z), ((1, 0, 0), over_x)]
    return quarter + [((j, 1, 0), swap(value, "y")) for (j, _, _), value in quarter]


def both_cores(half):
    return half + [((j, m, 1), swap(value, "c")) for (j, m, _), value in half]


def placing(plan, outs_at, place_ref, stacks, outs, sem, steps=True):
    copies = []
    for stack, (j, m, k) in zip(stacks, plan):
        x, y, c = (lax.bitwise_xor(place_ref[n], step) for n, step in ((1, j), (3, m), (2, k)))
        for i in range(4):
            shard = (lax.bitwise_xor(place_ref[0], i) if steps else i) * 2 + x
            for source, target in outs_at(stack.at[i], outs, shard, y, c):
                copies.append(pltpu.make_async_copy(source, target, sem.at[len(copies)]))
    return copies


def place_kernel(plan, outs_at, place_ref, *refs):
    stacks = refs[: len(plan)]
    copies = placing(plan, outs_at, place_ref, stacks, refs[len(plan) : -1], refs[-1])
    for copy in copies:
        copy.start()
    for copy in copies:
        copy.wait()


def placed_pieces(pieces, outs_at, outs, place, count):
    anywhere = pl.BlockSpec(memory_space=pl.ANY)
    return pl.pallas_call(
        partial(place_kernel, [step for step, _ in pieces], outs_at),
        in_specs=[pl.BlockSpec(memory_space=pltpu.SMEM)] + [anywhere] * len(pieces),
        out_specs=[pl.BlockSpec(memory_space=pltpu.VMEM)] * len(outs),
        out_shape=[jax.ShapeDtypeStruct(shape, jnp.bfloat16) for shape in outs],
        scratch_shapes=[pltpu.SemaphoreType.DMA((count,))],
        compiler_params=pltpu.CompilerParams(
            vmem_limit_bytes=sum(2 * math.prod(s) for s in outs) + 2 * 2**20
        ),
    )(place, *[value for _, value in pieces])


def row_attn_at(ref, outs, shard, y, c):
    depth = outs[0].shape[0] // 16
    at = pl.multiple_of((shard * 2 + y) * depth, depth)
    return [(ref, outs[0].at[pl.ds(at, depth)])]


def ffn_at(ref, outs, shard, y, c):
    depth = ref.shape[0]
    at = pl.multiple_of((y * 8 + shard) * depth, depth)
    return [(ref, outs[0].at[pl.ds(at, depth)])]


def col_attn_at(ref, outs, shard, y, c):
    depth, half = ref.shape[1], ref.shape[2]
    at = pl.multiple_of((shard * 2 + y) * depth, depth)
    moves = []
    slots = [(o, n) for o, out in enumerate(outs) for n in range(out.shape[1] // (2 * half))]
    for k, (o, n) in enumerate(slots):
        lane = pl.multiple_of(c * half + n * 2 * half, TILE)
        moves.append((ref.at[k], outs[o].at[pl.ds(at, depth), pl.ds(lane, half)]))
    return moves


def contract(a, b, dims):
    return lax.dot_general(a, b, (dims, ((), ())), preferred_element_type=jnp.float32)


LAST = ((1,), (1,))
FIRST = ((0,), (0,))
PLAIN = ((1,), (0,))


def softmax_of(scores, keep):
    scores = jnp.where(keep, scores, masked_score)
    expo = jnp.exp(scores - jnp.max(scores, axis=-1, keepdims=True))
    return expo / jnp.sum(expo, axis=-1, keepdims=True)


def head_lanes(lanes):
    side = lax.broadcasted_iota(jnp.int32, (1, lanes), 1) % TILE < DH
    return (side, jnp.logical_not(side))


def only(keep, value):
    return jnp.where(keep, value, jnp.zeros_like(value))


def column_keep(info_ref, own_cols, near, part):
    key = lax.broadcasted_iota(jnp.int32, (1, 2 * near), 1)
    far = key >= near
    inner = key % near
    x = jnp.where(far, 1 - info_ref[1], info_ref[1])
    c = jnp.where(inner >= part, 1 - info_ref[2], info_ref[2])
    column = x * near + c * part + inner % part
    return column < info_ref[3]


def live_pair(value, row, info_ref):
    lane = lax.broadcasted_iota(jnp.int32, (1, value.shape[1]), 1) // TILE + row
    return only(lane < info_ref[4], value)


def head_pair(ref, row, lane):
    blocks, _, part, _ = ref.shape
    found = [ref[:, row + n, :, lane : lane + TILE].reshape(blocks * part, TILE) for n in (0, 1)]
    return jnp.concatenate(found, axis=1)


def row_fwd_kernel(token_plan, weight_plan, place_ref, info_ref, tie_ref, *refs):
    bf16 = jnp.bfloat16
    f32 = jnp.float32
    tokens, refs = refs[: len(token_plan)], refs[len(token_plan) :]
    stacks, refs = refs[: len(weight_plan)], refs[len(weight_plan) :]
    own_ref, near_tokens_ref, far_tokens_ref, w_ref, gain_ref, near_ref, far_ref, o_ref = refs[:8]
    all_ref, norm_ref, token_sem, weight_sem = refs[8:]
    blocks, rows, part, lanes = near_ref.shape
    half = lanes // 3
    count = rows * part
    near = blocks * part
    copies = []
    for stack, (j, k) in zip(tokens, token_plan):
        x = lax.bitwise_xor(place_ref[1], j)
        for i in range(4):
            row = lax.bitwise_xor(place_ref[0], i) * 2 + x
            moves = [(stack.at[i, pl.ds(0, 2 * part)], all_ref.at[k, row])]
            if k == 0:
                moves.append((stack.at[i, pl.ds(2 * part, 16)], norm_ref.at[j * 4 + i]))
            for source, target in moves:
                copies.append(pltpu.make_async_copy(source, target, token_sem.at[len(copies)]))
    weights = placing(weight_plan, row_attn_at, place_ref, stacks, [w_ref], weight_sem)
    for copy in copies + weights:
        copy.start()
    for copy in copies:
        copy.wait()
    gains = jnp.sum(norm_ref[...].astype(f32), axis=0)
    gain_ref[...] = gains
    x = info_ref[1]
    for ref, side in ((near_tokens_ref, x), (far_tokens_ref, 1 - x)):
        at = pl.ds(pl.multiple_of(side * part, part), part)
        for k in range(blocks):
            value = all_ref[k, :, at, :].reshape(count, -1)
            if k == 0:
                @pl.when(side == x)
                def _():
                    own_ref[...] = value
            found = normed(value.astype(f32), gains[0:1], gains[1:2])[0]
            ref[k * count : (k + 1) * count] = found.astype(bf16)
    for copy in weights:
        copy.wait()
    for n in range(3):
        at = slice(n * half, (n + 1) * half)
        found = contract(near_tokens_ref[...], w_ref[:, at], PLAIN).astype(bf16)
        near_ref[:, :, :, at] = found.reshape(blocks, rows, part, half)
        if n > 0:
            found = contract(far_tokens_ref[...], w_ref[:, at], PLAIN).astype(bf16)
            far_ref[:, :, :, (n - 1) * half : n * half] = found.reshape(blocks, rows, part, half)
    sides = head_lanes(2 * TILE)
    keep = column_keep(info_ref, near, near, part)
    tie = tie_ref[0]
    for lane in range(0, half, TILE):
        scores = [jnp.zeros((near, 2 * near), f32) for _ in sides]
        for row in range(0, rows, 2):
            query = live_pair(head_pair(near_ref, row, lane), row, info_ref)
            key = jnp.concatenate(
                [head_pair(near_ref, row, half + lane), head_pair(far_ref, row, lane)], axis=0
            )
            for n, side in enumerate(sides):
                scores[n] = scores[n] + contract(only(side, query), key, LAST)
        probs = [softmax_of(s * tie, keep).astype(bf16) for s in scores]
        for row in range(0, rows, 2):
            value = jnp.concatenate(
                [head_pair(near_ref, row, 2 * half + lane), head_pair(far_ref, row, half + lane)],
                axis=0,
            )
            mixed = jnp.where(
                sides[0], contract(probs[0], value, PLAIN), contract(probs[1], value, PLAIN)
            ).astype(bf16)
            for n in (0, 1):
                o_ref[:, row + n, :, lane : lane + TILE] = mixed[:, n * TILE : (n + 1) * TILE].reshape(
                    blocks, part, TILE
                )


def row_bwd_kernel(
    info_ref, tie_ref, near_ref, far_ref, own_ref, got_ref, w_ref, near_tokens_ref, far_tokens_ref,
    y_kept_ref, y_got_ref, x_kept_ref, x_got_ref,
    near_part_ref, near_theirs_ref, far_part_ref, far_theirs_ref, sent_ref, kept_ref,
    to_x_ref, with_x_ref, to_y_ref, with_y_ref, do_ref, d_near_ref, d_far_ref,
):
    bf16 = jnp.bfloat16
    blocks, rows, part, lanes = near_ref.shape
    half = lanes // 3
    near = blocks * part
    sides = head_lanes(2 * TILE)
    keep = column_keep(info_ref, near, near, part)
    tie = tie_ref[0]
    do_ref[0] = own_ref[...].reshape(rows, part, half)
    do_ref[1] = got_ref[...].reshape(rows, part, half)

    for lane in range(0, half, TILE):

        def pair(ref, row, first):
            at = slice(first + lane, first + lane + TILE)
            found = [ref[:, row + n, :, at].reshape(near, TILE) for n in (0, 1)]
            return jnp.concatenate(found, axis=1)

        def both(row, first):
            return jnp.concatenate(
                [pair(near_ref, row, first), pair(far_ref, row, first - half)], axis=0
            )

        scores = [jnp.zeros((near, 2 * near), jnp.float32) for _ in sides]
        grads = [jnp.zeros((near, 2 * near), jnp.float32) for _ in sides]
        for row in range(0, rows, 2):
            query = live_pair(pair(near_ref, row, 0), row, info_ref)
            key, value = both(row, half), both(row, 2 * half)
            out = pair(do_ref, row, 0)
            for n, side in enumerate(sides):
                scores[n] = scores[n] + contract(only(side, query), key, LAST)
                grads[n] = grads[n] + contract(only(side, out), value, LAST)
        probs = [softmax_of(s * tie, keep) for s in scores]
        lows = [p.astype(bf16) for p in probs]
        deltas = [softmax_back(p, g).astype(bf16) for p, g in zip(probs, grads)]
        low_turned = [p.T for p in lows]
        delta_turned = [d.T for d in deltas]
        for row in range(0, rows, 2):
            query = live_pair(pair(near_ref, row, 0), row, info_ref)
            key, out = both(row, half), pair(do_ref, row, 0)
            dq = [contract(d, key, PLAIN) for d in deltas]
            dk = [contract(d, query, PLAIN) for d in delta_turned]
            dv = [contract(p, out, PLAIN) for p in low_turned]
            dq = live_pair(jnp.where(sides[0], dq[0], dq[1]) * tie, row, info_ref).astype(bf16)
            dk = (jnp.where(sides[0], dk[0], dk[1]) * tie).astype(bf16)
            dv = jnp.where(sides[0], dv[0], dv[1]).astype(bf16)

            def put(ref, first, value):
                for n in (0, 1):
                    piece = value[:, n * TILE : (n + 1) * TILE].reshape(blocks, part, TILE)
                    ref[:, row + n, :, first + lane : first + lane + TILE] = piece

            put(d_near_ref, 0, dq)
            put(d_near_ref, half, dk[:near])
            put(d_near_ref, 2 * half, dv[:near])
            put(d_far_ref, 0, dk[near:])
            put(d_far_ref, half, dv[near:])

    count = rows * part
    d_far = d_far_ref[...].reshape(blocks * count, 2 * half)
    far_weights = w_ref[:, half:]
    far_part_ref[...] = contract(d_far[:count], far_weights, LAST)
    far_theirs_ref[...] = contract(d_far[count:], far_weights, LAST).astype(bf16)
    d_near = d_near_ref[...].reshape(blocks * count, lanes)
    near_part_ref[...] = contract(d_near[:count], w_ref[...], LAST)
    near_theirs_ref[...] = contract(d_near[count:], w_ref[...], LAST).astype(bf16)
    near_turned = near_tokens_ref[...].T
    far_turned = far_tokens_ref[...].T
    zs, depth = kept_ref.shape[0], kept_ref.shape[1]
    first = info_ref[1] == 0
    first_y = info_ref[5] == 0
    summed = added(y_kept_ref[...], y_got_ref[...]).reshape(zs, 2, depth, -1)
    with_x_ref[...] = jnp.where(first, summed[:, 0], summed[:, 1])
    to_x_ref[...] = jnp.where(first, summed[:, 1], summed[:, 0])
    summed = added(x_kept_ref[...], x_got_ref[...])
    with_y_ref[...] = jnp.where(first_y, summed[:, 0], summed[:, 1])
    to_y_ref[...] = jnp.where(first_y, summed[:, 1], summed[:, 0])
    for n in range(3):
        at = slice(n * half, (n + 1) * half)
        terms = contract(near_turned, d_near[:, at], PLAIN)
        if n > 0:
            terms = terms + contract(far_turned, d_far[:, (n - 1) * half : n * half], PLAIN)
        terms = terms.astype(bf16).reshape(zs, 2, depth, half)
        kept_ref[:, :, at] = jnp.where(first, terms[:, 0], terms[:, 1])
        sent_ref[:, :, at] = jnp.where(first, terms[:, 1], terms[:, 0])


def row_attention(place, info, tie, tokens, weights, rows, half):
    f32, bf16 = jnp.float32, jnp.bfloat16
    zs, deep, width = tokens[0][1].shape
    part = (deep - 16) // 2
    count = rows * part
    small = pl.BlockSpec(memory_space=pltpu.SMEM)
    anywhere = pl.BlockSpec(memory_space=pl.ANY)
    inside = pl.BlockSpec(memory_space=pltpu.VMEM)
    shapes = [
        ((count, width), bf16),
        ((2 * count, width), bf16),
        ((2 * count, width), bf16),
        ((width, 3 * half), bf16),
        ((16, width), f32),
        ((2, rows, part, 3 * half), bf16),
        ((2, rows, part, 2 * half), bf16),
        ((2, rows, part, half), bf16),
    ]
    return pl.pallas_call(
        partial(row_fwd_kernel, [step for step, _ in tokens], [step for step, _ in weights]),
        in_specs=[small] * 3 + [anywhere] * (len(tokens) + len(weights)),
        out_specs=[inside] * len(shapes),
        out_shape=[jax.ShapeDtypeStruct(shape, kind) for shape, kind in shapes],
        scratch_shapes=[
            pltpu.VMEM((2, rows, 2 * part, width), bf16),
            pltpu.VMEM((8, 16, width), bf16),
            pltpu.SemaphoreType.DMA((24,)),
            pltpu.SemaphoreType.DMA((16,)),
        ],
        compiler_params=pltpu.CompilerParams(vmem_limit_bytes=56 * 2**20),
    )(place, info, tie, *[v for _, v in tokens], *[v for _, v in weights])


def row_attention_back(info, tie, near, far, own, got, weights, near_tokens, far_tokens, *ffn_terms):
    blocks, rows, part, lanes = near.shape
    count, width = rows * part, weights.shape[0]
    half = lanes // 3
    f32, bf16 = jnp.float32, jnp.bfloat16
    small = pl.BlockSpec(memory_space=pltpu.SMEM)
    inside = pl.BlockSpec(memory_space=pltpu.VMEM)
    shapes = [((count, width), kind) for kind in (f32, bf16) * 2]
    shapes = shapes + [((4, width // 8, lanes), bf16)] * 2
    shapes = shapes + [((4, width // 8, ffn_terms[0].shape[1]), bf16)] * 4
    return pl.pallas_call(
        row_bwd_kernel,
        in_specs=[small, small] + [inside] * 11,
        out_specs=[inside] * 10,
        out_shape=[jax.ShapeDtypeStruct(shape, kind) for shape, kind in shapes],
        scratch_shapes=[
            pltpu.VMEM((blocks, rows, part, half), bf16),
            pltpu.VMEM((blocks, rows, part, lanes), bf16),
            pltpu.VMEM((blocks, rows, part, 2 * half), bf16),
        ],
        compiler_params=pltpu.CompilerParams(vmem_limit_bytes=56 * 2**20),
    )(info, tie, near, far, own, got, weights, near_tokens, far_tokens, *ffn_terms)


def normed(value, gain, shift):
    centred = value - jnp.mean(value, axis=-1, keepdims=True)
    scale = lax.rsqrt(jnp.mean(centred * centred, axis=-1, keepdims=True) + eps_norm)
    unit = centred * scale
    return unit * gain + shift, unit, scale


def normed_back(grad, unit, scale, gain):
    inner = grad * gain
    mean = jnp.mean(inner, axis=-1, keepdims=True)
    along = jnp.mean(inner * unit, axis=-1, keepdims=True)
    return scale * (inner - mean - unit * along)


def column_masks(info_ref, rows, part):
    tokens = rows * part
    key = lax.broadcasted_iota(jnp.int32, (tokens, tokens), 0)
    query = lax.broadcasted_iota(jnp.int32, (tokens, tokens), 1)
    same = key % part == query % part
    return jnp.logical_and(same, key // part < info_ref[4])


def stacked(value, sides):
    return jnp.concatenate([only(side, value) for side in sides], axis=0)


def column_probs(query, key, keep, sides):
    scores = contract(stacked(key, sides), query, LAST) * (1.0 / math.sqrt(DH))
    tokens = query.shape[0]
    probs = []
    for n in (0, 1):
        part = jnp.where(keep, scores[n * tokens : (n + 1) * tokens], masked_score)
        expo = jnp.exp(part - jnp.max(part, axis=0, keepdims=True))
        probs.append(expo / jnp.sum(expo, axis=0, keepdims=True))
    return probs


def col_fwd_kernel(plan, info_ref, place_ref, *refs):
    stacks, refs = refs[: len(plan)], refs[len(plan) :]
    x_ref, own_ref, other_ref, gain_ref, acts_ref, one_ref, qkv_ref = refs[:7]
    resid_ref, normed_three_ref, mixed_ref, three_ref, col_ref, seven_ref, sem = refs[7:]
    copies = placing(plan, col_attn_at, place_ref, stacks, [three_ref, col_ref, seven_ref], sem)
    for copy in copies:
        copy.start()
    bf16 = jnp.bfloat16
    rows, cols, lanes = qkv_ref.shape
    width = lanes // 3
    part = 16
    own, other = own_ref[...], other_ref[...]
    flip = info_ref[2] == 0
    mixed_one = jnp.concatenate(
        [jnp.where(flip, own, other), jnp.where(flip, other, own)], axis=1
    )
    acts_ref[:, :width] = mixed_one
    for copy in copies:
        copy.wait()
    stream = (x_ref[...].astype(jnp.float32) + contract(mixed_one, three_ref[...], PLAIN)).astype(bf16)
    one_ref[...] = stream
    normed_two = normed(stream.astype(jnp.float32), gain_ref[2:3], gain_ref[3:4])[0].astype(bf16)
    acts_ref[:, width : 2 * width] = normed_two
    for n in range(3):
        at = slice(n * width, (n + 1) * width)
        found = contract(normed_two, col_ref[:, at], PLAIN).astype(bf16)
        qkv_ref[:, :, at] = found.reshape(rows, cols, width)
    keep = column_masks(info_ref, rows, part)
    sides = head_lanes(TILE)

    def attend(b, carry):
        at = pl.ds(pl.multiple_of(b * part, part), part)
        def tile(n, t):
            lane = n * width + t * TILE
            return qkv_ref[:, at, lane : lane + TILE].reshape(rows * part, TILE)
        tiles = range(width // TILE)
        probs = [column_probs(tile(0, t), tile(1, t), keep, sides) for t in tiles]
        for t in tiles:
            low = jnp.concatenate(probs[t], axis=0).astype(bf16)
            mixed = contract(low, stacked(tile(2, t), sides), FIRST).astype(bf16)
            mixed_ref[:, at, t * TILE : (t + 1) * TILE] = mixed.reshape(rows, part, TILE)
        return carry

    lax.fori_loop(0, cols // part, attend, 0)
    mixed = mixed_ref[...].reshape(rows * cols, width)
    acts_ref[:, 2 * width :] = mixed
    resid = one_ref[...].astype(jnp.float32) + contract(mixed, seven_ref[...], PLAIN)
    resid_ref[...] = resid
    normed_three_ref[...] = normed(resid, gain_ref[4:5], gain_ref[5:6])[0].astype(bf16)


def col_bwd_kernel(plan, info_ref, place_ref, *refs):
    stacks, refs = refs[: len(plan)], refs[len(plan) :]
    up_ref, da_ref, da_got_ref, out_ref, out_got_ref, resid_ref, one_ref, qkv_ref, gain_ref = refs[:9]
    result_ref, stream_ref, own_ref, other_ref, mine_ref, theirs_ref, norms_ref = refs[9:16]
    dqkv_ref, do_ref, three_ref, col_ref, seven_ref, sem = refs[16:]
    copies = placing(plan, col_attn_at, place_ref, stacks, [three_ref, col_ref, seven_ref], sem)
    for copy in copies:
        copy.start()
    bf16 = jnp.bfloat16
    f32 = jnp.float32
    rows, cols, lanes = qkv_ref.shape
    width = lanes // 3
    part = 16
    result_ref[...] = (resid_ref[...] + out_ref[...] + out_got_ref[...].astype(f32)).astype(bf16)
    da = da_ref[...] + da_got_ref[...].astype(f32)
    gain = gain_ref[4:5]
    _, unit, scale = normed(resid_ref[...], gain, 0.0)
    grad_three = up_ref[...].astype(f32) + normed_back(da, unit, scale, gain)
    norms_ref[2:3] = jnp.sum(da * unit, axis=0, keepdims=True)
    norms_ref[3:4] = jnp.sum(da, axis=0, keepdims=True)
    branch = grad_three.astype(bf16)
    half = width // 2
    flip = info_ref[2] == 0

    def put_halves(first, value):
        at = slice(first, first + half)
        mine_ref[:, at] = jnp.where(flip, value[:, :half], value[:, half:])
        theirs_ref[:, at] = jnp.where(flip, value[:, half:], value[:, :half])

    put_halves(4 * half, branch)
    for copy in copies:
        copy.wait()
    do_ref[...] = contract(branch, seven_ref[...], LAST).astype(bf16).reshape(rows, cols, width)
    keep = column_masks(info_ref, rows, part)
    sides = head_lanes(TILE)
    ratio = 1.0 / math.sqrt(DH)

    def attend(b, carry):
        at = pl.ds(pl.multiple_of(b * part, part), part)
        tokens = rows * part

        def tile(n, t):
            lane = n * width + t * TILE
            return qkv_ref[:, at, lane : lane + TILE].reshape(tokens, TILE)

        def out_tile(t):
            return do_ref[:, at, t * TILE : (t + 1) * TILE].reshape(tokens, TILE)

        def put(n, t, value):
            lane = n * width + t * TILE
            dqkv_ref[:, at, lane : lane + TILE] = value.astype(bf16).reshape(rows, part, TILE)

        for t in range(width // TILE):
            query, key, out = tile(0, t), tile(1, t), out_tile(t)
            keys = stacked(key, sides)
            probs = column_probs(query, key, keep, sides)
            grads = contract(stacked(tile(2, t), sides), out, LAST)
            deltas = []
            for n, p in enumerate(probs):
                g = grads[n * tokens : (n + 1) * tokens]
                deltas.append((p * (g - jnp.sum(p * g, axis=0, keepdims=True))).astype(bf16))
            put(0, t, contract(jnp.concatenate(deltas, axis=0), keys, FIRST) * ratio)
            wide = jnp.concatenate(deltas, axis=1)
            put(1, t, contract(wide, stacked(query, sides), PLAIN) * ratio)
            wide = jnp.concatenate([p.astype(bf16) for p in probs], axis=1)
            put(2, t, contract(wide, stacked(out, sides), PLAIN))
        return carry

    lax.fori_loop(0, cols // part, attend, 0)
    dqkv = dqkv_ref[...].reshape(rows * cols, lanes)
    for n in range(3):
        put_halves((n + 1) * half, dqkv[:, n * width : (n + 1) * width])
    grad_normed = contract(dqkv, col_ref[...], LAST)
    gain = gain_ref[2:3]
    _, unit, scale = normed(one_ref[...].astype(f32), gain, 0.0)
    norms_ref[0:1] = jnp.sum(grad_normed * unit, axis=0, keepdims=True)
    norms_ref[1:2] = jnp.sum(grad_normed, axis=0, keepdims=True)
    stream = (grad_three + normed_back(grad_normed, unit, scale, gain)).astype(bf16)
    stream_ref[...] = stream
    put_halves(0, stream)
    mixed = contract(stream, three_ref[...], LAST).astype(bf16)
    own_ref[...] = jnp.where(flip, mixed[:, :half], mixed[:, half:])
    other_ref[...] = jnp.where(flip, mixed[:, half:], mixed[:, :half])


def attn_terms_kernel(place_ref, acts_ref, got_ref, mine_ref, theirs_ref, sent_ref, kept_ref):
    width = acts_ref.shape[1] // 3
    half = width // 2
    depth = sent_ref.shape[1]
    turned = [
        jnp.concatenate([ref[:, n * width : (n + 1) * width].T for ref in (acts_ref, got_ref)], axis=1)
        for n in range(3)
    ]
    first = place_ref[3] == 0
    for n, m in enumerate((0, 1, 1, 1, 2)):
        at = slice(n * half, (n + 1) * half)
        grads = jnp.concatenate([mine_ref[:, at], theirs_ref[:, at]], axis=0)
        terms = contract(turned[m], grads, PLAIN).astype(jnp.bfloat16)
        terms = terms.reshape(sent_ref.shape[0], 2, depth, half)
        kept_ref[:, :, at] = jnp.where(first, terms[:, 0], terms[:, 1])
        sent_ref[:, :, at] = jnp.where(first, terms[:, 1], terms[:, 0])


def column_call(kernel, info, place, pieces, args, outs, scratch):
    width = args[-1].shape[1]
    bf16 = jnp.bfloat16
    small = pl.BlockSpec(memory_space=pltpu.SMEM)
    inside = pl.BlockSpec(memory_space=pltpu.VMEM)
    anywhere = pl.BlockSpec(memory_space=pl.ANY)
    return pl.pallas_call(
        partial(kernel, [step for step, _ in pieces]),
        in_specs=[small] * 2 + [anywhere] * len(pieces) + [inside] * len(args),
        out_specs=[inside] * len(outs),
        out_shape=[jax.ShapeDtypeStruct(shape, kind) for shape, kind in outs],
        scratch_shapes=[
            *scratch,
            pltpu.VMEM((width, width), bf16),
            pltpu.VMEM((width, 3 * width), bf16),
            pltpu.VMEM((width, width), bf16),
            pltpu.SemaphoreType.DMA((20 * len(pieces),)),
        ],
        compiler_params=pltpu.CompilerParams(vmem_limit_bytes=56 * 2**20),
    )(info, place, *[value for _, value in pieces], *args)


def adam_kernel(place_ref, factor_ref, own_ref, other_ref, w_ref, first_ref, second_ref, *outs):
    half = w_ref.shape[2] // 2
    at = pl.ds(pl.multiple_of(pl.program_id(0) * half, TILE), half)
    own, other = own_ref[:, at], other_ref[:, at]
    low = place_ref[2] == 0
    grad = jnp.concatenate([jnp.where(low, own, other), jnp.where(low, other, own)], axis=1)
    grad = grad.astype(jnp.float32) * factor_ref[0]
    first, second, weight = adam_update(w_ref[0], first_ref[0], second_ref[0], grad, matrix_rate)
    for ref, value in zip(outs, (first, second, weight, weight.astype(jnp.bfloat16))):
        ref[0] = value


def attn_adam(place, factor, own, other, weight, first, second):
    small = pl.BlockSpec(memory_space=pltpu.SMEM)
    inside = pl.BlockSpec(memory_space=pltpu.VMEM)
    block = pl.BlockSpec((1, *weight.shape[1:]), lambda m: (m, 0, 0))
    kinds = [jnp.float32] * 3 + [jnp.bfloat16]
    return pl.pallas_call(
        adam_kernel,
        grid=(weight.shape[0],),
        in_specs=[small, small, inside, inside] + [block] * 3,
        out_specs=[block] * 4,
        out_shape=[jax.ShapeDtypeStruct(weight.shape, kind) for kind in kinds],
    )(place, factor.reshape(1), own, other, weight, first, second)


def whole_call(kernel, info, args, outs, scratch=()):
    inside = pl.BlockSpec(memory_space=pltpu.VMEM)
    return pl.pallas_call(
        kernel,
        in_specs=[pl.BlockSpec(memory_space=pltpu.SMEM)] + [inside] * len(args),
        out_specs=[inside] * len(outs),
        out_shape=[jax.ShapeDtypeStruct(shape, kind) for shape, kind in outs],
        scratch_shapes=list(scratch),
        compiler_params=pltpu.CompilerParams(vmem_limit_bytes=56 * 2**20),
    )(info, *args)


def gelu_pair(u):
    ratio = math.sqrt(2.0 / math.pi)
    square = u * u
    tanh = jnp.tanh(ratio * u * (1.0 + 0.044715 * square))
    rise = 0.5 * (1.0 + tanh)
    slope = (0.5 * ratio) * (1.0 - tanh * tanh) * (1.0 + (3.0 * 0.044715) * square)
    return u * rise, rise + u * slope


def ffn_kernel(
    plan, place_ref, a_ref, a_got_ref, up_ref, up_got_ref, *refs
):
    bf16 = jnp.bfloat16
    stacks, refs = refs[: len(plan)], refs[len(plan) :]
    out_ref, out_other_ref, da_ref, da_other_ref = refs[:4]
    y_sent_ref, y_kept_ref, x_sent_ref, x_kept_ref = refs[4:8]
    w_ref, tokens_ref, turned_ref, out_sum, da_sum, sem = refs[8:]
    step = pl.program_id(0)
    count, width = a_ref.shape
    chunk = x_sent_ref.shape[3]
    last = pl.num_programs(0) - 1

    @pl.when(step == 0)
    def _():
        copies = placing(plan, ffn_at, place_ref, stacks, [w_ref], sem, steps=False)
        for copy in copies:
            copy.start()
        for n, ref in enumerate((a_ref, a_got_ref, up_ref, up_got_ref)):
            k, at = n // 2, slice((n % 2) * count, (n % 2 + 1) * count)
            tokens_ref[k, at] = ref[...]
            turned_ref[k, :, at] = ref[...].T
        out_sum[...] = jnp.zeros_like(out_sum)
        da_sum[...] = jnp.zeros_like(da_sum)
        for copy in copies:
            copy.wait()

    lane = pl.ds(pl.multiple_of(step * chunk, chunk), chunk)
    w_in = w_ref[:width, lane]
    w_out = w_ref[width:, lane]
    activs, grads = [], []
    for n in (0, 1):
        at = slice(n * count, (n + 1) * count)
        activ, slope = gelu_pair(contract(tokens_ref[0, at], w_in, PLAIN))
        activ = activ.astype(bf16)
        grad = (contract(tokens_ref[1, at], w_out, PLAIN) * slope).astype(bf16)
        out_sum[at] += contract(activ, w_out, LAST)
        da_sum[at] += contract(grad, w_in, LAST)
        activs.append(activ)
        grads.append(grad)
    in_terms = contract(turned_ref[0], jnp.concatenate(grads, axis=0), PLAIN).astype(bf16)
    out_terms = contract(turned_ref[1], jnp.concatenate(activs, axis=0), PLAIN).astype(bf16)

    @pl.when(step < last)
    def _():
        first = place_ref[3] == 0
        y_kept_ref[...] = jnp.where(first, in_terms, out_terms)
        y_sent_ref[...] = jnp.where(first, out_terms, in_terms)

    @pl.when(step == last)
    def _():
        first = place_ref[1] == 0
        zs, _, depth, _ = x_sent_ref.shape
        for n, terms in enumerate((in_terms, out_terms)):
            terms = terms.reshape(zs, 2, depth, chunk)
            x_kept_ref[:, n] = jnp.where(first, terms[:, 0], terms[:, 1])
            x_sent_ref[:, n] = jnp.where(first, terms[:, 1], terms[:, 0])

    @pl.when(step == last)
    def _():
        out_ref[...] = out_sum[:count]
        out_other_ref[...] = out_sum[count:].astype(bf16)
        da_ref[...] = da_sum[:count]
        da_other_ref[...] = da_sum[count:].astype(bf16)


def feed_forward(place, normed_own, normed_got, up_own, up_got, pieces, chunk=768):
    count, width = normed_own.shape
    half = pieces[0][1].shape[-1]
    anywhere = pl.BlockSpec(memory_space=pl.ANY)
    inside = pl.BlockSpec(memory_space=pltpu.VMEM)
    steps = half // chunk
    lanes = pl.BlockSpec((width, chunk), lambda n: (0, jnp.minimum(n, steps - 2)))
    f32, bf16 = jnp.float32, jnp.bfloat16
    shapes = [((count, width), kind) for kind in (f32, bf16, f32, bf16)]
    shapes = shapes + [((width, half - chunk), bf16)] * 2 + [((4, 2, width // 8, chunk), bf16)] * 2
    return pl.pallas_call(
        partial(ffn_kernel, [step for step, _ in pieces]),
        grid=(steps,),
        in_specs=[pl.BlockSpec(memory_space=pltpu.SMEM)] + [inside] * 4 + [anywhere] * len(pieces),
        out_specs=[inside] * 4 + [lanes] * 2 + [inside] * 2,
        out_shape=[jax.ShapeDtypeStruct(shape, kind) for shape, kind in shapes],
        scratch_shapes=[
            pltpu.VMEM((2 * width, half), bf16),
            pltpu.VMEM((2, 2 * count, width), bf16),
            pltpu.VMEM((2, width, 2 * count), bf16),
            pltpu.VMEM((2 * count, width), f32),
            pltpu.VMEM((2 * count, width), f32),
            pltpu.SemaphoreType.DMA((16,)),
        ],
        compiler_params=pltpu.CompilerParams(vmem_limit_bytes=56 * 2**20),
    )(place, normed_own, normed_got, up_own, up_got, *[value for _, value in pieces])


def added(a, b):
    return (a.astype(jnp.float32) + b.astype(jnp.float32)).astype(jnp.bfloat16)


def z_summed(column, z):
    shard = pick(column, z, 0).astype(jnp.float32)
    for i in (1, 2, 3):
        other = pick(column, lax.bitwise_xor(z, i), 0)
        got = lax.ppermute(other, "z", [(k, k ^ i) for k in range(4)])
        shard = shard + got.astype(jnp.float32)
    return shard.astype(jnp.bfloat16)


def paired_body(
    tokens,
    cotangent,
    col_count,
    row_count,
    attn_weight,
    in_weight,
    out_weight,
    norm_param,
    attn_first,
    attn_second,
    in_first,
    in_second,
    out_first,
    out_second,
    norm_first,
    norm_second,
):
    f32 = jnp.float32
    bf16 = jnp.bfloat16
    z, x, y, c = (lax.axis_index(name) for name in ("z", "x", "y", "c"))
    width = tokens.shape[-1]
    hidden = in_weight.shape[1]
    depth = in_weight.shape[0]
    half = width // 2
    hidden_half = hidden // 2

    counts = jnp.stack([col_count, row_count])
    other_counts = swap(counts, "c")
    mine = jnp.where(z // 2 == c, counts, other_counts)
    mine = pick(mine, z % 2, 1)
    cols_live, rows_live = mine[0], mine[1]
    place = jnp.stack([z, x, c, y]).astype(jnp.int32)
    info = jnp.concatenate([place[:3], mine, place[3:]])
    tie = (lax.rsqrt(rows_live.astype(f32)) * (1.0 / math.sqrt(DH))).reshape(1)

    attn_low = attn_weight.astype(bf16)
    halves = attn_low.reshape(8, depth, 2, half)
    row_half = jnp.moveaxis(pick(halves[:3], c, 2), 0, 1).reshape(2, depth // 2, 3 * half)
    row_quarter = pick(row_half, y, 0)
    col_quarter = pick(pick(halves[3:], c, 2).reshape(5, 2, depth // 2, half), y, 1)
    row_z = gather_z(row_quarter)
    ffn_low = [in_weight.astype(bf16), out_weight.astype(bf16).T]
    ffn_low = [
        jnp.where(c == 0, low[:, :hidden_half], low[:, hidden_half:]) for low in ffn_low
    ]
    ffn_quarter = jnp.where(y == 0, *ffn_low)

    lanes = jnp.arange(width, dtype=jnp.int32) // depth
    norm_low = jnp.tile(norm_param.astype(bf16), (1, width // depth))
    norm_rows = jnp.where(lanes[None] == z * 2 + x, norm_low, jnp.zeros_like(norm_low))
    norm_rows = jnp.pad(norm_rows, ((0, 10), (0, 0)))
    part = tokens.shape[2] // 4
    tokens_here = merge_cores(tokens, c).reshape(4, 2 * part, width)
    parts = [
        jnp.concatenate([pick(tokens_here, lax.bitwise_xor(z, i), 0), norm_rows]) for i in range(4)
    ]
    parts = [parts[0]] + [
        lax.ppermute(parts[i], "z", [(k, k ^ i) for k in range(4)]) for i in (1, 2, 3)
    ]
    row_pieces = spread(jnp.stack(row_z))
    row_x, row_y, *parts, col_quarter = together(
        row_pieces[1][1], row_pieces[2][1], *parts, col_quarter
    )
    row_pieces = [
        row_pieces[0],
        ((1, 0, 0), row_x),
        ((0, 1, 0), row_y),
        row_pieces[3],
    ]
    tokens_z = jnp.stack(parts)
    col_z = gather_z(col_quarter)
    tokens_x, row_last, ffn_quarter, *col_z = together(
        swap(tokens_z, "x"), row_pieces[3][1], ffn_quarter, *col_z
    )
    row_pieces[3] = (row_pieces[3][0], row_last)
    col_pieces = spread(jnp.stack(col_z))
    ffn_z = lax.all_to_all(
        jnp.broadcast_to(ffn_quarter, (4, *ffn_quarter.shape)), "z", 0, 0, tiled=True
    )
    tokens_far = swap(tokens_x, "c")
    tokens_far, col_x, col_y, ffn_z, up = together(
        tokens_far, col_pieces[1][1], col_pieces[2][1], ffn_z, merge_cores(cotangent, c)
    )
    up = lax.all_to_all(up, ("z", "x"), 0, 0, tiled=True)
    col_pieces[1] = (col_pieces[1][0], col_x)

    rows = 8
    count = rows * part
    stream_zero, near_normed, far_normed, w_row, norm_gain, near, far, mixed_heads = row_attention(
        place,
        info,
        tie,
        [((0, 0), tokens_z), ((1, 0), tokens_x), ((0, 1), swap(tokens_z, "c")), ((1, 1), tokens_far)],
        row_pieces,
        rows,
        half,
    )
    resid_one = stream_zero.astype(f32)
    mixed_heads = mixed_heads.reshape(2, count, half)
    ffn_pieces = spread(ffn_z)
    col_quarters = [col_pieces[0][1], col_x, col_y]
    mixed_heads, up, last, ffn_x, ffn_y, *col_others = together(
        mixed_heads, up, swap(col_x, "y"), ffn_pieces[1][1], ffn_pieces[2][1],
        *[swap(value, "c") for value in col_quarters],
    )
    ffn_pieces[1:] = [
        (ffn_pieces[1][0], ffn_x),
        (ffn_pieces[2][0], ffn_y),
        (ffn_pieces[3][0], swap(ffn_x, "y")),
    ]
    steps = [(j, m) for m in (0, 1) for j in (0, 1)]
    col_pieces = [((*step, 0), v) for step, v in zip(steps, [*col_quarters, last])]
    col_others = [*col_others, swap(last, "c")]
    col_pieces = col_pieces + [((*step, 1), v) for step, v in zip(steps, col_others)]

    whole_shape, wide_shape = ((count, width), bf16), ((rows, part, 3 * width), bf16)
    acts, stream_one, qkv_two, resid_three, normed_three = column_call(
        col_fwd_kernel,
        info,
        place,
        col_pieces,
        [stream_zero, mixed_heads[0], swap(mixed_heads[1], "c"), norm_gain],
        [((count, 3 * width), bf16), whole_shape, wide_shape, ((count, width), f32), whole_shape],
        [pltpu.VMEM((rows, part, width), bf16)],
    )

    column = x * (2 * part) + c * part + jnp.arange(part, dtype=jnp.int32)
    live = jnp.logical_and(
        (jnp.arange(rows, dtype=jnp.int32) < rows_live)[:, None], (column < cols_live)[None, :]
    )
    up = jnp.where(live[..., None], up, jnp.zeros_like(up)).reshape(count, width)
    out_own, out_other, da_own, da_other, *ffn_terms = feed_forward(
        place, normed_three, swap(normed_three, "c"), up, swap(up, "c"), ffn_pieces
    )
    da_got = swap(da_other, "c")
    out_got = swap(out_other, "c")
    y_sent, y_kept, x_sent, x_kept = ffn_terms
    y_got, x_got = swap(y_sent, "y"), swap(x_sent, "x")

    acts_got = swap(acts, "c")
    result, grad_stream, grad_own, grad_other, attn_mine, attn_theirs, col_norms = column_call(
        col_bwd_kernel,
        info,
        place,
        col_pieces,
        [up, da_own, da_got, out_own, out_got, resid_three, stream_one, qkv_two, norm_gain],
        [whole_shape] * 2
        + [((count, half), bf16)] * 2
        + [((count, 5 * half), bf16)] * 2
        + [((4, width), f32)],
        [pltpu.VMEM((rows, part, 3 * width), bf16), pltpu.VMEM((rows, part, width), bf16)],
    )

    result, x_got, y_got = together(result, x_got, y_got)
    block_out = to_blocks(result.reshape(rows, part, width))
    (
        near_part, near_theirs, far_part, far_theirs, row_sent, row_kept,
        ffn_to_x, ffn_x, ffn_to_y, ffn_y,
    ) = row_attention_back(
        info, tie, near, far, grad_own, swap(grad_other, "c"), w_row, near_normed, far_normed,
        y_kept, y_got, x_kept, x_got,
    )
    row_sent, far_theirs, near_theirs, attn_theirs, block_out, ffn_to_x, ffn_to_y = together(
        row_sent, far_theirs, near_theirs, attn_theirs, block_out, ffn_to_x, ffn_to_y
    )
    ffn_x_got, ffn_y_got = swap(ffn_to_x, "x"), swap(ffn_to_y, "y")
    row_got = swap(row_sent, "x")
    far_sum = added(far_part, swap(far_theirs, "c"))
    far_got = swap(far_sum, "x")
    near_got = swap(near_theirs, "c")
    attn_sent, attn_kept = whole_call(
        attn_terms_kernel,
        place,
        [acts, acts_got, attn_mine, swap(attn_theirs, "c")],
        [((8, depth // 2, 5 * half), bf16)] * 2,
    )
    attn_got = swap(attn_sent, "y")
    attn_kept, ffn_y_got, ffn_x_got = together(attn_kept, ffn_y_got, ffn_x_got)
    ffn_column = jnp.concatenate([added(ffn_x, ffn_x_got), added(ffn_y, ffn_y_got)], axis=2)
    ffn_own = z_summed(ffn_column, z)
    row_column, ffn_own = together(added(row_kept, row_got), ffn_own)
    row_own = z_summed(row_column, z)
    far_got, attn_got, block_out = together(far_got, attn_got, block_out)
    block_out = to_rows(block_out, c)
    attn_pair_terms = added(attn_kept, attn_got).reshape(4, 2, depth // 2, 5 * half)
    grad_normed_one = near_part + near_got.astype(f32) + far_got.astype(f32)
    _, norm_back_one = jax.vjp(layer_norm, resid_one, norm_gain[0], norm_gain[1])
    part_one, gain_grad_one, shift_grad_one = norm_back_one(grad_normed_one)
    grad_input = (grad_stream.astype(f32) + part_one).astype(bf16)
    grad_tokens = to_blocks(grad_input.reshape(rows, part, width))

    norm_stack = jnp.concatenate([jnp.stack([gain_grad_one, shift_grad_one]), col_norms])
    norm_terms = jnp.moveaxis(norm_stack.reshape(6, 4, 2, depth), 0, 2).reshape(4, 2, depth // 2, 12)
    norm_terms = jnp.pad(norm_terms.astype(bf16), ((0, 0), (0, 0), (0, 0), (0, TILE - 12)))
    attn_blocks = jnp.concatenate([attn_pair_terms, norm_terms], axis=3)
    attn_column = added(pick(attn_blocks, x, 1), swap(pick(attn_blocks, 1 - x, 1), "x"))
    attn_column, row_own, grad_tokens = together(attn_column, row_own, grad_tokens)
    attn_own = z_summed(attn_column, z)
    grad_tokens = to_rows(grad_tokens, c).astype(f32)
    row_grad = added(row_own, swap(row_own, "y"))
    attn_y = swap(attn_own, "y")
    attn_grad_b = joined(attn_own[:, : 5 * half], attn_y[:, : 5 * half], y, 0)
    norm_grad = added(attn_own[:, 5 * half :], attn_y[:, 5 * half :])
    ffn_grads = [ffn_own, swap(ffn_own, "y")]

    row_other = swap(row_grad, "c")
    attn_other = swap(attn_grad_b, "c")
    norm_grad = norm_grad.astype(f32) + swap(norm_grad, "c").astype(f32)
    norm_grad = norm_grad[:, :12].reshape(6, depth)
    ffn_whole = [joined(piece, swap(piece, "c"), c, 1) for piece in ffn_grads]

    in_grad = jnp.where(y == 0, *ffn_whole).astype(f32)
    out_grad = jnp.where(y == 0, *ffn_whole[::-1]).astype(f32).T

    squares = sum(
        jnp.sum(jnp.square(g.astype(f32))) for g in (row_grad, attn_grad_b, *ffn_grads)
    )
    squares = squares + swap(squares, "c") + jnp.sum(norm_grad * norm_grad)
    squares = jnp.broadcast_to(squares, (8, 8, TILE))
    squares = lax.all_to_all(squares, ("z", "x"), 0, 0, tiled=True)
    grad_norm = jnp.sqrt(jnp.sum(squares[:, 0, 0]))
    factor = clip_bound / jnp.maximum(grad_norm, clip_bound)
    attn_first_new, attn_second_new, attn_weight_new, attn_copy = attn_adam(
        place,
        factor,
        jnp.concatenate([row_grad, attn_grad_b], axis=1),
        jnp.concatenate([row_other, attn_other], axis=1),
        attn_weight,
        attn_first,
        attn_second,
    )
    in_first_new, in_second_new, in_weight_new = adam_update(
        in_weight, in_first, in_second, in_grad * factor, matrix_rate
    )
    out_first_new, out_second_new, out_weight_new = adam_update(
        out_weight, out_first, out_second, out_grad * factor, matrix_rate
    )
    norm_first_new, norm_second_new, norm_new = adam_update(
        norm_param, norm_first, norm_second, norm_grad * factor, norm_rate
    )
    return (
        block_out,
        grad_tokens,
        grad_norm,
        attn_first_new,
        attn_second_new,
        attn_weight_new,
        attn_copy,
        in_first_new,
        in_second_new,
        in_weight_new,
        in_weight_new.astype(bf16),
        out_first_new,
        out_second_new,
        out_weight_new,
        out_weight_new.astype(bf16),
        norm_first_new,
        norm_second_new,
        norm_new,
    )


def paired_layout(mesh):
    return dict(mesh.shape) == {"seq": 8, "grp": 4}


def mapped(run, mesh, seq, grp):
    placed = (
        P(grp, seq, None, None),
        P(grp, seq, None, None),
        P(grp),
        P(grp),
        P(None, seq, None),
        P(seq, None),
        P(None, seq),
        P(None, seq),
        P(None, seq, None),
        P(None, seq, None),
        P(seq, None),
        P(seq, None),
        P(None, seq),
        P(None, seq),
        P(None, seq),
        P(None, seq),
    )
    return jax.shard_map(
        run,
        mesh=mesh,
        in_specs=placed,
        out_specs=(
            P(grp, seq, None, None),
            P(grp, seq, None, None),
            P(),
            P(None, seq, None),
            P(None, seq, None),
            P(None, seq, None),
            P(None, seq, None),
            P(seq, None),
            P(seq, None),
            P(seq, None),
            P(seq, None),
            P(None, seq),
            P(None, seq),
            P(None, seq),
            P(None, seq),
            P(None, seq),
            P(None, seq),
            P(None, seq),
        ),
        check_vma=False,
    )


def solution(mesh):
    if not paired_layout(mesh):
        return mapped(general_body, mesh, "seq", "grp")
    fine = Mesh(mesh.devices.reshape(4, 2, 2, 2), ("z", "x", "y", "c"))
    return mapped(paired_body, fine, ("z", "x"), ("y", "c"))
```

```python
from functools import partial
import math

import jax
import jax.numpy as jnp
from jax import lax
from jax.experimental import pallas as pl
from jax.experimental.pallas import tpu as pltpu
from jax.sharding import Mesh
from jax.sharding import PartitionSpec as P

H = 12
DH = 64
STEP = 5


eps_norm = 1e-05
masked_score = -1000000000.0
clip_bound = 1.0
beta_one = 0.5
beta_two = 0.5
matrix_rate = 0.06
norm_rate = 0.3
decay_rate = 0.01
adam_eps = 1e-08


def in_blocks(x, dim, length):
    lengths = x.shape
    pieces = x.reshape(*lengths[:dim], length, lengths[dim] // length, *lengths[dim + 1 :])
    return jnp.moveaxis(pieces, dim, 0)


def sent_and_summed(x, axis, dim):
    length = lax.axis_size(axis)
    pieces = lax.all_to_all(in_blocks(x, dim, length), axis, 0, 0, tiled=True)
    return jnp.sum(pieces.astype(jnp.float32), axis=0)


def layer_norm(value, gain, shift):
    mean = jnp.mean(value, axis=-1, keepdims=True)
    centred = value - mean
    spread = jnp.mean(centred * centred, axis=-1, keepdims=True)
    return centred * lax.rsqrt(spread + eps_norm) * gain + shift


def softmax_rows(scores, keep):
    scores = jnp.where(keep, scores, masked_score)
    top = jnp.max(scores, axis=-1, keepdims=True)
    expo = jnp.exp(scores - top)
    return expo / jnp.sum(expo, axis=-1, keepdims=True)


def softmax_back(probs, grads):
    return probs * (grads - jnp.sum(probs * grads, axis=-1, keepdims=True))


def adam_update(weight, first, second, grad, rate):
    first_new = beta_one * first + (1.0 - beta_one) * grad
    second_new = beta_two * second + (1.0 - beta_two) * grad * grad
    first_hat = first_new / (1.0 - beta_one**STEP)
    second_hat = second_new / (1.0 - beta_two**STEP)
    weight_new = weight - rate * (
        first_hat / (jnp.sqrt(second_hat) + adam_eps) + decay_rate * weight
    )
    return (first_new, second_new, weight_new)


def attn_pair(normed, grad_proj, mixed, grad_branch):
    width = normed.shape[-1]
    qkv_terms = jnp.einsum("prcd,kprce->dke", normed, grad_proj, preferred_element_type=jnp.float32)
    output_terms = jnp.einsum(
        "prcd,prce->de", mixed, grad_branch, preferred_element_type=jnp.float32
    )
    return jnp.concatenate([qkv_terms, output_terms[:, None, :]], axis=1).reshape(width, 4 * width)


def general_body(
    tokens,
    cotangent,
    col_count,
    row_count,
    attn_weight,
    in_weight,
    out_weight,
    norm_param,
    attn_first,
    attn_second,
    in_first,
    in_second,
    out_first,
    out_second,
    norm_first,
    norm_second,
):
    f32 = jnp.float32
    bf16 = jnp.bfloat16
    prot, rows_dev, cols, width = tokens.shape
    hidden = in_weight.shape[1]
    head_scale = 1.0 / math.sqrt(DH)
    attn_full, in_full, out_full, norm_full = (
        lax.all_gather(attn_weight.astype(bf16), "seq", axis=1, tiled=True),
        lax.all_gather(in_weight.astype(bf16), "seq", axis=0, tiled=True),
        lax.all_gather(out_weight.astype(bf16), "seq", axis=1, tiled=True),
        lax.all_gather(norm_param.astype(bf16), "seq", axis=1, tiled=True),
    )
    norm_gain = norm_full.astype(f32)
    row_ids = lax.axis_index("seq") * rows_dev + jnp.arange(rows_dev, dtype=jnp.int32)
    row_live = (row_ids[None, :] < row_count[:, None]).astype(f32)
    col_live = jnp.arange(cols, dtype=jnp.int32)[None, :] < col_count[:, None]
    tie_scale = lax.rsqrt(row_count.astype(f32)) * head_scale
    live = row_live[:, :, None] * col_live.astype(f32)[:, None, :]
    grad_out = (cotangent.astype(f32) * live[..., None]).astype(bf16)
    resid_one = tokens.astype(f32)
    normed_one = layer_norm(resid_one, norm_gain[0], norm_gain[1]).astype(bf16)
    proj_one = jnp.einsum(
        "prcd,kde->kprce", normed_one, attn_full[0:3], preferred_element_type=f32
    ).astype(bf16)
    proj_one = proj_one.reshape(3, prot, rows_dev, cols, H, DH)
    query_one, key_one, value_one = (proj_one[0], proj_one[1], proj_one[2])
    masked_query = query_one * row_live[:, :, None, None, None].astype(bf16)
    partial_scores = (
        jnp.einsum("prihe,prjhe->phij", masked_query, key_one, preferred_element_type=f32)
        * tie_scale[:, None, None, None]
    )
    keep_cols = col_live[:, None, None, :]
    score_part = lax.psum_scatter(partial_scores, "seq", scatter_dimension=2, tiled=True)
    probs_one = softmax_rows(score_part, keep_cols)
    probs_low = lax.all_gather(probs_one.astype(bf16), "seq", axis=2, tiled=True)
    mixed_one = jnp.einsum(
        "phij,prjhe->prihe", probs_low, value_one, preferred_element_type=f32
    ).astype(bf16)
    mixed_one = mixed_one.reshape(prot, rows_dev, cols, width)
    branch_one = jnp.einsum("prcd,de->prce", mixed_one, attn_full[3], preferred_element_type=f32)
    stream_one = (resid_one + branch_one).astype(bf16)
    stream_cols, up_grad = (
        lax.all_to_all(stream_one, "seq", split_axis=2, concat_axis=1, tiled=True),
        lax.all_to_all(grad_out, "seq", split_axis=2, concat_axis=1, tiled=True),
    )
    rows = stream_cols.shape[1]
    cols_dev = stream_cols.shape[2]
    row_live_all = jnp.arange(rows, dtype=jnp.int32)[None, :] < row_count[:, None]
    resid_two = stream_cols.astype(f32)
    normed_two = layer_norm(resid_two, norm_gain[2], norm_gain[3]).astype(bf16)
    proj_two = jnp.einsum(
        "prcd,kde->kprce", normed_two, attn_full[4:7], preferred_element_type=f32
    ).astype(bf16)
    proj_two = proj_two.reshape(3, prot, rows, cols_dev, H, DH)
    query_two, key_two, value_two = (proj_two[0], proj_two[1], proj_two[2])
    scores_two = (
        jnp.einsum("prche,psche->pchrs", query_two, key_two, preferred_element_type=f32)
        * head_scale
    )
    probs_two = softmax_rows(scores_two, row_live_all[:, None, None, None, :])
    probs_two_low = probs_two.astype(bf16)
    mixed_two = jnp.einsum(
        "pchrs,psche->prche", probs_two_low, value_two, preferred_element_type=f32
    ).astype(bf16)
    mixed_two = mixed_two.reshape(prot, rows, cols_dev, width)
    resid_three = resid_two + jnp.einsum(
        "prcd,de->prce", mixed_two, attn_full[7], preferred_element_type=f32
    )
    normed_three = layer_norm(resid_three, norm_gain[4], norm_gain[5]).astype(bf16)
    inner = jnp.einsum("prcd,df->prcf", normed_three, in_full, preferred_element_type=f32)
    activ = jax.nn.gelu(inner, approximate=True).astype(bf16)
    result = (
        resid_three + jnp.einsum("prcf,fd->prcd", activ, out_full, preferred_element_type=f32)
    ).astype(bf16)
    block_out = lax.all_to_all(result, "seq", split_axis=1, concat_axis=2, tiled=True)
    grad_act = jnp.einsum("prcd,fd->prcf", up_grad, out_full, preferred_element_type=f32)
    _, gelu_back = jax.vjp(partial(jax.nn.gelu, approximate=True), inner)
    grad_inner = gelu_back(grad_act)[0].astype(bf16)
    grad_normed_three = jnp.einsum("prcf,df->prcd", grad_inner, in_full, preferred_element_type=f32)
    _, norm_back_three = jax.vjp(layer_norm, resid_three, norm_gain[4], norm_gain[5])
    part_three, gain_grad_three, shift_grad_three = norm_back_three(grad_normed_three)
    grad_three = up_grad.astype(f32) + part_three
    grad_branch_two = grad_three.astype(bf16)
    grad_mixed_two = jnp.einsum(
        "prce,de->prcd", grad_branch_two, attn_full[7], preferred_element_type=f32
    ).astype(bf16)
    grad_mixed_two = grad_mixed_two.reshape(prot, rows, cols_dev, H, DH)
    grad_probs_two = jnp.einsum(
        "prche,psche->pchrs", grad_mixed_two, value_two, preferred_element_type=f32
    )
    grad_value_two = jnp.einsum(
        "pchrs,prche->psche", probs_two_low, grad_mixed_two, preferred_element_type=f32
    )
    grad_scores_two = softmax_back(probs_two, grad_probs_two).astype(bf16)
    grad_query_two = (
        jnp.einsum("pchrs,psche->prche", grad_scores_two, key_two, preferred_element_type=f32)
        * head_scale
    )
    grad_key_two = (
        jnp.einsum("pchrs,prche->psche", grad_scores_two, query_two, preferred_element_type=f32)
        * head_scale
    )
    grad_proj_two = jnp.stack([grad_query_two, grad_key_two, grad_value_two]).astype(bf16)
    grad_proj_two = grad_proj_two.reshape(3, prot, rows, cols_dev, width)
    grad_normed_two = jnp.einsum(
        "kprce,kde->prcd", grad_proj_two, attn_full[4:7], preferred_element_type=f32
    )
    _, norm_back_two = jax.vjp(layer_norm, resid_two, norm_gain[2], norm_gain[3])
    part_two, gain_grad_two, shift_grad_two = norm_back_two(grad_normed_two)
    grad_stream = (grad_three + part_two).astype(bf16)
    col_attn_terms = attn_pair(normed_two, grad_proj_two, mixed_two, grad_branch_two)
    in_terms = jnp.einsum("prcd,prcf->df", normed_three, grad_inner, preferred_element_type=f32)
    out_terms = jnp.einsum("prcf,prcd->df", activ, up_grad, preferred_element_type=f32)
    grad_rows = lax.all_to_all(grad_stream, "seq", split_axis=1, concat_axis=2, tiled=True)
    grad_mixed_one = jnp.einsum(
        "prce,de->prcd", grad_rows, attn_full[3], preferred_element_type=f32
    ).astype(bf16)
    grad_mixed_one = grad_mixed_one.reshape(prot, rows_dev, cols, H, DH)
    partial_grads = jnp.einsum(
        "prihe,prjhe->phij", grad_mixed_one, value_one, preferred_element_type=f32
    )
    grad_value_one = jnp.einsum(
        "phij,prihe->prjhe", probs_low, grad_mixed_one, preferred_element_type=f32
    )
    grad_part = sent_and_summed(partial_grads.astype(jnp.bfloat16), "seq", 2)
    grad_scores_one = lax.all_gather(
        softmax_back(probs_one, grad_part).astype(bf16), "seq", axis=2, tiled=True
    )
    tie_rows = row_live[:, :, None, None, None] * tie_scale[:, None, None, None, None]
    grad_query_one = (
        jnp.einsum("phij,prjhe->prihe", grad_scores_one, key_one, preferred_element_type=f32)
        * tie_rows
    )
    grad_key_one = (
        jnp.einsum("phij,prihe->prjhe", grad_scores_one, masked_query, preferred_element_type=f32)
        * tie_scale[:, None, None, None, None]
    )
    grad_proj_one = jnp.stack([grad_query_one, grad_key_one, grad_value_one]).astype(bf16)
    grad_proj_one = grad_proj_one.reshape(3, prot, rows_dev, cols, width)
    grad_normed_one = jnp.einsum(
        "kprce,kde->prcd", grad_proj_one, attn_full[0:3], preferred_element_type=f32
    )
    _, norm_back_one = jax.vjp(layer_norm, resid_one, norm_gain[0], norm_gain[1])
    part_one, gain_grad_one, shift_grad_one = norm_back_one(grad_normed_one)
    grad_tokens = grad_rows.astype(f32) + part_one
    norm_stack = jnp.stack(
        [
            gain_grad_one,
            shift_grad_one,
            gain_grad_two,
            shift_grad_two,
            gain_grad_three,
            shift_grad_three,
        ]
    )
    row_attn_terms = attn_pair(normed_one, grad_proj_one, mixed_one, grad_rows)
    owned = lax.psum_scatter(
        jnp.concatenate(
            [row_attn_terms, col_attn_terms, in_terms, out_terms, norm_stack.T], axis=1
        ),
        "seq",
        scatter_dimension=0,
        tiled=True,
    )
    width_dev = owned.shape[0]
    row_part = owned[:, : 4 * width].reshape(width_dev, 4, width)
    col_part = owned[:, 4 * width : 8 * width].reshape(width_dev, 4, width)
    in_part = owned[:, 8 * width : 8 * width + hidden]
    out_part = owned[:, 8 * width + hidden : 8 * width + 2 * hidden].T
    norm_part = owned[:, 8 * width + 2 * hidden :].T
    attn_part = jnp.concatenate([row_part, col_part], axis=1).transpose(1, 0, 2)
    attn_grad, in_grad, out_grad, norm_grad = (
        lax.psum(attn_part.astype(jnp.bfloat16), "grp").astype(jnp.float32),
        lax.psum(in_part.astype(jnp.bfloat16), "grp").astype(jnp.float32),
        lax.psum(out_part.astype(jnp.bfloat16), "grp").astype(jnp.float32),
        lax.psum(norm_part.astype(jnp.bfloat16), "grp").astype(jnp.float32),
    )
    squares = (
        jnp.sum(attn_grad * attn_grad)
        + jnp.sum(in_grad * in_grad)
        + jnp.sum(out_grad * out_grad)
        + jnp.sum(norm_grad * norm_grad)
    )
    grad_norm = jnp.sqrt(lax.psum(squares, "seq"))
    factor = clip_bound / jnp.maximum(grad_norm, clip_bound)
    attn_first_new, attn_second_new, attn_weight_new = adam_update(
        attn_weight, attn_first, attn_second, attn_grad * factor, matrix_rate
    )
    in_first_new, in_second_new, in_weight_new = adam_update(
        in_weight, in_first, in_second, in_grad * factor, matrix_rate
    )
    out_first_new, out_second_new, out_weight_new = adam_update(
        out_weight, out_first, out_second, out_grad * factor, matrix_rate
    )
    norm_first_new, norm_second_new, norm_new = adam_update(
        norm_param, norm_first, norm_second, norm_grad * factor, norm_rate
    )
    return (
        block_out,
        grad_tokens,
        grad_norm,
        attn_first_new,
        attn_second_new,
        attn_weight_new,
        attn_weight_new.astype(bf16),
        in_first_new,
        in_second_new,
        in_weight_new,
        in_weight_new.astype(bf16),
        out_first_new,
        out_second_new,
        out_weight_new,
        out_weight_new.astype(bf16),
        norm_first_new,
        norm_second_new,
        norm_new,
    )


PAIR = [(0, 1), (1, 0)]
TILE = 128


def swap(value, axis):
    return lax.ppermute(value, axis, PAIR)


def pick(value, index, axis):
    return lax.dynamic_index_in_dim(value, index, axis, keepdims=False)


def joined(own, other, place, axis):
    return jnp.where(
        place == 0,
        jnp.concatenate([own, other], axis=axis),
        jnp.concatenate([other, own], axis=axis),
    )


def merge(own, other, place, axis):
    return jnp.where(
        place == 0,
        jnp.stack([own, other], axis=axis),
        jnp.stack([other, own], axis=axis),
    )


def merge_cores(value, c):
    prot, _, cols, width = value.shape
    part = cols // 4
    split = value.reshape(prot, 2, 2, part, width)
    got = swap(pick(split, 1 - c, 2), "c")
    both = merge(pick(split, c, 2), got, c, 0)
    return both.reshape(8, part, width)


def to_blocks(value):
    return lax.all_to_all(value, ("z", "x"), 0, 0, tiled=True)


def to_rows(got, c):
    _, part, width = got.shape
    got = got.reshape(2, 2, 2, part, width)
    other = swap(pick(got, 1 - c, 0), "c")
    both = merge(pick(got, c, 0), other, c, 2)
    return both.reshape(2, 1, 4 * part, width)


def together(*values):
    return lax.optimization_barrier(values)


def gather_z(own):
    return [own] + [lax.ppermute(own, "z", [(k, k ^ i) for k in range(4)]) for i in (1, 2, 3)]


def spread(over_z):
    over_x = swap(over_z, "x")
    quarter = [((0, 0, 0), over_z, 0), ((1, 0, 0), over_x, 0)]
    return quarter + [((j, 1, 0), swap(value, "y"), 0) for (j, _, _), value, _ in quarter]


def across(over_x, over_y):
    half = over_x.shape[0] // 2
    return swap(over_x[:half], "y"), swap(over_y[half:], "x")


def across_pieces(by_y, by_x):
    return [((1, 1, 0), by_y, 0), ((1, 1, 0), by_x, by_y.shape[0])]


def plan_of(pieces):
    return [(step, first) for step, _, first in pieces]


def placing(plan, outs_at, place_ref, stacks, outs, sem, steps=True):
    copies = []
    for stack, ((j, m, k), first) in zip(stacks, plan):
        x, y, c = (lax.bitwise_xor(place_ref[n], step) for n, step in ((1, j), (3, m), (2, k)))
        for i in range(stack.shape[0]):
            z = first + i
            shard = (lax.bitwise_xor(place_ref[0], z) if steps else z) * 2 + x
            for source, target in outs_at(stack.at[i], outs, shard, y, c):
                copies.append(pltpu.make_async_copy(source, target, sem.at[len(copies)]))
    return copies


def row_attn_at(ref, outs, shard, y, c):
    depth = outs[0].shape[0] // 16
    at = pl.multiple_of((shard * 2 + y) * depth, depth)
    return [(ref, outs[0].at[pl.ds(at, depth)])]


def ffn_at(ref, outs, shard, y, c):
    depth = ref.shape[0]
    at = pl.multiple_of((y * 8 + shard) * depth, depth)
    return [(ref, outs[0].at[pl.ds(at, depth)])]


def col_attn_at(ref, outs, shard, y, c):
    depth, half = ref.shape[1], ref.shape[2]
    at = pl.multiple_of((shard * 2 + y) * depth, depth)
    moves = []
    slots = [(o, n) for o, out in enumerate(outs) for n in range(out.shape[1] // (2 * half))]
    for k, (o, n) in enumerate(slots):
        lane = pl.multiple_of(c * half + n * 2 * half, TILE)
        moves.append((ref.at[k], outs[o].at[pl.ds(at, depth), pl.ds(lane, half)]))
    return moves


def contract(a, b, dims):
    return lax.dot_general(a, b, (dims, ((), ())), preferred_element_type=jnp.float32)


LAST = ((1,), (1,))
FIRST = ((0,), (0,))
PLAIN = ((1,), (0,))


def softmax_of(scores, keep):
    scores = jnp.where(keep, scores, masked_score)
    expo = jnp.exp(scores - jnp.max(scores, axis=-1, keepdims=True))
    return expo / jnp.sum(expo, axis=-1, keepdims=True)


def head_lanes(lanes):
    side = lax.broadcasted_iota(jnp.int32, (1, lanes), 1) % TILE < DH
    return (side, jnp.logical_not(side))


def only(keep, value):
    return jnp.where(keep, value, jnp.zeros_like(value))


def column_keep(info_ref, own_cols, near, part):
    key = lax.broadcasted_iota(jnp.int32, (1, 2 * near), 1)
    far = key >= near
    inner = key % near
    x = jnp.where(far, 1 - info_ref[1], info_ref[1])
    c = jnp.where(inner >= part, 1 - info_ref[2], info_ref[2])
    column = x * near + c * part + inner % part
    return column < info_ref[3]


def live_pair(value, row, info_ref):
    lane = lax.broadcasted_iota(jnp.int32, (1, value.shape[1]), 1) // TILE + row
    return only(lane < info_ref[4], value)


def head_pair(ref, row, lane):
    blocks, _, part, _ = ref.shape
    found = [ref[:, row + n, :, lane : lane + TILE].reshape(blocks * part, TILE) for n in (0, 1)]
    return jnp.concatenate(found, axis=1)


def row_fwd_kernel(token_plan, weight_plan, place_ref, info_ref, tie_ref, *refs):
    bf16 = jnp.bfloat16
    f32 = jnp.float32
    tokens, refs = refs[: len(token_plan)], refs[len(token_plan) :]
    stacks, refs = refs[: len(weight_plan)], refs[len(weight_plan) :]
    own_ref, near_tokens_ref, far_tokens_ref, w_ref, gain_ref, near_ref, far_ref, o_ref = refs[:8]
    all_ref, norm_ref, token_sem, weight_sem = refs[8:]
    blocks, rows, part, lanes = near_ref.shape
    half = lanes // 3
    count = rows * part
    near = blocks * part
    copies = []
    for stack, (j, k) in zip(tokens, token_plan):
        x = lax.bitwise_xor(place_ref[1], j)
        for i in range(4):
            row = lax.bitwise_xor(place_ref[0], i) * 2 + x
            moves = [(stack.at[i, pl.ds(0, 2 * part)], all_ref.at[k, row])]
            if k == 0:
                moves.append((stack.at[i, pl.ds(2 * part, 16)], norm_ref.at[j * 4 + i]))
            for source, target in moves:
                copies.append(pltpu.make_async_copy(source, target, token_sem.at[len(copies)]))
    weights = placing(weight_plan, row_attn_at, place_ref, stacks, [w_ref], weight_sem)
    for copy in copies + weights:
        copy.start()
    for copy in copies:
        copy.wait()
    gains = jnp.sum(norm_ref[...].astype(f32), axis=0)
    gain_ref[...] = gains
    x = info_ref[1]
    for ref, side in ((near_tokens_ref, x), (far_tokens_ref, 1 - x)):
        at = pl.ds(pl.multiple_of(side * part, part), part)
        for k in range(blocks):
            value = all_ref[k, :, at, :].reshape(count, -1)
            if k == 0:
                @pl.when(side == x)
                def _():
                    own_ref[...] = value
            found = normed(value.astype(f32), gains[0:1], gains[1:2])[0]
            ref[k * count : (k + 1) * count] = found.astype(bf16)
    for copy in weights:
        copy.wait()
    for n in range(3):
        at = slice(n * half, (n + 1) * half)
        found = contract(near_tokens_ref[...], w_ref[:, at], PLAIN).astype(bf16)
        near_ref[:, :, :, at] = found.reshape(blocks, rows, part, half)
        if n > 0:
            found = contract(far_tokens_ref[...], w_ref[:, at], PLAIN).astype(bf16)
            far_ref[:, :, :, (n - 1) * half : n * half] = found.reshape(blocks, rows, part, half)
    sides = head_lanes(2 * TILE)
    keep = column_keep(info_ref, near, near, part)
    tie = tie_ref[0]
    for lane in range(0, half, TILE):
        scores = [jnp.zeros((near, 2 * near), f32) for _ in sides]
        for row in range(0, rows, 2):
            query = live_pair(head_pair(near_ref, row, lane), row, info_ref)
            key = jnp.concatenate(
                [head_pair(near_ref, row, half + lane), head_pair(far_ref, row, lane)], axis=0
            )
            for n, side in enumerate(sides):
                scores[n] = scores[n] + contract(only(side, query), key, LAST)
        probs = [softmax_of(s * tie, keep).astype(bf16) for s in scores]
        for row in range(0, rows, 2):
            value = jnp.concatenate(
                [head_pair(near_ref, row, 2 * half + lane), head_pair(far_ref, row, half + lane)],
                axis=0,
            )
            mixed = jnp.where(
                sides[0], contract(probs[0], value, PLAIN), contract(probs[1], value, PLAIN)
            ).astype(bf16)
            for n in (0, 1):
                o_ref[:, row + n, :, lane : lane + TILE] = mixed[:, n * TILE : (n + 1) * TILE].reshape(
                    blocks, part, TILE
                )


def row_bwd_kernel(
    info_ref, tie_ref, near_ref, far_ref, own_ref, got_ref, w_ref, near_tokens_ref, far_tokens_ref,
    y_kept_ref, y_got_ref, x_kept_ref, x_got_ref,
    near_part_ref, near_theirs_ref, far_part_ref, far_theirs_ref, sent_ref, kept_ref,
    to_x_ref, with_x_ref, to_y_ref, with_y_ref, do_ref, d_near_ref, d_far_ref,
):
    bf16 = jnp.bfloat16
    blocks, rows, part, lanes = near_ref.shape
    half = lanes // 3
    near = blocks * part
    sides = head_lanes(2 * TILE)
    keep = column_keep(info_ref, near, near, part)
    tie = tie_ref[0]
    do_ref[0] = own_ref[...].reshape(rows, part, half)
    do_ref[1] = got_ref[...].reshape(rows, part, half)

    for lane in range(0, half, TILE):

        def pair(ref, row, first):
            at = slice(first + lane, first + lane + TILE)
            found = [ref[:, row + n, :, at].reshape(near, TILE) for n in (0, 1)]
            return jnp.concatenate(found, axis=1)

        def both(row, first):
            return jnp.concatenate(
                [pair(near_ref, row, first), pair(far_ref, row, first - half)], axis=0
            )

        scores = [jnp.zeros((near, 2 * near), jnp.float32) for _ in sides]
        grads = [jnp.zeros((near, 2 * near), jnp.float32) for _ in sides]
        for row in range(0, rows, 2):
            query = live_pair(pair(near_ref, row, 0), row, info_ref)
            key, value = both(row, half), both(row, 2 * half)
            out = pair(do_ref, row, 0)
            for n, side in enumerate(sides):
                scores[n] = scores[n] + contract(only(side, query), key, LAST)
                grads[n] = grads[n] + contract(only(side, out), value, LAST)
        probs = [softmax_of(s * tie, keep) for s in scores]
        lows = [p.astype(bf16) for p in probs]
        deltas = [softmax_back(p, g).astype(bf16) for p, g in zip(probs, grads)]
        low_turned = [p.T for p in lows]
        delta_turned = [d.T for d in deltas]
        for row in range(0, rows, 2):
            query = live_pair(pair(near_ref, row, 0), row, info_ref)
            key, out = both(row, half), pair(do_ref, row, 0)
            dq = [contract(d, key, PLAIN) for d in deltas]
            dk = [contract(d, query, PLAIN) for d in delta_turned]
            dv = [contract(p, out, PLAIN) for p in low_turned]
            dq = live_pair(jnp.where(sides[0], dq[0], dq[1]) * tie, row, info_ref).astype(bf16)
            dk = (jnp.where(sides[0], dk[0], dk[1]) * tie).astype(bf16)
            dv = jnp.where(sides[0], dv[0], dv[1]).astype(bf16)

            def put(ref, first, value):
                for n in (0, 1):
                    piece = value[:, n * TILE : (n + 1) * TILE].reshape(blocks, part, TILE)
                    ref[:, row + n, :, first + lane : first + lane + TILE] = piece

            put(d_near_ref, 0, dq)
            put(d_near_ref, half, dk[:near])
            put(d_near_ref, 2 * half, dv[:near])
            put(d_far_ref, 0, dk[near:])
            put(d_far_ref, half, dv[near:])

    count = rows * part
    d_far = d_far_ref[...].reshape(blocks * count, 2 * half)
    far_weights = w_ref[:, half:]
    far_part_ref[...] = contract(d_far[:count], far_weights, LAST)
    far_theirs_ref[...] = contract(d_far[count:], far_weights, LAST).astype(bf16)
    d_near = d_near_ref[...].reshape(blocks * count, lanes)
    near_part_ref[...] = contract(d_near[:count], w_ref[...], LAST)
    near_theirs_ref[...] = contract(d_near[count:], w_ref[...], LAST).astype(bf16)
    near_turned = near_tokens_ref[...].T
    far_turned = far_tokens_ref[...].T
    zs, depth = kept_ref.shape[0], kept_ref.shape[1]
    first = info_ref[1] == 0
    first_y = info_ref[5] == 0
    summed = added(y_kept_ref[...], y_got_ref[...]).reshape(zs, 2, depth, -1)
    with_x_ref[...] = jnp.where(first, summed[:, 0], summed[:, 1])
    to_x_ref[...] = jnp.where(first, summed[:, 1], summed[:, 0])
    summed = added(x_kept_ref[...], x_got_ref[...])
    with_y_ref[...] = jnp.where(first_y, summed[:, 0], summed[:, 1])
    to_y_ref[...] = jnp.where(first_y, summed[:, 1], summed[:, 0])
    for n in range(3):
        at = slice(n * half, (n + 1) * half)
        terms = contract(near_turned, d_near[:, at], PLAIN)
        if n > 0:
            terms = terms + contract(far_turned, d_far[:, (n - 1) * half : n * half], PLAIN)
        terms = terms.astype(bf16).reshape(zs, 2, depth, half)
        kept_ref[:, :, at] = jnp.where(first, terms[:, 0], terms[:, 1])
        sent_ref[:, :, at] = jnp.where(first, terms[:, 1], terms[:, 0])


def row_attention(place, info, tie, tokens, weights, rows, half):
    f32, bf16 = jnp.float32, jnp.bfloat16
    zs, deep, width = tokens[0][1].shape
    part = (deep - 16) // 2
    count = rows * part
    small = pl.BlockSpec(memory_space=pltpu.SMEM)
    anywhere = pl.BlockSpec(memory_space=pl.ANY)
    inside = pl.BlockSpec(memory_space=pltpu.VMEM)
    shapes = [
        ((count, width), bf16),
        ((2 * count, width), bf16),
        ((2 * count, width), bf16),
        ((width, 3 * half), bf16),
        ((16, width), f32),
        ((2, rows, part, 3 * half), bf16),
        ((2, rows, part, 2 * half), bf16),
        ((2, rows, part, half), bf16),
    ]
    return pl.pallas_call(
        partial(row_fwd_kernel, [step for step, _ in tokens], plan_of(weights)),
        in_specs=[small] * 3 + [anywhere] * (len(tokens) + len(weights)),
        out_specs=[inside] * len(shapes),
        out_shape=[jax.ShapeDtypeStruct(shape, kind) for shape, kind in shapes],
        scratch_shapes=[
            pltpu.VMEM((2, rows, 2 * part, width), bf16),
            pltpu.VMEM((8, 16, width), bf16),
            pltpu.SemaphoreType.DMA((24,)),
            pltpu.SemaphoreType.DMA((16,)),
        ],
        compiler_params=pltpu.CompilerParams(vmem_limit_bytes=56 * 2**20),
        cost_estimate=pl.CostEstimate(flops=7 * 10**9, bytes_accessed=10**7, transcendentals=10**6),
    )(place, info, tie, *[v for _, v in tokens], *[v for _, v, _ in weights])


def row_attention_back(info, tie, near, far, own, got, weights, near_tokens, far_tokens, *ffn_terms):
    blocks, rows, part, lanes = near.shape
    count, width = rows * part, weights.shape[0]
    half = lanes // 3
    f32, bf16 = jnp.float32, jnp.bfloat16
    small = pl.BlockSpec(memory_space=pltpu.SMEM)
    inside = pl.BlockSpec(memory_space=pltpu.VMEM)
    shapes = [((count, width), kind) for kind in (f32, bf16) * 2]
    shapes = shapes + [((4, width // 8, lanes), bf16)] * 2
    shapes = shapes + [((4, width // 8, ffn_terms[0].shape[1]), bf16)] * 4
    return pl.pallas_call(
        row_bwd_kernel,
        in_specs=[small, small] + [inside] * 11,
        out_specs=[inside] * 10,
        out_shape=[jax.ShapeDtypeStruct(shape, kind) for shape, kind in shapes],
        scratch_shapes=[
            pltpu.VMEM((blocks, rows, part, half), bf16),
            pltpu.VMEM((blocks, rows, part, lanes), bf16),
            pltpu.VMEM((blocks, rows, part, 2 * half), bf16),
        ],
        compiler_params=pltpu.CompilerParams(vmem_limit_bytes=56 * 2**20),
    )(info, tie, near, far, own, got, weights, near_tokens, far_tokens, *ffn_terms)


def normed(value, gain, shift):
    centred = value - jnp.mean(value, axis=-1, keepdims=True)
    scale = lax.rsqrt(jnp.mean(centred * centred, axis=-1, keepdims=True) + eps_norm)
    unit = centred * scale
    return unit * gain + shift, unit, scale


def normed_back(grad, unit, scale, gain):
    inner = grad * gain
    mean = jnp.mean(inner, axis=-1, keepdims=True)
    along = jnp.mean(inner * unit, axis=-1, keepdims=True)
    return scale * (inner - mean - unit * along)


def column_masks(info_ref, rows, part):
    tokens = rows * part
    key = lax.broadcasted_iota(jnp.int32, (tokens, tokens), 0)
    query = lax.broadcasted_iota(jnp.int32, (tokens, tokens), 1)
    same = key % part == query % part
    return jnp.logical_and(same, key // part < info_ref[4])


def stacked(value, sides):
    return jnp.concatenate([only(side, value) for side in sides], axis=0)


def column_probs(query, key, keep, sides):
    scores = contract(stacked(key, sides), query, LAST) * (1.0 / math.sqrt(DH))
    tokens = query.shape[0]
    probs = []
    for n in (0, 1):
        part = jnp.where(keep, scores[n * tokens : (n + 1) * tokens], masked_score)
        expo = jnp.exp(part - jnp.max(part, axis=0, keepdims=True))
        probs.append(expo / jnp.sum(expo, axis=0, keepdims=True))
    return probs


def col_fwd_kernel(plan, info_ref, place_ref, *refs):
    stacks, refs = refs[: len(plan)], refs[len(plan) :]
    x_ref, own_ref, other_ref, gain_ref, acts_ref, one_ref, qkv_ref = refs[:7]
    resid_ref, normed_three_ref, mixed_ref, three_ref, col_ref, seven_ref, sem = refs[7:]
    copies = placing(plan, col_attn_at, place_ref, stacks, [three_ref, col_ref, seven_ref], sem)
    for copy in copies:
        copy.start()
    bf16 = jnp.bfloat16
    rows, cols, lanes = qkv_ref.shape
    width = lanes // 3
    part = 16
    own, other = own_ref[...], other_ref[...]
    flip = info_ref[2] == 0
    mixed_one = jnp.concatenate(
        [jnp.where(flip, own, other), jnp.where(flip, other, own)], axis=1
    )
    acts_ref[:, :width] = mixed_one
    for copy in copies:
        copy.wait()
    stream = (x_ref[...].astype(jnp.float32) + contract(mixed_one, three_ref[...], PLAIN)).astype(bf16)
    one_ref[...] = stream
    normed_two = normed(stream.astype(jnp.float32), gain_ref[2:3], gain_ref[3:4])[0].astype(bf16)
    acts_ref[:, width : 2 * width] = normed_two
    for n in range(3):
        at = slice(n * width, (n + 1) * width)
        found = contract(normed_two, col_ref[:, at], PLAIN).astype(bf16)
        qkv_ref[:, :, at] = found.reshape(rows, cols, width)
    keep = column_masks(info_ref, rows, part)
    sides = head_lanes(TILE)

    def attend(b, carry):
        at = pl.ds(pl.multiple_of(b * part, part), part)
        def tile(n, t):
            lane = n * width + t * TILE
            return qkv_ref[:, at, lane : lane + TILE].reshape(rows * part, TILE)
        tiles = range(width // TILE)
        probs = [column_probs(tile(0, t), tile(1, t), keep, sides) for t in tiles]
        for t in tiles:
            low = jnp.concatenate(probs[t], axis=0).astype(bf16)
            mixed = contract(low, stacked(tile(2, t), sides), FIRST).astype(bf16)
            mixed_ref[:, at, t * TILE : (t + 1) * TILE] = mixed.reshape(rows, part, TILE)
        return carry

    lax.fori_loop(0, cols // part, attend, 0)
    mixed = mixed_ref[...].reshape(rows * cols, width)
    acts_ref[:, 2 * width :] = mixed
    resid = one_ref[...].astype(jnp.float32) + contract(mixed, seven_ref[...], PLAIN)
    resid_ref[...] = resid
    normed_three_ref[...] = normed(resid, gain_ref[4:5], gain_ref[5:6])[0].astype(bf16)


def col_bwd_kernel(plan, info_ref, place_ref, *refs):
    stacks, refs = refs[: len(plan)], refs[len(plan) :]
    up_ref, da_ref, da_got_ref, out_ref, out_got_ref, resid_ref, one_ref, qkv_ref, gain_ref = refs[:9]
    result_ref, stream_ref, own_ref, other_ref, mine_ref, theirs_ref, norms_ref = refs[9:16]
    dqkv_ref, do_ref, three_ref, col_ref, seven_ref, sem = refs[16:]
    copies = placing(plan, col_attn_at, place_ref, stacks, [three_ref, col_ref, seven_ref], sem)
    for copy in copies:
        copy.start()
    bf16 = jnp.bfloat16
    f32 = jnp.float32
    rows, cols, lanes = qkv_ref.shape
    width = lanes // 3
    part = 16
    result_ref[...] = (resid_ref[...] + out_ref[...] + out_got_ref[...].astype(f32)).astype(bf16)
    da = da_ref[...] + da_got_ref[...].astype(f32)
    gain = gain_ref[4:5]
    _, unit, scale = normed(resid_ref[...], gain, 0.0)
    grad_three = up_ref[...].astype(f32) + normed_back(da, unit, scale, gain)
    norms_ref[2:3] = jnp.sum(da * unit, axis=0, keepdims=True)
    norms_ref[3:4] = jnp.sum(da, axis=0, keepdims=True)
    branch = grad_three.astype(bf16)
    half = width // 2
    flip = info_ref[2] == 0

    def put_halves(first, value):
        at = slice(first, first + half)
        mine_ref[:, at] = jnp.where(flip, value[:, :half], value[:, half:])
        theirs_ref[:, at] = jnp.where(flip, value[:, half:], value[:, :half])

    put_halves(4 * half, branch)
    for copy in copies:
        copy.wait()
    do_ref[...] = contract(branch, seven_ref[...], LAST).astype(bf16).reshape(rows, cols, width)
    keep = column_masks(info_ref, rows, part)
    sides = head_lanes(TILE)
    ratio = 1.0 / math.sqrt(DH)

    def attend(b, carry):
        at = pl.ds(pl.multiple_of(b * part, part), part)
        tokens = rows * part

        def tile(n, t):
            lane = n * width + t * TILE
            return qkv_ref[:, at, lane : lane + TILE].reshape(tokens, TILE)

        def out_tile(t):
            return do_ref[:, at, t * TILE : (t + 1) * TILE].reshape(tokens, TILE)

        def put(n, t, value):
            lane = n * width + t * TILE
            dqkv_ref[:, at, lane : lane + TILE] = value.astype(bf16).reshape(rows, part, TILE)

        for t in range(width // TILE):
            query, key, out = tile(0, t), tile(1, t), out_tile(t)
            keys = stacked(key, sides)
            probs = column_probs(query, key, keep, sides)
            grads = contract(stacked(tile(2, t), sides), out, LAST)
            deltas = []
            for n, p in enumerate(probs):
                g = grads[n * tokens : (n + 1) * tokens]
                deltas.append((p * (g - jnp.sum(p * g, axis=0, keepdims=True))).astype(bf16))
            put(0, t, contract(jnp.concatenate(deltas, axis=0), keys, FIRST) * ratio)
            wide = jnp.concatenate(deltas, axis=1)
            put(1, t, contract(wide, stacked(query, sides), PLAIN) * ratio)
            wide = jnp.concatenate([p.astype(bf16) for p in probs], axis=1)
            put(2, t, contract(wide, stacked(out, sides), PLAIN))
        return carry

    lax.fori_loop(0, cols // part, attend, 0)
    dqkv = dqkv_ref[...].reshape(rows * cols, lanes)
    for n in range(3):
        put_halves((n + 1) * half, dqkv[:, n * width : (n + 1) * width])
    grad_normed = contract(dqkv, col_ref[...], LAST)
    gain = gain_ref[2:3]
    _, unit, scale = normed(one_ref[...].astype(f32), gain, 0.0)
    norms_ref[0:1] = jnp.sum(grad_normed * unit, axis=0, keepdims=True)
    norms_ref[1:2] = jnp.sum(grad_normed, axis=0, keepdims=True)
    stream = (grad_three + normed_back(grad_normed, unit, scale, gain)).astype(bf16)
    stream_ref[...] = stream
    put_halves(0, stream)
    mixed = contract(stream, three_ref[...], LAST).astype(bf16)
    own_ref[...] = jnp.where(flip, mixed[:, :half], mixed[:, half:])
    other_ref[...] = jnp.where(flip, mixed[:, half:], mixed[:, :half])


def tokens_back_kernel(
    info_ref, near_ref, near_got_ref, far_got_ref, x_ref, stream_ref, gain_ref, norms_ref,
    blocks_ref,
):
    f32 = jnp.float32
    grad = near_ref[...] + near_got_ref[...].astype(f32) + far_got_ref[...].astype(f32)
    gain = gain_ref[0:1]
    _, unit, scale = normed(x_ref[...].astype(f32), gain, 0.0)
    found = stream_ref[...].astype(f32) + normed_back(grad, unit, scale, gain)
    rows, deep, width = blocks_ref.shape
    part = deep - 16
    blocks_ref[:, :part] = found.astype(jnp.bfloat16).reshape(rows, part, width)
    sums = [
        jnp.sum(grad * unit, axis=0, keepdims=True),
        jnp.sum(grad, axis=0, keepdims=True),
        norms_ref[...],
        jnp.zeros((2, width), f32),
    ]
    sums = jnp.concatenate(sums, axis=0)
    depth = width // 8
    lane = lax.broadcasted_iota(jnp.int32, (width, TILE), 0)
    place = lax.broadcasted_iota(jnp.int32, (width, TILE), 1)
    for shard in range(8):
        chosen = jnp.logical_and(lane == shard * depth + place, place < depth)
        found = lax.dot_general(
            sums,
            chosen.astype(f32),
            (PLAIN, ((), ())),
            precision=lax.Precision.HIGHEST,
            preferred_element_type=f32,
        )
        found = jnp.concatenate([found, jnp.zeros((8, TILE), f32)], axis=0)
        blocks_ref[shard, part:, :TILE] = found.astype(jnp.bfloat16)
        blocks_ref[shard, part:, TILE:] = jnp.zeros((16, width - TILE), jnp.bfloat16)


def attn_terms_kernel(place_ref, acts_ref, got_ref, mine_ref, theirs_ref, sent_ref, kept_ref):
    width = acts_ref.shape[1] // 3
    half = width // 2
    depth = sent_ref.shape[1]
    turned = [
        jnp.concatenate([ref[:, n * width : (n + 1) * width].T for ref in (acts_ref, got_ref)], axis=1)
        for n in range(3)
    ]
    first = place_ref[3] == 0
    for n, m in enumerate((0, 1, 1, 1, 2)):
        at = slice(n * half, (n + 1) * half)
        grads = jnp.concatenate([mine_ref[:, at], theirs_ref[:, at]], axis=0)
        terms = contract(turned[m], grads, PLAIN).astype(jnp.bfloat16)
        terms = terms.reshape(sent_ref.shape[0], 2, depth, half)
        kept_ref[:, :, at] = jnp.where(first, terms[:, 0], terms[:, 1])
        sent_ref[:, :, at] = jnp.where(first, terms[:, 1], terms[:, 0])


def column_call(kernel, info, place, pieces, args, outs, scratch):
    width = args[-1].shape[1]
    bf16 = jnp.bfloat16
    small = pl.BlockSpec(memory_space=pltpu.SMEM)
    inside = pl.BlockSpec(memory_space=pltpu.VMEM)
    anywhere = pl.BlockSpec(memory_space=pl.ANY)
    return pl.pallas_call(
        partial(kernel, plan_of(pieces)),
        in_specs=[small] * 2 + [anywhere] * len(pieces) + [inside] * len(args),
        out_specs=[inside] * len(outs),
        out_shape=[jax.ShapeDtypeStruct(shape, kind) for shape, kind in outs],
        scratch_shapes=[
            *scratch,
            pltpu.VMEM((width, width), bf16),
            pltpu.VMEM((width, 3 * width), bf16),
            pltpu.VMEM((width, width), bf16),
            pltpu.SemaphoreType.DMA((160,)),
        ],
        compiler_params=pltpu.CompilerParams(vmem_limit_bytes=56 * 2**20),
    )(info, place, *[value for _, value, _ in pieces], *args)


def adam_kernel(place_ref, factor_ref, own_ref, other_ref, w_ref, first_ref, second_ref, *outs):
    count, _, width = w_ref.shape
    half = width // 2
    low = place_ref[2] == 0
    for n in range(count):
        at = pl.ds(pl.multiple_of((pl.program_id(0) * count + n) * half, TILE), half)
        own, other = own_ref[:, at], other_ref[:, at]
        grad = jnp.concatenate([jnp.where(low, own, other), jnp.where(low, other, own)], axis=1)
        grad = grad.astype(jnp.float32) * factor_ref[0]
        first, second, weight = adam_update(w_ref[n], first_ref[n], second_ref[n], grad, matrix_rate)
        for ref, value in zip(outs, (first, second, weight, weight.astype(jnp.bfloat16))):
            ref[n] = value


def attn_adam(place, factor, own, other, weight, first, second):
    small = pl.BlockSpec(memory_space=pltpu.SMEM)
    inside = pl.BlockSpec(memory_space=pltpu.VMEM)
    block = pl.BlockSpec((4, *weight.shape[1:]), lambda m: (m, 0, 0))
    kinds = [jnp.float32] * 3 + [jnp.bfloat16]
    return pl.pallas_call(
        adam_kernel,
        grid=(weight.shape[0] // 4,),
        in_specs=[small, small, inside, inside] + [block] * 3,
        out_specs=[block] * 4,
        out_shape=[jax.ShapeDtypeStruct(weight.shape, kind) for kind in kinds],
        compiler_params=pltpu.CompilerParams(vmem_limit_bytes=40 * 2**20),
    )(place, factor.reshape(1), own, other, weight, first, second)


def whole_call(kernel, info, args, outs, scratch=()):
    inside = pl.BlockSpec(memory_space=pltpu.VMEM)
    return pl.pallas_call(
        kernel,
        in_specs=[pl.BlockSpec(memory_space=pltpu.SMEM)] + [inside] * len(args),
        out_specs=[inside] * len(outs),
        out_shape=[jax.ShapeDtypeStruct(shape, kind) for shape, kind in outs],
        scratch_shapes=list(scratch),
        compiler_params=pltpu.CompilerParams(vmem_limit_bytes=56 * 2**20),
    )(info, *args)


def gelu_pair(u):
    ratio = math.sqrt(2.0 / math.pi)
    square = u * u
    tanh = jnp.tanh(ratio * u * (1.0 + 0.044715 * square))
    rise = 0.5 * (1.0 + tanh)
    slope = (0.5 * ratio) * (1.0 - tanh * tanh) * (1.0 + (3.0 * 0.044715) * square)
    return u * rise, rise + u * slope


def ffn_kernel(
    plan, place_ref, a_ref, a_got_ref, up_ref, up_got_ref, *refs
):
    bf16 = jnp.bfloat16
    stacks, refs = refs[: len(plan)], refs[len(plan) :]
    out_ref, out_other_ref, da_ref, da_other_ref = refs[:4]
    y_sent_ref, y_kept_ref, x_sent_ref, x_kept_ref = refs[4:8]
    w_ref, tokens_ref, turned_ref, out_sum, da_sum, sem = refs[8:]
    step = pl.program_id(0)
    count, width = a_ref.shape
    chunk = x_sent_ref.shape[3]
    last = pl.num_programs(0) - 1

    @pl.when(step == 0)
    def _():
        copies = placing(plan, ffn_at, place_ref, stacks, [w_ref], sem, steps=False)
        for copy in copies:
            copy.start()
        for n, ref in enumerate((a_ref, a_got_ref, up_ref, up_got_ref)):
            k, at = n // 2, slice((n % 2) * count, (n % 2 + 1) * count)
            tokens_ref[k, at] = ref[...]
            turned_ref[k, :, at] = ref[...].T
        out_sum[...] = jnp.zeros_like(out_sum)
        da_sum[...] = jnp.zeros_like(da_sum)
        for copy in copies:
            copy.wait()

    lane = pl.ds(pl.multiple_of(step * chunk, chunk), chunk)
    w_in = w_ref[:width, lane]
    w_out = w_ref[width:, lane]
    activs, grads = [], []
    for n in (0, 1):
        at = slice(n * count, (n + 1) * count)
        activ, slope = gelu_pair(contract(tokens_ref[0, at], w_in, PLAIN))
        activ = activ.astype(bf16)
        grad = (contract(tokens_ref[1, at], w_out, PLAIN) * slope).astype(bf16)
        out_sum[at] += contract(activ, w_out, LAST)
        da_sum[at] += contract(grad, w_in, LAST)
        activs.append(activ)
        grads.append(grad)
    in_terms = contract(turned_ref[0], jnp.concatenate(grads, axis=0), PLAIN).astype(bf16)
    out_terms = contract(turned_ref[1], jnp.concatenate(activs, axis=0), PLAIN).astype(bf16)

    @pl.when(step < last)
    def _():
        first = place_ref[3] == 0
        y_kept_ref[...] = jnp.where(first, in_terms, out_terms)
        y_sent_ref[...] = jnp.where(first, out_terms, in_terms)

    @pl.when(step == last)
    def _():
        first = place_ref[1] == 0
        zs, _, depth, _ = x_sent_ref.shape
        for n, terms in enumerate((in_terms, out_terms)):
            terms = terms.reshape(zs, 2, depth, chunk)
            x_kept_ref[:, n] = jnp.where(first, terms[:, 0], terms[:, 1])
            x_sent_ref[:, n] = jnp.where(first, terms[:, 1], terms[:, 0])

    @pl.when(step == last)
    def _():
        out_ref[...] = out_sum[:count]
        out_other_ref[...] = out_sum[count:].astype(bf16)
        da_ref[...] = da_sum[:count]
        da_other_ref[...] = da_sum[count:].astype(bf16)


def feed_forward(place, normed_own, normed_got, up_own, up_got, pieces, chunk=768):
    count, width = normed_own.shape
    half = pieces[0][1].shape[-1]
    anywhere = pl.BlockSpec(memory_space=pl.ANY)
    inside = pl.BlockSpec(memory_space=pltpu.VMEM)
    steps = half // chunk
    lanes = pl.BlockSpec((width, chunk), lambda n: (0, jnp.minimum(n, steps - 2)))
    f32, bf16 = jnp.float32, jnp.bfloat16
    shapes = [((count, width), kind) for kind in (f32, bf16, f32, bf16)]
    shapes = shapes + [((width, half - chunk), bf16)] * 2 + [((4, 2, width // 8, chunk), bf16)] * 2
    return pl.pallas_call(
        partial(ffn_kernel, plan_of(pieces)),
        grid=(steps,),
        in_specs=[pl.BlockSpec(memory_space=pltpu.SMEM)] + [inside] * 4 + [anywhere] * len(pieces),
        out_specs=[inside] * 4 + [lanes] * 2 + [inside] * 2,
        out_shape=[jax.ShapeDtypeStruct(shape, kind) for shape, kind in shapes],
        scratch_shapes=[
            pltpu.VMEM((2 * width, half), bf16),
            pltpu.VMEM((2, 2 * count, width), bf16),
            pltpu.VMEM((2, width, 2 * count), bf16),
            pltpu.VMEM((2 * count, width), f32),
            pltpu.VMEM((2 * count, width), f32),
            pltpu.SemaphoreType.DMA((16,)),
        ],
        compiler_params=pltpu.CompilerParams(vmem_limit_bytes=56 * 2**20),
    )(place, normed_own, normed_got, up_own, up_got, *[value for _, value, _ in pieces])


def added(a, b):
    return (a.astype(jnp.float32) + b.astype(jnp.float32)).astype(jnp.bfloat16)


def z_summed(column, z):
    shard = pick(column, z, 0).astype(jnp.float32)
    for i in (1, 2, 3):
        other = pick(column, lax.bitwise_xor(z, i), 0)
        got = lax.ppermute(other, "z", [(k, k ^ i) for k in range(4)])
        shard = shard + got.astype(jnp.float32)
    return shard.astype(jnp.bfloat16)


def paired_body(
    tokens,
    cotangent,
    col_count,
    row_count,
    attn_weight,
    in_weight,
    out_weight,
    norm_param,
    attn_first,
    attn_second,
    in_first,
    in_second,
    out_first,
    out_second,
    norm_first,
    norm_second,
):
    f32 = jnp.float32
    bf16 = jnp.bfloat16
    z, x, y, c = (lax.axis_index(name) for name in ("z", "x", "y", "c"))
    width = tokens.shape[-1]
    hidden = in_weight.shape[1]
    depth = in_weight.shape[0]
    half = width // 2
    hidden_half = hidden // 2

    counts = jnp.stack([col_count, row_count])
    other_counts = swap(counts, "c")
    mine = jnp.where(z // 2 == c, counts, other_counts)
    mine = pick(mine, z % 2, 1)
    cols_live, rows_live = mine[0], mine[1]
    place = jnp.stack([z, x, c, y]).astype(jnp.int32)
    info = jnp.concatenate([place[:3], mine, place[3:]])
    tie = (lax.rsqrt(rows_live.astype(f32)) * (1.0 / math.sqrt(DH))).reshape(1)

    attn_low = attn_weight.astype(bf16)
    halves = attn_low.reshape(8, depth, 2, half)
    row_half = jnp.moveaxis(pick(halves[:3], c, 2), 0, 1).reshape(2, depth // 2, 3 * half)
    row_quarter = pick(row_half, y, 0)
    col_quarter = pick(pick(halves[3:], c, 2).reshape(5, 2, depth // 2, half), y, 1)
    row_z = gather_z(row_quarter)
    ffn_low = [in_weight.astype(bf16), out_weight.astype(bf16).T]
    ffn_low = [
        jnp.where(c == 0, low[:, :hidden_half], low[:, hidden_half:]) for low in ffn_low
    ]
    ffn_quarter = jnp.where(y == 0, *ffn_low)

    lanes = jnp.arange(width, dtype=jnp.int32) // depth
    norm_low = jnp.tile(norm_param.astype(bf16), (1, width // depth))
    norm_rows = jnp.where(lanes[None] == z * 2 + x, norm_low, jnp.zeros_like(norm_low))
    norm_rows = jnp.pad(norm_rows, ((0, 10), (0, 0)))
    part = tokens.shape[2] // 4
    tokens_here = merge_cores(tokens, c).reshape(4, 2 * part, width)
    parts = [
        jnp.concatenate([pick(tokens_here, lax.bitwise_xor(z, i), 0), norm_rows]) for i in range(4)
    ]
    parts = [parts[0]] + [
        lax.ppermute(parts[i], "z", [(k, k ^ i) for k in range(4)]) for i in (1, 2, 3)
    ]
    row_pieces = spread(jnp.stack(row_z))
    row_x, row_y, *parts, col_quarter = together(
        row_pieces[1][1], row_pieces[2][1], *parts, col_quarter
    )
    tokens_z = jnp.stack(parts)
    up = merge_cores(cotangent, c).reshape(4, 2, part, width)
    up = joined(pick(up, x, 1)[:, None], swap(pick(up, 1 - x, 1), "x")[:, None], x, 1)
    col_z = gather_z(col_quarter)
    tokens_x, row_last, ffn_quarter, up, *col_z = together(
        swap(tokens_z, "x"), swap(row_x, "y"), ffn_quarter, up, *col_z
    )
    steps = [(0, 0, 0), (1, 0, 0), (0, 1, 0), (1, 1, 0)]
    row_stacks = [row_pieces[0][1], row_x, row_y, row_last]
    row_pieces = [(step, value, 0) for step, value in zip(steps, row_stacks)]
    col_z = jnp.stack(col_z)
    ffn_z = lax.all_to_all(
        jnp.broadcast_to(ffn_quarter, (4, *ffn_quarter.shape)), "z", 0, 0, tiled=True
    )
    col_x = swap(col_z, "x")
    col_last = swap(col_x, "y")
    col_x, col_y, ffn_z = together(col_x, swap(col_z, "y"), ffn_z)
    tokens_far, col_last = together(swap(tokens_x, "c"), col_last)
    ffn_x, ffn_y = swap(ffn_z, "x"), swap(ffn_z, "y")
    ups = [pick(up, z, 0)] + [
        lax.ppermute(pick(up, lax.bitwise_xor(z, i), 0), "z", [(k, k ^ i) for k in range(4)])
        for i in (1, 2, 3)
    ]

    rows = 8
    count = rows * part
    stream_zero, near_normed, far_normed, w_row, norm_gain, near, far, mixed_heads = row_attention(
        place,
        info,
        tie,
        [((0, 0), tokens_z), ((1, 0), tokens_x), ((0, 1), swap(tokens_z, "c")), ((1, 1), tokens_far)],
        row_pieces,
        rows,
        half,
    )
    mixed_heads = mixed_heads.reshape(2, count, half)
    col_stacks = [col_z, col_x, col_y]
    mixed_heads, ffn_x, ffn_y, *rest = together(
        mixed_heads, ffn_x, ffn_y, *ups, *[swap(value, "c") for value in col_stacks]
    )
    ups, col_others = rest[:4], rest[4:]
    ups = [jnp.where(z % 2 == 0, a, b) for a, b in zip(ups, (ups[1], ups[0], ups[3], ups[2]))]
    ups = [jnp.where(z < 2, a, b) for a, b in zip(ups, ups[2:] + ups[:2])]
    up = jnp.concatenate(ups)
    col_stacks, col_others = [*col_stacks, col_last], [*col_others, swap(col_last, "c")]
    col_pieces = [(step, v, 0) for step, v in zip(steps, col_stacks)]
    col_pieces = col_pieces + [((j, m, 1), v, 0) for (j, m, _), v in zip(steps, col_others)]
    ffn_pieces = [(step, v, 0) for step, v in zip(steps, [ffn_z, ffn_x, ffn_y])]

    whole_shape, wide_shape = ((count, width), bf16), ((rows, part, 3 * width), bf16)
    acts, stream_one, qkv_two, resid_three, normed_three = column_call(
        col_fwd_kernel,
        info,
        place,
        col_pieces,
        [stream_zero, mixed_heads[0], swap(mixed_heads[1], "c"), norm_gain],
        [((count, 3 * width), bf16), whole_shape, wide_shape, ((count, width), f32), whole_shape],
        [pltpu.VMEM((rows, part, width), bf16)],
    )
    normed_three, *ffn_across = together(normed_three, *across(ffn_x, ffn_y))
    ffn_pieces = ffn_pieces + across_pieces(*ffn_across)

    column = x * (2 * part) + c * part + jnp.arange(part, dtype=jnp.int32)
    live = jnp.logical_and(
        (jnp.arange(rows, dtype=jnp.int32) < rows_live)[:, None], (column < cols_live)[None, :]
    )
    up = jnp.where(live[..., None], up, jnp.zeros_like(up)).reshape(count, width)
    out_own, out_other, da_own, da_other, *ffn_terms = feed_forward(
        place, normed_three, swap(normed_three, "c"), up, swap(up, "c"), ffn_pieces
    )
    da_got = swap(da_other, "c")
    out_got = swap(out_other, "c")
    y_sent, y_kept, x_sent, x_kept = ffn_terms
    y_got, x_got = swap(y_sent, "y"), swap(x_sent, "x")

    acts_got = swap(acts, "c")
    result, grad_stream, grad_own, grad_other, attn_mine, attn_theirs, col_norms = column_call(
        col_bwd_kernel,
        info,
        place,
        col_pieces,
        [up, da_own, da_got, out_own, out_got, resid_three, stream_one, qkv_two, norm_gain],
        [whole_shape] * 2
        + [((count, half), bf16)] * 2
        + [((count, 5 * half), bf16)] * 2
        + [((4, width), f32)],
        [pltpu.VMEM((rows, part, 3 * width), bf16), pltpu.VMEM((rows, part, width), bf16)],
    )

    result, x_got, y_got = together(result, x_got, y_got)
    block_out = to_blocks(result.reshape(rows, part, width))
    (
        near_part, near_theirs, far_part, far_theirs, row_sent, row_kept,
        ffn_to_x, ffn_x, ffn_to_y, ffn_y,
    ) = row_attention_back(
        info, tie, near, far, grad_own, swap(grad_other, "c"), w_row, near_normed, far_normed,
        y_kept, y_got, x_kept, x_got,
    )
    row_sent, far_theirs, near_theirs, attn_theirs, block_out, ffn_to_x, ffn_to_y = together(
        row_sent, far_theirs, near_theirs, attn_theirs, block_out, ffn_to_x, ffn_to_y
    )
    ffn_x_got, ffn_y_got = swap(ffn_to_x, "x"), swap(ffn_to_y, "y")
    row_got = swap(row_sent, "x")
    far_sum = added(far_part, swap(far_theirs, "c"))
    far_got = swap(far_sum, "x")
    near_got = swap(near_theirs, "c")
    attn_sent, attn_kept = whole_call(
        attn_terms_kernel,
        place,
        [acts, acts_got, attn_mine, swap(attn_theirs, "c")],
        [((8, depth // 2, 5 * half), bf16)] * 2,
    )
    attn_got = swap(attn_sent, "y")
    attn_kept, ffn_y_got, ffn_x_got = together(attn_kept, ffn_y_got, ffn_x_got)
    ffn_column = jnp.concatenate([added(ffn_x, ffn_x_got), added(ffn_y, ffn_y_got)], axis=2)
    ffn_own = lax.all_to_all(ffn_column, "z", 0, 0, tiled=True)
    ffn_own = jnp.sum(ffn_own.astype(f32), axis=0).astype(bf16)
    ffn_own, row_got, block_out = together(ffn_own, row_got, block_out)
    row_own = z_summed(added(row_kept, row_got), z)
    attn_pair_terms = added(attn_kept, attn_got).reshape(4, 2, depth // 2, 5 * half)
    attn_column = pick(attn_pair_terms, x, 1)
    attn_x_got = swap(pick(attn_pair_terms, 1 - x, 1), "x")
    blocks = whole_call(
        tokens_back_kernel,
        info,
        [near_part, near_got, far_got, stream_zero, grad_stream, norm_gain, col_norms],
        [((rows, part + 16, width), bf16)],
    )[0]
    blocks, row_own = together(blocks, row_own)
    blocks = to_blocks(blocks)
    grad_tokens = to_rows(blocks[:, :part], c).astype(f32)
    norm_grad = jnp.sum(blocks[:, part : part + 8, :TILE].astype(f32), axis=0)
    block_out = to_rows(block_out, c)
    attn_column = added(attn_column, attn_x_got)
    norm_parts = [norm_grad] + [
        lax.ppermute(norm_grad, ("y", "c"), [(k, k ^ i) for k in range(4)]) for i in (1, 2, 3)
    ]
    norm_grad = (norm_parts[0] + norm_parts[1]) + (norm_parts[2] + norm_parts[3])
    norm_grad = norm_grad[:6, :depth]
    attn_own = z_summed(attn_column, z)
    row_grad = added(row_own, swap(row_own, "y"))
    attn_grad_b = joined(attn_own, swap(attn_own, "y"), y, 0)
    ffn_grads = [ffn_own, swap(ffn_own, "y")]

    row_other = swap(row_grad, "c")
    attn_other = swap(attn_grad_b, "c")
    ffn_whole = [joined(piece, swap(piece, "c"), c, 1) for piece in ffn_grads]

    in_grad = jnp.where(y == 0, *ffn_whole).astype(f32)
    out_grad = jnp.where(y == 0, *ffn_whole[::-1]).astype(f32).T

    attn_own, block_out = together(attn_own, block_out)
    squares = sum(jnp.sum(jnp.square(g.astype(f32))) for g in (attn_own, ffn_own))
    squares = squares + 0.5 * jnp.sum(jnp.square(row_grad.astype(f32)))
    squares = squares + 0.25 * jnp.sum(norm_grad * norm_grad)
    squares = jnp.broadcast_to(squares, (32, 8, TILE))
    squares = lax.all_to_all(squares, ("z", "x", "y", "c"), 0, 0, tiled=True)
    grad_norm = jnp.sqrt(jnp.sum(squares[:, 0, 0]))
    factor = clip_bound / jnp.maximum(grad_norm, clip_bound)
    attn_first_new, attn_second_new, attn_weight_new, attn_copy = attn_adam(
        place,
        factor,
        jnp.concatenate([row_grad, attn_grad_b], axis=1),
        jnp.concatenate([row_other, attn_other], axis=1),
        attn_weight,
        attn_first,
        attn_second,
    )
    in_first_new, in_second_new, in_weight_new = adam_update(
        in_weight, in_first, in_second, in_grad * factor, matrix_rate
    )
    out_first_new, out_second_new, out_weight_new = adam_update(
        out_weight, out_first, out_second, out_grad * factor, matrix_rate
    )
    norm_first_new, norm_second_new, norm_new = adam_update(
        norm_param, norm_first, norm_second, norm_grad * factor, norm_rate
    )
    return (
        block_out,
        grad_tokens,
        grad_norm,
        attn_first_new,
        attn_second_new,
        attn_weight_new,
        attn_copy,
        in_first_new,
        in_second_new,
        in_weight_new,
        in_weight_new.astype(bf16),
        out_first_new,
        out_second_new,
        out_weight_new,
        out_weight_new.astype(bf16),
        norm_first_new,
        norm_second_new,
        norm_new,
    )


def paired_layout(mesh):
    return dict(mesh.shape) == {"seq": 8, "grp": 4}


def mapped(run, mesh, seq, grp):
    placed = (
        P(grp, seq, None, None),
        P(grp, seq, None, None),
        P(grp),
        P(grp),
        P(None, seq, None),
        P(seq, None),
        P(None, seq),
        P(None, seq),
        P(None, seq, None),
        P(None, seq, None),
        P(seq, None),
        P(seq, None),
        P(None, seq),
        P(None, seq),
        P(None, seq),
        P(None, seq),
    )
    return jax.shard_map(
        run,
        mesh=mesh,
        in_specs=placed,
        out_specs=(
            P(grp, seq, None, None),
            P(grp, seq, None, None),
            P(),
            P(None, seq, None),
            P(None, seq, None),
            P(None, seq, None),
            P(None, seq, None),
            P(seq, None),
            P(seq, None),
            P(seq, None),
            P(seq, None),
            P(None, seq),
            P(None, seq),
            P(None, seq),
            P(None, seq),
            P(None, seq),
            P(None, seq),
            P(None, seq),
        ),
        check_vma=False,
    )


def solution(mesh):
    if not paired_layout(mesh):
        return mapped(general_body, mesh, "seq", "grp")
    fine = Mesh(mesh.devices.reshape(4, 2, 2, 2), ("z", "x", "y", "c"))
    return mapped(paired_body, fine, ("z", "x"), ("y", "c"))
```

```python
from functools import partial
import math

import jax
import jax.numpy as jnp
from jax import lax
from jax.experimental import pallas as pl
from jax.experimental.pallas import tpu as pltpu
from jax.sharding import Mesh
from jax.sharding import PartitionSpec as P

H = 12
DH = 64
STEP = 5


eps_norm = 1e-05
masked_score = -1000000000.0
clip_bound = 1.0
beta_one = 0.5
beta_two = 0.5
matrix_rate = 0.06
norm_rate = 0.3
decay_rate = 0.01
adam_eps = 1e-08


def in_blocks(x, dim, length):
    lengths = x.shape
    pieces = x.reshape(*lengths[:dim], length, lengths[dim] // length, *lengths[dim + 1 :])
    return jnp.moveaxis(pieces, dim, 0)


def sent_and_summed(x, axis, dim):
    length = lax.axis_size(axis)
    pieces = lax.all_to_all(in_blocks(x, dim, length), axis, 0, 0, tiled=True)
    return jnp.sum(pieces.astype(jnp.float32), axis=0)


def layer_norm(value, gain, shift):
    mean = jnp.mean(value, axis=-1, keepdims=True)
    centred = value - mean
    spread = jnp.mean(centred * centred, axis=-1, keepdims=True)
    return centred * lax.rsqrt(spread + eps_norm) * gain + shift


def softmax_rows(scores, keep):
    scores = jnp.where(keep, scores, masked_score)
    top = jnp.max(scores, axis=-1, keepdims=True)
    expo = jnp.exp(scores - top)
    return expo / jnp.sum(expo, axis=-1, keepdims=True)


def softmax_back(probs, grads):
    return probs * (grads - jnp.sum(probs * grads, axis=-1, keepdims=True))


def adam_update(weight, first, second, grad, rate):
    first_new = beta_one * first + (1.0 - beta_one) * grad
    second_new = beta_two * second + (1.0 - beta_two) * grad * grad
    first_hat = first_new / (1.0 - beta_one**STEP)
    second_hat = second_new / (1.0 - beta_two**STEP)
    weight_new = weight - rate * (
        first_hat / (jnp.sqrt(second_hat) + adam_eps) + decay_rate * weight
    )
    return (first_new, second_new, weight_new)


def attn_pair(normed, grad_proj, mixed, grad_branch):
    width = normed.shape[-1]
    qkv_terms = jnp.einsum("prcd,kprce->dke", normed, grad_proj, preferred_element_type=jnp.float32)
    output_terms = jnp.einsum(
        "prcd,prce->de", mixed, grad_branch, preferred_element_type=jnp.float32
    )
    return jnp.concatenate([qkv_terms, output_terms[:, None, :]], axis=1).reshape(width, 4 * width)


def general_body(
    tokens,
    cotangent,
    col_count,
    row_count,
    attn_weight,
    in_weight,
    out_weight,
    norm_param,
    attn_first,
    attn_second,
    in_first,
    in_second,
    out_first,
    out_second,
    norm_first,
    norm_second,
):
    f32 = jnp.float32
    bf16 = jnp.bfloat16
    prot, rows_dev, cols, width = tokens.shape
    hidden = in_weight.shape[1]
    head_scale = 1.0 / math.sqrt(DH)
    attn_full, in_full, out_full, norm_full = (
        lax.all_gather(attn_weight.astype(bf16), "seq", axis=1, tiled=True),
        lax.all_gather(in_weight.astype(bf16), "seq", axis=0, tiled=True),
        lax.all_gather(out_weight.astype(bf16), "seq", axis=1, tiled=True),
        lax.all_gather(norm_param.astype(bf16), "seq", axis=1, tiled=True),
    )
    norm_gain = norm_full.astype(f32)
    row_ids = lax.axis_index("seq") * rows_dev + jnp.arange(rows_dev, dtype=jnp.int32)
    row_live = (row_ids[None, :] < row_count[:, None]).astype(f32)
    col_live = jnp.arange(cols, dtype=jnp.int32)[None, :] < col_count[:, None]
    tie_scale = lax.rsqrt(row_count.astype(f32)) * head_scale
    live = row_live[:, :, None] * col_live.astype(f32)[:, None, :]
    grad_out = (cotangent.astype(f32) * live[..., None]).astype(bf16)
    resid_one = tokens.astype(f32)
    normed_one = layer_norm(resid_one, norm_gain[0], norm_gain[1]).astype(bf16)
    proj_one = jnp.einsum(
        "prcd,kde->kprce", normed_one, attn_full[0:3], preferred_element_type=f32
    ).astype(bf16)
    proj_one = proj_one.reshape(3, prot, rows_dev, cols, H, DH)
    query_one, key_one, value_one = (proj_one[0], proj_one[1], proj_one[2])
    masked_query = query_one * row_live[:, :, None, None, None].astype(bf16)
    partial_scores = (
        jnp.einsum("prihe,prjhe->phij", masked_query, key_one, preferred_element_type=f32)
        * tie_scale[:, None, None, None]
    )
    keep_cols = col_live[:, None, None, :]
    score_part = lax.psum_scatter(partial_scores, "seq", scatter_dimension=2, tiled=True)
    probs_one = softmax_rows(score_part, keep_cols)
    probs_low = lax.all_gather(probs_one.astype(bf16), "seq", axis=2, tiled=True)
    mixed_one = jnp.einsum(
        "phij,prjhe->prihe", probs_low, value_one, preferred_element_type=f32
    ).astype(bf16)
    mixed_one = mixed_one.reshape(prot, rows_dev, cols, width)
    branch_one = jnp.einsum("prcd,de->prce", mixed_one, attn_full[3], preferred_element_type=f32)
    stream_one = (resid_one + branch_one).astype(bf16)
    stream_cols, up_grad = (
        lax.all_to_all(stream_one, "seq", split_axis=2, concat_axis=1, tiled=True),
        lax.all_to_all(grad_out, "seq", split_axis=2, concat_axis=1, tiled=True),
    )
    rows = stream_cols.shape[1]
    cols_dev = stream_cols.shape[2]
    row_live_all = jnp.arange(rows, dtype=jnp.int32)[None, :] < row_count[:, None]
    resid_two = stream_cols.astype(f32)
    normed_two = layer_norm(resid_two, norm_gain[2], norm_gain[3]).astype(bf16)
    proj_two = jnp.einsum(
        "prcd,kde->kprce", normed_two, attn_full[4:7], preferred_element_type=f32
    ).astype(bf16)
    proj_two = proj_two.reshape(3, prot, rows, cols_dev, H, DH)
    query_two, key_two, value_two = (proj_two[0], proj_two[1], proj_two[2])
    scores_two = (
        jnp.einsum("prche,psche->pchrs", query_two, key_two, preferred_element_type=f32)
        * head_scale
    )
    probs_two = softmax_rows(scores_two, row_live_all[:, None, None, None, :])
    probs_two_low = probs_two.astype(bf16)
    mixed_two = jnp.einsum(
        "pchrs,psche->prche", probs_two_low, value_two, preferred_element_type=f32
    ).astype(bf16)
    mixed_two = mixed_two.reshape(prot, rows, cols_dev, width)
    resid_three = resid_two + jnp.einsum(
        "prcd,de->prce", mixed_two, attn_full[7], preferred_element_type=f32
    )
    normed_three = layer_norm(resid_three, norm_gain[4], norm_gain[5]).astype(bf16)
    inner = jnp.einsum("prcd,df->prcf", normed_three, in_full, preferred_element_type=f32)
    activ = jax.nn.gelu(inner, approximate=True).astype(bf16)
    result = (
        resid_three + jnp.einsum("prcf,fd->prcd", activ, out_full, preferred_element_type=f32)
    ).astype(bf16)
    block_out = lax.all_to_all(result, "seq", split_axis=1, concat_axis=2, tiled=True)
    grad_act = jnp.einsum("prcd,fd->prcf", up_grad, out_full, preferred_element_type=f32)
    _, gelu_back = jax.vjp(partial(jax.nn.gelu, approximate=True), inner)
    grad_inner = gelu_back(grad_act)[0].astype(bf16)
    grad_normed_three = jnp.einsum("prcf,df->prcd", grad_inner, in_full, preferred_element_type=f32)
    _, norm_back_three = jax.vjp(layer_norm, resid_three, norm_gain[4], norm_gain[5])
    part_three, gain_grad_three, shift_grad_three = norm_back_three(grad_normed_three)
    grad_three = up_grad.astype(f32) + part_three
    grad_branch_two = grad_three.astype(bf16)
    grad_mixed_two = jnp.einsum(
        "prce,de->prcd", grad_branch_two, attn_full[7], preferred_element_type=f32
    ).astype(bf16)
    grad_mixed_two = grad_mixed_two.reshape(prot, rows, cols_dev, H, DH)
    grad_probs_two = jnp.einsum(
        "prche,psche->pchrs", grad_mixed_two, value_two, preferred_element_type=f32
    )
    grad_value_two = jnp.einsum(
        "pchrs,prche->psche", probs_two_low, grad_mixed_two, preferred_element_type=f32
    )
    grad_scores_two = softmax_back(probs_two, grad_probs_two).astype(bf16)
    grad_query_two = (
        jnp.einsum("pchrs,psche->prche", grad_scores_two, key_two, preferred_element_type=f32)
        * head_scale
    )
    grad_key_two = (
        jnp.einsum("pchrs,prche->psche", grad_scores_two, query_two, preferred_element_type=f32)
        * head_scale
    )
    grad_proj_two = jnp.stack([grad_query_two, grad_key_two, grad_value_two]).astype(bf16)
    grad_proj_two = grad_proj_two.reshape(3, prot, rows, cols_dev, width)
    grad_normed_two = jnp.einsum(
        "kprce,kde->prcd", grad_proj_two, attn_full[4:7], preferred_element_type=f32
    )
    _, norm_back_two = jax.vjp(layer_norm, resid_two, norm_gain[2], norm_gain[3])
    part_two, gain_grad_two, shift_grad_two = norm_back_two(grad_normed_two)
    grad_stream = (grad_three + part_two).astype(bf16)
    col_attn_terms = attn_pair(normed_two, grad_proj_two, mixed_two, grad_branch_two)
    in_terms = jnp.einsum("prcd,prcf->df", normed_three, grad_inner, preferred_element_type=f32)
    out_terms = jnp.einsum("prcf,prcd->df", activ, up_grad, preferred_element_type=f32)
    grad_rows = lax.all_to_all(grad_stream, "seq", split_axis=1, concat_axis=2, tiled=True)
    grad_mixed_one = jnp.einsum(
        "prce,de->prcd", grad_rows, attn_full[3], preferred_element_type=f32
    ).astype(bf16)
    grad_mixed_one = grad_mixed_one.reshape(prot, rows_dev, cols, H, DH)
    partial_grads = jnp.einsum(
        "prihe,prjhe->phij", grad_mixed_one, value_one, preferred_element_type=f32
    )
    grad_value_one = jnp.einsum(
        "phij,prihe->prjhe", probs_low, grad_mixed_one, preferred_element_type=f32
    )
    grad_part = sent_and_summed(partial_grads.astype(jnp.bfloat16), "seq", 2)
    grad_scores_one = lax.all_gather(
        softmax_back(probs_one, grad_part).astype(bf16), "seq", axis=2, tiled=True
    )
    tie_rows = row_live[:, :, None, None, None] * tie_scale[:, None, None, None, None]
    grad_query_one = (
        jnp.einsum("phij,prjhe->prihe", grad_scores_one, key_one, preferred_element_type=f32)
        * tie_rows
    )
    grad_key_one = (
        jnp.einsum("phij,prihe->prjhe", grad_scores_one, masked_query, preferred_element_type=f32)
        * tie_scale[:, None, None, None, None]
    )
    grad_proj_one = jnp.stack([grad_query_one, grad_key_one, grad_value_one]).astype(bf16)
    grad_proj_one = grad_proj_one.reshape(3, prot, rows_dev, cols, width)
    grad_normed_one = jnp.einsum(
        "kprce,kde->prcd", grad_proj_one, attn_full[0:3], preferred_element_type=f32
    )
    _, norm_back_one = jax.vjp(layer_norm, resid_one, norm_gain[0], norm_gain[1])
    part_one, gain_grad_one, shift_grad_one = norm_back_one(grad_normed_one)
    grad_tokens = grad_rows.astype(f32) + part_one
    norm_stack = jnp.stack(
        [
            gain_grad_one,
            shift_grad_one,
            gain_grad_two,
            shift_grad_two,
            gain_grad_three,
            shift_grad_three,
        ]
    )
    row_attn_terms = attn_pair(normed_one, grad_proj_one, mixed_one, grad_rows)
    owned = lax.psum_scatter(
        jnp.concatenate(
            [row_attn_terms, col_attn_terms, in_terms, out_terms, norm_stack.T], axis=1
        ),
        "seq",
        scatter_dimension=0,
        tiled=True,
    )
    width_dev = owned.shape[0]
    row_part = owned[:, : 4 * width].reshape(width_dev, 4, width)
    col_part = owned[:, 4 * width : 8 * width].reshape(width_dev, 4, width)
    in_part = owned[:, 8 * width : 8 * width + hidden]
    out_part = owned[:, 8 * width + hidden : 8 * width + 2 * hidden].T
    norm_part = owned[:, 8 * width + 2 * hidden :].T
    attn_part = jnp.concatenate([row_part, col_part], axis=1).transpose(1, 0, 2)
    attn_grad, in_grad, out_grad, norm_grad = (
        lax.psum(attn_part.astype(jnp.bfloat16), "grp").astype(jnp.float32),
        lax.psum(in_part.astype(jnp.bfloat16), "grp").astype(jnp.float32),
        lax.psum(out_part.astype(jnp.bfloat16), "grp").astype(jnp.float32),
        lax.psum(norm_part.astype(jnp.bfloat16), "grp").astype(jnp.float32),
    )
    squares = (
        jnp.sum(attn_grad * attn_grad)
        + jnp.sum(in_grad * in_grad)
        + jnp.sum(out_grad * out_grad)
        + jnp.sum(norm_grad * norm_grad)
    )
    grad_norm = jnp.sqrt(lax.psum(squares, "seq"))
    factor = clip_bound / jnp.maximum(grad_norm, clip_bound)
    attn_first_new, attn_second_new, attn_weight_new = adam_update(
        attn_weight, attn_first, attn_second, attn_grad * factor, matrix_rate
    )
    in_first_new, in_second_new, in_weight_new = adam_update(
        in_weight, in_first, in_second, in_grad * factor, matrix_rate
    )
    out_first_new, out_second_new, out_weight_new = adam_update(
        out_weight, out_first, out_second, out_grad * factor, matrix_rate
    )
    norm_first_new, norm_second_new, norm_new = adam_update(
        norm_param, norm_first, norm_second, norm_grad * factor, norm_rate
    )
    return (
        block_out,
        grad_tokens,
        grad_norm,
        attn_first_new,
        attn_second_new,
        attn_weight_new,
        attn_weight_new.astype(bf16),
        in_first_new,
        in_second_new,
        in_weight_new,
        in_weight_new.astype(bf16),
        out_first_new,
        out_second_new,
        out_weight_new,
        out_weight_new.astype(bf16),
        norm_first_new,
        norm_second_new,
        norm_new,
    )


PAIR = [(0, 1), (1, 0)]
TILE = 128


def swap(value, axis):
    return lax.ppermute(value, axis, PAIR)


def pick(value, index, axis):
    return lax.dynamic_index_in_dim(value, index, axis, keepdims=False)


def joined(own, other, place, axis):
    return jnp.where(
        place == 0,
        jnp.concatenate([own, other], axis=axis),
        jnp.concatenate([other, own], axis=axis),
    )


def merge(own, other, place, axis):
    return jnp.where(
        place == 0,
        jnp.stack([own, other], axis=axis),
        jnp.stack([other, own], axis=axis),
    )


def merge_cores(value, c):
    prot, _, cols, width = value.shape
    part = cols // 4
    split = value.reshape(prot, 2, 2, part, width)
    got = swap(pick(split, 1 - c, 2), "c")
    both = merge(pick(split, c, 2), got, c, 0)
    return both.reshape(8, part, width)


def to_blocks(value):
    return lax.all_to_all(value, ("z", "x"), 0, 0, tiled=True)


def to_rows(got, c):
    _, part, width = got.shape
    got = got.reshape(2, 2, 2, part, width)
    other = swap(pick(got, 1 - c, 0), "c")
    both = merge(pick(got, c, 0), other, c, 2)
    return both.reshape(2, 1, 4 * part, width)


def together(*values):
    return lax.optimization_barrier(values)


def gather_z(own):
    return [own] + [lax.ppermute(own, "z", [(k, k ^ i) for k in range(4)]) for i in (1, 2, 3)]


def spread(over_z):
    over_x = swap(over_z, "x")
    quarter = [((0, 0, 0), over_z, 0), ((1, 0, 0), over_x, 0)]
    return quarter + [((j, 1, 0), swap(value, "y"), 0) for (j, _, _), value, _ in quarter]


def across(over_x, over_y):
    half = over_x.shape[0] // 2
    return swap(over_x[:half], "y"), swap(over_y[half:], "x")


def across_pieces(by_y, by_x):
    return [((1, 1, 0), by_y, 0), ((1, 1, 0), by_x, by_y.shape[0])]


def plan_of(pieces):
    return [(step, first) for step, _, first in pieces]


def placing(plan, outs_at, place_ref, stacks, outs, sem, steps=True):
    copies = []
    for stack, ((j, m, k), first) in zip(stacks, plan):
        x, y, c = (lax.bitwise_xor(place_ref[n], step) for n, step in ((1, j), (3, m), (2, k)))
        for i in range(stack.shape[0]):
            z = first + i
            shard = (lax.bitwise_xor(place_ref[0], z) if steps else z) * 2 + x
            for source, target in outs_at(stack.at[i], outs, shard, y, c):
                copies.append(pltpu.make_async_copy(source, target, sem.at[len(copies)]))
    return copies


def row_attn_at(ref, outs, shard, y, c):
    depth = outs[0].shape[0] // 16
    at = pl.multiple_of((shard * 2 + y) * depth, depth)
    return [(ref, outs[0].at[pl.ds(at, depth)])]


def ffn_at(ref, outs, shard, y, c):
    depth = ref.shape[0]
    at = pl.multiple_of((y * 8 + shard) * depth, depth)
    return [(ref, outs[0].at[pl.ds(at, depth)])]


def col_attn_at(ref, outs, shard, y, c):
    depth, half = ref.shape[1], ref.shape[2]
    at = pl.multiple_of((shard * 2 + y) * depth, depth)
    moves = []
    slots = [(o, n) for o, out in enumerate(outs) for n in range(out.shape[1] // (2 * half))]
    for k, (o, n) in enumerate(slots):
        lane = pl.multiple_of(c * half + n * 2 * half, TILE)
        moves.append((ref.at[k], outs[o].at[pl.ds(at, depth), pl.ds(lane, half)]))
    return moves


def contract(a, b, dims):
    return lax.dot_general(a, b, (dims, ((), ())), preferred_element_type=jnp.float32)


LAST = ((1,), (1,))
FIRST = ((0,), (0,))
PLAIN = ((1,), (0,))


def softmax_of(scores, keep):
    scores = jnp.where(keep, scores, masked_score)
    expo = jnp.exp(scores - jnp.max(scores, axis=-1, keepdims=True))
    return expo / jnp.sum(expo, axis=-1, keepdims=True)


def head_lanes(lanes):
    side = lax.broadcasted_iota(jnp.int32, (1, lanes), 1) % TILE < DH
    return (side, jnp.logical_not(side))


def only(keep, value):
    return jnp.where(keep, value, jnp.zeros_like(value))


def column_keep(info_ref, own_cols, near, part):
    key = lax.broadcasted_iota(jnp.int32, (1, 2 * near), 1)
    far = key >= near
    inner = key % near
    x = jnp.where(far, 1 - info_ref[1], info_ref[1])
    c = jnp.where(inner >= part, 1 - info_ref[2], info_ref[2])
    column = x * near + c * part + inner % part
    return column < info_ref[3]


def live_pair(value, row, info_ref):
    lane = lax.broadcasted_iota(jnp.int32, (1, value.shape[1]), 1) // TILE + row
    return only(lane < info_ref[4], value)


def head_pair(ref, row, lane):
    blocks, _, part, _ = ref.shape
    found = [ref[:, row + n, :, lane : lane + TILE].reshape(blocks * part, TILE) for n in (0, 1)]
    return jnp.concatenate(found, axis=1)


def row_fwd_kernel(token_plan, weight_plan, place_ref, info_ref, tie_ref, *refs):
    bf16 = jnp.bfloat16
    f32 = jnp.float32
    tokens, refs = refs[: len(token_plan)], refs[len(token_plan) :]
    stacks, refs = refs[: len(weight_plan)], refs[len(weight_plan) :]
    own_ref, near_tokens_ref, far_tokens_ref, w_ref, gain_ref, near_ref, far_ref, o_ref = refs[:8]
    all_ref, norm_ref, token_sem, weight_sem = refs[8:]
    blocks, rows, part, lanes = near_ref.shape
    half = lanes // 3
    count = rows * part
    near = blocks * part
    copies = []
    for stack, (j, k) in zip(tokens, token_plan):
        x = lax.bitwise_xor(place_ref[1], j)
        for i in range(4):
            row = lax.bitwise_xor(place_ref[0], i) * 2 + x
            moves = [(stack.at[i, pl.ds(0, 2 * part)], all_ref.at[k, row])]
            if k == 0:
                moves.append((stack.at[i, pl.ds(2 * part, 16)], norm_ref.at[j * 4 + i]))
            for source, target in moves:
                copies.append(pltpu.make_async_copy(source, target, token_sem.at[len(copies)]))
    weights = placing(weight_plan, row_attn_at, place_ref, stacks, [w_ref], weight_sem)
    for copy in copies + weights:
        copy.start()
    for copy in copies:
        copy.wait()
    gains = jnp.sum(norm_ref[...].astype(f32), axis=0)
    gain_ref[...] = gains
    x = info_ref[1]
    for ref, side in ((near_tokens_ref, x), (far_tokens_ref, 1 - x)):
        at = pl.ds(pl.multiple_of(side * part, part), part)
        for k in range(blocks):
            value = all_ref[k, :, at, :].reshape(count, -1)
            if k == 0:
                @pl.when(side == x)
                def _():
                    own_ref[...] = value
            found = normed(value.astype(f32), gains[0:1], gains[1:2])[0]
            ref[k * count : (k + 1) * count] = found.astype(bf16)
    for copy in weights:
        copy.wait()
    for n in range(3):
        at = slice(n * half, (n + 1) * half)
        found = contract(near_tokens_ref[...], w_ref[:, at], PLAIN).astype(bf16)
        near_ref[:, :, :, at] = found.reshape(blocks, rows, part, half)
        if n > 0:
            found = contract(far_tokens_ref[...], w_ref[:, at], PLAIN).astype(bf16)
            far_ref[:, :, :, (n - 1) * half : n * half] = found.reshape(blocks, rows, part, half)
    sides = head_lanes(2 * TILE)
    keep = column_keep(info_ref, near, near, part)
    tie = tie_ref[0]
    for lane in range(0, half, TILE):
        scores = [jnp.zeros((near, 2 * near), f32) for _ in sides]
        for row in range(0, rows, 2):
            query = live_pair(head_pair(near_ref, row, lane), row, info_ref)
            key = jnp.concatenate(
                [head_pair(near_ref, row, half + lane), head_pair(far_ref, row, lane)], axis=0
            )
            for n, side in enumerate(sides):
                scores[n] = scores[n] + contract(only(side, query), key, LAST)
        probs = [softmax_of(s * tie, keep).astype(bf16) for s in scores]
        for row in range(0, rows, 2):
            value = jnp.concatenate(
                [head_pair(near_ref, row, 2 * half + lane), head_pair(far_ref, row, half + lane)],
                axis=0,
            )
            mixed = jnp.where(
                sides[0], contract(probs[0], value, PLAIN), contract(probs[1], value, PLAIN)
            ).astype(bf16)
            for n in (0, 1):
                o_ref[:, row + n, :, lane : lane + TILE] = mixed[:, n * TILE : (n + 1) * TILE].reshape(
                    blocks, part, TILE
                )


def next_sums_kernel(
    place_ref, y_kept_ref, y_got_ref, x_kept_ref, x_got_ref, to_x_ref, with_x_ref, to_y_ref, with_y_ref
):
    _, depth, lanes = to_x_ref.shape
    first, first_y = place_ref[1] == 0, place_ref[3] == 0
    summed = added(y_kept_ref[...], y_got_ref[...]).reshape(2, depth, lanes)
    with_x_ref[0] = jnp.where(first, summed[0], summed[1])
    to_x_ref[0] = jnp.where(first, summed[1], summed[0])
    summed = added(x_kept_ref[0], x_got_ref[0])
    with_y_ref[0] = jnp.where(first_y, summed[0], summed[1])
    to_y_ref[0] = jnp.where(first_y, summed[1], summed[0])


def next_sums(place, y_kept, y_got, x_kept, x_got):
    zs, _, depth, lanes = x_kept.shape
    by_rows = pl.BlockSpec((2 * depth, lanes), lambda n: (n, 0))
    by_z = pl.BlockSpec((1, 2, depth, lanes), lambda n: (n, 0, 0, 0))
    return pl.pallas_call(
        next_sums_kernel,
        grid=(zs,),
        in_specs=[pl.BlockSpec(memory_space=pltpu.SMEM), by_rows, by_rows, by_z, by_z],
        out_specs=[pl.BlockSpec((1, depth, lanes), lambda n: (n, 0, 0))] * 4,
        out_shape=[jax.ShapeDtypeStruct((zs, depth, lanes), jnp.bfloat16)] * 4,
        compiler_params=pltpu.CompilerParams(vmem_limit_bytes=56 * 2**20),
    )(place, y_kept, y_got, x_kept, x_got)


def row_bwd_kernel(
    info_ref, tie_ref, near_ref, far_ref, own_ref, got_ref, w_ref, near_tokens_ref, far_tokens_ref,
    near_part_ref, near_theirs_ref, far_part_ref, far_theirs_ref, sent_ref, kept_ref,
    do_ref, d_near_ref, d_far_ref,
):
    bf16 = jnp.bfloat16
    blocks, rows, part, lanes = near_ref.shape
    half = lanes // 3
    near = blocks * part
    sides = head_lanes(2 * TILE)
    keep = column_keep(info_ref, near, near, part)
    tie = tie_ref[0]
    do_ref[0] = own_ref[...].reshape(rows, part, half)
    do_ref[1] = got_ref[...].reshape(rows, part, half)

    for lane in range(0, half, TILE):

        def pair(ref, row, first):
            at = slice(first + lane, first + lane + TILE)
            found = [ref[:, row + n, :, at].reshape(near, TILE) for n in (0, 1)]
            return jnp.concatenate(found, axis=1)

        def both(row, first):
            return jnp.concatenate(
                [pair(near_ref, row, first), pair(far_ref, row, first - half)], axis=0
            )

        scores = [jnp.zeros((near, 2 * near), jnp.float32) for _ in sides]
        grads = [jnp.zeros((near, 2 * near), jnp.float32) for _ in sides]
        for row in range(0, rows, 2):
            query = live_pair(pair(near_ref, row, 0), row, info_ref)
            key, value = both(row, half), both(row, 2 * half)
            out = pair(do_ref, row, 0)
            for n, side in enumerate(sides):
                scores[n] = scores[n] + contract(only(side, query), key, LAST)
                grads[n] = grads[n] + contract(only(side, out), value, LAST)
        probs = [softmax_of(s * tie, keep) for s in scores]
        lows = [p.astype(bf16) for p in probs]
        deltas = [softmax_back(p, g).astype(bf16) for p, g in zip(probs, grads)]
        low_turned = [p.T for p in lows]
        delta_turned = [d.T for d in deltas]
        for row in range(0, rows, 2):
            query = live_pair(pair(near_ref, row, 0), row, info_ref)
            key, out = both(row, half), pair(do_ref, row, 0)
            dq = [contract(d, key, PLAIN) for d in deltas]
            dk = [contract(d, query, PLAIN) for d in delta_turned]
            dv = [contract(p, out, PLAIN) for p in low_turned]
            dq = live_pair(jnp.where(sides[0], dq[0], dq[1]) * tie, row, info_ref).astype(bf16)
            dk = (jnp.where(sides[0], dk[0], dk[1]) * tie).astype(bf16)
            dv = jnp.where(sides[0], dv[0], dv[1]).astype(bf16)

            def put(ref, first, value):
                for n in (0, 1):
                    piece = value[:, n * TILE : (n + 1) * TILE].reshape(blocks, part, TILE)
                    ref[:, row + n, :, first + lane : first + lane + TILE] = piece

            put(d_near_ref, 0, dq)
            put(d_near_ref, half, dk[:near])
            put(d_near_ref, 2 * half, dv[:near])
            put(d_far_ref, 0, dk[near:])
            put(d_far_ref, half, dv[near:])

    count = rows * part
    d_far = d_far_ref[...].reshape(blocks * count, 2 * half)
    far_weights = w_ref[:, half:]
    far_part_ref[...] = contract(d_far[:count], far_weights, LAST)
    far_theirs_ref[...] = contract(d_far[count:], far_weights, LAST).astype(bf16)
    d_near = d_near_ref[...].reshape(blocks * count, lanes)
    near_part_ref[...] = contract(d_near[:count], w_ref[...], LAST)
    near_theirs_ref[...] = contract(d_near[count:], w_ref[...], LAST).astype(bf16)
    near_turned = near_tokens_ref[...].T
    far_turned = far_tokens_ref[...].T
    zs, depth = kept_ref.shape[0], kept_ref.shape[1]
    first = info_ref[1] == 0
    for n in range(3):
        at = slice(n * half, (n + 1) * half)
        terms = contract(near_turned, d_near[:, at], PLAIN)
        if n > 0:
            terms = terms + contract(far_turned, d_far[:, (n - 1) * half : n * half], PLAIN)
        terms = terms.astype(bf16).reshape(zs, 2, depth, half)
        kept_ref[:, :, at] = jnp.where(first, terms[:, 0], terms[:, 1])
        sent_ref[:, :, at] = jnp.where(first, terms[:, 1], terms[:, 0])


def row_attention(place, info, tie, tokens, weights, rows, half):
    f32, bf16 = jnp.float32, jnp.bfloat16
    zs, deep, width = tokens[0][1].shape
    part = (deep - 16) // 2
    count = rows * part
    small = pl.BlockSpec(memory_space=pltpu.SMEM)
    anywhere = pl.BlockSpec(memory_space=pl.ANY)
    inside = pl.BlockSpec(memory_space=pltpu.VMEM)
    shapes = [
        ((count, width), bf16),
        ((2 * count, width), bf16),
        ((2 * count, width), bf16),
        ((width, 3 * half), bf16),
        ((16, width), f32),
        ((2, rows, part, 3 * half), bf16),
        ((2, rows, part, 2 * half), bf16),
        ((2, rows, part, half), bf16),
    ]
    return pl.pallas_call(
        partial(row_fwd_kernel, [step for step, _ in tokens], plan_of(weights)),
        in_specs=[small] * 3 + [anywhere] * (len(tokens) + len(weights)),
        out_specs=[inside] * len(shapes),
        out_shape=[jax.ShapeDtypeStruct(shape, kind) for shape, kind in shapes],
        scratch_shapes=[
            pltpu.VMEM((2, rows, 2 * part, width), bf16),
            pltpu.VMEM((8, 16, width), bf16),
            pltpu.SemaphoreType.DMA((24,)),
            pltpu.SemaphoreType.DMA((16,)),
        ],
        compiler_params=pltpu.CompilerParams(vmem_limit_bytes=56 * 2**20),
        cost_estimate=pl.CostEstimate(flops=7 * 10**9, bytes_accessed=10**7, transcendentals=10**6),
    )(place, info, tie, *[v for _, v in tokens], *[v for _, v, _ in weights])


def row_attention_back(info, tie, near, far, own, got, weights, near_tokens, far_tokens):
    blocks, rows, part, lanes = near.shape
    count, width = rows * part, weights.shape[0]
    half = lanes // 3
    f32, bf16 = jnp.float32, jnp.bfloat16
    small = pl.BlockSpec(memory_space=pltpu.SMEM)
    inside = pl.BlockSpec(memory_space=pltpu.VMEM)
    shapes = [((count, width), kind) for kind in (f32, bf16) * 2]
    shapes = shapes + [((4, width // 8, lanes), bf16)] * 2
    return pl.pallas_call(
        row_bwd_kernel,
        in_specs=[small, small] + [inside] * 7,
        out_specs=[inside] * 6,
        out_shape=[jax.ShapeDtypeStruct(shape, kind) for shape, kind in shapes],
        scratch_shapes=[
            pltpu.VMEM((blocks, rows, part, half), bf16),
            pltpu.VMEM((blocks, rows, part, lanes), bf16),
            pltpu.VMEM((blocks, rows, part, 2 * half), bf16),
        ],
        compiler_params=pltpu.CompilerParams(vmem_limit_bytes=56 * 2**20),
    )(info, tie, near, far, own, got, weights, near_tokens, far_tokens)


def normed(value, gain, shift):
    centred = value - jnp.mean(value, axis=-1, keepdims=True)
    scale = lax.rsqrt(jnp.mean(centred * centred, axis=-1, keepdims=True) + eps_norm)
    unit = centred * scale
    return unit * gain + shift, unit, scale


def normed_back(grad, unit, scale, gain):
    inner = grad * gain
    mean = jnp.mean(inner, axis=-1, keepdims=True)
    along = jnp.mean(inner * unit, axis=-1, keepdims=True)
    return scale * (inner - mean - unit * along)


def column_masks(info_ref, rows, part):
    tokens = rows * part
    key = lax.broadcasted_iota(jnp.int32, (tokens, tokens), 0)
    query = lax.broadcasted_iota(jnp.int32, (tokens, tokens), 1)
    same = key % part == query % part
    return jnp.logical_and(same, key // part < info_ref[4])


def stacked(value, sides):
    return jnp.concatenate([only(side, value) for side in sides], axis=0)


def column_probs(query, key, keep, sides):
    scores = contract(stacked(key, sides), query, LAST) * (1.0 / math.sqrt(DH))
    tokens = query.shape[0]
    probs = []
    for n in (0, 1):
        part = jnp.where(keep, scores[n * tokens : (n + 1) * tokens], masked_score)
        expo = jnp.exp(part - jnp.max(part, axis=0, keepdims=True))
        probs.append(expo / jnp.sum(expo, axis=0, keepdims=True))
    return probs


def col_fwd_kernel(plan, info_ref, place_ref, *refs):
    stacks, refs = refs[: len(plan)], refs[len(plan) :]
    x_ref, own_ref, other_ref, gain_ref, acts_ref, one_ref, qkv_ref = refs[:7]
    resid_ref, normed_three_ref, mixed_ref, three_ref, col_ref, seven_ref, sem = refs[7:]
    copies = placing(plan, col_attn_at, place_ref, stacks, [three_ref, col_ref, seven_ref], sem)
    for copy in copies:
        copy.start()
    bf16 = jnp.bfloat16
    rows, cols, lanes = qkv_ref.shape
    width = lanes // 3
    part = 16
    own, other = own_ref[...], other_ref[...]
    flip = info_ref[2] == 0
    mixed_one = jnp.concatenate(
        [jnp.where(flip, own, other), jnp.where(flip, other, own)], axis=1
    )
    acts_ref[:, :width] = mixed_one
    for copy in copies:
        copy.wait()
    stream = (x_ref[...].astype(jnp.float32) + contract(mixed_one, three_ref[...], PLAIN)).astype(bf16)
    one_ref[...] = stream
    normed_two = normed(stream.astype(jnp.float32), gain_ref[2:3], gain_ref[3:4])[0].astype(bf16)
    acts_ref[:, width : 2 * width] = normed_two
    for n in range(3):
        at = slice(n * width, (n + 1) * width)
        found = contract(normed_two, col_ref[:, at], PLAIN).astype(bf16)
        qkv_ref[:, :, at] = found.reshape(rows, cols, width)
    keep = column_masks(info_ref, rows, part)
    sides = head_lanes(TILE)

    def attend(b, carry):
        at = pl.ds(pl.multiple_of(b * part, part), part)
        def tile(n, t):
            lane = n * width + t * TILE
            return qkv_ref[:, at, lane : lane + TILE].reshape(rows * part, TILE)
        tiles = range(width // TILE)
        probs = [column_probs(tile(0, t), tile(1, t), keep, sides) for t in tiles]
        for t in tiles:
            low = jnp.concatenate(probs[t], axis=0).astype(bf16)
            mixed = contract(low, stacked(tile(2, t), sides), FIRST).astype(bf16)
            mixed_ref[:, at, t * TILE : (t + 1) * TILE] = mixed.reshape(rows, part, TILE)
        return carry

    lax.fori_loop(0, cols // part, attend, 0)
    mixed = mixed_ref[...].reshape(rows * cols, width)
    acts_ref[:, 2 * width :] = mixed
    resid = one_ref[...].astype(jnp.float32) + contract(mixed, seven_ref[...], PLAIN)
    resid_ref[...] = resid
    normed_three_ref[...] = normed(resid, gain_ref[4:5], gain_ref[5:6])[0].astype(bf16)


def col_bwd_kernel(plan, info_ref, place_ref, *refs):
    stacks, refs = refs[: len(plan)], refs[len(plan) :]
    up_ref, da_ref, da_got_ref, out_ref, out_got_ref, resid_ref, one_ref, qkv_ref, gain_ref = refs[:9]
    result_ref, stream_ref, own_ref, other_ref, mine_ref, theirs_ref, norms_ref = refs[9:16]
    dqkv_ref, do_ref, three_ref, col_ref, seven_ref, sem = refs[16:]
    copies = placing(plan, col_attn_at, place_ref, stacks, [three_ref, col_ref, seven_ref], sem)
    for copy in copies:
        copy.start()
    bf16 = jnp.bfloat16
    f32 = jnp.float32
    rows, cols, lanes = qkv_ref.shape
    width = lanes // 3
    part = 16
    result_ref[...] = (resid_ref[...] + out_ref[...] + out_got_ref[...].astype(f32)).astype(bf16)
    da = da_ref[...] + da_got_ref[...].astype(f32)
    gain = gain_ref[4:5]
    _, unit, scale = normed(resid_ref[...], gain, 0.0)
    grad_three = up_ref[...].astype(f32) + normed_back(da, unit, scale, gain)
    norms_ref[2:3] = jnp.sum(da * unit, axis=0, keepdims=True)
    norms_ref[3:4] = jnp.sum(da, axis=0, keepdims=True)
    branch = grad_three.astype(bf16)
    half = width // 2
    flip = info_ref[2] == 0

    def put_halves(first, value):
        at = slice(first, first + half)
        mine_ref[:, at] = jnp.where(flip, value[:, :half], value[:, half:])
        theirs_ref[:, at] = jnp.where(flip, value[:, half:], value[:, :half])

    put_halves(4 * half, branch)
    for copy in copies:
        copy.wait()
    do_ref[...] = contract(branch, seven_ref[...], LAST).astype(bf16).reshape(rows, cols, width)
    keep = column_masks(info_ref, rows, part)
    sides = head_lanes(TILE)
    ratio = 1.0 / math.sqrt(DH)

    def attend(b, carry):
        at = pl.ds(pl.multiple_of(b * part, part), part)
        tokens = rows * part

        def tile(n, t):
            lane = n * width + t * TILE
            return qkv_ref[:, at, lane : lane + TILE].reshape(tokens, TILE)

        def out_tile(t):
            return do_ref[:, at, t * TILE : (t + 1) * TILE].reshape(tokens, TILE)

        def put(n, t, value):
            lane = n * width + t * TILE
            dqkv_ref[:, at, lane : lane + TILE] = value.astype(bf16).reshape(rows, part, TILE)

        for t in range(width // TILE):
            query, key, out = tile(0, t), tile(1, t), out_tile(t)
            keys = stacked(key, sides)
            probs = column_probs(query, key, keep, sides)
            grads = contract(stacked(tile(2, t), sides), out, LAST)
            deltas = []
            for n, p in enumerate(probs):
                g = grads[n * tokens : (n + 1) * tokens]
                deltas.append((p * (g - jnp.sum(p * g, axis=0, keepdims=True))).astype(bf16))
            put(0, t, contract(jnp.concatenate(deltas, axis=0), keys, FIRST) * ratio)
            wide = jnp.concatenate(deltas, axis=1)
            put(1, t, contract(wide, stacked(query, sides), PLAIN) * ratio)
            wide = jnp.concatenate([p.astype(bf16) for p in probs], axis=1)
            put(2, t, contract(wide, stacked(out, sides), PLAIN))
        return carry

    lax.fori_loop(0, cols // part, attend, 0)
    dqkv = dqkv_ref[...].reshape(rows * cols, lanes)
    for n in range(3):
        put_halves((n + 1) * half, dqkv[:, n * width : (n + 1) * width])
    grad_normed = contract(dqkv, col_ref[...], LAST)
    gain = gain_ref[2:3]
    _, unit, scale = normed(one_ref[...].astype(f32), gain, 0.0)
    norms_ref[0:1] = jnp.sum(grad_normed * unit, axis=0, keepdims=True)
    norms_ref[1:2] = jnp.sum(grad_normed, axis=0, keepdims=True)
    stream = (grad_three + normed_back(grad_normed, unit, scale, gain)).astype(bf16)
    stream_ref[...] = stream
    put_halves(0, stream)
    mixed = contract(stream, three_ref[...], LAST).astype(bf16)
    own_ref[...] = jnp.where(flip, mixed[:, :half], mixed[:, half:])
    other_ref[...] = jnp.where(flip, mixed[:, half:], mixed[:, :half])


def tokens_back_kernel(
    info_ref, near_ref, near_got_ref, far_got_ref, x_ref, stream_ref, gain_ref, norms_ref,
    blocks_ref,
):
    f32 = jnp.float32
    grad = near_ref[...] + near_got_ref[...].astype(f32) + far_got_ref[...].astype(f32)
    gain = gain_ref[0:1]
    _, unit, scale = normed(x_ref[...].astype(f32), gain, 0.0)
    found = stream_ref[...].astype(f32) + normed_back(grad, unit, scale, gain)
    rows, deep, width = blocks_ref.shape
    part = deep - 16
    blocks_ref[:, :part] = found.astype(jnp.bfloat16).reshape(rows, part, width)
    sums = [
        jnp.sum(grad * unit, axis=0, keepdims=True),
        jnp.sum(grad, axis=0, keepdims=True),
        norms_ref[...],
        jnp.zeros((2, width), f32),
    ]
    sums = jnp.concatenate(sums, axis=0)
    depth = width // 8
    lane = lax.broadcasted_iota(jnp.int32, (width, TILE), 0)
    place = lax.broadcasted_iota(jnp.int32, (width, TILE), 1)
    for shard in range(8):
        chosen = jnp.logical_and(lane == shard * depth + place, place < depth)
        found = lax.dot_general(
            sums,
            chosen.astype(f32),
            (PLAIN, ((), ())),
            precision=lax.Precision.HIGHEST,
            preferred_element_type=f32,
        )
        found = jnp.concatenate([found, jnp.zeros((8, TILE), f32)], axis=0)
        blocks_ref[shard, part:, :TILE] = found.astype(jnp.bfloat16)
        blocks_ref[shard, part:, TILE:] = jnp.zeros((16, width - TILE), jnp.bfloat16)


def attn_terms_kernel(place_ref, acts_ref, got_ref, mine_ref, theirs_ref, sent_ref, kept_ref):
    width = acts_ref.shape[1] // 3
    half = width // 2
    depth = sent_ref.shape[1]
    turned = [
        jnp.concatenate([ref[:, n * width : (n + 1) * width].T for ref in (acts_ref, got_ref)], axis=1)
        for n in range(3)
    ]
    first = place_ref[3] == 0
    for n, m in enumerate((0, 1, 1, 1, 2)):
        at = slice(n * half, (n + 1) * half)
        grads = jnp.concatenate([mine_ref[:, at], theirs_ref[:, at]], axis=0)
        terms = contract(turned[m], grads, PLAIN).astype(jnp.bfloat16)
        terms = terms.reshape(sent_ref.shape[0], 2, depth, half)
        kept_ref[:, :, at] = jnp.where(first, terms[:, 0], terms[:, 1])
        sent_ref[:, :, at] = jnp.where(first, terms[:, 1], terms[:, 0])


def column_call(kernel, info, place, pieces, args, outs, scratch):
    width = args[-1].shape[1]
    bf16 = jnp.bfloat16
    small = pl.BlockSpec(memory_space=pltpu.SMEM)
    inside = pl.BlockSpec(memory_space=pltpu.VMEM)
    anywhere = pl.BlockSpec(memory_space=pl.ANY)
    return pl.pallas_call(
        partial(kernel, plan_of(pieces)),
        in_specs=[small] * 2 + [anywhere] * len(pieces) + [inside] * len(args),
        out_specs=[inside] * len(outs),
        out_shape=[jax.ShapeDtypeStruct(shape, kind) for shape, kind in outs],
        scratch_shapes=[
            *scratch,
            pltpu.VMEM((width, width), bf16),
            pltpu.VMEM((width, 3 * width), bf16),
            pltpu.VMEM((width, width), bf16),
            pltpu.SemaphoreType.DMA((160,)),
        ],
        compiler_params=pltpu.CompilerParams(vmem_limit_bytes=56 * 2**20),
    )(info, place, *[value for _, value, _ in pieces], *args)


def adam_kernel(place_ref, factor_ref, own_ref, other_ref, w_ref, first_ref, second_ref, *outs):
    count, _, width = w_ref.shape
    half = width // 2
    low = place_ref[2] == 0
    for n in range(count):
        at = pl.ds(pl.multiple_of((pl.program_id(0) * count + n) * half, TILE), half)
        own, other = own_ref[:, at], other_ref[:, at]
        grad = jnp.concatenate([jnp.where(low, own, other), jnp.where(low, other, own)], axis=1)
        grad = grad.astype(jnp.float32) * factor_ref[0]
        first, second, weight = adam_update(w_ref[n], first_ref[n], second_ref[n], grad, matrix_rate)
        for ref, value in zip(outs, (first, second, weight, weight.astype(jnp.bfloat16))):
            ref[n] = value


def attn_adam(place, factor, own, other, weight, first, second):
    small = pl.BlockSpec(memory_space=pltpu.SMEM)
    inside = pl.BlockSpec(memory_space=pltpu.VMEM)
    block = pl.BlockSpec((4, *weight.shape[1:]), lambda m: (m, 0, 0))
    kinds = [jnp.float32] * 3 + [jnp.bfloat16]
    return pl.pallas_call(
        adam_kernel,
        grid=(weight.shape[0] // 4,),
        in_specs=[small, small, inside, inside] + [block] * 3,
        out_specs=[block] * 4,
        out_shape=[jax.ShapeDtypeStruct(weight.shape, kind) for kind in kinds],
        compiler_params=pltpu.CompilerParams(vmem_limit_bytes=58 * 2**20),
    )(place, factor.reshape(1), own, other, weight, first, second)


def ffn_adam_kernel(place_ref, factor_ref, *refs):
    pieces, refs = refs[:4], refs[4:]
    low, even = place_ref[2] == 0, place_ref[3] == 0
    factor = factor_ref[0]
    depth = pieces[0].shape[0]
    part = depth // 2
    half = pl.program_id(0)

    def by_matrix(first, second):
        return jnp.where(even, first, second), jnp.where(even, second, first)

    def put(grad, ins, outs):
        values = adam_update(*[ref[...] for ref in ins], grad * factor, matrix_rate)
        for ref, value in zip(outs, (*values, values[2].astype(jnp.bfloat16))):
            ref[...] = value

    rows = pl.ds(pl.multiple_of(half * part, 16), part)
    owns = by_matrix(pieces[0][rows], pieces[1][rows])
    others = by_matrix(pieces[2][rows], pieces[3][rows])
    for n, (own, other) in enumerate(zip(owns, others)):
        grad = jnp.concatenate([jnp.where(low, own, other), jnp.where(low, other, own)], axis=1)
        put(grad.astype(jnp.float32), refs[3 * n : 3 * n + 3], refs[6 + 4 * n : 10 + 4 * n])


def ffn_adam(place, factor, pieces, ins, outs):
    small = pl.BlockSpec(memory_space=pltpu.SMEM)
    inside = pl.BlockSpec(memory_space=pltpu.VMEM)
    depth, hidden = ins[0].shape
    block = pl.BlockSpec((depth // 2, hidden), lambda n: (n, 0))
    kinds = [jnp.float32] * 3 + [jnp.bfloat16]
    return pl.pallas_call(
        ffn_adam_kernel,
        grid=(2,),
        in_specs=[small, small] + [inside] * 4 + [block] * 6,
        out_specs=[block] * 8,
        out_shape=[jax.ShapeDtypeStruct((depth, hidden), kind) for kind in kinds * 2],
        compiler_params=pltpu.CompilerParams(vmem_limit_bytes=58 * 2**20),
    )(place, factor.reshape(1), *pieces, *ins, *[value.T for value in outs])


def whole_call(kernel, info, args, outs, scratch=()):
    inside = pl.BlockSpec(memory_space=pltpu.VMEM)
    return pl.pallas_call(
        kernel,
        in_specs=[pl.BlockSpec(memory_space=pltpu.SMEM)] + [inside] * len(args),
        out_specs=[inside] * len(outs),
        out_shape=[jax.ShapeDtypeStruct(shape, kind) for shape, kind in outs],
        scratch_shapes=list(scratch),
        compiler_params=pltpu.CompilerParams(vmem_limit_bytes=56 * 2**20),
    )(info, *args)


def gelu_pair(u):
    ratio = math.sqrt(2.0 / math.pi)
    square = u * u
    tanh = jnp.tanh(ratio * u * (1.0 + 0.044715 * square))
    rise = 0.5 * (1.0 + tanh)
    slope = (0.5 * ratio) * (1.0 - tanh * tanh) * (1.0 + (3.0 * 0.044715) * square)
    return u * rise, rise + u * slope


def ffn_kernel(plan, place_ref, a_ref, a_got_ref, up_ref, up_got_ref, *refs):
    bf16 = jnp.bfloat16
    stacks, refs = refs[: len(plan)], refs[len(plan) :]
    out_ref, out_other_ref, da_ref, da_other_ref = refs[:4]
    y_sent_ref, y_kept_ref, x_sent_ref, x_kept_ref = refs[4:8]
    w_ref, turned_ref, out_sum, da_sum, sem = refs[8:]
    count, width = a_ref.shape
    chunk = w_ref.shape[1] // 2
    copies = placing(plan, ffn_at, place_ref, stacks, [w_ref], sem, steps=False)
    for copy in copies:
        copy.start()
    for n, ref in enumerate((a_ref, a_got_ref, up_ref, up_got_ref)):
        turned_ref[n // 2, :, (n % 2) * count : (n % 2 + 1) * count] = ref[...].T
    for copy in copies:
        copy.wait()
    for step in (0, 1):
        lane = slice(step * chunk, (step + 1) * chunk)
        w_in = w_ref[:width, lane]
        w_out = w_ref[width:, lane]
        activs, grads = [], []
        for n, (tokens, ups) in enumerate(((a_ref, up_ref), (a_got_ref, up_got_ref))):
            at = slice(n * count, (n + 1) * count)
            activ, slope = gelu_pair(contract(tokens[...], w_in, PLAIN))
            activ = activ.astype(bf16)
            grad = (contract(ups[...], w_out, PLAIN) * slope).astype(bf16)
            out, da = contract(activ, w_out, LAST), contract(grad, w_in, LAST)
            if step == 0:
                out_sum[at] = out
                da_sum[at] = da
            elif n == 0:
                out_ref[...] = out_sum[at] + out
                da_ref[...] = da_sum[at] + da
            else:
                out_other_ref[...] = (out_sum[at] + out).astype(bf16)
                da_other_ref[...] = (da_sum[at] + da).astype(bf16)
            activs.append(activ)
            grads.append(grad)
        in_terms = contract(turned_ref[0], jnp.concatenate(grads, axis=0), PLAIN).astype(bf16)
        out_terms = contract(turned_ref[1], jnp.concatenate(activs, axis=0), PLAIN).astype(bf16)
        if step == 0:
            first = place_ref[3] == 0
            y_kept_ref[...] = jnp.where(first, in_terms, out_terms)
            y_sent_ref[...] = jnp.where(first, out_terms, in_terms)
        else:
            first = place_ref[1] == 0
            zs, _, depth, _ = x_sent_ref.shape
            for n, terms in enumerate((in_terms, out_terms)):
                terms = terms.reshape(zs, 2, depth, chunk)
                x_kept_ref[:, n] = jnp.where(first, terms[:, 0], terms[:, 1])
                x_sent_ref[:, n] = jnp.where(first, terms[:, 1], terms[:, 0])


def feed_forward(place, normed_own, normed_got, up_own, up_got, pieces):
    count, width = normed_own.shape
    half = pieces[0][1].shape[-1]
    anywhere = pl.BlockSpec(memory_space=pl.ANY)
    inside = pl.BlockSpec(memory_space=pltpu.VMEM)
    f32, bf16 = jnp.float32, jnp.bfloat16
    shapes = [((count, width), kind) for kind in (f32, bf16, f32, bf16)]
    shapes = shapes + [((width, half // 2), bf16)] * 2 + [((4, 2, width // 8, half // 2), bf16)] * 2
    return pl.pallas_call(
        partial(ffn_kernel, plan_of(pieces)),
        in_specs=[pl.BlockSpec(memory_space=pltpu.SMEM)] + [inside] * 4 + [anywhere] * len(pieces),
        out_specs=[inside] * 8,
        out_shape=[jax.ShapeDtypeStruct(shape, kind) for shape, kind in shapes],
        scratch_shapes=[
            pltpu.VMEM((2 * width, half), bf16),
            pltpu.VMEM((2, width, 2 * count), bf16),
            pltpu.VMEM((2 * count, width), f32),
            pltpu.VMEM((2 * count, width), f32),
            pltpu.SemaphoreType.DMA((16,)),
        ],
        compiler_params=pltpu.CompilerParams(vmem_limit_bytes=56 * 2**20),
    )(place, normed_own, normed_got, up_own, up_got, *[value for _, value, _ in pieces])


def added(a, b):
    return (a.astype(jnp.float32) + b.astype(jnp.float32)).astype(jnp.bfloat16)


def z_summed(column, z):
    shard = pick(column, z, 0).astype(jnp.float32)
    for i in (1, 2, 3):
        other = pick(column, lax.bitwise_xor(z, i), 0)
        got = lax.ppermute(other, "z", [(k, k ^ i) for k in range(4)])
        shard = shard + got.astype(jnp.float32)
    return shard.astype(jnp.bfloat16)


def paired_body(
    tokens,
    cotangent,
    col_count,
    row_count,
    attn_weight,
    in_weight,
    out_weight,
    norm_param,
    attn_first,
    attn_second,
    in_first,
    in_second,
    out_first,
    out_second,
    norm_first,
    norm_second,
):
    f32 = jnp.float32
    bf16 = jnp.bfloat16
    z, x, y, c = (lax.axis_index(name) for name in ("z", "x", "y", "c"))
    width = tokens.shape[-1]
    hidden = in_weight.shape[1]
    depth = in_weight.shape[0]
    half = width // 2
    hidden_half = hidden // 2

    counts = jnp.stack([col_count, row_count])
    other_counts = swap(counts, "c")
    mine = jnp.where(z // 2 == c, counts, other_counts)
    mine = pick(mine, z % 2, 1)
    cols_live, rows_live = mine[0], mine[1]
    place = jnp.stack([z, x, c, y]).astype(jnp.int32)
    info = jnp.concatenate([place[:3], mine, place[3:]])
    tie = (lax.rsqrt(rows_live.astype(f32)) * (1.0 / math.sqrt(DH))).reshape(1)

    attn_low = attn_weight.astype(bf16)
    halves = attn_low.reshape(8, depth, 2, half)
    row_half = jnp.moveaxis(pick(halves[:3], c, 2), 0, 1).reshape(2, depth // 2, 3 * half)
    row_quarter = pick(row_half, y, 0)
    col_quarter = pick(pick(halves[3:], c, 2).reshape(5, 2, depth // 2, half), y, 1)
    row_z = gather_z(row_quarter)
    ffn_low = [in_weight.astype(bf16), out_weight.astype(bf16).T]
    ffn_low = [
        jnp.where(c == 0, low[:, :hidden_half], low[:, hidden_half:]) for low in ffn_low
    ]
    ffn_quarter = jnp.where(y == 0, *ffn_low)

    lanes = jnp.arange(width, dtype=jnp.int32) // depth
    norm_low = jnp.tile(norm_param.astype(bf16), (1, width // depth))
    norm_rows = jnp.where(lanes[None] == z * 2 + x, norm_low, jnp.zeros_like(norm_low))
    norm_rows = jnp.pad(norm_rows, ((0, 10), (0, 0)))
    part = tokens.shape[2] // 4
    tokens_here = merge_cores(tokens, c).reshape(4, 2 * part, width)
    parts = [
        jnp.concatenate([pick(tokens_here, lax.bitwise_xor(z, i), 0), norm_rows]) for i in range(4)
    ]
    parts = [parts[0]] + [
        lax.ppermute(parts[i], "z", [(k, k ^ i) for k in range(4)]) for i in (1, 2, 3)
    ]
    row_pieces = spread(jnp.stack(row_z))
    row_x, row_y, *parts, col_quarter = together(
        row_pieces[1][1], row_pieces[2][1], *parts, col_quarter
    )
    tokens_z = jnp.stack(parts)
    up = merge_cores(cotangent, c).reshape(4, 2, part, width)
    up = joined(pick(up, x, 1)[:, None], swap(pick(up, 1 - x, 1), "x")[:, None], x, 1)
    col_z = gather_z(col_quarter)
    tokens_x, row_last, ffn_quarter, up, *col_z = together(
        swap(tokens_z, "x"), swap(row_x, "y"), ffn_quarter, up, *col_z
    )
    steps = [(0, 0, 0), (1, 0, 0), (0, 1, 0), (1, 1, 0)]
    row_stacks = [row_pieces[0][1], row_x, row_y, row_last]
    row_pieces = [(step, value, 0) for step, value in zip(steps, row_stacks)]
    col_z = jnp.stack(col_z)
    ffn_z = lax.all_to_all(
        jnp.broadcast_to(ffn_quarter, (4, *ffn_quarter.shape)), "z", 0, 0, tiled=True
    )
    col_x = swap(col_z, "x")
    col_last = swap(col_x, "y")
    col_x, col_y, ffn_z, up = together(col_x, swap(col_z, "y"), ffn_z, up)
    tokens_far, col_last = together(swap(tokens_x, "c"), col_last)
    ffn_x, ffn_y = swap(ffn_z, "x"), swap(ffn_z, "y")
    ups = [pick(up, z, 0)] + [
        lax.ppermute(pick(up, lax.bitwise_xor(z, i), 0), "z", [(k, k ^ i) for k in range(4)])
        for i in (1, 2, 3)
    ]

    rows = 8
    count = rows * part
    stream_zero, near_normed, far_normed, w_row, norm_gain, near, far, mixed_heads = row_attention(
        place,
        info,
        tie,
        [((0, 0), tokens_z), ((1, 0), tokens_x), ((0, 1), swap(tokens_z, "c")), ((1, 1), tokens_far)],
        row_pieces,
        rows,
        half,
    )
    mixed_heads = mixed_heads.reshape(2, count, half)
    col_stacks = [col_z, col_x, col_y]
    mixed_heads, ffn_x, ffn_y, *rest = together(
        mixed_heads, ffn_x, ffn_y, *ups, *[swap(value, "c") for value in col_stacks]
    )
    ups, col_others = rest[:4], rest[4:]
    ups = [jnp.where(z % 2 == 0, a, b) for a, b in zip(ups, (ups[1], ups[0], ups[3], ups[2]))]
    ups = [jnp.where(z < 2, a, b) for a, b in zip(ups, ups[2:] + ups[:2])]
    up = jnp.concatenate(ups)
    col_stacks, col_others = [*col_stacks, col_last], [*col_others, swap(col_last, "c")]
    col_pieces = [(step, v, 0) for step, v in zip(steps, col_stacks)]
    col_pieces = col_pieces + [((j, m, 1), v, 0) for (j, m, _), v in zip(steps, col_others)]
    ffn_pieces = [(step, v, 0) for step, v in zip(steps, [ffn_z, ffn_x, ffn_y])]

    whole_shape, wide_shape = ((count, width), bf16), ((rows, part, 3 * width), bf16)
    acts, stream_one, qkv_two, resid_three, normed_three = column_call(
        col_fwd_kernel,
        info,
        place,
        col_pieces,
        [stream_zero, mixed_heads[0], swap(mixed_heads[1], "c"), norm_gain],
        [((count, 3 * width), bf16), whole_shape, wide_shape, ((count, width), f32), whole_shape],
        [pltpu.VMEM((rows, part, width), bf16)],
    )
    normed_three, *ffn_across = together(normed_three, *across(ffn_x, ffn_y))
    ffn_pieces = ffn_pieces + across_pieces(*ffn_across)

    column = x * (2 * part) + c * part + jnp.arange(part, dtype=jnp.int32)
    live = jnp.logical_and(
        (jnp.arange(rows, dtype=jnp.int32) < rows_live)[:, None], (column < cols_live)[None, :]
    )
    up = jnp.where(live[..., None], up, jnp.zeros_like(up)).reshape(count, width)
    out_own, out_other, da_own, da_other, *ffn_terms = feed_forward(
        place, normed_three, swap(normed_three, "c"), up, swap(up, "c"), ffn_pieces
    )
    da_got = swap(da_other, "c")
    out_got = swap(out_other, "c")
    y_sent, y_kept, x_sent, x_kept = ffn_terms
    y_got, x_got = swap(y_sent, "y"), swap(x_sent, "x")

    acts_got = swap(acts, "c")
    result, grad_stream, grad_own, grad_other, attn_mine, attn_theirs, col_norms = column_call(
        col_bwd_kernel,
        info,
        place,
        col_pieces,
        [up, da_own, da_got, out_own, out_got, resid_three, stream_one, qkv_two, norm_gain],
        [whole_shape] * 2
        + [((count, half), bf16)] * 2
        + [((count, 5 * half), bf16)] * 2
        + [((4, width), f32)],
        [pltpu.VMEM((rows, part, 3 * width), bf16), pltpu.VMEM((rows, part, width), bf16)],
    )

    result, x_got, y_got = together(result, x_got, y_got)
    block_out = to_blocks(result.reshape(rows, part, width))
    ffn_to_x, ffn_x, ffn_to_y, ffn_y = next_sums(place, y_kept, y_got, x_kept, x_got)
    near_part, near_theirs, far_part, far_theirs, row_sent, row_kept = row_attention_back(
        info, tie, near, far, grad_own, swap(grad_other, "c"), w_row, near_normed, far_normed
    )
    (
        row_sent, far_theirs, near_theirs, attn_theirs, block_out, ffn_x_got, ffn_y_got
    ) = together(
        row_sent, far_theirs, near_theirs, attn_theirs, block_out,
        swap(ffn_to_x, "x"), swap(ffn_to_y, "y"),
    )
    row_got = swap(row_sent, "x")
    far_sum = added(far_part, swap(far_theirs, "c"))
    far_got = swap(far_sum, "x")
    near_got = swap(near_theirs, "c")
    attn_sent, attn_kept = whole_call(
        attn_terms_kernel,
        place,
        [acts, acts_got, attn_mine, swap(attn_theirs, "c")],
        [((8, depth // 2, 5 * half), bf16)] * 2,
    )
    ffn_column = jnp.concatenate([added(ffn_x, ffn_x_got), added(ffn_y, ffn_y_got)], axis=2)
    ffn_own = lax.all_to_all(ffn_column, "z", 0, 0, tiled=True)
    attn_sent, attn_kept, ffn_own, row_got = together(attn_sent, attn_kept, ffn_own, row_got)
    attn_got = swap(attn_sent, "y")
    ffn_own = jnp.sum(ffn_own.astype(f32), axis=0).astype(bf16)
    ffn_own, row_got, block_out = together(ffn_own, row_got, block_out)
    row_own = z_summed(added(row_kept, row_got), z)
    attn_pair_terms = added(attn_kept, attn_got).reshape(4, 2, depth // 2, 5 * half)
    attn_column = pick(attn_pair_terms, x, 1)
    attn_x_got = swap(pick(attn_pair_terms, 1 - x, 1), "x")
    blocks = whole_call(
        tokens_back_kernel,
        info,
        [near_part, near_got, far_got, stream_zero, grad_stream, norm_gain, col_norms],
        [((rows, part + 16, width), bf16)],
    )[0]
    blocks, row_own = together(blocks, row_own)
    blocks = to_blocks(blocks)
    grad_tokens = to_rows(blocks[:, :part], c).astype(f32)
    norm_grad = jnp.sum(blocks[:, part : part + 8, :TILE].astype(f32), axis=0)
    block_out = to_rows(block_out, c)
    attn_column = added(attn_column, attn_x_got)
    norm_parts = [norm_grad] + [
        lax.ppermute(norm_grad, ("y", "c"), [(k, k ^ i) for k in range(4)]) for i in (1, 2, 3)
    ]
    norm_grad = (norm_parts[0] + norm_parts[1]) + (norm_parts[2] + norm_parts[3])
    norm_grad = norm_grad[:6, :depth]
    attn_own = z_summed(attn_column, z)
    row_grad = added(row_own, swap(row_own, "y"))
    attn_grad_b = joined(attn_own, swap(attn_own, "y"), y, 0)
    ffn_grads = [ffn_own, swap(ffn_own, "y")]

    row_other = swap(row_grad, "c")
    attn_other = swap(attn_grad_b, "c")
    ffn_others = [swap(piece, "c") for piece in ffn_grads]

    attn_own, block_out = together(attn_own, block_out)
    squares = sum(jnp.sum(jnp.square(g.astype(f32))) for g in (attn_own, ffn_own))
    squares = squares + 0.5 * jnp.sum(jnp.square(row_grad.astype(f32)))
    squares = squares + 0.25 * jnp.sum(norm_grad * norm_grad)
    squares = jnp.broadcast_to(squares, (32, 8, TILE))
    squares = lax.all_to_all(squares, ("z", "x", "y", "c"), 0, 0, tiled=True)
    grad_norm = jnp.sqrt(jnp.sum(squares[:, 0, 0]))
    factor = clip_bound / jnp.maximum(grad_norm, clip_bound)
    attn_first_new, attn_second_new, attn_weight_new, attn_copy = attn_adam(
        place,
        factor,
        jnp.concatenate([row_grad, attn_grad_b], axis=1),
        jnp.concatenate([row_other, attn_other], axis=1),
        attn_weight,
        attn_first,
        attn_second,
    )
    in_first_new, in_second_new, in_weight_new, in_copy, *turned = ffn_adam(
        place,
        factor,
        [*ffn_grads, *ffn_others],
        (in_weight, in_first, in_second),
        (out_weight, out_first, out_second),
    )
    out_first_new, out_second_new, out_weight_new, out_copy = [value.T for value in turned]
    norm_first_new, norm_second_new, norm_new = adam_update(
        norm_param, norm_first, norm_second, norm_grad * factor, norm_rate
    )
    return (
        block_out,
        grad_tokens,
        grad_norm,
        attn_first_new,
        attn_second_new,
        attn_weight_new,
        attn_copy,
        in_first_new,
        in_second_new,
        in_weight_new,
        in_copy,
        out_first_new,
        out_second_new,
        out_weight_new,
        out_copy,
        norm_first_new,
        norm_second_new,
        norm_new,
    )


def paired_layout(mesh):
    return dict(mesh.shape) == {"seq": 8, "grp": 4}


def mapped(run, mesh, seq, grp):
    placed = (
        P(grp, seq, None, None),
        P(grp, seq, None, None),
        P(grp),
        P(grp),
        P(None, seq, None),
        P(seq, None),
        P(None, seq),
        P(None, seq),
        P(None, seq, None),
        P(None, seq, None),
        P(seq, None),
        P(seq, None),
        P(None, seq),
        P(None, seq),
        P(None, seq),
        P(None, seq),
    )
    return jax.shard_map(
        run,
        mesh=mesh,
        in_specs=placed,
        out_specs=(
            P(grp, seq, None, None),
            P(grp, seq, None, None),
            P(),
            P(None, seq, None),
            P(None, seq, None),
            P(None, seq, None),
            P(None, seq, None),
            P(seq, None),
            P(seq, None),
            P(seq, None),
            P(seq, None),
            P(None, seq),
            P(None, seq),
            P(None, seq),
            P(None, seq),
            P(None, seq),
            P(None, seq),
            P(None, seq),
        ),
        check_vma=False,
    )


def solution(mesh):
    if not paired_layout(mesh):
        return mapped(general_body, mesh, "seq", "grp")
    fine = Mesh(mesh.devices.reshape(4, 2, 2, 2), ("z", "x", "y", "c"))
    return mapped(paired_body, fine, ("z", "x"), ("y", "c"))
```

```python
from functools import partial
import math

import jax
import jax.numpy as jnp
from jax import lax
from jax.experimental import pallas as pl
from jax.experimental.pallas import tpu as pltpu
from jax.sharding import Mesh
from jax.sharding import PartitionSpec as P

H = 12
DH = 64
STEP = 5


eps_norm = 1e-05
masked_score = -1000000000.0
clip_bound = 1.0
beta_one = 0.5
beta_two = 0.5
matrix_rate = 0.06
norm_rate = 0.3
decay_rate = 0.01
adam_eps = 1e-08


def in_blocks(x, dim, length):
    lengths = x.shape
    pieces = x.reshape(*lengths[:dim], length, lengths[dim] // length, *lengths[dim + 1 :])
    return jnp.moveaxis(pieces, dim, 0)


def sent_and_summed(x, axis, dim):
    length = lax.axis_size(axis)
    pieces = lax.all_to_all(in_blocks(x, dim, length), axis, 0, 0, tiled=True)
    return jnp.sum(pieces.astype(jnp.float32), axis=0)


def layer_norm(value, gain, shift):
    mean = jnp.mean(value, axis=-1, keepdims=True)
    centred = value - mean
    spread = jnp.mean(centred * centred, axis=-1, keepdims=True)
    return centred * lax.rsqrt(spread + eps_norm) * gain + shift


def softmax_rows(scores, keep):
    scores = jnp.where(keep, scores, masked_score)
    top = jnp.max(scores, axis=-1, keepdims=True)
    expo = jnp.exp(scores - top)
    return expo / jnp.sum(expo, axis=-1, keepdims=True)


def softmax_back(probs, grads):
    return probs * (grads - jnp.sum(probs * grads, axis=-1, keepdims=True))


def adam_update(weight, first, second, grad, rate):
    first_new = beta_one * first + (1.0 - beta_one) * grad
    second_new = beta_two * second + (1.0 - beta_two) * grad * grad
    first_hat = first_new / (1.0 - beta_one**STEP)
    second_hat = second_new / (1.0 - beta_two**STEP)
    weight_new = weight - rate * (
        first_hat / (jnp.sqrt(second_hat) + adam_eps) + decay_rate * weight
    )
    return (first_new, second_new, weight_new)


def attn_pair(normed, grad_proj, mixed, grad_branch):
    width = normed.shape[-1]
    qkv_terms = jnp.einsum("prcd,kprce->dke", normed, grad_proj, preferred_element_type=jnp.float32)
    output_terms = jnp.einsum(
        "prcd,prce->de", mixed, grad_branch, preferred_element_type=jnp.float32
    )
    return jnp.concatenate([qkv_terms, output_terms[:, None, :]], axis=1).reshape(width, 4 * width)


def general_body(
    tokens,
    cotangent,
    col_count,
    row_count,
    attn_weight,
    in_weight,
    out_weight,
    norm_param,
    attn_first,
    attn_second,
    in_first,
    in_second,
    out_first,
    out_second,
    norm_first,
    norm_second,
):
    f32 = jnp.float32
    bf16 = jnp.bfloat16
    prot, rows_dev, cols, width = tokens.shape
    hidden = in_weight.shape[1]
    head_scale = 1.0 / math.sqrt(DH)
    attn_full, in_full, out_full, norm_full = (
        lax.all_gather(attn_weight.astype(bf16), "seq", axis=1, tiled=True),
        lax.all_gather(in_weight.astype(bf16), "seq", axis=0, tiled=True),
        lax.all_gather(out_weight.astype(bf16), "seq", axis=1, tiled=True),
        lax.all_gather(norm_param.astype(bf16), "seq", axis=1, tiled=True),
    )
    norm_gain = norm_full.astype(f32)
    row_ids = lax.axis_index("seq") * rows_dev + jnp.arange(rows_dev, dtype=jnp.int32)
    row_live = (row_ids[None, :] < row_count[:, None]).astype(f32)
    col_live = jnp.arange(cols, dtype=jnp.int32)[None, :] < col_count[:, None]
    tie_scale = lax.rsqrt(row_count.astype(f32)) * head_scale
    live = row_live[:, :, None] * col_live.astype(f32)[:, None, :]
    grad_out = (cotangent.astype(f32) * live[..., None]).astype(bf16)
    resid_one = tokens.astype(f32)
    normed_one = layer_norm(resid_one, norm_gain[0], norm_gain[1]).astype(bf16)
    proj_one = jnp.einsum(
        "prcd,kde->kprce", normed_one, attn_full[0:3], preferred_element_type=f32
    ).astype(bf16)
    proj_one = proj_one.reshape(3, prot, rows_dev, cols, H, DH)
    query_one, key_one, value_one = (proj_one[0], proj_one[1], proj_one[2])
    masked_query = query_one * row_live[:, :, None, None, None].astype(bf16)
    partial_scores = (
        jnp.einsum("prihe,prjhe->phij", masked_query, key_one, preferred_element_type=f32)
        * tie_scale[:, None, None, None]
    )
    keep_cols = col_live[:, None, None, :]
    score_part = lax.psum_scatter(partial_scores, "seq", scatter_dimension=2, tiled=True)
    probs_one = softmax_rows(score_part, keep_cols)
    probs_low = lax.all_gather(probs_one.astype(bf16), "seq", axis=2, tiled=True)
    mixed_one = jnp.einsum(
        "phij,prjhe->prihe", probs_low, value_one, preferred_element_type=f32
    ).astype(bf16)
    mixed_one = mixed_one.reshape(prot, rows_dev, cols, width)
    branch_one = jnp.einsum("prcd,de->prce", mixed_one, attn_full[3], preferred_element_type=f32)
    stream_one = (resid_one + branch_one).astype(bf16)
    stream_cols, up_grad = (
        lax.all_to_all(stream_one, "seq", split_axis=2, concat_axis=1, tiled=True),
        lax.all_to_all(grad_out, "seq", split_axis=2, concat_axis=1, tiled=True),
    )
    rows = stream_cols.shape[1]
    cols_dev = stream_cols.shape[2]
    row_live_all = jnp.arange(rows, dtype=jnp.int32)[None, :] < row_count[:, None]
    resid_two = stream_cols.astype(f32)
    normed_two = layer_norm(resid_two, norm_gain[2], norm_gain[3]).astype(bf16)
    proj_two = jnp.einsum(
        "prcd,kde->kprce", normed_two, attn_full[4:7], preferred_element_type=f32
    ).astype(bf16)
    proj_two = proj_two.reshape(3, prot, rows, cols_dev, H, DH)
    query_two, key_two, value_two = (proj_two[0], proj_two[1], proj_two[2])
    scores_two = (
        jnp.einsum("prche,psche->pchrs", query_two, key_two, preferred_element_type=f32)
        * head_scale
    )
    probs_two = softmax_rows(scores_two, row_live_all[:, None, None, None, :])
    probs_two_low = probs_two.astype(bf16)
    mixed_two = jnp.einsum(
        "pchrs,psche->prche", probs_two_low, value_two, preferred_element_type=f32
    ).astype(bf16)
    mixed_two = mixed_two.reshape(prot, rows, cols_dev, width)
    resid_three = resid_two + jnp.einsum(
        "prcd,de->prce", mixed_two, attn_full[7], preferred_element_type=f32
    )
    normed_three = layer_norm(resid_three, norm_gain[4], norm_gain[5]).astype(bf16)
    inner = jnp.einsum("prcd,df->prcf", normed_three, in_full, preferred_element_type=f32)
    activ = jax.nn.gelu(inner, approximate=True).astype(bf16)
    result = (
        resid_three + jnp.einsum("prcf,fd->prcd", activ, out_full, preferred_element_type=f32)
    ).astype(bf16)
    block_out = lax.all_to_all(result, "seq", split_axis=1, concat_axis=2, tiled=True)
    grad_act = jnp.einsum("prcd,fd->prcf", up_grad, out_full, preferred_element_type=f32)
    _, gelu_back = jax.vjp(partial(jax.nn.gelu, approximate=True), inner)
    grad_inner = gelu_back(grad_act)[0].astype(bf16)
    grad_normed_three = jnp.einsum("prcf,df->prcd", grad_inner, in_full, preferred_element_type=f32)
    _, norm_back_three = jax.vjp(layer_norm, resid_three, norm_gain[4], norm_gain[5])
    part_three, gain_grad_three, shift_grad_three = norm_back_three(grad_normed_three)
    grad_three = up_grad.astype(f32) + part_three
    grad_branch_two = grad_three.astype(bf16)
    grad_mixed_two = jnp.einsum(
        "prce,de->prcd", grad_branch_two, attn_full[7], preferred_element_type=f32
    ).astype(bf16)
    grad_mixed_two = grad_mixed_two.reshape(prot, rows, cols_dev, H, DH)
    grad_probs_two = jnp.einsum(
        "prche,psche->pchrs", grad_mixed_two, value_two, preferred_element_type=f32
    )
    grad_value_two = jnp.einsum(
        "pchrs,prche->psche", probs_two_low, grad_mixed_two, preferred_element_type=f32
    )
    grad_scores_two = softmax_back(probs_two, grad_probs_two).astype(bf16)
    grad_query_two = (
        jnp.einsum("pchrs,psche->prche", grad_scores_two, key_two, preferred_element_type=f32)
        * head_scale
    )
    grad_key_two = (
        jnp.einsum("pchrs,prche->psche", grad_scores_two, query_two, preferred_element_type=f32)
        * head_scale
    )
    grad_proj_two = jnp.stack([grad_query_two, grad_key_two, grad_value_two]).astype(bf16)
    grad_proj_two = grad_proj_two.reshape(3, prot, rows, cols_dev, width)
    grad_normed_two = jnp.einsum(
        "kprce,kde->prcd", grad_proj_two, attn_full[4:7], preferred_element_type=f32
    )
    _, norm_back_two = jax.vjp(layer_norm, resid_two, norm_gain[2], norm_gain[3])
    part_two, gain_grad_two, shift_grad_two = norm_back_two(grad_normed_two)
    grad_stream = (grad_three + part_two).astype(bf16)
    col_attn_terms = attn_pair(normed_two, grad_proj_two, mixed_two, grad_branch_two)
    in_terms = jnp.einsum("prcd,prcf->df", normed_three, grad_inner, preferred_element_type=f32)
    out_terms = jnp.einsum("prcf,prcd->df", activ, up_grad, preferred_element_type=f32)
    grad_rows = lax.all_to_all(grad_stream, "seq", split_axis=1, concat_axis=2, tiled=True)
    grad_mixed_one = jnp.einsum(
        "prce,de->prcd", grad_rows, attn_full[3], preferred_element_type=f32
    ).astype(bf16)
    grad_mixed_one = grad_mixed_one.reshape(prot, rows_dev, cols, H, DH)
    partial_grads = jnp.einsum(
        "prihe,prjhe->phij", grad_mixed_one, value_one, preferred_element_type=f32
    )
    grad_value_one = jnp.einsum(
        "phij,prihe->prjhe", probs_low, grad_mixed_one, preferred_element_type=f32
    )
    grad_part = sent_and_summed(partial_grads.astype(jnp.bfloat16), "seq", 2)
    grad_scores_one = lax.all_gather(
        softmax_back(probs_one, grad_part).astype(bf16), "seq", axis=2, tiled=True
    )
    tie_rows = row_live[:, :, None, None, None] * tie_scale[:, None, None, None, None]
    grad_query_one = (
        jnp.einsum("phij,prjhe->prihe", grad_scores_one, key_one, preferred_element_type=f32)
        * tie_rows
    )
    grad_key_one = (
        jnp.einsum("phij,prihe->prjhe", grad_scores_one, masked_query, preferred_element_type=f32)
        * tie_scale[:, None, None, None, None]
    )
    grad_proj_one = jnp.stack([grad_query_one, grad_key_one, grad_value_one]).astype(bf16)
    grad_proj_one = grad_proj_one.reshape(3, prot, rows_dev, cols, width)
    grad_normed_one = jnp.einsum(
        "kprce,kde->prcd", grad_proj_one, attn_full[0:3], preferred_element_type=f32
    )
    _, norm_back_one = jax.vjp(layer_norm, resid_one, norm_gain[0], norm_gain[1])
    part_one, gain_grad_one, shift_grad_one = norm_back_one(grad_normed_one)
    grad_tokens = grad_rows.astype(f32) + part_one
    norm_stack = jnp.stack(
        [
            gain_grad_one,
            shift_grad_one,
            gain_grad_two,
            shift_grad_two,
            gain_grad_three,
            shift_grad_three,
        ]
    )
    row_attn_terms = attn_pair(normed_one, grad_proj_one, mixed_one, grad_rows)
    owned = lax.psum_scatter(
        jnp.concatenate(
            [row_attn_terms, col_attn_terms, in_terms, out_terms, norm_stack.T], axis=1
        ),
        "seq",
        scatter_dimension=0,
        tiled=True,
    )
    width_dev = owned.shape[0]
    row_part = owned[:, : 4 * width].reshape(width_dev, 4, width)
    col_part = owned[:, 4 * width : 8 * width].reshape(width_dev, 4, width)
    in_part = owned[:, 8 * width : 8 * width + hidden]
    out_part = owned[:, 8 * width + hidden : 8 * width + 2 * hidden].T
    norm_part = owned[:, 8 * width + 2 * hidden :].T
    attn_part = jnp.concatenate([row_part, col_part], axis=1).transpose(1, 0, 2)
    attn_grad, in_grad, out_grad, norm_grad = (
        lax.psum(attn_part.astype(jnp.bfloat16), "grp").astype(jnp.float32),
        lax.psum(in_part.astype(jnp.bfloat16), "grp").astype(jnp.float32),
        lax.psum(out_part.astype(jnp.bfloat16), "grp").astype(jnp.float32),
        lax.psum(norm_part.astype(jnp.bfloat16), "grp").astype(jnp.float32),
    )
    squares = (
        jnp.sum(attn_grad * attn_grad)
        + jnp.sum(in_grad * in_grad)
        + jnp.sum(out_grad * out_grad)
        + jnp.sum(norm_grad * norm_grad)
    )
    grad_norm = jnp.sqrt(lax.psum(squares, "seq"))
    factor = clip_bound / jnp.maximum(grad_norm, clip_bound)
    attn_first_new, attn_second_new, attn_weight_new = adam_update(
        attn_weight, attn_first, attn_second, attn_grad * factor, matrix_rate
    )
    in_first_new, in_second_new, in_weight_new = adam_update(
        in_weight, in_first, in_second, in_grad * factor, matrix_rate
    )
    out_first_new, out_second_new, out_weight_new = adam_update(
        out_weight, out_first, out_second, out_grad * factor, matrix_rate
    )
    norm_first_new, norm_second_new, norm_new = adam_update(
        norm_param, norm_first, norm_second, norm_grad * factor, norm_rate
    )
    return (
        block_out,
        grad_tokens,
        grad_norm,
        attn_first_new,
        attn_second_new,
        attn_weight_new,
        attn_weight_new.astype(bf16),
        in_first_new,
        in_second_new,
        in_weight_new,
        in_weight_new.astype(bf16),
        out_first_new,
        out_second_new,
        out_weight_new,
        out_weight_new.astype(bf16),
        norm_first_new,
        norm_second_new,
        norm_new,
    )


PAIR = [(0, 1), (1, 0)]
TILE = 128


def swap(value, axis):
    return lax.ppermute(value, axis, PAIR)


def pick(value, index, axis):
    return lax.dynamic_index_in_dim(value, index, axis, keepdims=False)


def joined(own, other, place, axis):
    return jnp.where(
        place == 0,
        jnp.concatenate([own, other], axis=axis),
        jnp.concatenate([other, own], axis=axis),
    )


def merge(own, other, place, axis):
    return jnp.where(
        place == 0,
        jnp.stack([own, other], axis=axis),
        jnp.stack([other, own], axis=axis),
    )


def merge_cores(value, c):
    prot, _, cols, width = value.shape
    part = cols // 4
    split = value.reshape(prot, 2, 2, part, width)
    got = swap(pick(split, 1 - c, 2), "c")
    both = merge(pick(split, c, 2), got, c, 0)
    return both.reshape(8, part, width)


def to_blocks(value):
    return lax.all_to_all(value, ("z", "x"), 0, 0, tiled=True)


def to_rows(got, c):
    _, part, width = got.shape
    got = got.reshape(2, 2, 2, part, width)
    other = swap(pick(got, 1 - c, 0), "c")
    both = merge(pick(got, c, 0), other, c, 2)
    return both.reshape(2, 1, 4 * part, width)


def together(*values):
    return lax.optimization_barrier(values)


def gather_z(own):
    return [own] + [lax.ppermute(own, "z", [(k, k ^ i) for k in range(4)]) for i in (1, 2, 3)]


def spread(over_z):
    over_x = swap(over_z, "x")
    quarter = [((0, 0, 0), over_z, 0), ((1, 0, 0), over_x, 0)]
    return quarter + [((j, 1, 0), swap(value, "y"), 0) for (j, _, _), value, _ in quarter]


def across(over_x, over_y):
    half = over_x.shape[0] // 2
    return swap(over_x[:half], "y"), swap(over_y[half:], "x")


def across_pieces(by_y, by_x):
    return [((1, 1, 0), by_y, 0), ((1, 1, 0), by_x, by_y.shape[0])]


def plan_of(pieces):
    return [(step, first) for step, _, first in pieces]


def placing(plan, outs_at, place_ref, stacks, outs, sem, steps=True):
    copies = []
    for stack, ((j, m, k), first) in zip(stacks, plan):
        x, y, c = (lax.bitwise_xor(place_ref[n], step) for n, step in ((1, j), (3, m), (2, k)))
        for i in range(stack.shape[0]):
            z = first + i
            shard = (lax.bitwise_xor(place_ref[0], z) if steps else z) * 2 + x
            for source, target in outs_at(stack.at[i], outs, shard, y, c):
                copies.append(pltpu.make_async_copy(source, target, sem.at[len(copies)]))
    return copies


def row_attn_at(ref, outs, shard, y, c):
    depth = outs[0].shape[0] // 16
    at = pl.multiple_of((shard * 2 + y) * depth, depth)
    return [(ref, outs[0].at[pl.ds(at, depth)])]


def ffn_at(ref, outs, shard, y, c):
    depth = ref.shape[0]
    at = pl.multiple_of((y * 8 + shard) * depth, depth)
    return [(ref, outs[0].at[pl.ds(at, depth)])]


def col_attn_at(ref, outs, shard, y, c):
    depth, half = ref.shape[1], ref.shape[2]
    at = pl.multiple_of((shard * 2 + y) * depth, depth)
    moves = []
    slots = [(o, n) for o, out in enumerate(outs) for n in range(out.shape[1] // (2 * half))]
    for k, (o, n) in enumerate(slots):
        lane = pl.multiple_of(c * half + n * 2 * half, TILE)
        moves.append((ref.at[k], outs[o].at[pl.ds(at, depth), pl.ds(lane, half)]))
    return moves


def contract(a, b, dims):
    return lax.dot_general(a, b, (dims, ((), ())), preferred_element_type=jnp.float32)


LAST = ((1,), (1,))
FIRST = ((0,), (0,))
PLAIN = ((1,), (0,))


def softmax_of(scores, keep):
    scores = jnp.where(keep, scores, masked_score)
    expo = jnp.exp(scores - jnp.max(scores, axis=-1, keepdims=True))
    return expo / jnp.sum(expo, axis=-1, keepdims=True)


def head_lanes(lanes):
    side = lax.broadcasted_iota(jnp.int32, (1, lanes), 1) % TILE < DH
    return (side, jnp.logical_not(side))


def lasting(microseconds):
    return pl.CostEstimate(
        flops=int(microseconds * 0.58e9), bytes_accessed=0, transcendentals=0
    )


def moved(pairs, sem, first=0):
    copies = [pltpu.make_async_copy(a, b, sem.at[first + n]) for n, (a, b) in enumerate(pairs)]
    for copy in copies:
        copy.start()
    return copies


def wait_all(copies):
    for copy in copies:
        copy.wait()


def only(keep, value):
    return jnp.where(keep, value, jnp.zeros_like(value))


def column_keep(info_ref, own_cols, near, part):
    key = lax.broadcasted_iota(jnp.int32, (1, 2 * near), 1)
    far = key >= near
    inner = key % near
    x = jnp.where(far, 1 - info_ref[1], info_ref[1])
    c = jnp.where(inner >= part, 1 - info_ref[2], info_ref[2])
    column = x * near + c * part + inner % part
    return column < info_ref[3]


def live_pair(value, row, info_ref):
    lane = lax.broadcasted_iota(jnp.int32, (1, value.shape[1]), 1) // TILE + row
    return only(lane < info_ref[4], value)


def head_pair(ref, row, lane):
    blocks, _, part, _ = ref.shape
    found = [ref[:, row + n, :, lane : lane + TILE].reshape(blocks * part, TILE) for n in (0, 1)]
    return jnp.concatenate(found, axis=1)


def row_fwd_kernel(token_plan, weight_plan, place_ref, info_ref, tie_ref, *refs):
    bf16 = jnp.bfloat16
    f32 = jnp.float32
    tokens, refs = refs[: len(token_plan)], refs[len(token_plan) :]
    stacks, refs = refs[: len(weight_plan)], refs[len(weight_plan) :]
    own_ref, near_tokens_ref, far_tokens_ref, w_ref, gain_ref, near_ref, far_ref, o_ref = refs[:8]
    all_ref, norm_ref, token_sem, weight_sem = refs[8:]
    blocks, rows, part, lanes = near_ref.shape
    half = lanes // 3
    count = rows * part
    near = blocks * part
    copies = []
    for stack, (j, k) in zip(tokens, token_plan):
        x = lax.bitwise_xor(place_ref[1], j)
        for i in range(4):
            row = lax.bitwise_xor(place_ref[0], i) * 2 + x
            moves = [(stack.at[i, pl.ds(0, 2 * part)], all_ref.at[k, row])]
            if k == 0:
                moves.append((stack.at[i, pl.ds(2 * part, 16)], norm_ref.at[j * 4 + i]))
            for source, target in moves:
                copies.append(pltpu.make_async_copy(source, target, token_sem.at[len(copies)]))
    weights = placing(weight_plan, row_attn_at, place_ref, stacks, [w_ref], weight_sem)
    for copy in copies + weights:
        copy.start()
    for copy in copies:
        copy.wait()
    gains = jnp.sum(norm_ref[...].astype(f32), axis=0)
    gain_ref[...] = gains
    x = info_ref[1]
    for ref, side in ((near_tokens_ref, x), (far_tokens_ref, 1 - x)):
        at = pl.ds(pl.multiple_of(side * part, part), part)
        for k in range(blocks):
            value = all_ref[k, :, at, :].reshape(count, -1)
            if k == 0:
                @pl.when(side == x)
                def _():
                    own_ref[...] = value
            found = normed(value.astype(f32), gains[0:1], gains[1:2])[0]
            ref[k * count : (k + 1) * count] = found.astype(bf16)
    for copy in weights:
        copy.wait()
    for n in range(3):
        at = slice(n * half, (n + 1) * half)
        found = contract(near_tokens_ref[...], w_ref[:, at], PLAIN).astype(bf16)
        near_ref[:, :, :, at] = found.reshape(blocks, rows, part, half)
        if n > 0:
            found = contract(far_tokens_ref[...], w_ref[:, at], PLAIN).astype(bf16)
            far_ref[:, :, :, (n - 1) * half : n * half] = found.reshape(blocks, rows, part, half)
    sides = head_lanes(2 * TILE)
    keep = column_keep(info_ref, near, near, part)
    tie = tie_ref[0]
    for lane in range(0, half, TILE):
        scores = [jnp.zeros((near, 2 * near), f32) for _ in sides]
        for row in range(0, rows, 2):
            query = live_pair(head_pair(near_ref, row, lane), row, info_ref)
            key = jnp.concatenate(
                [head_pair(near_ref, row, half + lane), head_pair(far_ref, row, lane)], axis=0
            )
            for n, side in enumerate(sides):
                scores[n] = scores[n] + contract(only(side, query), key, LAST)
        probs = [softmax_of(s * tie, keep).astype(bf16) for s in scores]
        for row in range(0, rows, 2):
            value = jnp.concatenate(
                [head_pair(near_ref, row, 2 * half + lane), head_pair(far_ref, row, half + lane)],
                axis=0,
            )
            mixed = jnp.where(
                sides[0], contract(probs[0], value, PLAIN), contract(probs[1], value, PLAIN)
            ).astype(bf16)
            for n in (0, 1):
                o_ref[:, row + n, :, lane : lane + TILE] = mixed[:, n * TILE : (n + 1) * TILE].reshape(
                    blocks, part, TILE
                )


def next_sums_kernel(
    place_ref, y_kept_ref, y_got_ref, x_kept_ref, x_got_ref, to_x_ref, with_x_ref, to_y_ref, with_y_ref
):
    _, depth, lanes = to_x_ref.shape
    first, first_y = place_ref[1] == 0, place_ref[3] == 0
    summed = added(y_kept_ref[...], y_got_ref[...]).reshape(2, depth, lanes)
    with_x_ref[0] = jnp.where(first, summed[0], summed[1])
    to_x_ref[0] = jnp.where(first, summed[1], summed[0])
    summed = added(x_kept_ref[0], x_got_ref[0])
    with_y_ref[0] = jnp.where(first_y, summed[0], summed[1])
    to_y_ref[0] = jnp.where(first_y, summed[1], summed[0])


def next_sums(place, y_kept, y_got, x_kept, x_got):
    zs, _, depth, lanes = x_kept.shape
    by_rows = pl.BlockSpec((2 * depth, lanes), lambda n: (n, 0))
    by_z = pl.BlockSpec((1, 2, depth, lanes), lambda n: (n, 0, 0, 0))
    return pl.pallas_call(
        next_sums_kernel,
        grid=(zs,),
        in_specs=[pl.BlockSpec(memory_space=pltpu.SMEM), by_rows, by_rows, by_z, by_z],
        out_specs=[pl.BlockSpec((1, depth, lanes), lambda n: (n, 0, 0))] * 4,
        out_shape=[jax.ShapeDtypeStruct((zs, depth, lanes), jnp.bfloat16)] * 4,
        cost_estimate=lasting(4),
        compiler_params=pltpu.CompilerParams(vmem_limit_bytes=56 * 2**20),
    )(place, y_kept, y_got, x_kept, x_got)


def row_bwd_kernel(
    info_ref, tie_ref, near_ref, far_ref, own_ref, got_ref, w_any, near_any, far_any,
    near_part_any, near_theirs_any, far_part_any, far_theirs_any, sent_ref, kept_ref,
    do_ref, d_near_ref, d_far_ref, w_ref, near_tokens_ref, far_tokens_ref,
    near_part_ref, near_theirs_ref, far_part_ref, far_theirs_ref, sem,
):
    arriving = moved(
        [(w_any, w_ref), (near_any, near_tokens_ref), (far_any, far_tokens_ref)], sem
    )
    bf16 = jnp.bfloat16
    blocks, rows, part, lanes = near_ref.shape
    half = lanes // 3
    near = blocks * part
    sides = head_lanes(2 * TILE)
    keep = column_keep(info_ref, near, near, part)
    tie = tie_ref[0]
    do_ref[0] = own_ref[...].reshape(rows, part, half)
    do_ref[1] = got_ref[...].reshape(rows, part, half)

    for lane in range(0, half, TILE):

        def pair(ref, row, first):
            at = slice(first + lane, first + lane + TILE)
            found = [ref[:, row + n, :, at].reshape(near, TILE) for n in (0, 1)]
            return jnp.concatenate(found, axis=1)

        def both(row, first):
            return jnp.concatenate(
                [pair(near_ref, row, first), pair(far_ref, row, first - half)], axis=0
            )

        scores = [jnp.zeros((near, 2 * near), jnp.float32) for _ in sides]
        grads = [jnp.zeros((near, 2 * near), jnp.float32) for _ in sides]
        for row in range(0, rows, 2):
            query = live_pair(pair(near_ref, row, 0), row, info_ref)
            key, value = both(row, half), both(row, 2 * half)
            out = pair(do_ref, row, 0)
            for n, side in enumerate(sides):
                scores[n] = scores[n] + contract(only(side, query), key, LAST)
                grads[n] = grads[n] + contract(only(side, out), value, LAST)
        probs = [softmax_of(s * tie, keep) for s in scores]
        lows = [p.astype(bf16) for p in probs]
        deltas = [softmax_back(p, g).astype(bf16) for p, g in zip(probs, grads)]
        low_turned = [p.T for p in lows]
        delta_turned = [d.T for d in deltas]
        for row in range(0, rows, 2):
            query = live_pair(pair(near_ref, row, 0), row, info_ref)
            key, out = both(row, half), pair(do_ref, row, 0)
            dq = [contract(d, key, PLAIN) for d in deltas]
            dk = [contract(d, query, PLAIN) for d in delta_turned]
            dv = [contract(p, out, PLAIN) for p in low_turned]
            dq = live_pair(jnp.where(sides[0], dq[0], dq[1]) * tie, row, info_ref).astype(bf16)
            dk = (jnp.where(sides[0], dk[0], dk[1]) * tie).astype(bf16)
            dv = jnp.where(sides[0], dv[0], dv[1]).astype(bf16)

            def put(ref, first, value):
                for n in (0, 1):
                    piece = value[:, n * TILE : (n + 1) * TILE].reshape(blocks, part, TILE)
                    ref[:, row + n, :, first + lane : first + lane + TILE] = piece

            put(d_near_ref, 0, dq)
            put(d_near_ref, half, dk[:near])
            put(d_near_ref, 2 * half, dv[:near])
            put(d_far_ref, 0, dk[near:])
            put(d_far_ref, half, dv[near:])

    count = rows * part
    wait_all(arriving)
    d_far = d_far_ref[...].reshape(blocks * count, 2 * half)
    far_weights = w_ref[:, half:]
    far_part_ref[...] = contract(d_far[:count], far_weights, LAST)
    far_theirs_ref[...] = contract(d_far[count:], far_weights, LAST).astype(bf16)
    d_near = d_near_ref[...].reshape(blocks * count, lanes)
    near_part_ref[...] = contract(d_near[:count], w_ref[...], LAST)
    near_theirs_ref[...] = contract(d_near[count:], w_ref[...], LAST).astype(bf16)
    leaving = moved(
        [
            (far_theirs_ref, far_theirs_any),
            (near_theirs_ref, near_theirs_any),
            (far_part_ref, far_part_any),
            (near_part_ref, near_part_any),
        ],
        sem,
        3,
    )
    near_turned = near_tokens_ref[...].T
    far_turned = far_tokens_ref[...].T
    zs, depth = kept_ref.shape[0], kept_ref.shape[1]
    first = info_ref[1] == 0
    for n in range(3):
        at = slice(n * half, (n + 1) * half)
        terms = contract(near_turned, d_near[:, at], PLAIN)
        if n > 0:
            terms = terms + contract(far_turned, d_far[:, (n - 1) * half : n * half], PLAIN)
        terms = terms.astype(bf16).reshape(zs, 2, depth, half)
        kept_ref[:, :, at] = jnp.where(first, terms[:, 0], terms[:, 1])
        sent_ref[:, :, at] = jnp.where(first, terms[:, 1], terms[:, 0])
    wait_all(leaving)


def row_attention(place, info, tie, tokens, weights, rows, half):
    f32, bf16 = jnp.float32, jnp.bfloat16
    zs, deep, width = tokens[0][1].shape
    part = (deep - 16) // 2
    count = rows * part
    small = pl.BlockSpec(memory_space=pltpu.SMEM)
    anywhere = pl.BlockSpec(memory_space=pl.ANY)
    inside = pl.BlockSpec(memory_space=pltpu.VMEM)
    shapes = [
        ((count, width), bf16),
        ((2 * count, width), bf16),
        ((2 * count, width), bf16),
        ((width, 3 * half), bf16),
        ((16, width), f32),
        ((2, rows, part, 3 * half), bf16),
        ((2, rows, part, 2 * half), bf16),
        ((2, rows, part, half), bf16),
    ]
    return pl.pallas_call(
        partial(row_fwd_kernel, [step for step, _ in tokens], plan_of(weights)),
        in_specs=[small] * 3 + [anywhere] * (len(tokens) + len(weights)),
        out_specs=[inside] * len(shapes),
        out_shape=[jax.ShapeDtypeStruct(shape, kind) for shape, kind in shapes],
        scratch_shapes=[
            pltpu.VMEM((2, rows, 2 * part, width), bf16),
            pltpu.VMEM((8, 16, width), bf16),
            pltpu.SemaphoreType.DMA((24,)),
            pltpu.SemaphoreType.DMA((16,)),
        ],
        compiler_params=pltpu.CompilerParams(vmem_limit_bytes=56 * 2**20),
        cost_estimate=lasting(13),
    )(place, info, tie, *[v for _, v in tokens], *[v for _, v, _ in weights])


def row_attention_back(info, tie, near, far, own, got, weights, near_tokens, far_tokens):
    blocks, rows, part, lanes = near.shape
    count, width = rows * part, weights.shape[0]
    half = lanes // 3
    f32, bf16 = jnp.float32, jnp.bfloat16
    small = pl.BlockSpec(memory_space=pltpu.SMEM)
    anywhere = pl.BlockSpec(memory_space=pl.ANY)
    inside = pl.BlockSpec(memory_space=pltpu.VMEM)
    shapes = [((count, width), kind) for kind in (f32, bf16) * 2]
    shapes = shapes + [((4, width // 8, lanes), bf16)] * 2
    return pl.pallas_call(
        row_bwd_kernel,
        in_specs=[small, small] + [inside] * 4 + [anywhere] * 3,
        out_specs=[anywhere] * 4 + [inside] * 2,
        out_shape=[jax.ShapeDtypeStruct(shape, kind) for shape, kind in shapes],
        scratch_shapes=[
            pltpu.VMEM((blocks, rows, part, half), bf16),
            pltpu.VMEM((blocks, rows, part, lanes), bf16),
            pltpu.VMEM((blocks, rows, part, 2 * half), bf16),
            pltpu.VMEM(weights.shape, bf16),
            pltpu.VMEM(near_tokens.shape, bf16),
            pltpu.VMEM(far_tokens.shape, bf16),
            *[pltpu.VMEM(shape, kind) for shape, kind in shapes[:4]],
            pltpu.SemaphoreType.DMA((7,)),
        ],
        cost_estimate=lasting(16),
        compiler_params=pltpu.CompilerParams(vmem_limit_bytes=56 * 2**20),
    )(info, tie, near, far, own, got, weights, near_tokens, far_tokens)


def normed(value, gain, shift):
    centred = value - jnp.mean(value, axis=-1, keepdims=True)
    scale = lax.rsqrt(jnp.mean(centred * centred, axis=-1, keepdims=True) + eps_norm)
    unit = centred * scale
    return unit * gain + shift, unit, scale


def normed_back(grad, unit, scale, gain):
    inner = grad * gain
    mean = jnp.mean(inner, axis=-1, keepdims=True)
    along = jnp.mean(inner * unit, axis=-1, keepdims=True)
    return scale * (inner - mean - unit * along)


def column_masks(info_ref, rows, part):
    tokens = rows * part
    key = lax.broadcasted_iota(jnp.int32, (tokens, tokens), 0)
    query = lax.broadcasted_iota(jnp.int32, (tokens, tokens), 1)
    same = key % part == query % part
    return jnp.logical_and(same, key // part < info_ref[4])


def stacked(value, sides):
    return jnp.concatenate([only(side, value) for side in sides], axis=0)


def column_probs(query, key, keep, sides):
    scores = contract(stacked(key, sides), query, LAST) * (1.0 / math.sqrt(DH))
    tokens = query.shape[0]
    probs = []
    for n in (0, 1):
        part = jnp.where(keep, scores[n * tokens : (n + 1) * tokens], masked_score)
        expo = jnp.exp(part - jnp.max(part, axis=0, keepdims=True))
        probs.append(expo / jnp.sum(expo, axis=0, keepdims=True))
    return probs


def col_fwd_kernel(plan, info_ref, place_ref, *refs):
    stacks, refs = refs[: len(plan)], refs[len(plan) :]
    x_ref, own_ref, other_ref, gain_ref, acts_ref, one_ref, qkv_ref = refs[:7]
    resid_ref, normed_three_ref, mixed_ref, three_ref, col_ref, seven_ref, sem = refs[7:]
    copies = placing(plan, col_attn_at, place_ref, stacks, [three_ref, col_ref, seven_ref], sem)
    for copy in copies:
        copy.start()
    bf16 = jnp.bfloat16
    rows, cols, lanes = qkv_ref.shape
    width = lanes // 3
    part = 16
    own, other = own_ref[...], other_ref[...]
    flip = info_ref[2] == 0
    mixed_one = jnp.concatenate(
        [jnp.where(flip, own, other), jnp.where(flip, other, own)], axis=1
    )
    acts_ref[:, :width] = mixed_one
    for copy in copies:
        copy.wait()
    stream = (x_ref[...].astype(jnp.float32) + contract(mixed_one, three_ref[...], PLAIN)).astype(bf16)
    one_ref[...] = stream
    normed_two = normed(stream.astype(jnp.float32), gain_ref[2:3], gain_ref[3:4])[0].astype(bf16)
    acts_ref[:, width : 2 * width] = normed_two
    for n in range(3):
        at = slice(n * width, (n + 1) * width)
        found = contract(normed_two, col_ref[:, at], PLAIN).astype(bf16)
        qkv_ref[:, :, at] = found.reshape(rows, cols, width)
    keep = column_masks(info_ref, rows, part)
    sides = head_lanes(TILE)

    def attend(b, carry):
        at = pl.ds(pl.multiple_of(b * part, part), part)
        def tile(n, t):
            lane = n * width + t * TILE
            return qkv_ref[:, at, lane : lane + TILE].reshape(rows * part, TILE)
        tiles = range(width // TILE)
        probs = [column_probs(tile(0, t), tile(1, t), keep, sides) for t in tiles]
        for t in tiles:
            low = jnp.concatenate(probs[t], axis=0).astype(bf16)
            mixed = contract(low, stacked(tile(2, t), sides), FIRST).astype(bf16)
            mixed_ref[:, at, t * TILE : (t + 1) * TILE] = mixed.reshape(rows, part, TILE)
        return carry

    lax.fori_loop(0, cols // part, attend, 0)
    mixed = mixed_ref[...].reshape(rows * cols, width)
    acts_ref[:, 2 * width :] = mixed
    resid = one_ref[...].astype(jnp.float32) + contract(mixed, seven_ref[...], PLAIN)
    resid_ref[...] = resid
    normed_three_ref[...] = normed(resid, gain_ref[4:5], gain_ref[5:6])[0].astype(bf16)


def col_bwd_kernel(plan, info_ref, place_ref, *refs):
    stacks, refs = refs[: len(plan)], refs[len(plan) :]
    up_ref, da_ref, out_ref, got_ref, resid_ref, one_ref, qkv_ref, gain_ref = refs[:8]
    result_ref, stream_ref, own_ref, other_ref, mine_ref, theirs_ref, norms_ref = refs[8:15]
    dqkv_ref, do_ref, three_ref, col_ref, seven_ref, sem = refs[15:]
    copies = placing(plan, col_attn_at, place_ref, stacks, [three_ref, col_ref, seven_ref], sem)
    for copy in copies:
        copy.start()
    bf16 = jnp.bfloat16
    f32 = jnp.float32
    rows, cols, lanes = qkv_ref.shape
    width = lanes // 3
    part = 16
    result_ref[...] = (resid_ref[...] + out_ref[...] + got_ref[0].astype(f32)).astype(bf16)
    da = da_ref[...] + got_ref[1].astype(f32)
    gain = gain_ref[4:5]
    _, unit, scale = normed(resid_ref[...], gain, 0.0)
    grad_three = up_ref[...].astype(f32) + normed_back(da, unit, scale, gain)
    norms_ref[2:3] = jnp.sum(da * unit, axis=0, keepdims=True)
    norms_ref[3:4] = jnp.sum(da, axis=0, keepdims=True)
    branch = grad_three.astype(bf16)
    half = width // 2
    flip = info_ref[2] == 0

    def put_halves(first, value):
        at = slice(first, first + half)
        mine_ref[:, at] = jnp.where(flip, value[:, :half], value[:, half:])
        theirs_ref[:, at] = jnp.where(flip, value[:, half:], value[:, :half])

    put_halves(4 * half, branch)
    for copy in copies:
        copy.wait()
    do_ref[...] = contract(branch, seven_ref[...], LAST).astype(bf16).reshape(rows, cols, width)
    keep = column_masks(info_ref, rows, part)
    sides = head_lanes(TILE)
    ratio = 1.0 / math.sqrt(DH)

    def attend(b, carry):
        at = pl.ds(pl.multiple_of(b * part, part), part)
        tokens = rows * part

        def tile(n, t):
            lane = n * width + t * TILE
            return qkv_ref[:, at, lane : lane + TILE].reshape(tokens, TILE)

        def out_tile(t):
            return do_ref[:, at, t * TILE : (t + 1) * TILE].reshape(tokens, TILE)

        def put(n, t, value):
            lane = n * width + t * TILE
            dqkv_ref[:, at, lane : lane + TILE] = value.astype(bf16).reshape(rows, part, TILE)

        for t in range(width // TILE):
            query, key, out = tile(0, t), tile(1, t), out_tile(t)
            keys = stacked(key, sides)
            probs = column_probs(query, key, keep, sides)
            grads = contract(stacked(tile(2, t), sides), out, LAST)
            deltas = []
            for n, p in enumerate(probs):
                g = grads[n * tokens : (n + 1) * tokens]
                deltas.append((p * (g - jnp.sum(p * g, axis=0, keepdims=True))).astype(bf16))
            put(0, t, contract(jnp.concatenate(deltas, axis=0), keys, FIRST) * ratio)
            wide = jnp.concatenate(deltas, axis=1)
            put(1, t, contract(wide, stacked(query, sides), PLAIN) * ratio)
            wide = jnp.concatenate([p.astype(bf16) for p in probs], axis=1)
            put(2, t, contract(wide, stacked(out, sides), PLAIN))
        return carry

    lax.fori_loop(0, cols // part, attend, 0)
    dqkv = dqkv_ref[...].reshape(rows * cols, lanes)
    for n in range(3):
        put_halves((n + 1) * half, dqkv[:, n * width : (n + 1) * width])
    grad_normed = contract(dqkv, col_ref[...], LAST)
    gain = gain_ref[2:3]
    _, unit, scale = normed(one_ref[...].astype(f32), gain, 0.0)
    norms_ref[0:1] = jnp.sum(grad_normed * unit, axis=0, keepdims=True)
    norms_ref[1:2] = jnp.sum(grad_normed, axis=0, keepdims=True)
    stream = (grad_three + normed_back(grad_normed, unit, scale, gain)).astype(bf16)
    stream_ref[...] = stream
    put_halves(0, stream)
    mixed = contract(stream, three_ref[...], LAST).astype(bf16)
    own_ref[...] = jnp.where(flip, mixed[:, :half], mixed[:, half:])
    other_ref[...] = jnp.where(flip, mixed[:, half:], mixed[:, :half])


def tokens_back_kernel(
    info_ref, near_ref, near_got_ref, far_got_ref, x_ref, stream_ref, gain_ref, norms_ref,
    blocks_ref,
):
    f32 = jnp.float32
    grad = near_ref[...] + near_got_ref[...].astype(f32) + far_got_ref[...].astype(f32)
    gain = gain_ref[0:1]
    _, unit, scale = normed(x_ref[...].astype(f32), gain, 0.0)
    found = stream_ref[...].astype(f32) + normed_back(grad, unit, scale, gain)
    rows, deep, width = blocks_ref.shape
    part = deep - 16
    blocks_ref[:, :part] = found.astype(jnp.bfloat16).reshape(rows, part, width)
    sums = [
        jnp.sum(grad * unit, axis=0, keepdims=True),
        jnp.sum(grad, axis=0, keepdims=True),
        norms_ref[...],
        jnp.zeros((2, width), f32),
    ]
    sums = jnp.concatenate(sums, axis=0)
    depth = width // 8
    lane = lax.broadcasted_iota(jnp.int32, (width, TILE), 0)
    place = lax.broadcasted_iota(jnp.int32, (width, TILE), 1)
    for shard in range(8):
        chosen = jnp.logical_and(lane == shard * depth + place, place < depth)
        found = lax.dot_general(
            sums,
            chosen.astype(f32),
            (PLAIN, ((), ())),
            precision=lax.Precision.HIGHEST,
            preferred_element_type=f32,
        )
        found = jnp.concatenate([found, jnp.zeros((8, TILE), f32)], axis=0)
        blocks_ref[shard, part:, :TILE] = found.astype(jnp.bfloat16)
        blocks_ref[shard, part:, TILE:] = jnp.zeros((16, width - TILE), jnp.bfloat16)


def attn_terms_kernel(place_ref, acts_ref, got_ref, mine_ref, theirs_ref, sent_ref, kept_ref):
    width = acts_ref.shape[1] // 3
    half = width // 2
    depth = sent_ref.shape[1]
    turned = [
        jnp.concatenate([ref[:, n * width : (n + 1) * width].T for ref in (acts_ref, got_ref)], axis=1)
        for n in range(3)
    ]
    first = place_ref[3] == 0
    for n, m in enumerate((0, 1, 1, 1, 2)):
        at = slice(n * half, (n + 1) * half)
        grads = jnp.concatenate([mine_ref[:, at], theirs_ref[:, at]], axis=0)
        terms = contract(turned[m], grads, PLAIN).astype(jnp.bfloat16)
        terms = terms.reshape(sent_ref.shape[0], 2, depth, half)
        kept_ref[:, :, at] = jnp.where(first, terms[:, 0], terms[:, 1])
        sent_ref[:, :, at] = jnp.where(first, terms[:, 1], terms[:, 0])


def column_call(kernel, info, place, pieces, args, outs, scratch, time):
    width = args[-1].shape[1]
    bf16 = jnp.bfloat16
    small = pl.BlockSpec(memory_space=pltpu.SMEM)
    inside = pl.BlockSpec(memory_space=pltpu.VMEM)
    anywhere = pl.BlockSpec(memory_space=pl.ANY)
    return pl.pallas_call(
        partial(kernel, plan_of(pieces)),
        in_specs=[small] * 2 + [anywhere] * len(pieces) + [inside] * len(args),
        out_specs=[inside] * len(outs),
        out_shape=[jax.ShapeDtypeStruct(shape, kind) for shape, kind in outs],
        scratch_shapes=[
            *scratch,
            pltpu.VMEM((width, width), bf16),
            pltpu.VMEM((width, 3 * width), bf16),
            pltpu.VMEM((width, width), bf16),
            pltpu.SemaphoreType.DMA((160,)),
        ],
        cost_estimate=lasting(time),
        compiler_params=pltpu.CompilerParams(vmem_limit_bytes=56 * 2**20),
    )(info, place, *[value for _, value, _ in pieces], *args)


def last_sums_kernel(place_ref, own_ref, *refs):
    f32 = jnp.float32
    got, (before_ref, sum_ref, squares_ref) = refs[:3], refs[3:]
    total = own_ref[...].astype(f32)
    for ref in got:
        total = total + ref[...].astype(f32)
    low = total.astype(jnp.bfloat16)
    sum_ref[...] = low
    low = low.astype(f32)
    squares = jnp.sum(low * low, axis=1, keepdims=True)
    squares = jnp.sum(squares, axis=0, keepdims=True) + before_ref[0:1, 0:1]
    squares_ref[...] = jnp.broadcast_to(squares[None], squares_ref.shape)


def clip_factor(squares_ref):
    total = jnp.sum(squares_ref[:, 0:1, 0:1], axis=0)
    return clip_bound / jnp.maximum(jnp.sqrt(total), clip_bound)


def adam_kernel(
    place_ref, squares_ref, row_ref, row_other_ref, col_ref, col_other_ref, w_ref, first_ref, second_ref, *outs
):
    count, _, width = w_ref.shape
    half = width // 2
    low = place_ref[2] == 0
    early = pl.program_id(0) == 0
    factor = clip_factor(squares_ref)
    for n in range(count):
        at = slice((n + 1) * half, (n + 2) * half)
        own, other = col_ref[:, at], col_other_ref[:, at]
        if n < 3:
            at = slice(n * half, (n + 1) * half)
            sooner, sooner_other = row_ref[:, at], row_other_ref[:, at]
        else:
            sooner, sooner_other = col_ref[:, :half], col_other_ref[:, :half]
        own, other = jnp.where(early, sooner, own), jnp.where(early, sooner_other, other)
        grad = jnp.concatenate([jnp.where(low, own, other), jnp.where(low, other, own)], axis=1)
        grad = grad.astype(jnp.float32) * factor
        first, second, weight = adam_update(w_ref[n], first_ref[n], second_ref[n], grad, matrix_rate)
        for ref, value in zip(outs, (first, second, weight, weight.astype(jnp.bfloat16))):
            ref[n] = value


def attn_adam(place, squares, grads, weight, first, second):
    small = pl.BlockSpec(memory_space=pltpu.SMEM)
    inside = pl.BlockSpec(memory_space=pltpu.VMEM)
    block = pl.BlockSpec((4, *weight.shape[1:]), lambda m: (m, 0, 0))
    kinds = [jnp.float32] * 3 + [jnp.bfloat16]
    return pl.pallas_call(
        adam_kernel,
        grid=(weight.shape[0] // 4,),
        in_specs=[small] + [inside] * 5 + [block] * 3,
        out_specs=[block] * 4,
        out_shape=[jax.ShapeDtypeStruct(weight.shape, kind) for kind in kinds],
        compiler_params=pltpu.CompilerParams(vmem_limit_bytes=40 * 2**20),
    )(place, squares, *grads, weight, first, second)


def ffn_adam_kernel(place_ref, squares_ref, *refs):
    pieces, refs = refs[:4], refs[4:]
    low, even = place_ref[2] == 0, place_ref[3] == 0
    factor = clip_factor(squares_ref)
    depth = pieces[0].shape[0]
    part = depth // 2
    half = pl.program_id(0)

    def by_matrix(first, second):
        return jnp.where(even, first, second), jnp.where(even, second, first)

    def put(grad, ins, outs):
        values = adam_update(*[ref[...] for ref in ins], grad * factor, matrix_rate)
        for ref, value in zip(outs, (*values, values[2].astype(jnp.bfloat16))):
            ref[...] = value

    rows = pl.ds(pl.multiple_of(half * part, 16), part)
    owns = by_matrix(pieces[0][rows], pieces[1][rows])
    others = by_matrix(pieces[2][rows], pieces[3][rows])
    for n, (own, other) in enumerate(zip(owns, others)):
        grad = jnp.concatenate([jnp.where(low, own, other), jnp.where(low, other, own)], axis=1)
        put(grad.astype(jnp.float32), refs[3 * n : 3 * n + 3], refs[6 + 4 * n : 10 + 4 * n])


def ffn_adam(place, squares, pieces, ins, outs):
    small = pl.BlockSpec(memory_space=pltpu.SMEM)
    inside = pl.BlockSpec(memory_space=pltpu.VMEM)
    depth, hidden = ins[0].shape
    block = pl.BlockSpec((depth // 2, hidden), lambda n: (n, 0))
    kinds = [jnp.float32] * 3 + [jnp.bfloat16]
    return pl.pallas_call(
        ffn_adam_kernel,
        grid=(2,),
        in_specs=[small] + [inside] * 5 + [block] * 6,
        out_specs=[block] * 8,
        out_shape=[jax.ShapeDtypeStruct((depth, hidden), kind) for kind in kinds * 2],
        compiler_params=pltpu.CompilerParams(vmem_limit_bytes=58 * 2**20),
    )(place, squares, *pieces, *ins, *[value.T for value in outs])


def whole_call(kernel, info, args, outs, time):
    inside = pl.BlockSpec(memory_space=pltpu.VMEM)
    return pl.pallas_call(
        kernel,
        in_specs=[pl.BlockSpec(memory_space=pltpu.SMEM)] + [inside] * len(args),
        out_specs=[inside] * len(outs),
        out_shape=[jax.ShapeDtypeStruct(shape, kind) for shape, kind in outs],
        cost_estimate=lasting(time),
        compiler_params=pltpu.CompilerParams(vmem_limit_bytes=56 * 2**20),
    )(info, *args)


def gelu_pair(u):
    ratio = math.sqrt(2.0 / math.pi)
    square = u * u
    tanh = jnp.tanh(ratio * u * (1.0 + 0.044715 * square))
    rise = 0.5 * (1.0 + tanh)
    slope = (0.5 * ratio) * (1.0 - tanh * tanh) * (1.0 + (3.0 * 0.044715) * square)
    return u * rise, rise + u * slope


def ffn_kernel(plan, place_ref, a_ref, a_got_ref, up_ref, up_got_ref, *refs):
    bf16 = jnp.bfloat16
    stacks, refs = refs[: len(plan)], refs[len(plan) :]
    out_ref, da_ref, others_ref = refs[:3]
    y_sent_ref, y_kept_ref, x_sent_ref, x_kept_ref = refs[3:7]
    w_ref, turned_ref, out_sum, da_sum, sem = refs[7:]
    count, width = a_ref.shape
    chunk = w_ref.shape[1] // 2
    copies = placing(plan, ffn_at, place_ref, stacks, [w_ref], sem, steps=False)
    for copy in copies:
        copy.start()
    for n, ref in enumerate((a_ref, a_got_ref, up_ref, up_got_ref)):
        turned_ref[n // 2, :, (n % 2) * count : (n % 2 + 1) * count] = ref[...].T
    for copy in copies:
        copy.wait()
    for step in (0, 1):
        lane = slice(step * chunk, (step + 1) * chunk)
        w_in = w_ref[:width, lane]
        w_out = w_ref[width:, lane]
        activs, grads = [], []
        for n, (tokens, ups) in enumerate(((a_ref, up_ref), (a_got_ref, up_got_ref))):
            at = slice(n * count, (n + 1) * count)
            activ, slope = gelu_pair(contract(tokens[...], w_in, PLAIN))
            activ = activ.astype(bf16)
            grad = (contract(ups[...], w_out, PLAIN) * slope).astype(bf16)
            out, da = contract(activ, w_out, LAST), contract(grad, w_in, LAST)
            if step == 0:
                out_sum[at] = out
                da_sum[at] = da
            elif n == 0:
                out_ref[...] = out_sum[at] + out
                da_ref[...] = da_sum[at] + da
            else:
                others_ref[0] = (out_sum[at] + out).astype(bf16)
                others_ref[1] = (da_sum[at] + da).astype(bf16)
            activs.append(activ)
            grads.append(grad)
        in_terms = contract(turned_ref[0], jnp.concatenate(grads, axis=0), PLAIN).astype(bf16)
        out_terms = contract(turned_ref[1], jnp.concatenate(activs, axis=0), PLAIN).astype(bf16)
        if step == 0:
            first = place_ref[3] == 0
            y_kept_ref[...] = jnp.where(first, in_terms, out_terms)
            y_sent_ref[...] = jnp.where(first, out_terms, in_terms)
        else:
            first = place_ref[1] == 0
            zs, _, depth, _ = x_sent_ref.shape
            for n, terms in enumerate((in_terms, out_terms)):
                terms = terms.reshape(zs, 2, depth, chunk)
                x_kept_ref[:, n] = jnp.where(first, terms[:, 0], terms[:, 1])
                x_sent_ref[:, n] = jnp.where(first, terms[:, 1], terms[:, 0])


def feed_forward(place, normed_own, normed_got, up_own, up_got, pieces):
    count, width = normed_own.shape
    half = pieces[0][1].shape[-1]
    anywhere = pl.BlockSpec(memory_space=pl.ANY)
    inside = pl.BlockSpec(memory_space=pltpu.VMEM)
    f32, bf16 = jnp.float32, jnp.bfloat16
    shapes = [((count, width), f32)] * 2 + [((2, count, width), bf16)]
    shapes = shapes + [((width, half // 2), bf16)] * 2 + [((4, 2, width // 8, half // 2), bf16)] * 2
    return pl.pallas_call(
        partial(ffn_kernel, plan_of(pieces)),
        in_specs=[pl.BlockSpec(memory_space=pltpu.SMEM)] + [inside] * 4 + [anywhere] * len(pieces),
        out_specs=[inside] * 7,
        out_shape=[jax.ShapeDtypeStruct(shape, kind) for shape, kind in shapes],
        scratch_shapes=[
            pltpu.VMEM((2 * width, half), bf16),
            pltpu.VMEM((2, width, 2 * count), bf16),
            pltpu.VMEM((2 * count, width), f32),
            pltpu.VMEM((2 * count, width), f32),
            pltpu.SemaphoreType.DMA((16,)),
        ],
        cost_estimate=lasting(22),
        compiler_params=pltpu.CompilerParams(vmem_limit_bytes=56 * 2**20),
    )(place, normed_own, normed_got, up_own, up_got, *[value for _, value, _ in pieces])


def added(a, b):
    return (a.astype(jnp.float32) + b.astype(jnp.float32)).astype(jnp.bfloat16)


def gather_turned(column, z):
    return [
        lax.ppermute(pick(column, lax.bitwise_xor(z, i), 0), "z", [(k, k ^ i) for k in range(4)])
        for i in (1, 2, 3)
    ]


def z_summed(column, z):
    parts = [pick(column, z, 0)] + gather_turned(column, z)
    return sum(part.astype(jnp.float32) for part in parts).astype(jnp.bfloat16)


def paired_body(
    tokens,
    cotangent,
    col_count,
    row_count,
    attn_weight,
    in_weight,
    out_weight,
    norm_param,
    attn_first,
    attn_second,
    in_first,
    in_second,
    out_first,
    out_second,
    norm_first,
    norm_second,
):
    f32 = jnp.float32
    bf16 = jnp.bfloat16
    z, x, y, c = (lax.axis_index(name) for name in ("z", "x", "y", "c"))
    width = tokens.shape[-1]
    hidden = in_weight.shape[1]
    depth = in_weight.shape[0]
    half = width // 2
    hidden_half = hidden // 2

    counts = jnp.stack([col_count, row_count])
    other_counts = swap(counts, "c")
    mine = jnp.where(z // 2 == c, counts, other_counts)
    mine = pick(mine, z % 2, 1)
    cols_live, rows_live = mine[0], mine[1]
    place = jnp.stack([z, x, c, y]).astype(jnp.int32)
    info = jnp.concatenate([place[:3], mine, place[3:]])
    tie = (lax.rsqrt(rows_live.astype(f32)) * (1.0 / math.sqrt(DH))).reshape(1)

    attn_low = attn_weight.astype(bf16)
    halves = attn_low.reshape(8, depth, 2, half)
    row_half = jnp.moveaxis(pick(halves[:3], c, 2), 0, 1).reshape(2, depth // 2, 3 * half)
    row_quarter = pick(row_half, y, 0)
    col_quarter = pick(pick(halves[3:], c, 2).reshape(5, 2, depth // 2, half), y, 1)
    row_z = gather_z(row_quarter)
    ffn_low = [in_weight.astype(bf16), out_weight.astype(bf16).T]
    ffn_low = [
        jnp.where(c == 0, low[:, :hidden_half], low[:, hidden_half:]) for low in ffn_low
    ]
    ffn_quarter = jnp.where(y == 0, *ffn_low)

    lanes = jnp.arange(width, dtype=jnp.int32) // depth
    norm_low = jnp.tile(norm_param.astype(bf16), (1, width // depth))
    norm_rows = jnp.where(lanes[None] == z * 2 + x, norm_low, jnp.zeros_like(norm_low))
    norm_rows = jnp.pad(norm_rows, ((0, 10), (0, 0)))
    part = tokens.shape[2] // 4
    tokens_here = merge_cores(tokens, c).reshape(4, 2 * part, width)
    parts = [
        jnp.concatenate([pick(tokens_here, lax.bitwise_xor(z, i), 0), norm_rows]) for i in range(4)
    ]
    parts = [parts[0]] + [
        lax.ppermute(parts[i], "z", [(k, k ^ i) for k in range(4)]) for i in (1, 2, 3)
    ]
    row_pieces = spread(jnp.stack(row_z))
    row_x, row_y, *parts, col_quarter = together(
        row_pieces[1][1], row_pieces[2][1], *parts, col_quarter
    )
    tokens_z = jnp.stack(parts)
    up = merge_cores(cotangent, c).reshape(4, 2, part, width)
    up = joined(pick(up, x, 1)[:, None], swap(pick(up, 1 - x, 1), "x")[:, None], x, 1)
    col_z = gather_z(col_quarter)
    tokens_x, row_last, ffn_quarter, up, *col_z = together(
        swap(tokens_z, "x"), swap(row_x, "y"), ffn_quarter, up, *col_z
    )
    steps = [(0, 0, 0), (1, 0, 0), (0, 1, 0), (1, 1, 0)]
    row_stacks = [row_pieces[0][1], row_x, row_y, row_last]
    row_pieces = [(step, value, 0) for step, value in zip(steps, row_stacks)]
    col_z = jnp.stack(col_z)
    ffn_z = lax.all_to_all(
        jnp.broadcast_to(ffn_quarter, (4, *ffn_quarter.shape)), "z", 0, 0, tiled=True
    )
    col_x = swap(col_z, "x")
    col_last = swap(col_x, "y")
    col_x, col_y, ffn_z, up = together(col_x, swap(col_z, "y"), ffn_z, up)
    tokens_far, col_last = together(swap(tokens_x, "c"), col_last)
    ffn_x, ffn_y = swap(ffn_z, "x"), swap(ffn_z, "y")
    ups = [pick(up, z, 0)] + [
        lax.ppermute(pick(up, lax.bitwise_xor(z, i), 0), "z", [(k, k ^ i) for k in range(4)])
        for i in (1, 2, 3)
    ]

    rows = 8
    count = rows * part
    stream_zero, near_normed, far_normed, w_row, norm_gain, near, far, mixed_heads = row_attention(
        place,
        info,
        tie,
        [((0, 0), tokens_z), ((1, 0), tokens_x), ((0, 1), swap(tokens_z, "c")), ((1, 1), tokens_far)],
        row_pieces,
        rows,
        half,
    )
    mixed_heads = mixed_heads.reshape(2, count, half)
    col_stacks = [col_z, col_x, col_y]
    mixed_heads, ffn_x, ffn_y, *rest = together(
        mixed_heads, ffn_x, ffn_y, *ups, *[swap(value, "c") for value in col_stacks]
    )
    ups, col_others = rest[:4], rest[4:]
    ups = [jnp.where(z % 2 == 0, a, b) for a, b in zip(ups, (ups[1], ups[0], ups[3], ups[2]))]
    ups = [jnp.where(z < 2, a, b) for a, b in zip(ups, ups[2:] + ups[:2])]
    up = jnp.concatenate(ups)
    col_stacks, col_others = [*col_stacks, col_last], [*col_others, swap(col_last, "c")]
    col_pieces = [(step, v, 0) for step, v in zip(steps, col_stacks)]
    col_pieces = col_pieces + [((j, m, 1), v, 0) for (j, m, _), v in zip(steps, col_others)]
    ffn_pieces = [(step, v, 0) for step, v in zip(steps, [ffn_z, ffn_x, ffn_y])]

    whole_shape, wide_shape = ((count, width), bf16), ((rows, part, 3 * width), bf16)
    acts, stream_one, qkv_two, resid_three, normed_three = column_call(
        col_fwd_kernel,
        info,
        place,
        col_pieces,
        [stream_zero, mixed_heads[0], swap(mixed_heads[1], "c"), norm_gain],
        [((count, 3 * width), bf16), whole_shape, wide_shape, ((count, width), f32), whole_shape],
        [pltpu.VMEM((rows, part, width), bf16)],
        14,
    )
    normed_three, *ffn_across = together(normed_three, *across(ffn_x, ffn_y))
    ffn_pieces = ffn_pieces + across_pieces(*ffn_across)

    column = x * (2 * part) + c * part + jnp.arange(part, dtype=jnp.int32)
    live = jnp.logical_and(
        (jnp.arange(rows, dtype=jnp.int32) < rows_live)[:, None], (column < cols_live)[None, :]
    )
    up = jnp.where(live[..., None], up, jnp.zeros_like(up)).reshape(count, width)
    out_own, da_own, other_parts, *ffn_terms = feed_forward(
        place, normed_three, swap(normed_three, "c"), up, swap(up, "c"), ffn_pieces
    )
    other_parts = swap(other_parts, "c")
    y_sent, y_kept, x_sent, x_kept = ffn_terms
    y_got, x_got = swap(y_sent, "y"), swap(x_sent, "x")

    acts_got = swap(acts, "c")
    result, grad_stream, grad_own, grad_other, attn_mine, attn_theirs, col_norms = column_call(
        col_bwd_kernel,
        info,
        place,
        col_pieces,
        [up, da_own, out_own, other_parts, resid_three, stream_one, qkv_two, norm_gain],
        [whole_shape] * 2
        + [((count, half), bf16)] * 2
        + [((count, 5 * half), bf16)] * 2
        + [((4, width), f32)],
        [pltpu.VMEM((rows, part, 3 * width), bf16), pltpu.VMEM((rows, part, width), bf16)],
        23,
    )

    result, x_got, y_got = together(result, x_got, y_got)
    block_out = to_blocks(result.reshape(rows, part, width))
    ffn_to_x, ffn_x, ffn_to_y, ffn_y = next_sums(place, y_kept, y_got, x_kept, x_got)
    near_part, near_theirs, far_part, far_theirs, row_sent, row_kept = row_attention_back(
        info, tie, near, far, grad_own, swap(grad_other, "c"), w_row, near_normed, far_normed
    )
    (
        row_sent, far_theirs, near_theirs, attn_theirs, block_out, ffn_x_got, ffn_y_got
    ) = together(
        row_sent, far_theirs, near_theirs, attn_theirs, block_out,
        swap(ffn_to_x, "x"), swap(ffn_to_y, "y"),
    )
    row_got = swap(row_sent, "x")
    far_sum = added(far_part, swap(far_theirs, "c"))
    far_got = swap(far_sum, "x")
    near_got = swap(near_theirs, "c")
    attn_sent, attn_kept = whole_call(
        attn_terms_kernel,
        place,
        [acts, acts_got, attn_mine, swap(attn_theirs, "c")],
        [((8, depth // 2, 5 * half), bf16)] * 2,
        9,
    )
    ffn_column = jnp.concatenate([added(ffn_x, ffn_x_got), added(ffn_y, ffn_y_got)], axis=2)
    ffn_own = lax.all_to_all(ffn_column, "z", 0, 0, tiled=True)
    attn_sent, attn_kept, ffn_own, row_got = together(attn_sent, attn_kept, ffn_own, row_got)
    attn_got = swap(attn_sent, "y")
    ffn_own = jnp.sum(ffn_own.astype(f32), axis=0).astype(bf16)
    ffn_own, row_got, block_out = together(ffn_own, row_got, block_out)
    row_own = z_summed(added(row_kept, row_got), z)
    attn_pair_terms = added(attn_kept, attn_got).reshape(4, 2, depth // 2, 5 * half)
    attn_column = pick(attn_pair_terms, x, 1)
    attn_x_got = swap(pick(attn_pair_terms, 1 - x, 1), "x")
    blocks = whole_call(
        tokens_back_kernel,
        info,
        [near_part, near_got, far_got, stream_zero, grad_stream, norm_gain, col_norms],
        [((rows, part + 16, width), bf16)],
        5,
    )[0]
    blocks, row_own = together(blocks, row_own)
    blocks = to_blocks(blocks)
    grad_tokens = to_rows(blocks[:, :part], c).astype(f32)
    norm_grad = jnp.sum(blocks[:, part : part + 8, :TILE].astype(f32), axis=0)
    block_out = to_rows(block_out, c)
    attn_column = added(attn_column, attn_x_got)
    norm_parts = [norm_grad] + [
        lax.ppermute(norm_grad, ("y", "c"), [(k, k ^ i) for k in range(4)]) for i in (1, 2, 3)
    ]
    norm_grad = (norm_parts[0] + norm_parts[1]) + (norm_parts[2] + norm_parts[3])
    norm_grad = norm_grad[:6, :depth]
    row_grad = added(row_own, swap(row_own, "y"))
    before = jnp.sum(jnp.square(ffn_own.astype(f32)))
    before = before + 0.5 * jnp.sum(jnp.square(row_grad.astype(f32)))
    before = before + 0.25 * jnp.sum(norm_grad * norm_grad)
    attn_own, squares = whole_call(
        last_sums_kernel,
        place,
        [
            pick(attn_column, z, 0),
            *gather_turned(attn_column, z),
            jnp.broadcast_to(before, (8, TILE)),
        ],
        [((depth // 2, 5 * half), bf16), ((32, 8, TILE), f32)],
        2,
    )
    attn_own, block_out = together(attn_own, block_out)
    squares = lax.all_to_all(squares, ("z", "x", "y", "c"), 0, 0, tiled=True)
    attn_grad_b = joined(attn_own, swap(attn_own, "y"), y, 0)
    ffn_grads = [ffn_own, swap(ffn_own, "y")]

    row_other = swap(row_grad, "c")
    attn_other = swap(attn_grad_b, "c")
    ffn_others = [swap(piece, "c") for piece in ffn_grads]

    grad_norm = jnp.sqrt(jnp.sum(squares[:, 0, 0]))
    factor = clip_bound / jnp.maximum(grad_norm, clip_bound)
    attn_first_new, attn_second_new, attn_weight_new, attn_copy = attn_adam(
        place,
        squares,
        (row_grad, row_other, attn_grad_b, attn_other),
        attn_weight,
        attn_first,
        attn_second,
    )
    in_first_new, in_second_new, in_weight_new, in_copy, *turned = ffn_adam(
        place,
        squares,
        [*ffn_grads, *ffn_others],
        (in_weight, in_first, in_second),
        (out_weight, out_first, out_second),
    )
    out_first_new, out_second_new, out_weight_new, out_copy = [value.T for value in turned]
    norm_first_new, norm_second_new, norm_new = adam_update(
        norm_param, norm_first, norm_second, norm_grad * factor, norm_rate
    )
    return (
        block_out,
        grad_tokens,
        grad_norm,
        attn_first_new,
        attn_second_new,
        attn_weight_new,
        attn_copy,
        in_first_new,
        in_second_new,
        in_weight_new,
        in_copy,
        out_first_new,
        out_second_new,
        out_weight_new,
        out_copy,
        norm_first_new,
        norm_second_new,
        norm_new,
    )


def paired_layout(mesh):
    return dict(mesh.shape) == {"seq": 8, "grp": 4}


def mapped(run, mesh, seq, grp):
    placed = (
        P(grp, seq, None, None),
        P(grp, seq, None, None),
        P(grp),
        P(grp),
        P(None, seq, None),
        P(seq, None),
        P(None, seq),
        P(None, seq),
        P(None, seq, None),
        P(None, seq, None),
        P(seq, None),
        P(seq, None),
        P(None, seq),
        P(None, seq),
        P(None, seq),
        P(None, seq),
    )
    return jax.shard_map(
        run,
        mesh=mesh,
        in_specs=placed,
        out_specs=(
            P(grp, seq, None, None),
            P(grp, seq, None, None),
            P(),
            P(None, seq, None),
            P(None, seq, None),
            P(None, seq, None),
            P(None, seq, None),
            P(seq, None),
            P(seq, None),
            P(seq, None),
            P(seq, None),
            P(None, seq),
            P(None, seq),
            P(None, seq),
            P(None, seq),
            P(None, seq),
            P(None, seq),
            P(None, seq),
        ),
        check_vma=False,
    )


def solution(mesh):
    if not paired_layout(mesh):
        return mapped(general_body, mesh, "seq", "grp")
    fine = Mesh(mesh.devices.reshape(4, 2, 2, 2), ("z", "x", "y", "c"))
    return mapped(paired_body, fine, ("z", "x"), ("y", "c"))
```

```python
from functools import partial
import math

import jax
import jax.numpy as jnp
from jax import lax
from jax.experimental import pallas as pl
from jax.experimental.pallas import tpu as pltpu
from jax.sharding import Mesh
from jax.sharding import PartitionSpec as P

H = 12
DH = 64
STEP = 5


eps_norm = 1e-05
masked_score = -1000000000.0
clip_bound = 1.0
beta_one = 0.5
beta_two = 0.5
matrix_rate = 0.06
norm_rate = 0.3
decay_rate = 0.01
adam_eps = 1e-08


def in_blocks(x, dim, length):
    lengths = x.shape
    pieces = x.reshape(*lengths[:dim], length, lengths[dim] // length, *lengths[dim + 1 :])
    return jnp.moveaxis(pieces, dim, 0)


def sent_and_summed(x, axis, dim):
    length = lax.axis_size(axis)
    pieces = lax.all_to_all(in_blocks(x, dim, length), axis, 0, 0, tiled=True)
    return jnp.sum(pieces.astype(jnp.float32), axis=0)


def layer_norm(value, gain, shift):
    mean = jnp.mean(value, axis=-1, keepdims=True)
    centred = value - mean
    spread = jnp.mean(centred * centred, axis=-1, keepdims=True)
    return centred * lax.rsqrt(spread + eps_norm) * gain + shift


def softmax_rows(scores, keep):
    scores = jnp.where(keep, scores, masked_score)
    top = jnp.max(scores, axis=-1, keepdims=True)
    expo = jnp.exp(scores - top)
    return expo / jnp.sum(expo, axis=-1, keepdims=True)


def softmax_back(probs, grads):
    return probs * (grads - jnp.sum(probs * grads, axis=-1, keepdims=True))


def adam_update(weight, first, second, grad, rate):
    first_new = beta_one * first + (1.0 - beta_one) * grad
    second_new = beta_two * second + (1.0 - beta_two) * grad * grad
    first_hat = first_new / (1.0 - beta_one**STEP)
    second_hat = second_new / (1.0 - beta_two**STEP)
    weight_new = weight - rate * (
        first_hat / (jnp.sqrt(second_hat) + adam_eps) + decay_rate * weight
    )
    return (first_new, second_new, weight_new)


def attn_pair(normed, grad_proj, mixed, grad_branch):
    width = normed.shape[-1]
    qkv_terms = jnp.einsum("prcd,kprce->dke", normed, grad_proj, preferred_element_type=jnp.float32)
    output_terms = jnp.einsum(
        "prcd,prce->de", mixed, grad_branch, preferred_element_type=jnp.float32
    )
    return jnp.concatenate([qkv_terms, output_terms[:, None, :]], axis=1).reshape(width, 4 * width)


def general_body(
    tokens,
    cotangent,
    col_count,
    row_count,
    attn_weight,
    in_weight,
    out_weight,
    norm_param,
    attn_first,
    attn_second,
    in_first,
    in_second,
    out_first,
    out_second,
    norm_first,
    norm_second,
):
    f32 = jnp.float32
    bf16 = jnp.bfloat16
    prot, rows_dev, cols, width = tokens.shape
    hidden = in_weight.shape[1]
    head_scale = 1.0 / math.sqrt(DH)
    attn_full, in_full, out_full, norm_full = (
        lax.all_gather(attn_weight.astype(bf16), "seq", axis=1, tiled=True),
        lax.all_gather(in_weight.astype(bf16), "seq", axis=0, tiled=True),
        lax.all_gather(out_weight.astype(bf16), "seq", axis=1, tiled=True),
        lax.all_gather(norm_param.astype(bf16), "seq", axis=1, tiled=True),
    )
    norm_gain = norm_full.astype(f32)
    row_ids = lax.axis_index("seq") * rows_dev + jnp.arange(rows_dev, dtype=jnp.int32)
    row_live = (row_ids[None, :] < row_count[:, None]).astype(f32)
    col_live = jnp.arange(cols, dtype=jnp.int32)[None, :] < col_count[:, None]
    tie_scale = lax.rsqrt(row_count.astype(f32)) * head_scale
    live = row_live[:, :, None] * col_live.astype(f32)[:, None, :]
    grad_out = (cotangent.astype(f32) * live[..., None]).astype(bf16)
    resid_one = tokens.astype(f32)
    normed_one = layer_norm(resid_one, norm_gain[0], norm_gain[1]).astype(bf16)
    proj_one = jnp.einsum(
        "prcd,kde->kprce", normed_one, attn_full[0:3], preferred_element_type=f32
    ).astype(bf16)
    proj_one = proj_one.reshape(3, prot, rows_dev, cols, H, DH)
    query_one, key_one, value_one = (proj_one[0], proj_one[1], proj_one[2])
    masked_query = query_one * row_live[:, :, None, None, None].astype(bf16)
    partial_scores = (
        jnp.einsum("prihe,prjhe->phij", masked_query, key_one, preferred_element_type=f32)
        * tie_scale[:, None, None, None]
    )
    keep_cols = col_live[:, None, None, :]
    score_part = lax.psum_scatter(partial_scores, "seq", scatter_dimension=2, tiled=True)
    probs_one = softmax_rows(score_part, keep_cols)
    probs_low = lax.all_gather(probs_one.astype(bf16), "seq", axis=2, tiled=True)
    mixed_one = jnp.einsum(
        "phij,prjhe->prihe", probs_low, value_one, preferred_element_type=f32
    ).astype(bf16)
    mixed_one = mixed_one.reshape(prot, rows_dev, cols, width)
    branch_one = jnp.einsum("prcd,de->prce", mixed_one, attn_full[3], preferred_element_type=f32)
    stream_one = (resid_one + branch_one).astype(bf16)
    stream_cols, up_grad = (
        lax.all_to_all(stream_one, "seq", split_axis=2, concat_axis=1, tiled=True),
        lax.all_to_all(grad_out, "seq", split_axis=2, concat_axis=1, tiled=True),
    )
    rows = stream_cols.shape[1]
    cols_dev = stream_cols.shape[2]
    row_live_all = jnp.arange(rows, dtype=jnp.int32)[None, :] < row_count[:, None]
    resid_two = stream_cols.astype(f32)
    normed_two = layer_norm(resid_two, norm_gain[2], norm_gain[3]).astype(bf16)
    proj_two = jnp.einsum(
        "prcd,kde->kprce", normed_two, attn_full[4:7], preferred_element_type=f32
    ).astype(bf16)
    proj_two = proj_two.reshape(3, prot, rows, cols_dev, H, DH)
    query_two, key_two, value_two = (proj_two[0], proj_two[1], proj_two[2])
    scores_two = (
        jnp.einsum("prche,psche->pchrs", query_two, key_two, preferred_element_type=f32)
        * head_scale
    )
    probs_two = softmax_rows(scores_two, row_live_all[:, None, None, None, :])
    probs_two_low = probs_two.astype(bf16)
    mixed_two = jnp.einsum(
        "pchrs,psche->prche", probs_two_low, value_two, preferred_element_type=f32
    ).astype(bf16)
    mixed_two = mixed_two.reshape(prot, rows, cols_dev, width)
    resid_three = resid_two + jnp.einsum(
        "prcd,de->prce", mixed_two, attn_full[7], preferred_element_type=f32
    )
    normed_three = layer_norm(resid_three, norm_gain[4], norm_gain[5]).astype(bf16)
    inner = jnp.einsum("prcd,df->prcf", normed_three, in_full, preferred_element_type=f32)
    activ = jax.nn.gelu(inner, approximate=True).astype(bf16)
    result = (
        resid_three + jnp.einsum("prcf,fd->prcd", activ, out_full, preferred_element_type=f32)
    ).astype(bf16)
    block_out = lax.all_to_all(result, "seq", split_axis=1, concat_axis=2, tiled=True)
    grad_act = jnp.einsum("prcd,fd->prcf", up_grad, out_full, preferred_element_type=f32)
    _, gelu_back = jax.vjp(partial(jax.nn.gelu, approximate=True), inner)
    grad_inner = gelu_back(grad_act)[0].astype(bf16)
    grad_normed_three = jnp.einsum("prcf,df->prcd", grad_inner, in_full, preferred_element_type=f32)
    _, norm_back_three = jax.vjp(layer_norm, resid_three, norm_gain[4], norm_gain[5])
    part_three, gain_grad_three, shift_grad_three = norm_back_three(grad_normed_three)
    grad_three = up_grad.astype(f32) + part_three
    grad_branch_two = grad_three.astype(bf16)
    grad_mixed_two = jnp.einsum(
        "prce,de->prcd", grad_branch_two, attn_full[7], preferred_element_type=f32
    ).astype(bf16)
    grad_mixed_two = grad_mixed_two.reshape(prot, rows, cols_dev, H, DH)
    grad_probs_two = jnp.einsum(
        "prche,psche->pchrs", grad_mixed_two, value_two, preferred_element_type=f32
    )
    grad_value_two = jnp.einsum(
        "pchrs,prche->psche", probs_two_low, grad_mixed_two, preferred_element_type=f32
    )
    grad_scores_two = softmax_back(probs_two, grad_probs_two).astype(bf16)
    grad_query_two = (
        jnp.einsum("pchrs,psche->prche", grad_scores_two, key_two, preferred_element_type=f32)
        * head_scale
    )
    grad_key_two = (
        jnp.einsum("pchrs,prche->psche", grad_scores_two, query_two, preferred_element_type=f32)
        * head_scale
    )
    grad_proj_two = jnp.stack([grad_query_two, grad_key_two, grad_value_two]).astype(bf16)
    grad_proj_two = grad_proj_two.reshape(3, prot, rows, cols_dev, width)
    grad_normed_two = jnp.einsum(
        "kprce,kde->prcd", grad_proj_two, attn_full[4:7], preferred_element_type=f32
    )
    _, norm_back_two = jax.vjp(layer_norm, resid_two, norm_gain[2], norm_gain[3])
    part_two, gain_grad_two, shift_grad_two = norm_back_two(grad_normed_two)
    grad_stream = (grad_three + part_two).astype(bf16)
    col_attn_terms = attn_pair(normed_two, grad_proj_two, mixed_two, grad_branch_two)
    in_terms = jnp.einsum("prcd,prcf->df", normed_three, grad_inner, preferred_element_type=f32)
    out_terms = jnp.einsum("prcf,prcd->df", activ, up_grad, preferred_element_type=f32)
    grad_rows = lax.all_to_all(grad_stream, "seq", split_axis=1, concat_axis=2, tiled=True)
    grad_mixed_one = jnp.einsum(
        "prce,de->prcd", grad_rows, attn_full[3], preferred_element_type=f32
    ).astype(bf16)
    grad_mixed_one = grad_mixed_one.reshape(prot, rows_dev, cols, H, DH)
    partial_grads = jnp.einsum(
        "prihe,prjhe->phij", grad_mixed_one, value_one, preferred_element_type=f32
    )
    grad_value_one = jnp.einsum(
        "phij,prihe->prjhe", probs_low, grad_mixed_one, preferred_element_type=f32
    )
    grad_part = sent_and_summed(partial_grads.astype(jnp.bfloat16), "seq", 2)
    grad_scores_one = lax.all_gather(
        softmax_back(probs_one, grad_part).astype(bf16), "seq", axis=2, tiled=True
    )
    tie_rows = row_live[:, :, None, None, None] * tie_scale[:, None, None, None, None]
    grad_query_one = (
        jnp.einsum("phij,prjhe->prihe", grad_scores_one, key_one, preferred_element_type=f32)
        * tie_rows
    )
    grad_key_one = (
        jnp.einsum("phij,prihe->prjhe", grad_scores_one, masked_query, preferred_element_type=f32)
        * tie_scale[:, None, None, None, None]
    )
    grad_proj_one = jnp.stack([grad_query_one, grad_key_one, grad_value_one]).astype(bf16)
    grad_proj_one = grad_proj_one.reshape(3, prot, rows_dev, cols, width)
    grad_normed_one = jnp.einsum(
        "kprce,kde->prcd", grad_proj_one, attn_full[0:3], preferred_element_type=f32
    )
    _, norm_back_one = jax.vjp(layer_norm, resid_one, norm_gain[0], norm_gain[1])
    part_one, gain_grad_one, shift_grad_one = norm_back_one(grad_normed_one)
    grad_tokens = grad_rows.astype(f32) + part_one
    norm_stack = jnp.stack(
        [
            gain_grad_one,
            shift_grad_one,
            gain_grad_two,
            shift_grad_two,
            gain_grad_three,
            shift_grad_three,
        ]
    )
    row_attn_terms = attn_pair(normed_one, grad_proj_one, mixed_one, grad_rows)
    owned = lax.psum_scatter(
        jnp.concatenate(
            [row_attn_terms, col_attn_terms, in_terms, out_terms, norm_stack.T], axis=1
        ),
        "seq",
        scatter_dimension=0,
        tiled=True,
    )
    width_dev = owned.shape[0]
    row_part = owned[:, : 4 * width].reshape(width_dev, 4, width)
    col_part = owned[:, 4 * width : 8 * width].reshape(width_dev, 4, width)
    in_part = owned[:, 8 * width : 8 * width + hidden]
    out_part = owned[:, 8 * width + hidden : 8 * width + 2 * hidden].T
    norm_part = owned[:, 8 * width + 2 * hidden :].T
    attn_part = jnp.concatenate([row_part, col_part], axis=1).transpose(1, 0, 2)
    attn_grad, in_grad, out_grad, norm_grad = (
        lax.psum(attn_part.astype(jnp.bfloat16), "grp").astype(jnp.float32),
        lax.psum(in_part.astype(jnp.bfloat16), "grp").astype(jnp.float32),
        lax.psum(out_part.astype(jnp.bfloat16), "grp").astype(jnp.float32),
        lax.psum(norm_part.astype(jnp.bfloat16), "grp").astype(jnp.float32),
    )
    squares = (
        jnp.sum(attn_grad * attn_grad)
        + jnp.sum(in_grad * in_grad)
        + jnp.sum(out_grad * out_grad)
        + jnp.sum(norm_grad * norm_grad)
    )
    grad_norm = jnp.sqrt(lax.psum(squares, "seq"))
    factor = clip_bound / jnp.maximum(grad_norm, clip_bound)
    attn_first_new, attn_second_new, attn_weight_new = adam_update(
        attn_weight, attn_first, attn_second, attn_grad * factor, matrix_rate
    )
    in_first_new, in_second_new, in_weight_new = adam_update(
        in_weight, in_first, in_second, in_grad * factor, matrix_rate
    )
    out_first_new, out_second_new, out_weight_new = adam_update(
        out_weight, out_first, out_second, out_grad * factor, matrix_rate
    )
    norm_first_new, norm_second_new, norm_new = adam_update(
        norm_param, norm_first, norm_second, norm_grad * factor, norm_rate
    )
    return (
        block_out,
        grad_tokens,
        grad_norm,
        attn_first_new,
        attn_second_new,
        attn_weight_new,
        attn_weight_new.astype(bf16),
        in_first_new,
        in_second_new,
        in_weight_new,
        in_weight_new.astype(bf16),
        out_first_new,
        out_second_new,
        out_weight_new,
        out_weight_new.astype(bf16),
        norm_first_new,
        norm_second_new,
        norm_new,
    )


PAIR = [(0, 1), (1, 0)]
TILE = 128


def swap(value, axis):
    return lax.ppermute(value, axis, PAIR)


def pick(value, index, axis):
    return lax.dynamic_index_in_dim(value, index, axis, keepdims=False)


def joined(own, other, place, axis):
    return jnp.where(
        place == 0,
        jnp.concatenate([own, other], axis=axis),
        jnp.concatenate([other, own], axis=axis),
    )


def merge(own, other, place, axis):
    return jnp.where(
        place == 0,
        jnp.stack([own, other], axis=axis),
        jnp.stack([other, own], axis=axis),
    )


def merge_cores(value, c):
    prot, _, cols, width = value.shape
    part = cols // 4
    split = value.reshape(prot, 2, 2, part, width)
    got = swap(pick(split, 1 - c, 2), "c")
    both = merge(pick(split, c, 2), got, c, 0)
    return both.reshape(8, part, width)


def to_blocks(value):
    return lax.all_to_all(value, ("z", "x"), 0, 0, tiled=True)


def to_rows(got, c):
    _, part, width = got.shape
    got = got.reshape(2, 2, 2, part, width)
    other = swap(pick(got, 1 - c, 0), "c")
    both = merge(pick(got, c, 0), other, c, 2)
    return both.reshape(2, 1, 4 * part, width)


def together(*values):
    return lax.optimization_barrier(values)


def gather_z(own):
    return [own] + [lax.ppermute(own, "z", [(k, k ^ i) for k in range(4)]) for i in (1, 2, 3)]


def spread(over_z):
    over_x = swap(over_z, "x")
    quarter = [((0, 0, 0), over_z, 0), ((1, 0, 0), over_x, 0)]
    return quarter + [((j, 1, 0), swap(value, "y"), 0) for (j, _, _), value, _ in quarter]


def across(over_x, over_y):
    half = over_x.shape[0] // 2
    return swap(over_x[:half], "y"), swap(over_y[half:], "x")


def across_pieces(by_y, by_x):
    return [((1, 1, 0), by_y, 0), ((1, 1, 0), by_x, by_y.shape[0])]


def plan_of(pieces):
    return [(step, first) for step, _, first in pieces]


def placing(plan, outs_at, place_ref, stacks, outs, sem, steps=True):
    copies = []
    for stack, ((j, m, k), first) in zip(stacks, plan):
        x, y, c = (lax.bitwise_xor(place_ref[n], step) for n, step in ((1, j), (3, m), (2, k)))
        for i in range(stack.shape[0]):
            z = first + i
            shard = (lax.bitwise_xor(place_ref[0], z) if steps else z) * 2 + x
            for source, target in outs_at(stack.at[i], outs, shard, y, c):
                copies.append(pltpu.make_async_copy(source, target, sem.at[len(copies)]))
    return copies


def row_attn_at(ref, outs, shard, y, c):
    depth = outs[0].shape[0] // 16
    at = pl.multiple_of((shard * 2 + y) * depth, depth)
    return [(ref, outs[0].at[pl.ds(at, depth)])]


def ffn_at(ref, outs, shard, y, c):
    depth = ref.shape[0]
    at = pl.multiple_of((y * 8 + shard) * depth, depth)
    return [(ref, outs[0].at[pl.ds(at, depth)])]


def col_attn_at(ref, outs, shard, y, c):
    depth, half = ref.shape[1], ref.shape[2]
    at = pl.multiple_of((shard * 2 + y) * depth, depth)
    moves = []
    slots = [(o, n) for o, out in enumerate(outs) for n in range(out.shape[1] // (2 * half))]
    for k, (o, n) in enumerate(slots):
        lane = pl.multiple_of(c * half + n * 2 * half, TILE)
        moves.append((ref.at[k], outs[o].at[pl.ds(at, depth), pl.ds(lane, half)]))
    return moves


def contract(a, b, dims):
    return lax.dot_general(a, b, (dims, ((), ())), preferred_element_type=jnp.float32)


LAST = ((1,), (1,))
FIRST = ((0,), (0,))
PLAIN = ((1,), (0,))


def softmax_of(scores, keep):
    scores = jnp.where(keep, scores, masked_score)
    expo = jnp.exp(scores - jnp.max(scores, axis=-1, keepdims=True))
    return expo / jnp.sum(expo, axis=-1, keepdims=True)


def head_lanes(lanes):
    side = lax.broadcasted_iota(jnp.int32, (1, lanes), 1) % TILE < DH
    return (side, jnp.logical_not(side))


def lasting(microseconds):
    return pl.CostEstimate(
        flops=int(microseconds * 0.58e9), bytes_accessed=0, transcendentals=0
    )


def moved(pairs, sem, first=0):
    copies = [pltpu.make_async_copy(a, b, sem.at[first + n]) for n, (a, b) in enumerate(pairs)]
    for copy in copies:
        copy.start()
    return copies


def wait_all(copies):
    for copy in copies:
        copy.wait()


def only(keep, value):
    return jnp.where(keep, value, jnp.zeros_like(value))


def column_keep(info_ref, own_cols, near, part):
    key = lax.broadcasted_iota(jnp.int32, (1, 2 * near), 1)
    far = key >= near
    inner = key % near
    x = jnp.where(far, 1 - info_ref[1], info_ref[1])
    c = jnp.where(inner >= part, 1 - info_ref[2], info_ref[2])
    column = x * near + c * part + inner % part
    return column < info_ref[3]


def live_pair(value, row, info_ref):
    lane = lax.broadcasted_iota(jnp.int32, (1, value.shape[1]), 1) // TILE + row
    return only(lane < info_ref[4], value)


def head_pair(ref, row, lane):
    blocks, _, part, _ = ref.shape
    found = [ref[:, row + n, :, lane : lane + TILE].reshape(blocks * part, TILE) for n in (0, 1)]
    return jnp.concatenate(found, axis=1)


def row_fwd_kernel(token_plan, weight_plan, place_ref, info_ref, tie_ref, *refs):
    bf16 = jnp.bfloat16
    f32 = jnp.float32
    tokens, refs = refs[: len(token_plan)], refs[len(token_plan) :]
    stacks, refs = refs[: len(weight_plan)], refs[len(weight_plan) :]
    own_ref, near_tokens_ref, far_tokens_ref, w_ref, gain_ref, near_ref, far_ref, o_ref = refs[:8]
    all_ref, norm_ref, token_sem, weight_sem = refs[8:]
    blocks, rows, part, lanes = near_ref.shape
    half = lanes // 3
    count = rows * part
    near = blocks * part
    copies = []
    for stack, (j, k) in zip(tokens, token_plan):
        x = lax.bitwise_xor(place_ref[1], j)
        for i in range(4):
            row = lax.bitwise_xor(place_ref[0], i) * 2 + x
            moves = [(stack.at[i, pl.ds(0, 2 * part)], all_ref.at[k, row])]
            if k == 0:
                moves.append((stack.at[i, pl.ds(2 * part, 16)], norm_ref.at[j * 4 + i]))
            for source, target in moves:
                copies.append(pltpu.make_async_copy(source, target, token_sem.at[len(copies)]))
    weights = placing(weight_plan, row_attn_at, place_ref, stacks, [w_ref], weight_sem)
    for copy in copies + weights:
        copy.start()
    for copy in copies:
        copy.wait()
    gains = jnp.sum(norm_ref[...].astype(f32), axis=0)
    gain_ref[...] = gains
    x = info_ref[1]
    for ref, side in ((near_tokens_ref, x), (far_tokens_ref, 1 - x)):
        at = pl.ds(pl.multiple_of(side * part, part), part)
        for k in range(blocks):
            value = all_ref[k, :, at, :].reshape(count, -1)
            if k == 0:
                @pl.when(side == x)
                def _():
                    own_ref[...] = value
            found = normed(value.astype(f32), gains[0:1], gains[1:2])[0]
            ref[k * count : (k + 1) * count] = found.astype(bf16)
    for copy in weights:
        copy.wait()
    for n in range(3):
        at = slice(n * half, (n + 1) * half)
        found = contract(near_tokens_ref[...], w_ref[:, at], PLAIN).astype(bf16)
        near_ref[:, :, :, at] = found.reshape(blocks, rows, part, half)
        if n > 0:
            found = contract(far_tokens_ref[...], w_ref[:, at], PLAIN).astype(bf16)
            far_ref[:, :, :, (n - 1) * half : n * half] = found.reshape(blocks, rows, part, half)
    sides = head_lanes(2 * TILE)
    keep = column_keep(info_ref, near, near, part)
    tie = tie_ref[0]
    for lane in range(0, half, TILE):
        scores = [jnp.zeros((near, 2 * near), f32) for _ in sides]
        for row in range(0, rows, 2):
            query = live_pair(head_pair(near_ref, row, lane), row, info_ref)
            key = jnp.concatenate(
                [head_pair(near_ref, row, half + lane), head_pair(far_ref, row, lane)], axis=0
            )
            for n, side in enumerate(sides):
                scores[n] = scores[n] + contract(only(side, query), key, LAST)
        probs = [softmax_of(s * tie, keep).astype(bf16) for s in scores]
        for row in range(0, rows, 2):
            value = jnp.concatenate(
                [head_pair(near_ref, row, 2 * half + lane), head_pair(far_ref, row, half + lane)],
                axis=0,
            )
            mixed = jnp.where(
                sides[0], contract(probs[0], value, PLAIN), contract(probs[1], value, PLAIN)
            ).astype(bf16)
            for n in (0, 1):
                o_ref[:, row + n, :, lane : lane + TILE] = mixed[:, n * TILE : (n + 1) * TILE].reshape(
                    blocks, part, TILE
                )


def next_sums_kernel(
    place_ref, y_kept_ref, y_got_ref, x_kept_ref, x_got_ref, to_x_ref, with_x_ref, to_y_ref, with_y_ref
):
    _, depth, lanes = to_x_ref.shape
    first, first_y = place_ref[1] == 0, place_ref[3] == 0
    summed = added(y_kept_ref[...], y_got_ref[...]).reshape(2, depth, lanes)
    with_x_ref[0] = jnp.where(first, summed[0], summed[1])
    to_x_ref[0] = jnp.where(first, summed[1], summed[0])
    summed = added(x_kept_ref[0], x_got_ref[0])
    with_y_ref[0] = jnp.where(first_y, summed[0], summed[1])
    to_y_ref[0] = jnp.where(first_y, summed[1], summed[0])


def next_sums(place, y_kept, y_got, x_kept, x_got):
    zs, _, depth, lanes = x_kept.shape
    by_rows = pl.BlockSpec((2 * depth, lanes), lambda n: (n, 0))
    by_z = pl.BlockSpec((1, 2, depth, lanes), lambda n: (n, 0, 0, 0))
    return pl.pallas_call(
        next_sums_kernel,
        grid=(zs,),
        in_specs=[pl.BlockSpec(memory_space=pltpu.SMEM), by_rows, by_rows, by_z, by_z],
        out_specs=[pl.BlockSpec((1, depth, lanes), lambda n: (n, 0, 0))] * 4,
        out_shape=[jax.ShapeDtypeStruct((zs, depth, lanes), jnp.bfloat16)] * 4,
        cost_estimate=lasting(4),
        compiler_params=pltpu.CompilerParams(vmem_limit_bytes=56 * 2**20),
    )(place, y_kept, y_got, x_kept, x_got)


def row_bwd_kernel(
    info_ref, tie_ref, near_ref, far_ref, own_ref, got_ref, w_any, near_any, far_any,
    near_part_any, near_theirs_any, far_part_any, far_theirs_any, sent_ref, kept_ref,
    do_ref, d_near_ref, d_far_ref, w_ref, near_tokens_ref, far_tokens_ref,
    near_part_ref, near_theirs_ref, far_part_ref, far_theirs_ref, sem,
):
    arriving = moved(
        [(w_any, w_ref), (near_any, near_tokens_ref), (far_any, far_tokens_ref)], sem
    )
    bf16 = jnp.bfloat16
    blocks, rows, part, lanes = near_ref.shape
    half = lanes // 3
    near = blocks * part
    sides = head_lanes(2 * TILE)
    keep = column_keep(info_ref, near, near, part)
    tie = tie_ref[0]
    do_ref[0] = own_ref[...].reshape(rows, part, half)
    do_ref[1] = got_ref[...].reshape(rows, part, half)

    for lane in range(0, half, TILE):

        def pair(ref, row, first):
            at = slice(first + lane, first + lane + TILE)
            found = [ref[:, row + n, :, at].reshape(near, TILE) for n in (0, 1)]
            return jnp.concatenate(found, axis=1)

        def both(row, first):
            return jnp.concatenate(
                [pair(near_ref, row, first), pair(far_ref, row, first - half)], axis=0
            )

        scores = [jnp.zeros((near, 2 * near), jnp.float32) for _ in sides]
        grads = [jnp.zeros((near, 2 * near), jnp.float32) for _ in sides]
        for row in range(0, rows, 2):
            query = live_pair(pair(near_ref, row, 0), row, info_ref)
            key, value = both(row, half), both(row, 2 * half)
            out = pair(do_ref, row, 0)
            for n, side in enumerate(sides):
                scores[n] = scores[n] + contract(only(side, query), key, LAST)
                grads[n] = grads[n] + contract(only(side, out), value, LAST)
        probs = [softmax_of(s * tie, keep) for s in scores]
        lows = [p.astype(bf16) for p in probs]
        deltas = [softmax_back(p, g).astype(bf16) for p, g in zip(probs, grads)]
        low_turned = [p.T for p in lows]
        delta_turned = [d.T for d in deltas]
        for row in range(0, rows, 2):
            query = live_pair(pair(near_ref, row, 0), row, info_ref)
            key, out = both(row, half), pair(do_ref, row, 0)
            dq = [contract(d, key, PLAIN) for d in deltas]
            dk = [contract(d, query, PLAIN) for d in delta_turned]
            dv = [contract(p, out, PLAIN) for p in low_turned]
            dq = live_pair(jnp.where(sides[0], dq[0], dq[1]) * tie, row, info_ref).astype(bf16)
            dk = (jnp.where(sides[0], dk[0], dk[1]) * tie).astype(bf16)
            dv = jnp.where(sides[0], dv[0], dv[1]).astype(bf16)

            def put(ref, first, value):
                for n in (0, 1):
                    piece = value[:, n * TILE : (n + 1) * TILE].reshape(blocks, part, TILE)
                    ref[:, row + n, :, first + lane : first + lane + TILE] = piece

            put(d_near_ref, 0, dq)
            put(d_near_ref, half, dk[:near])
            put(d_near_ref, 2 * half, dv[:near])
            put(d_far_ref, 0, dk[near:])
            put(d_far_ref, half, dv[near:])

    count = rows * part
    wait_all(arriving)
    d_far = d_far_ref[...].reshape(blocks * count, 2 * half)
    far_weights = w_ref[:, half:]
    far_part_ref[...] = contract(d_far[:count], far_weights, LAST)
    far_theirs_ref[...] = contract(d_far[count:], far_weights, LAST).astype(bf16)
    d_near = d_near_ref[...].reshape(blocks * count, lanes)
    near_part_ref[...] = contract(d_near[:count], w_ref[...], LAST)
    near_theirs_ref[...] = contract(d_near[count:], w_ref[...], LAST).astype(bf16)
    leaving = moved(
        [
            (far_theirs_ref, far_theirs_any),
            (near_theirs_ref, near_theirs_any),
            (far_part_ref, far_part_any),
            (near_part_ref, near_part_any),
        ],
        sem,
        3,
    )
    near_turned = near_tokens_ref[...].T
    far_turned = far_tokens_ref[...].T
    zs, depth = kept_ref.shape[0], kept_ref.shape[1]
    first = info_ref[1] == 0
    for n in range(3):
        at = slice(n * half, (n + 1) * half)
        terms = contract(near_turned, d_near[:, at], PLAIN)
        if n > 0:
            terms = terms + contract(far_turned, d_far[:, (n - 1) * half : n * half], PLAIN)
        terms = terms.astype(bf16).reshape(zs, 2, depth, half)
        kept_ref[:, :, at] = jnp.where(first, terms[:, 0], terms[:, 1])
        sent_ref[:, :, at] = jnp.where(first, terms[:, 1], terms[:, 0])
    wait_all(leaving)


def row_attention(place, info, tie, tokens, weights, rows, half):
    f32, bf16 = jnp.float32, jnp.bfloat16
    zs, deep, width = tokens[0][1].shape
    part = (deep - 16) // 2
    count = rows * part
    small = pl.BlockSpec(memory_space=pltpu.SMEM)
    anywhere = pl.BlockSpec(memory_space=pl.ANY)
    inside = pl.BlockSpec(memory_space=pltpu.VMEM)
    shapes = [
        ((count, width), bf16),
        ((2 * count, width), bf16),
        ((2 * count, width), bf16),
        ((width, 3 * half), bf16),
        ((16, width), f32),
        ((2, rows, part, 3 * half), bf16),
        ((2, rows, part, 2 * half), bf16),
        ((2, rows, part, half), bf16),
    ]
    return pl.pallas_call(
        partial(row_fwd_kernel, [step for step, _ in tokens], plan_of(weights)),
        in_specs=[small] * 3 + [anywhere] * (len(tokens) + len(weights)),
        out_specs=[inside] * len(shapes),
        out_shape=[jax.ShapeDtypeStruct(shape, kind) for shape, kind in shapes],
        scratch_shapes=[
            pltpu.VMEM((2, rows, 2 * part, width), bf16),
            pltpu.VMEM((8, 16, width), bf16),
            pltpu.SemaphoreType.DMA((24,)),
            pltpu.SemaphoreType.DMA((16,)),
        ],
        compiler_params=pltpu.CompilerParams(vmem_limit_bytes=56 * 2**20),
        cost_estimate=lasting(13),
    )(place, info, tie, *[v for _, v in tokens], *[v for _, v, _ in weights])


def row_attention_back(info, tie, near, far, own, got, weights, near_tokens, far_tokens):
    blocks, rows, part, lanes = near.shape
    count, width = rows * part, weights.shape[0]
    half = lanes // 3
    f32, bf16 = jnp.float32, jnp.bfloat16
    small = pl.BlockSpec(memory_space=pltpu.SMEM)
    anywhere = pl.BlockSpec(memory_space=pl.ANY)
    inside = pl.BlockSpec(memory_space=pltpu.VMEM)
    shapes = [((count, width), kind) for kind in (f32, bf16) * 2]
    shapes = shapes + [((4, width // 8, lanes), bf16)] * 2
    return pl.pallas_call(
        row_bwd_kernel,
        in_specs=[small, small] + [inside] * 4 + [anywhere] * 3,
        out_specs=[anywhere] * 4 + [inside] * 2,
        out_shape=[jax.ShapeDtypeStruct(shape, kind) for shape, kind in shapes],
        scratch_shapes=[
            pltpu.VMEM((blocks, rows, part, half), bf16),
            pltpu.VMEM((blocks, rows, part, lanes), bf16),
            pltpu.VMEM((blocks, rows, part, 2 * half), bf16),
            pltpu.VMEM(weights.shape, bf16),
            pltpu.VMEM(near_tokens.shape, bf16),
            pltpu.VMEM(far_tokens.shape, bf16),
            *[pltpu.VMEM(shape, kind) for shape, kind in shapes[:4]],
            pltpu.SemaphoreType.DMA((7,)),
        ],
        cost_estimate=lasting(16),
        compiler_params=pltpu.CompilerParams(vmem_limit_bytes=56 * 2**20),
    )(info, tie, near, far, own, got, weights, near_tokens, far_tokens)


def normed(value, gain, shift):
    centred = value - jnp.mean(value, axis=-1, keepdims=True)
    scale = lax.rsqrt(jnp.mean(centred * centred, axis=-1, keepdims=True) + eps_norm)
    unit = centred * scale
    return unit * gain + shift, unit, scale


def normed_back(grad, unit, scale, gain):
    inner = grad * gain
    mean = jnp.mean(inner, axis=-1, keepdims=True)
    along = jnp.mean(inner * unit, axis=-1, keepdims=True)
    return scale * (inner - mean - unit * along)


def column_masks(info_ref, rows, part):
    tokens = rows * part
    key = lax.broadcasted_iota(jnp.int32, (tokens, tokens), 0)
    query = lax.broadcasted_iota(jnp.int32, (tokens, tokens), 1)
    same = key % part == query % part
    return jnp.logical_and(same, key // part < info_ref[4])


def stacked(value, sides):
    return jnp.concatenate([only(side, value) for side in sides], axis=0)


def column_probs(query, key, keep, sides):
    scores = contract(stacked(key, sides), query, LAST) * (1.0 / math.sqrt(DH))
    tokens = query.shape[0]
    probs = []
    for n in (0, 1):
        part = jnp.where(keep, scores[n * tokens : (n + 1) * tokens], masked_score)
        expo = jnp.exp(part - jnp.max(part, axis=0, keepdims=True))
        probs.append(expo / jnp.sum(expo, axis=0, keepdims=True))
    return probs


def col_fwd_kernel(plan, info_ref, place_ref, *refs):
    stacks, refs = refs[: len(plan)], refs[len(plan) :]
    x_ref, own_ref, other_ref, gain_ref, acts_ref, one_ref, qkv_ref = refs[:7]
    resid_ref, normed_three_ref, mixed_ref, three_ref, col_ref, seven_ref, sem = refs[7:]
    copies = placing(plan, col_attn_at, place_ref, stacks, [three_ref, col_ref, seven_ref], sem)
    for copy in copies:
        copy.start()
    bf16 = jnp.bfloat16
    rows, cols, lanes = qkv_ref.shape
    width = lanes // 3
    part = 16
    own, other = own_ref[...], other_ref[...]
    flip = info_ref[2] == 0
    mixed_one = jnp.concatenate(
        [jnp.where(flip, own, other), jnp.where(flip, other, own)], axis=1
    )
    acts_ref[:, :width] = mixed_one
    for copy in copies:
        copy.wait()
    stream = (x_ref[...].astype(jnp.float32) + contract(mixed_one, three_ref[...], PLAIN)).astype(bf16)
    one_ref[...] = stream
    normed_two = normed(stream.astype(jnp.float32), gain_ref[2:3], gain_ref[3:4])[0].astype(bf16)
    acts_ref[:, width : 2 * width] = normed_two
    for n in range(3):
        at = slice(n * width, (n + 1) * width)
        found = contract(normed_two, col_ref[:, at], PLAIN).astype(bf16)
        qkv_ref[:, :, at] = found.reshape(rows, cols, width)
    keep = column_masks(info_ref, rows, part)
    sides = head_lanes(TILE)

    def attend(b, carry):
        at = pl.ds(pl.multiple_of(b * part, part), part)
        def tile(n, t):
            lane = n * width + t * TILE
            return qkv_ref[:, at, lane : lane + TILE].reshape(rows * part, TILE)
        tiles = range(width // TILE)
        probs = [column_probs(tile(0, t), tile(1, t), keep, sides) for t in tiles]
        for t in tiles:
            low = jnp.concatenate(probs[t], axis=0).astype(bf16)
            mixed = contract(low, stacked(tile(2, t), sides), FIRST).astype(bf16)
            mixed_ref[:, at, t * TILE : (t + 1) * TILE] = mixed.reshape(rows, part, TILE)
        return carry

    lax.fori_loop(0, cols // part, attend, 0)
    mixed = mixed_ref[...].reshape(rows * cols, width)
    acts_ref[:, 2 * width :] = mixed
    resid = one_ref[...].astype(jnp.float32) + contract(mixed, seven_ref[...], PLAIN)
    resid_ref[...] = resid
    normed_three_ref[...] = normed(resid, gain_ref[4:5], gain_ref[5:6])[0].astype(bf16)


def col_bwd_kernel(plan, info_ref, place_ref, *refs):
    stacks, refs = refs[: len(plan)], refs[len(plan) :]
    up_ref, da_ref, out_ref, got_ref, resid_ref, one_ref, qkv_ref, gain_ref = refs[:8]
    result_ref, stream_ref, own_ref, other_ref, mine_ref, theirs_ref, norms_ref = refs[8:15]
    dqkv_ref, do_ref, three_ref, col_ref, seven_ref, sem = refs[15:]
    copies = placing(plan, col_attn_at, place_ref, stacks, [three_ref, col_ref, seven_ref], sem)
    for copy in copies:
        copy.start()
    bf16 = jnp.bfloat16
    f32 = jnp.float32
    rows, cols, lanes = qkv_ref.shape
    width = lanes // 3
    part = 16
    result_ref[...] = (resid_ref[...] + out_ref[...] + got_ref[0].astype(f32)).astype(bf16)
    da = da_ref[...] + got_ref[1].astype(f32)
    gain = gain_ref[4:5]
    _, unit, scale = normed(resid_ref[...], gain, 0.0)
    grad_three = up_ref[...].astype(f32) + normed_back(da, unit, scale, gain)
    norms_ref[2:3] = jnp.sum(da * unit, axis=0, keepdims=True)
    norms_ref[3:4] = jnp.sum(da, axis=0, keepdims=True)
    branch = grad_three.astype(bf16)
    half = width // 2
    flip = info_ref[2] == 0

    def put_halves(first, value):
        at = slice(first, first + half)
        mine_ref[:, at] = jnp.where(flip, value[:, :half], value[:, half:])
        theirs_ref[:, at] = jnp.where(flip, value[:, half:], value[:, :half])

    put_halves(4 * half, branch)
    for copy in copies:
        copy.wait()
    do_ref[...] = contract(branch, seven_ref[...], LAST).astype(bf16).reshape(rows, cols, width)
    keep = column_masks(info_ref, rows, part)
    sides = head_lanes(TILE)
    ratio = 1.0 / math.sqrt(DH)

    def attend(b, carry):
        at = pl.ds(pl.multiple_of(b * part, part), part)
        tokens = rows * part

        def tile(n, t):
            lane = n * width + t * TILE
            return qkv_ref[:, at, lane : lane + TILE].reshape(tokens, TILE)

        def out_tile(t):
            return do_ref[:, at, t * TILE : (t + 1) * TILE].reshape(tokens, TILE)

        def put(n, t, value):
            lane = n * width + t * TILE
            dqkv_ref[:, at, lane : lane + TILE] = value.astype(bf16).reshape(rows, part, TILE)

        for t in range(width // TILE):
            query, key, out = tile(0, t), tile(1, t), out_tile(t)
            keys = stacked(key, sides)
            probs = column_probs(query, key, keep, sides)
            grads = contract(stacked(tile(2, t), sides), out, LAST)
            deltas = []
            for n, p in enumerate(probs):
                g = grads[n * tokens : (n + 1) * tokens]
                deltas.append((p * (g - jnp.sum(p * g, axis=0, keepdims=True))).astype(bf16))
            put(0, t, contract(jnp.concatenate(deltas, axis=0), keys, FIRST) * ratio)
            wide = jnp.concatenate(deltas, axis=1)
            put(1, t, contract(wide, stacked(query, sides), PLAIN) * ratio)
            wide = jnp.concatenate([p.astype(bf16) for p in probs], axis=1)
            put(2, t, contract(wide, stacked(out, sides), PLAIN))
        return carry

    lax.fori_loop(0, cols // part, attend, 0)
    dqkv = dqkv_ref[...].reshape(rows * cols, lanes)
    for n in range(3):
        put_halves((n + 1) * half, dqkv[:, n * width : (n + 1) * width])
    grad_normed = contract(dqkv, col_ref[...], LAST)
    gain = gain_ref[2:3]
    _, unit, scale = normed(one_ref[...].astype(f32), gain, 0.0)
    norms_ref[0:1] = jnp.sum(grad_normed * unit, axis=0, keepdims=True)
    norms_ref[1:2] = jnp.sum(grad_normed, axis=0, keepdims=True)
    stream = (grad_three + normed_back(grad_normed, unit, scale, gain)).astype(bf16)
    stream_ref[...] = stream
    put_halves(0, stream)
    mixed = contract(stream, three_ref[...], LAST).astype(bf16)
    own_ref[...] = jnp.where(flip, mixed[:, :half], mixed[:, half:])
    other_ref[...] = jnp.where(flip, mixed[:, half:], mixed[:, :half])


def tokens_back_kernel(
    info_ref, near_ref, near_got_ref, far_got_ref, x_ref, stream_ref, gain_ref, norms_ref,
    blocks_ref,
):
    f32 = jnp.float32
    grad = near_ref[...] + near_got_ref[...].astype(f32) + far_got_ref[...].astype(f32)
    gain = gain_ref[0:1]
    _, unit, scale = normed(x_ref[...].astype(f32), gain, 0.0)
    found = stream_ref[...].astype(f32) + normed_back(grad, unit, scale, gain)
    rows, deep, width = blocks_ref.shape
    part = deep - 16
    blocks_ref[:, :part] = found.astype(jnp.bfloat16).reshape(rows, part, width)
    sums = [
        jnp.sum(grad * unit, axis=0, keepdims=True),
        jnp.sum(grad, axis=0, keepdims=True),
        norms_ref[...],
        jnp.zeros((2, width), f32),
    ]
    sums = jnp.concatenate(sums, axis=0)
    depth = width // 8
    lane = lax.broadcasted_iota(jnp.int32, (width, TILE), 0)
    place = lax.broadcasted_iota(jnp.int32, (width, TILE), 1)
    for shard in range(8):
        chosen = jnp.logical_and(lane == shard * depth + place, place < depth)
        found = lax.dot_general(
            sums,
            chosen.astype(f32),
            (PLAIN, ((), ())),
            precision=lax.Precision.HIGHEST,
            preferred_element_type=f32,
        )
        found = jnp.concatenate([found, jnp.zeros((8, TILE), f32)], axis=0)
        blocks_ref[shard, part:, :TILE] = found.astype(jnp.bfloat16)
        blocks_ref[shard, part:, TILE:] = jnp.zeros((16, width - TILE), jnp.bfloat16)


def attn_terms_kernel(place_ref, acts_ref, got_ref, mine_ref, theirs_ref, sent_ref, kept_ref):
    width = acts_ref.shape[1] // 3
    half = width // 2
    depth = sent_ref.shape[1]
    turned = [
        jnp.concatenate([ref[:, n * width : (n + 1) * width].T for ref in (acts_ref, got_ref)], axis=1)
        for n in range(3)
    ]
    first = place_ref[3] == 0
    for n, m in enumerate((0, 1, 1, 1, 2)):
        at = slice(n * half, (n + 1) * half)
        grads = jnp.concatenate([mine_ref[:, at], theirs_ref[:, at]], axis=0)
        terms = contract(turned[m], grads, PLAIN).astype(jnp.bfloat16)
        terms = terms.reshape(sent_ref.shape[0], 2, depth, half)
        kept_ref[:, :, at] = jnp.where(first, terms[:, 0], terms[:, 1])
        sent_ref[:, :, at] = jnp.where(first, terms[:, 1], terms[:, 0])


def column_call(kernel, info, place, pieces, args, outs, scratch, time):
    width = args[-1].shape[1]
    bf16 = jnp.bfloat16
    small = pl.BlockSpec(memory_space=pltpu.SMEM)
    inside = pl.BlockSpec(memory_space=pltpu.VMEM)
    anywhere = pl.BlockSpec(memory_space=pl.ANY)
    return pl.pallas_call(
        partial(kernel, plan_of(pieces)),
        in_specs=[small] * 2 + [anywhere] * len(pieces) + [inside] * len(args),
        out_specs=[inside] * len(outs),
        out_shape=[jax.ShapeDtypeStruct(shape, kind) for shape, kind in outs],
        scratch_shapes=[
            *scratch,
            pltpu.VMEM((width, width), bf16),
            pltpu.VMEM((width, 3 * width), bf16),
            pltpu.VMEM((width, width), bf16),
            pltpu.SemaphoreType.DMA((160,)),
        ],
        cost_estimate=lasting(time),
        compiler_params=pltpu.CompilerParams(vmem_limit_bytes=56 * 2**20),
    )(info, place, *[value for _, value, _ in pieces], *args)


def last_sums_kernel(place_ref, own_ref, *refs):
    f32 = jnp.float32
    got, (before_ref, sum_ref, squares_ref) = refs[:3], refs[3:]
    total = own_ref[...].astype(f32)
    for ref in got:
        total = total + ref[...].astype(f32)
    low = total.astype(jnp.bfloat16)
    sum_ref[...] = low
    low = low.astype(f32)
    squares = jnp.sum(low * low, axis=1, keepdims=True)
    squares = jnp.sum(squares, axis=0, keepdims=True) + before_ref[0:1, 0:1]
    squares_ref[...] = jnp.broadcast_to(squares[None], squares_ref.shape)


def clip_factor(squares_ref):
    total = jnp.sum(squares_ref[:, 0:1, 0:1], axis=0)
    return clip_bound / jnp.maximum(jnp.sqrt(total), clip_bound)


def adam_kernel(
    place_ref, squares_ref, row_ref, row_other_ref, col_ref, col_other_ref, w_ref, first_ref, second_ref, *outs
):
    count, _, width = w_ref.shape
    half = width // 2
    low = place_ref[2] == 0
    early = pl.program_id(0) == 0
    factor = clip_factor(squares_ref)
    for n in range(count):
        at = slice((n + 1) * half, (n + 2) * half)
        own, other = col_ref[:, at], col_other_ref[:, at]
        if n < 3:
            at = slice(n * half, (n + 1) * half)
            sooner, sooner_other = row_ref[:, at], row_other_ref[:, at]
        else:
            sooner, sooner_other = col_ref[:, :half], col_other_ref[:, :half]
        own, other = jnp.where(early, sooner, own), jnp.where(early, sooner_other, other)
        grad = jnp.concatenate([jnp.where(low, own, other), jnp.where(low, other, own)], axis=1)
        grad = grad.astype(jnp.float32) * factor
        first, second, weight = adam_update(w_ref[n], first_ref[n], second_ref[n], grad, matrix_rate)
        for ref, value in zip(outs, (first, second, weight, weight.astype(jnp.bfloat16))):
            ref[n] = value


def attn_adam(place, squares, grads, weight, first, second):
    small = pl.BlockSpec(memory_space=pltpu.SMEM)
    inside = pl.BlockSpec(memory_space=pltpu.VMEM)
    block = pl.BlockSpec((4, *weight.shape[1:]), lambda m: (m, 0, 0))
    kinds = [jnp.float32] * 3 + [jnp.bfloat16]
    return pl.pallas_call(
        adam_kernel,
        grid=(weight.shape[0] // 4,),
        in_specs=[small] + [inside] * 5 + [block] * 3,
        out_specs=[block] * 4,
        out_shape=[jax.ShapeDtypeStruct(weight.shape, kind) for kind in kinds],
        compiler_params=pltpu.CompilerParams(vmem_limit_bytes=40 * 2**20),
    )(place, squares, *grads, weight, first, second)


def ffn_adam_kernel(place_ref, squares_ref, *refs):
    pieces, refs = refs[:4], refs[4:]
    low, even = place_ref[2] == 0, place_ref[3] == 0
    factor = clip_factor(squares_ref)
    depth = pieces[0].shape[0]
    part = depth // 2
    half = pl.program_id(0)

    def by_matrix(first, second):
        return jnp.where(even, first, second), jnp.where(even, second, first)

    def put(grad, ins, outs):
        values = adam_update(*[ref[...] for ref in ins], grad * factor, matrix_rate)
        for ref, value in zip(outs, (*values, values[2].astype(jnp.bfloat16))):
            ref[...] = value

    rows = pl.ds(pl.multiple_of(half * part, 16), part)
    owns = by_matrix(pieces[0][rows], pieces[1][rows])
    others = by_matrix(pieces[2][rows], pieces[3][rows])
    for n, (own, other) in enumerate(zip(owns, others)):
        grad = jnp.concatenate([jnp.where(low, own, other), jnp.where(low, other, own)], axis=1)
        put(grad.astype(jnp.float32), refs[3 * n : 3 * n + 3], refs[6 + 4 * n : 10 + 4 * n])


def ffn_adam(place, squares, pieces, ins, outs):
    small = pl.BlockSpec(memory_space=pltpu.SMEM)
    inside = pl.BlockSpec(memory_space=pltpu.VMEM)
    depth, hidden = ins[0].shape
    block = pl.BlockSpec((depth // 2, hidden), lambda n: (n, 0))
    kinds = [jnp.float32] * 3 + [jnp.bfloat16]
    return pl.pallas_call(
        ffn_adam_kernel,
        grid=(2,),
        in_specs=[small] + [inside] * 5 + [block] * 6,
        out_specs=[block] * 8,
        out_shape=[jax.ShapeDtypeStruct((depth, hidden), kind) for kind in kinds * 2],
        compiler_params=pltpu.CompilerParams(vmem_limit_bytes=58 * 2**20),
    )(place, squares, *pieces, *ins, *[value.T for value in outs])


def whole_call(kernel, info, args, outs, time):
    inside = pl.BlockSpec(memory_space=pltpu.VMEM)
    return pl.pallas_call(
        kernel,
        in_specs=[pl.BlockSpec(memory_space=pltpu.SMEM)] + [inside] * len(args),
        out_specs=[inside] * len(outs),
        out_shape=[jax.ShapeDtypeStruct(shape, kind) for shape, kind in outs],
        cost_estimate=lasting(time),
        compiler_params=pltpu.CompilerParams(vmem_limit_bytes=56 * 2**20),
    )(info, *args)


def gelu_pair(u):
    ratio = math.sqrt(2.0 / math.pi)
    square = u * u
    tanh = jnp.tanh(ratio * u * (1.0 + 0.044715 * square))
    rise = 0.5 * (1.0 + tanh)
    slope = (0.5 * ratio) * (1.0 - tanh * tanh) * (1.0 + (3.0 * 0.044715) * square)
    return u * rise, rise + u * slope


def ffn_kernel(plan, place_ref, a_ref, a_got_ref, up_ref, up_got_ref, *refs):
    bf16 = jnp.bfloat16
    stacks, refs = refs[: len(plan)], refs[len(plan) :]
    out_ref, da_ref, others_ref = refs[:3]
    y_sent_ref, y_kept_ref, x_sent_ref, x_kept_ref = refs[3:7]
    w_ref, turned_ref, out_sum, da_sum, sem = refs[7:]
    count, width = a_ref.shape
    chunk = w_ref.shape[1] // 2
    copies = placing(plan, ffn_at, place_ref, stacks, [w_ref], sem, steps=False)
    for copy in copies:
        copy.start()
    for n, ref in enumerate((a_ref, a_got_ref, up_ref, up_got_ref)):
        turned_ref[n // 2, :, (n % 2) * count : (n % 2 + 1) * count] = ref[...].T
    for copy in copies:
        copy.wait()
    for step in (0, 1):
        lane = slice(step * chunk, (step + 1) * chunk)
        w_in = w_ref[:width, lane]
        w_out = w_ref[width:, lane]
        activs, grads = [], []
        for n, (tokens, ups) in enumerate(((a_ref, up_ref), (a_got_ref, up_got_ref))):
            at = slice(n * count, (n + 1) * count)
            activ, slope = gelu_pair(contract(tokens[...], w_in, PLAIN))
            activ = activ.astype(bf16)
            grad = (contract(ups[...], w_out, PLAIN) * slope).astype(bf16)
            out, da = contract(activ, w_out, LAST), contract(grad, w_in, LAST)
            if step == 0:
                out_sum[at] = out
                da_sum[at] = da
            elif n == 0:
                out_ref[...] = out_sum[at] + out
                da_ref[...] = da_sum[at] + da
            else:
                others_ref[0] = (out_sum[at] + out).astype(bf16)
                others_ref[1] = (da_sum[at] + da).astype(bf16)
            activs.append(activ)
            grads.append(grad)
        in_terms = contract(turned_ref[0], jnp.concatenate(grads, axis=0), PLAIN).astype(bf16)
        out_terms = contract(turned_ref[1], jnp.concatenate(activs, axis=0), PLAIN).astype(bf16)
        if step == 0:
            first = place_ref[3] == 0
            y_kept_ref[...] = jnp.where(first, in_terms, out_terms)
            y_sent_ref[...] = jnp.where(first, out_terms, in_terms)
        else:
            first = place_ref[1] == 0
            zs, _, depth, _ = x_sent_ref.shape
            for n, terms in enumerate((in_terms, out_terms)):
                terms = terms.reshape(zs, 2, depth, chunk)
                x_kept_ref[:, n] = jnp.where(first, terms[:, 0], terms[:, 1])
                x_sent_ref[:, n] = jnp.where(first, terms[:, 1], terms[:, 0])


def feed_forward(place, normed_own, normed_got, up_own, up_got, pieces):
    count, width = normed_own.shape
    half = pieces[0][1].shape[-1]
    anywhere = pl.BlockSpec(memory_space=pl.ANY)
    inside = pl.BlockSpec(memory_space=pltpu.VMEM)
    f32, bf16 = jnp.float32, jnp.bfloat16
    shapes = [((count, width), f32)] * 2 + [((2, count, width), bf16)]
    shapes = shapes + [((width, half // 2), bf16)] * 2 + [((4, 2, width // 8, half // 2), bf16)] * 2
    return pl.pallas_call(
        partial(ffn_kernel, plan_of(pieces)),
        in_specs=[pl.BlockSpec(memory_space=pltpu.SMEM)] + [inside] * 4 + [anywhere] * len(pieces),
        out_specs=[inside] * 7,
        out_shape=[jax.ShapeDtypeStruct(shape, kind) for shape, kind in shapes],
        scratch_shapes=[
            pltpu.VMEM((2 * width, half), bf16),
            pltpu.VMEM((2, width, 2 * count), bf16),
            pltpu.VMEM((2 * count, width), f32),
            pltpu.VMEM((2 * count, width), f32),
            pltpu.SemaphoreType.DMA((16,)),
        ],
        cost_estimate=lasting(22),
        compiler_params=pltpu.CompilerParams(vmem_limit_bytes=56 * 2**20),
    )(place, normed_own, normed_got, up_own, up_got, *[value for _, value, _ in pieces])


def added(a, b):
    return (a.astype(jnp.float32) + b.astype(jnp.float32)).astype(jnp.bfloat16)


def gather_turned(column, z):
    return [
        lax.ppermute(pick(column, lax.bitwise_xor(z, i), 0), "z", [(k, k ^ i) for k in range(4)])
        for i in (1, 2, 3)
    ]


def z_summed(column, z):
    parts = [pick(column, z, 0)] + gather_turned(column, z)
    return sum(part.astype(jnp.float32) for part in parts).astype(jnp.bfloat16)


def paired_body(
    tokens,
    cotangent,
    col_count,
    row_count,
    attn_weight,
    in_weight,
    out_weight,
    norm_param,
    attn_first,
    attn_second,
    in_first,
    in_second,
    out_first,
    out_second,
    norm_first,
    norm_second,
):
    f32 = jnp.float32
    bf16 = jnp.bfloat16
    z, x, y, c = (lax.axis_index(name) for name in ("z", "x", "y", "c"))
    width = tokens.shape[-1]
    hidden = in_weight.shape[1]
    depth = in_weight.shape[0]
    half = width // 2
    hidden_half = hidden // 2

    counts = jnp.stack([col_count, row_count])
    other_counts = swap(counts, "c")
    mine = jnp.where(z // 2 == c, counts, other_counts)
    mine = pick(mine, z % 2, 1)
    cols_live, rows_live = mine[0], mine[1]
    place = jnp.stack([z, x, c, y]).astype(jnp.int32)
    info = jnp.concatenate([place[:3], mine, place[3:]])
    tie = (lax.rsqrt(rows_live.astype(f32)) * (1.0 / math.sqrt(DH))).reshape(1)

    attn_low = attn_weight.astype(bf16)
    halves = attn_low.reshape(8, depth, 2, half)
    row_half = jnp.moveaxis(pick(halves[:3], c, 2), 0, 1).reshape(2, depth // 2, 3 * half)
    row_quarter = pick(row_half, y, 0)
    col_quarter = pick(pick(halves[3:], c, 2).reshape(5, 2, depth // 2, half), y, 1)
    row_z = gather_z(row_quarter)
    ffn_low = [in_weight.astype(bf16), out_weight.astype(bf16).T]
    ffn_low = [
        jnp.where(c == 0, low[:, :hidden_half], low[:, hidden_half:]) for low in ffn_low
    ]
    ffn_quarter = jnp.where(y == 0, *ffn_low)

    lanes = jnp.arange(width, dtype=jnp.int32) // depth
    norm_low = jnp.tile(norm_param.astype(bf16), (1, width // depth))
    norm_rows = jnp.where(lanes[None] == z * 2 + x, norm_low, jnp.zeros_like(norm_low))
    norm_rows = jnp.pad(norm_rows, ((0, 10), (0, 0)))
    part = tokens.shape[2] // 4
    tokens_here = merge_cores(tokens, c).reshape(4, 2 * part, width)
    parts = [
        jnp.concatenate([pick(tokens_here, lax.bitwise_xor(z, i), 0), norm_rows]) for i in range(4)
    ]
    parts = [parts[0]] + [
        lax.ppermute(parts[i], "z", [(k, k ^ i) for k in range(4)]) for i in (1, 2, 3)
    ]
    row_pieces = spread(jnp.stack(row_z))
    row_x, row_y, *parts, col_quarter = together(
        row_pieces[1][1], row_pieces[2][1], *parts, col_quarter
    )
    tokens_z = jnp.stack(parts)
    up = merge_cores(cotangent, c).reshape(4, 2, part, width)
    up = joined(pick(up, x, 1)[:, None], swap(pick(up, 1 - x, 1), "x")[:, None], x, 1)
    col_z = gather_z(col_quarter)
    tokens_x, row_last, ffn_quarter, up, *col_z = together(
        swap(tokens_z, "x"), swap(row_x, "y"), ffn_quarter, up, *col_z
    )
    steps = [(0, 0, 0), (1, 0, 0), (0, 1, 0), (1, 1, 0)]
    row_stacks = [row_pieces[0][1], row_x, row_y, row_last]
    row_pieces = [(step, value, 0) for step, value in zip(steps, row_stacks)]
    col_z = jnp.stack(col_z)
    ffn_z = lax.all_to_all(
        jnp.broadcast_to(ffn_quarter, (4, *ffn_quarter.shape)), "z", 0, 0, tiled=True
    )
    col_x, col_y = swap(col_z, "x"), swap(col_z, "y")
    col_across = across(col_x, col_y)
    col_x, col_y, ffn_z, up = together(col_x, col_y, ffn_z, up)
    tokens_far, *col_across = together(swap(tokens_x, "c"), *col_across)
    ffn_x, ffn_y = swap(ffn_z, "x"), swap(ffn_z, "y")
    ups = [pick(up, z, 0)] + [
        lax.ppermute(pick(up, lax.bitwise_xor(z, i), 0), "z", [(k, k ^ i) for k in range(4)])
        for i in (1, 2, 3)
    ]

    rows = 8
    count = rows * part
    stream_zero, near_normed, far_normed, w_row, norm_gain, near, far, mixed_heads = row_attention(
        place,
        info,
        tie,
        [((0, 0), tokens_z), ((1, 0), tokens_x), ((0, 1), swap(tokens_z, "c")), ((1, 1), tokens_far)],
        row_pieces,
        rows,
        half,
    )
    mixed_heads = mixed_heads.reshape(2, count, half)
    col_stacks = [col_z, col_x, col_y]
    mixed_heads, ffn_x, ffn_y, *col_others = together(
        mixed_heads, ffn_x, ffn_y, *[swap(value, "c") for value in col_stacks]
    )
    ups = [jnp.where(z % 2 == 0, a, b) for a, b in zip(ups, (ups[1], ups[0], ups[3], ups[2]))]
    ups = [jnp.where(z < 2, a, b) for a, b in zip(ups, ups[2:] + ups[:2])]
    up = jnp.concatenate(ups)
    col_pieces = [(step, v, 0) for step, v in zip(steps, col_stacks)] + across_pieces(*col_across)
    col_others = [(step, v, 0) for step, v in zip(steps, col_others)]
    col_others = col_others + across_pieces(*[swap(v, "c") for v in col_across])
    col_pieces = col_pieces + [((j, m, 1), v, first) for (j, m, _), v, first in col_others]
    ffn_pieces = [(step, v, 0) for step, v in zip(steps, [ffn_z, ffn_x, ffn_y])]

    whole_shape, wide_shape = ((count, width), bf16), ((rows, part, 3 * width), bf16)
    acts, stream_one, qkv_two, resid_three, normed_three = column_call(
        col_fwd_kernel,
        info,
        place,
        col_pieces,
        [stream_zero, mixed_heads[0], swap(mixed_heads[1], "c"), norm_gain],
        [((count, 3 * width), bf16), whole_shape, wide_shape, ((count, width), f32), whole_shape],
        [pltpu.VMEM((rows, part, width), bf16)],
        14,
    )
    normed_three, *ffn_across = together(normed_three, *across(ffn_x, ffn_y))
    ffn_pieces = ffn_pieces + across_pieces(*ffn_across)

    column = x * (2 * part) + c * part + jnp.arange(part, dtype=jnp.int32)
    live = jnp.logical_and(
        (jnp.arange(rows, dtype=jnp.int32) < rows_live)[:, None], (column < cols_live)[None, :]
    )
    up = jnp.where(live[..., None], up, jnp.zeros_like(up)).reshape(count, width)
    out_own, da_own, other_parts, *ffn_terms = feed_forward(
        place, normed_three, swap(normed_three, "c"), up, swap(up, "c"), ffn_pieces
    )
    other_parts = swap(other_parts, "c")
    y_sent, y_kept, x_sent, x_kept = ffn_terms
    y_got, x_got = swap(y_sent, "y"), swap(x_sent, "x")

    acts_got = swap(acts, "c")
    result, grad_stream, grad_own, grad_other, attn_mine, attn_theirs, col_norms = column_call(
        col_bwd_kernel,
        info,
        place,
        col_pieces,
        [up, da_own, out_own, other_parts, resid_three, stream_one, qkv_two, norm_gain],
        [whole_shape] * 2
        + [((count, half), bf16)] * 2
        + [((count, 5 * half), bf16)] * 2
        + [((4, width), f32)],
        [pltpu.VMEM((rows, part, 3 * width), bf16), pltpu.VMEM((rows, part, width), bf16)],
        23,
    )

    result, x_got, y_got = together(result, x_got, y_got)
    block_out = to_blocks(result.reshape(rows, part, width))
    ffn_to_x, ffn_x, ffn_to_y, ffn_y = next_sums(place, y_kept, y_got, x_kept, x_got)
    near_part, near_theirs, far_part, far_theirs, row_sent, row_kept = row_attention_back(
        info, tie, near, far, grad_own, swap(grad_other, "c"), w_row, near_normed, far_normed
    )
    (
        row_sent, far_theirs, near_theirs, attn_theirs, block_out, ffn_x_got, ffn_y_got
    ) = together(
        row_sent, far_theirs, near_theirs, attn_theirs, block_out,
        swap(ffn_to_x, "x"), swap(ffn_to_y, "y"),
    )
    row_got = swap(row_sent, "x")
    far_sum = added(far_part, swap(far_theirs, "c"))
    far_sum, attn_mine = together(far_sum, attn_mine)
    far_got = swap(far_sum, "x")
    near_got = swap(near_theirs, "c")
    attn_sent, attn_kept = whole_call(
        attn_terms_kernel,
        place,
        [acts, acts_got, attn_mine, swap(attn_theirs, "c")],
        [((8, depth // 2, 5 * half), bf16)] * 2,
        9,
    )
    ffn_column = jnp.concatenate([added(ffn_x, ffn_x_got), added(ffn_y, ffn_y_got)], axis=2)
    ffn_own = lax.all_to_all(ffn_column, "z", 0, 0, tiled=True)
    attn_sent, attn_kept, ffn_own, row_got = together(attn_sent, attn_kept, ffn_own, row_got)
    attn_got = swap(attn_sent, "y")
    ffn_own = jnp.sum(ffn_own.astype(f32), axis=0).astype(bf16)
    ffn_own, row_got, block_out = together(ffn_own, row_got, block_out)
    row_own = z_summed(added(row_kept, row_got), z)
    attn_pair_terms = added(attn_kept, attn_got).reshape(4, 2, depth // 2, 5 * half)
    attn_column = pick(attn_pair_terms, x, 1)
    attn_x_got = swap(pick(attn_pair_terms, 1 - x, 1), "x")
    blocks = whole_call(
        tokens_back_kernel,
        info,
        [near_part, near_got, far_got, stream_zero, grad_stream, norm_gain, col_norms],
        [((rows, part + 16, width), bf16)],
        5,
    )[0]
    blocks, row_own = together(blocks, row_own)
    blocks = to_blocks(blocks)
    grad_tokens = to_rows(blocks[:, :part], c).astype(f32)
    norm_grad = jnp.sum(blocks[:, part : part + 8, :TILE].astype(f32), axis=0)
    block_out = to_rows(block_out, c)
    attn_column = added(attn_column, attn_x_got)
    norm_parts = [norm_grad] + [
        lax.ppermute(norm_grad, ("y", "c"), [(k, k ^ i) for k in range(4)]) for i in (1, 2, 3)
    ]
    norm_grad = (norm_parts[0] + norm_parts[1]) + (norm_parts[2] + norm_parts[3])
    norm_grad = norm_grad[:6, :depth]
    row_grad = added(row_own, swap(row_own, "y"))
    before = jnp.sum(jnp.square(ffn_own.astype(f32)))
    before = before + 0.5 * jnp.sum(jnp.square(row_grad.astype(f32)))
    before = before + 0.25 * jnp.sum(norm_grad * norm_grad)
    attn_own, squares = whole_call(
        last_sums_kernel,
        place,
        [
            pick(attn_column, z, 0),
            *gather_turned(attn_column, z),
            jnp.broadcast_to(before, (8, TILE)),
        ],
        [((depth // 2, 5 * half), bf16), ((32, 8, TILE), f32)],
        2,
    )
    attn_own, block_out = together(attn_own, block_out)
    squares = lax.all_to_all(squares, ("z", "x", "y", "c"), 0, 0, tiled=True)
    attn_grad_b = joined(attn_own, swap(attn_own, "y"), y, 0)
    ffn_grads = [ffn_own, swap(ffn_own, "y")]

    row_other = swap(row_grad, "c")
    attn_other = swap(attn_grad_b, "c")
    ffn_others = [swap(piece, "c") for piece in ffn_grads]

    grad_norm = jnp.sqrt(jnp.sum(squares[:, 0, 0]))
    factor = clip_bound / jnp.maximum(grad_norm, clip_bound)
    attn_first_new, attn_second_new, attn_weight_new, attn_copy = attn_adam(
        place,
        squares,
        (row_grad, row_other, attn_grad_b, attn_other),
        attn_weight,
        attn_first,
        attn_second,
    )
    in_first_new, in_second_new, in_weight_new, in_copy, *turned = ffn_adam(
        place,
        squares,
        [*ffn_grads, *ffn_others],
        (in_weight, in_first, in_second),
        (out_weight, out_first, out_second),
    )
    out_first_new, out_second_new, out_weight_new, out_copy = [value.T for value in turned]
    norm_first_new, norm_second_new, norm_new = adam_update(
        norm_param, norm_first, norm_second, norm_grad * factor, norm_rate
    )
    return (
        block_out,
        grad_tokens,
        grad_norm,
        attn_first_new,
        attn_second_new,
        attn_weight_new,
        attn_copy,
        in_first_new,
        in_second_new,
        in_weight_new,
        in_copy,
        out_first_new,
        out_second_new,
        out_weight_new,
        out_copy,
        norm_first_new,
        norm_second_new,
        norm_new,
    )


def paired_layout(mesh):
    return dict(mesh.shape) == {"seq": 8, "grp": 4}


def mapped(run, mesh, seq, grp):
    placed = (
        P(grp, seq, None, None),
        P(grp, seq, None, None),
        P(grp),
        P(grp),
        P(None, seq, None),
        P(seq, None),
        P(None, seq),
        P(None, seq),
        P(None, seq, None),
        P(None, seq, None),
        P(seq, None),
        P(seq, None),
        P(None, seq),
        P(None, seq),
        P(None, seq),
        P(None, seq),
    )
    return jax.shard_map(
        run,
        mesh=mesh,
        in_specs=placed,
        out_specs=(
            P(grp, seq, None, None),
            P(grp, seq, None, None),
            P(),
            P(None, seq, None),
            P(None, seq, None),
            P(None, seq, None),
            P(None, seq, None),
            P(seq, None),
            P(seq, None),
            P(seq, None),
            P(seq, None),
            P(None, seq),
            P(None, seq),
            P(None, seq),
            P(None, seq),
            P(None, seq),
            P(None, seq),
            P(None, seq),
        ),
        check_vma=False,
    )


def solution(mesh):
    if not paired_layout(mesh):
        return mapped(general_body, mesh, "seq", "grp")
    fine = Mesh(mesh.devices.reshape(4, 2, 2, 2), ("z", "x", "y", "c"))
    return mapped(paired_body, fine, ("z", "x"), ("y", "c"))
```

```python
from functools import partial
import math

import jax
import jax.numpy as jnp
from jax import lax
from jax.experimental import pallas as pl
from jax.experimental.pallas import tpu as pltpu
from jax.sharding import Mesh
from jax.sharding import PartitionSpec as P

H = 12
DH = 64
STEP = 5


eps_norm = 1e-05
masked_score = -1000000000.0
clip_bound = 1.0
beta_one = 0.5
beta_two = 0.5
matrix_rate = 0.06
norm_rate = 0.3
decay_rate = 0.01
adam_eps = 1e-08


def in_blocks(x, dim, length):
    lengths = x.shape
    pieces = x.reshape(*lengths[:dim], length, lengths[dim] // length, *lengths[dim + 1 :])
    return jnp.moveaxis(pieces, dim, 0)


def sent_and_summed(x, axis, dim):
    length = lax.axis_size(axis)
    pieces = lax.all_to_all(in_blocks(x, dim, length), axis, 0, 0, tiled=True)
    return jnp.sum(pieces.astype(jnp.float32), axis=0)


def layer_norm(value, gain, shift):
    mean = jnp.mean(value, axis=-1, keepdims=True)
    centred = value - mean
    spread = jnp.mean(centred * centred, axis=-1, keepdims=True)
    return centred * lax.rsqrt(spread + eps_norm) * gain + shift


def softmax_rows(scores, keep):
    scores = jnp.where(keep, scores, masked_score)
    top = jnp.max(scores, axis=-1, keepdims=True)
    expo = jnp.exp(scores - top)
    return expo / jnp.sum(expo, axis=-1, keepdims=True)


def softmax_back(probs, grads):
    return probs * (grads - jnp.sum(probs * grads, axis=-1, keepdims=True))


def adam_update(weight, first, second, grad, rate):
    first_new = beta_one * first + (1.0 - beta_one) * grad
    second_new = beta_two * second + (1.0 - beta_two) * grad * grad
    first_hat = first_new / (1.0 - beta_one**STEP)
    second_hat = second_new / (1.0 - beta_two**STEP)
    weight_new = weight - rate * (
        first_hat / (jnp.sqrt(second_hat) + adam_eps) + decay_rate * weight
    )
    return (first_new, second_new, weight_new)


def attn_pair(normed, grad_proj, mixed, grad_branch):
    width = normed.shape[-1]
    qkv_terms = jnp.einsum("prcd,kprce->dke", normed, grad_proj, preferred_element_type=jnp.float32)
    output_terms = jnp.einsum(
        "prcd,prce->de", mixed, grad_branch, preferred_element_type=jnp.float32
    )
    return jnp.concatenate([qkv_terms, output_terms[:, None, :]], axis=1).reshape(width, 4 * width)


def general_body(
    tokens,
    cotangent,
    col_count,
    row_count,
    attn_weight,
    in_weight,
    out_weight,
    norm_param,
    attn_first,
    attn_second,
    in_first,
    in_second,
    out_first,
    out_second,
    norm_first,
    norm_second,
):
    f32 = jnp.float32
    bf16 = jnp.bfloat16
    prot, rows_dev, cols, width = tokens.shape
    hidden = in_weight.shape[1]
    head_scale = 1.0 / math.sqrt(DH)
    attn_full, in_full, out_full, norm_full = (
        lax.all_gather(attn_weight.astype(bf16), "seq", axis=1, tiled=True),
        lax.all_gather(in_weight.astype(bf16), "seq", axis=0, tiled=True),
        lax.all_gather(out_weight.astype(bf16), "seq", axis=1, tiled=True),
        lax.all_gather(norm_param.astype(bf16), "seq", axis=1, tiled=True),
    )
    norm_gain = norm_full.astype(f32)
    row_ids = lax.axis_index("seq") * rows_dev + jnp.arange(rows_dev, dtype=jnp.int32)
    row_live = (row_ids[None, :] < row_count[:, None]).astype(f32)
    col_live = jnp.arange(cols, dtype=jnp.int32)[None, :] < col_count[:, None]
    tie_scale = lax.rsqrt(row_count.astype(f32)) * head_scale
    live = row_live[:, :, None] * col_live.astype(f32)[:, None, :]
    grad_out = (cotangent.astype(f32) * live[..., None]).astype(bf16)
    resid_one = tokens.astype(f32)
    normed_one = layer_norm(resid_one, norm_gain[0], norm_gain[1]).astype(bf16)
    proj_one = jnp.einsum(
        "prcd,kde->kprce", normed_one, attn_full[0:3], preferred_element_type=f32
    ).astype(bf16)
    proj_one = proj_one.reshape(3, prot, rows_dev, cols, H, DH)
    query_one, key_one, value_one = (proj_one[0], proj_one[1], proj_one[2])
    masked_query = query_one * row_live[:, :, None, None, None].astype(bf16)
    partial_scores = (
        jnp.einsum("prihe,prjhe->phij", masked_query, key_one, preferred_element_type=f32)
        * tie_scale[:, None, None, None]
    )
    keep_cols = col_live[:, None, None, :]
    score_part = lax.psum_scatter(partial_scores, "seq", scatter_dimension=2, tiled=True)
    probs_one = softmax_rows(score_part, keep_cols)
    probs_low = lax.all_gather(probs_one.astype(bf16), "seq", axis=2, tiled=True)
    mixed_one = jnp.einsum(
        "phij,prjhe->prihe", probs_low, value_one, preferred_element_type=f32
    ).astype(bf16)
    mixed_one = mixed_one.reshape(prot, rows_dev, cols, width)
    branch_one = jnp.einsum("prcd,de->prce", mixed_one, attn_full[3], preferred_element_type=f32)
    stream_one = (resid_one + branch_one).astype(bf16)
    stream_cols, up_grad = (
        lax.all_to_all(stream_one, "seq", split_axis=2, concat_axis=1, tiled=True),
        lax.all_to_all(grad_out, "seq", split_axis=2, concat_axis=1, tiled=True),
    )
    rows = stream_cols.shape[1]
    cols_dev = stream_cols.shape[2]
    row_live_all = jnp.arange(rows, dtype=jnp.int32)[None, :] < row_count[:, None]
    resid_two = stream_cols.astype(f32)
    normed_two = layer_norm(resid_two, norm_gain[2], norm_gain[3]).astype(bf16)
    proj_two = jnp.einsum(
        "prcd,kde->kprce", normed_two, attn_full[4:7], preferred_element_type=f32
    ).astype(bf16)
    proj_two = proj_two.reshape(3, prot, rows, cols_dev, H, DH)
    query_two, key_two, value_two = (proj_two[0], proj_two[1], proj_two[2])
    scores_two = (
        jnp.einsum("prche,psche->pchrs", query_two, key_two, preferred_element_type=f32)
        * head_scale
    )
    probs_two = softmax_rows(scores_two, row_live_all[:, None, None, None, :])
    probs_two_low = probs_two.astype(bf16)
    mixed_two = jnp.einsum(
        "pchrs,psche->prche", probs_two_low, value_two, preferred_element_type=f32
    ).astype(bf16)
    mixed_two = mixed_two.reshape(prot, rows, cols_dev, width)
    resid_three = resid_two + jnp.einsum(
        "prcd,de->prce", mixed_two, attn_full[7], preferred_element_type=f32
    )
    normed_three = layer_norm(resid_three, norm_gain[4], norm_gain[5]).astype(bf16)
    inner = jnp.einsum("prcd,df->prcf", normed_three, in_full, preferred_element_type=f32)
    activ = jax.nn.gelu(inner, approximate=True).astype(bf16)
    result = (
        resid_three + jnp.einsum("prcf,fd->prcd", activ, out_full, preferred_element_type=f32)
    ).astype(bf16)
    block_out = lax.all_to_all(result, "seq", split_axis=1, concat_axis=2, tiled=True)
    grad_act = jnp.einsum("prcd,fd->prcf", up_grad, out_full, preferred_element_type=f32)
    _, gelu_back = jax.vjp(partial(jax.nn.gelu, approximate=True), inner)
    grad_inner = gelu_back(grad_act)[0].astype(bf16)
    grad_normed_three = jnp.einsum("prcf,df->prcd", grad_inner, in_full, preferred_element_type=f32)
    _, norm_back_three = jax.vjp(layer_norm, resid_three, norm_gain[4], norm_gain[5])
    part_three, gain_grad_three, shift_grad_three = norm_back_three(grad_normed_three)
    grad_three = up_grad.astype(f32) + part_three
    grad_branch_two = grad_three.astype(bf16)
    grad_mixed_two = jnp.einsum(
        "prce,de->prcd", grad_branch_two, attn_full[7], preferred_element_type=f32
    ).astype(bf16)
    grad_mixed_two = grad_mixed_two.reshape(prot, rows, cols_dev, H, DH)
    grad_probs_two = jnp.einsum(
        "prche,psche->pchrs", grad_mixed_two, value_two, preferred_element_type=f32
    )
    grad_value_two = jnp.einsum(
        "pchrs,prche->psche", probs_two_low, grad_mixed_two, preferred_element_type=f32
    )
    grad_scores_two = softmax_back(probs_two, grad_probs_two).astype(bf16)
    grad_query_two = (
        jnp.einsum("pchrs,psche->prche", grad_scores_two, key_two, preferred_element_type=f32)
        * head_scale
    )
    grad_key_two = (
        jnp.einsum("pchrs,prche->psche", grad_scores_two, query_two, preferred_element_type=f32)
        * head_scale
    )
    grad_proj_two = jnp.stack([grad_query_two, grad_key_two, grad_value_two]).astype(bf16)
    grad_proj_two = grad_proj_two.reshape(3, prot, rows, cols_dev, width)
    grad_normed_two = jnp.einsum(
        "kprce,kde->prcd", grad_proj_two, attn_full[4:7], preferred_element_type=f32
    )
    _, norm_back_two = jax.vjp(layer_norm, resid_two, norm_gain[2], norm_gain[3])
    part_two, gain_grad_two, shift_grad_two = norm_back_two(grad_normed_two)
    grad_stream = (grad_three + part_two).astype(bf16)
    col_attn_terms = attn_pair(normed_two, grad_proj_two, mixed_two, grad_branch_two)
    in_terms = jnp.einsum("prcd,prcf->df", normed_three, grad_inner, preferred_element_type=f32)
    out_terms = jnp.einsum("prcf,prcd->df", activ, up_grad, preferred_element_type=f32)
    grad_rows = lax.all_to_all(grad_stream, "seq", split_axis=1, concat_axis=2, tiled=True)
    grad_mixed_one = jnp.einsum(
        "prce,de->prcd", grad_rows, attn_full[3], preferred_element_type=f32
    ).astype(bf16)
    grad_mixed_one = grad_mixed_one.reshape(prot, rows_dev, cols, H, DH)
    partial_grads = jnp.einsum(
        "prihe,prjhe->phij", grad_mixed_one, value_one, preferred_element_type=f32
    )
    grad_value_one = jnp.einsum(
        "phij,prihe->prjhe", probs_low, grad_mixed_one, preferred_element_type=f32
    )
    grad_part = sent_and_summed(partial_grads.astype(jnp.bfloat16), "seq", 2)
    grad_scores_one = lax.all_gather(
        softmax_back(probs_one, grad_part).astype(bf16), "seq", axis=2, tiled=True
    )
    tie_rows = row_live[:, :, None, None, None] * tie_scale[:, None, None, None, None]
    grad_query_one = (
        jnp.einsum("phij,prjhe->prihe", grad_scores_one, key_one, preferred_element_type=f32)
        * tie_rows
    )
    grad_key_one = (
        jnp.einsum("phij,prihe->prjhe", grad_scores_one, masked_query, preferred_element_type=f32)
        * tie_scale[:, None, None, None, None]
    )
    grad_proj_one = jnp.stack([grad_query_one, grad_key_one, grad_value_one]).astype(bf16)
    grad_proj_one = grad_proj_one.reshape(3, prot, rows_dev, cols, width)
    grad_normed_one = jnp.einsum(
        "kprce,kde->prcd", grad_proj_one, attn_full[0:3], preferred_element_type=f32
    )
    _, norm_back_one = jax.vjp(layer_norm, resid_one, norm_gain[0], norm_gain[1])
    part_one, gain_grad_one, shift_grad_one = norm_back_one(grad_normed_one)
    grad_tokens = grad_rows.astype(f32) + part_one
    norm_stack = jnp.stack(
        [
            gain_grad_one,
            shift_grad_one,
            gain_grad_two,
            shift_grad_two,
            gain_grad_three,
            shift_grad_three,
        ]
    )
    row_attn_terms = attn_pair(normed_one, grad_proj_one, mixed_one, grad_rows)
    owned = lax.psum_scatter(
        jnp.concatenate(
            [row_attn_terms, col_attn_terms, in_terms, out_terms, norm_stack.T], axis=1
        ),
        "seq",
        scatter_dimension=0,
        tiled=True,
    )
    width_dev = owned.shape[0]
    row_part = owned[:, : 4 * width].reshape(width_dev, 4, width)
    col_part = owned[:, 4 * width : 8 * width].reshape(width_dev, 4, width)
    in_part = owned[:, 8 * width : 8 * width + hidden]
    out_part = owned[:, 8 * width + hidden : 8 * width + 2 * hidden].T
    norm_part = owned[:, 8 * width + 2 * hidden :].T
    attn_part = jnp.concatenate([row_part, col_part], axis=1).transpose(1, 0, 2)
    attn_grad, in_grad, out_grad, norm_grad = (
        lax.psum(attn_part.astype(jnp.bfloat16), "grp").astype(jnp.float32),
        lax.psum(in_part.astype(jnp.bfloat16), "grp").astype(jnp.float32),
        lax.psum(out_part.astype(jnp.bfloat16), "grp").astype(jnp.float32),
        lax.psum(norm_part.astype(jnp.bfloat16), "grp").astype(jnp.float32),
    )
    squares = (
        jnp.sum(attn_grad * attn_grad)
        + jnp.sum(in_grad * in_grad)
        + jnp.sum(out_grad * out_grad)
        + jnp.sum(norm_grad * norm_grad)
    )
    grad_norm = jnp.sqrt(lax.psum(squares, "seq"))
    factor = clip_bound / jnp.maximum(grad_norm, clip_bound)
    attn_first_new, attn_second_new, attn_weight_new = adam_update(
        attn_weight, attn_first, attn_second, attn_grad * factor, matrix_rate
    )
    in_first_new, in_second_new, in_weight_new = adam_update(
        in_weight, in_first, in_second, in_grad * factor, matrix_rate
    )
    out_first_new, out_second_new, out_weight_new = adam_update(
        out_weight, out_first, out_second, out_grad * factor, matrix_rate
    )
    norm_first_new, norm_second_new, norm_new = adam_update(
        norm_param, norm_first, norm_second, norm_grad * factor, norm_rate
    )
    return (
        block_out,
        grad_tokens,
        grad_norm,
        attn_first_new,
        attn_second_new,
        attn_weight_new,
        attn_weight_new.astype(bf16),
        in_first_new,
        in_second_new,
        in_weight_new,
        in_weight_new.astype(bf16),
        out_first_new,
        out_second_new,
        out_weight_new,
        out_weight_new.astype(bf16),
        norm_first_new,
        norm_second_new,
        norm_new,
    )


PAIR = [(0, 1), (1, 0)]
TILE = 128


def swap(value, axis):
    return lax.ppermute(value, axis, PAIR)


def pick(value, index, axis):
    return lax.dynamic_index_in_dim(value, index, axis, keepdims=False)


def joined(own, other, place, axis):
    return jnp.where(
        place == 0,
        jnp.concatenate([own, other], axis=axis),
        jnp.concatenate([other, own], axis=axis),
    )


def merge(own, other, place, axis):
    return jnp.where(
        place == 0,
        jnp.stack([own, other], axis=axis),
        jnp.stack([other, own], axis=axis),
    )


def merge_cores(value, c):
    prot, _, cols, width = value.shape
    part = cols // 4
    split = value.reshape(prot, 2, 2, part, width)
    got = swap(pick(split, 1 - c, 2), "c")
    both = merge(pick(split, c, 2), got, c, 0)
    return both.reshape(8, part, width)


def to_blocks(value):
    return lax.all_to_all(value, ("z", "x"), 0, 0, tiled=True)


def to_rows(got, c):
    _, part, width = got.shape
    got = got.reshape(2, 2, 2, part, width)
    other = swap(pick(got, 1 - c, 0), "c")
    both = merge(pick(got, c, 0), other, c, 2)
    return both.reshape(2, 1, 4 * part, width)


def together(*values):
    return lax.optimization_barrier(values)


def gather_z(own):
    return [own] + [lax.ppermute(own, "z", [(k, k ^ i) for k in range(4)]) for i in (1, 2, 3)]


def spread(over_z):
    over_x = swap(over_z, "x")
    quarter = [((0, 0, 0), over_z, 0), ((1, 0, 0), over_x, 0)]
    return quarter + [((j, 1, 0), swap(value, "y"), 0) for (j, _, _), value, _ in quarter]


def across(over_x, over_y):
    half = over_x.shape[0] // 2
    return swap(over_x[:half], "y"), swap(over_y[half:], "x")


def across_pieces(by_y, by_x):
    return [((1, 1, 0), by_y, 0), ((1, 1, 0), by_x, by_y.shape[0])]


def plan_of(pieces):
    return [(step, first) for step, _, first in pieces]


def placing(plan, outs_at, place_ref, stacks, outs, sem, steps=True):
    copies = []
    for stack, ((j, m, k), first) in zip(stacks, plan):
        x, y, c = (lax.bitwise_xor(place_ref[n], step) for n, step in ((1, j), (3, m), (2, k)))
        for i in range(stack.shape[0]):
            z = first + i
            shard = (lax.bitwise_xor(place_ref[0], z) if steps else z) * 2 + x
            for source, target in outs_at(stack.at[i], outs, shard, y, c):
                copies.append(pltpu.make_async_copy(source, target, sem.at[len(copies)]))
    return copies


def row_attn_at(ref, outs, shard, y, c):
    depth = outs[0].shape[0] // 16
    at = pl.multiple_of((shard * 2 + y) * depth, depth)
    return [(ref, outs[0].at[pl.ds(at, depth)])]


def ffn_at(ref, outs, shard, y, c):
    depth = ref.shape[0]
    at = pl.multiple_of((y * 8 + shard) * depth, depth)
    return [(ref, outs[0].at[pl.ds(at, depth)])]


def col_attn_at(ref, outs, shard, y, c):
    depth, half = ref.shape[1], ref.shape[2]
    at = pl.multiple_of((shard * 2 + y) * depth, depth)
    moves = []
    slots = [(o, n) for o, out in enumerate(outs) for n in range(out.shape[1] // (2 * half))]
    for k, (o, n) in enumerate(slots):
        lane = pl.multiple_of(c * half + n * 2 * half, TILE)
        moves.append((ref.at[k], outs[o].at[pl.ds(at, depth), pl.ds(lane, half)]))
    return moves


def contract(a, b, dims):
    return lax.dot_general(a, b, (dims, ((), ())), preferred_element_type=jnp.float32)


LAST = ((1,), (1,))
FIRST = ((0,), (0,))
PLAIN = ((1,), (0,))


def softmax_of(scores, keep):
    scores = jnp.where(keep, scores, masked_score)
    expo = jnp.exp(scores - jnp.max(scores, axis=-1, keepdims=True))
    return expo / jnp.sum(expo, axis=-1, keepdims=True)


def head_lanes(lanes):
    side = lax.broadcasted_iota(jnp.int32, (1, lanes), 1) % TILE < DH
    return (side, jnp.logical_not(side))


def lasting(microseconds):
    return pl.CostEstimate(
        flops=int(microseconds * 0.58e9), bytes_accessed=0, transcendentals=0
    )


def moved(pairs, sem, first=0):
    copies = [pltpu.make_async_copy(a, b, sem.at[first + n]) for n, (a, b) in enumerate(pairs)]
    for copy in copies:
        copy.start()
    return copies


def wait_all(copies):
    for copy in copies:
        copy.wait()


def only(keep, value):
    return jnp.where(keep, value, jnp.zeros_like(value))


def column_keep(info_ref, own_cols, near, part):
    key = lax.broadcasted_iota(jnp.int32, (1, 2 * near), 1)
    far = key >= near
    inner = key % near
    x = jnp.where(far, 1 - info_ref[1], info_ref[1])
    c = jnp.where(inner >= part, 1 - info_ref[2], info_ref[2])
    column = x * near + c * part + inner % part
    return column < info_ref[3]


def live_pair(value, row, info_ref):
    lane = lax.broadcasted_iota(jnp.int32, (1, value.shape[1]), 1) // TILE + row
    return only(lane < info_ref[4], value)


def head_pair(ref, row, lane):
    blocks, _, part, _ = ref.shape
    found = [ref[:, row + n, :, lane : lane + TILE].reshape(blocks * part, TILE) for n in (0, 1)]
    return jnp.concatenate(found, axis=1)


def row_fwd_kernel(token_plan, weight_plan, place_ref, info_ref, tie_ref, *refs):
    bf16 = jnp.bfloat16
    f32 = jnp.float32
    tokens, refs = refs[: len(token_plan)], refs[len(token_plan) :]
    stacks, refs = refs[: len(weight_plan)], refs[len(weight_plan) :]
    own_ref, near_tokens_ref, far_tokens_ref, w_ref, gain_ref, near_ref, far_ref, o_ref = refs[:8]
    all_ref, norm_ref, token_sem, weight_sem = refs[8:]
    blocks, rows, part, lanes = near_ref.shape
    half = lanes // 3
    count = rows * part
    near = blocks * part
    copies = []
    for stack, (j, k) in zip(tokens, token_plan):
        x = lax.bitwise_xor(place_ref[1], j)
        for i in range(4):
            row = lax.bitwise_xor(place_ref[0], i) * 2 + x
            moves = [(stack.at[i, pl.ds(0, 2 * part)], all_ref.at[k, row])]
            if k == 0:
                moves.append((stack.at[i, pl.ds(2 * part, 16)], norm_ref.at[j * 4 + i]))
            for source, target in moves:
                copies.append(pltpu.make_async_copy(source, target, token_sem.at[len(copies)]))
    weights = placing(weight_plan, row_attn_at, place_ref, stacks, [w_ref], weight_sem)
    for copy in copies + weights:
        copy.start()
    for copy in copies:
        copy.wait()
    gains = jnp.sum(norm_ref[...].astype(f32), axis=0)
    gain_ref[...] = gains
    x = info_ref[1]
    for ref, side in ((near_tokens_ref, x), (far_tokens_ref, 1 - x)):
        at = pl.ds(pl.multiple_of(side * part, part), part)
        for k in range(blocks):
            value = all_ref[k, :, at, :].reshape(count, -1)
            if k == 0:
                @pl.when(side == x)
                def _():
                    own_ref[...] = value
            found = normed(value.astype(f32), gains[0:1], gains[1:2])[0]
            ref[k * count : (k + 1) * count] = found.astype(bf16)
    for copy in weights:
        copy.wait()
    for n in range(3):
        at = slice(n * half, (n + 1) * half)
        found = contract(near_tokens_ref[...], w_ref[:, at], PLAIN).astype(bf16)
        near_ref[:, :, :, at] = found.reshape(blocks, rows, part, half)
        if n > 0:
            found = contract(far_tokens_ref[...], w_ref[:, at], PLAIN).astype(bf16)
            far_ref[:, :, :, (n - 1) * half : n * half] = found.reshape(blocks, rows, part, half)
    sides = head_lanes(2 * TILE)
    keep = column_keep(info_ref, near, near, part)
    tie = tie_ref[0]
    for lane in range(0, half, TILE):
        scores = [jnp.zeros((near, 2 * near), f32) for _ in sides]
        for row in range(0, rows, 2):
            query = live_pair(head_pair(near_ref, row, lane), row, info_ref)
            key = jnp.concatenate(
                [head_pair(near_ref, row, half + lane), head_pair(far_ref, row, lane)], axis=0
            )
            for n, side in enumerate(sides):
                scores[n] = scores[n] + contract(only(side, query), key, LAST)
        probs = [softmax_of(s * tie, keep).astype(bf16) for s in scores]
        for row in range(0, rows, 2):
            value = jnp.concatenate(
                [head_pair(near_ref, row, 2 * half + lane), head_pair(far_ref, row, half + lane)],
                axis=0,
            )
            mixed = jnp.where(
                sides[0], contract(probs[0], value, PLAIN), contract(probs[1], value, PLAIN)
            ).astype(bf16)
            for n in (0, 1):
                o_ref[:, row + n, :, lane : lane + TILE] = mixed[:, n * TILE : (n + 1) * TILE].reshape(
                    blocks, part, TILE
                )


def next_sums_kernel(
    place_ref, y_kept_ref, y_got_ref, x_kept_ref, x_got_ref, to_x_ref, with_x_ref, to_y_ref, with_y_ref
):
    _, depth, lanes = to_x_ref.shape
    first, first_y = place_ref[1] == 0, place_ref[3] == 0
    summed = added(y_kept_ref[...], y_got_ref[...]).reshape(2, depth, lanes)
    with_x_ref[0] = jnp.where(first, summed[0], summed[1])
    to_x_ref[0] = jnp.where(first, summed[1], summed[0])
    summed = added(x_kept_ref[0], x_got_ref[0])
    with_y_ref[0] = jnp.where(first_y, summed[0], summed[1])
    to_y_ref[0] = jnp.where(first_y, summed[1], summed[0])


def next_sums(place, y_kept, y_got, x_kept, x_got):
    zs, _, depth, lanes = x_kept.shape
    by_rows = pl.BlockSpec((2 * depth, lanes), lambda n: (n, 0))
    by_z = pl.BlockSpec((1, 2, depth, lanes), lambda n: (n, 0, 0, 0))
    return pl.pallas_call(
        next_sums_kernel,
        grid=(zs,),
        in_specs=[pl.BlockSpec(memory_space=pltpu.SMEM), by_rows, by_rows, by_z, by_z],
        out_specs=[pl.BlockSpec((1, depth, lanes), lambda n: (n, 0, 0))] * 4,
        out_shape=[jax.ShapeDtypeStruct((zs, depth, lanes), jnp.bfloat16)] * 4,
        cost_estimate=lasting(4),
        compiler_params=pltpu.CompilerParams(vmem_limit_bytes=56 * 2**20),
    )(place, y_kept, y_got, x_kept, x_got)


def row_bwd_kernel(
    info_ref, tie_ref, near_ref, far_ref, own_ref, got_ref, w_any, near_any, far_any,
    near_part_any, near_theirs_any, far_part_any, far_theirs_any, sent_ref, kept_ref,
    do_ref, d_near_ref, d_far_ref, w_ref, near_tokens_ref, far_tokens_ref,
    near_part_ref, near_theirs_ref, far_part_ref, far_theirs_ref, sem,
):
    arriving = moved(
        [(w_any, w_ref), (near_any, near_tokens_ref), (far_any, far_tokens_ref)], sem
    )
    bf16 = jnp.bfloat16
    blocks, rows, part, lanes = near_ref.shape
    half = lanes // 3
    near = blocks * part
    sides = head_lanes(2 * TILE)
    keep = column_keep(info_ref, near, near, part)
    tie = tie_ref[0]
    do_ref[0] = own_ref[...].reshape(rows, part, half)
    do_ref[1] = got_ref[...].reshape(rows, part, half)

    for lane in range(0, half, TILE):

        def pair(ref, row, first):
            at = slice(first + lane, first + lane + TILE)
            found = [ref[:, row + n, :, at].reshape(near, TILE) for n in (0, 1)]
            return jnp.concatenate(found, axis=1)

        def both(row, first):
            return jnp.concatenate(
                [pair(near_ref, row, first), pair(far_ref, row, first - half)], axis=0
            )

        scores = [jnp.zeros((near, 2 * near), jnp.float32) for _ in sides]
        grads = [jnp.zeros((near, 2 * near), jnp.float32) for _ in sides]
        for row in range(0, rows, 2):
            query = live_pair(pair(near_ref, row, 0), row, info_ref)
            key, value = both(row, half), both(row, 2 * half)
            out = pair(do_ref, row, 0)
            for n, side in enumerate(sides):
                scores[n] = scores[n] + contract(only(side, query), key, LAST)
                grads[n] = grads[n] + contract(only(side, out), value, LAST)
        probs = [softmax_of(s * tie, keep) for s in scores]
        lows = [p.astype(bf16) for p in probs]
        deltas = [softmax_back(p, g).astype(bf16) for p, g in zip(probs, grads)]
        low_turned = [p.T for p in lows]
        delta_turned = [d.T for d in deltas]
        for row in range(0, rows, 2):
            query = live_pair(pair(near_ref, row, 0), row, info_ref)
            key, out = both(row, half), pair(do_ref, row, 0)
            dq = [contract(d, key, PLAIN) for d in deltas]
            dk = [contract(d, query, PLAIN) for d in delta_turned]
            dv = [contract(p, out, PLAIN) for p in low_turned]
            dq = live_pair(jnp.where(sides[0], dq[0], dq[1]) * tie, row, info_ref).astype(bf16)
            dk = (jnp.where(sides[0], dk[0], dk[1]) * tie).astype(bf16)
            dv = jnp.where(sides[0], dv[0], dv[1]).astype(bf16)

            def put(ref, first, value):
                for n in (0, 1):
                    piece = value[:, n * TILE : (n + 1) * TILE].reshape(blocks, part, TILE)
                    ref[:, row + n, :, first + lane : first + lane + TILE] = piece

            put(d_near_ref, 0, dq)
            put(d_near_ref, half, dk[:near])
            put(d_near_ref, 2 * half, dv[:near])
            put(d_far_ref, 0, dk[near:])
            put(d_far_ref, half, dv[near:])

    count = rows * part
    wait_all(arriving)
    d_far = d_far_ref[...].reshape(blocks * count, 2 * half)
    far_weights = w_ref[:, half:]
    far_part_ref[...] = contract(d_far[:count], far_weights, LAST)
    far_theirs_ref[...] = contract(d_far[count:], far_weights, LAST).astype(bf16)
    d_near = d_near_ref[...].reshape(blocks * count, lanes)
    near_part_ref[...] = contract(d_near[:count], w_ref[...], LAST)
    near_theirs_ref[...] = contract(d_near[count:], w_ref[...], LAST).astype(bf16)
    leaving = moved(
        [
            (far_theirs_ref, far_theirs_any),
            (near_theirs_ref, near_theirs_any),
            (far_part_ref, far_part_any),
            (near_part_ref, near_part_any),
        ],
        sem,
        3,
    )
    near_turned = near_tokens_ref[...].T
    far_turned = far_tokens_ref[...].T
    zs, depth = kept_ref.shape[0], kept_ref.shape[1]
    first = info_ref[1] == 0
    for n in range(3):
        at = slice(n * half, (n + 1) * half)
        terms = contract(near_turned, d_near[:, at], PLAIN)
        if n > 0:
            terms = terms + contract(far_turned, d_far[:, (n - 1) * half : n * half], PLAIN)
        terms = terms.astype(bf16).reshape(zs, 2, depth, half)
        kept_ref[:, :, at] = jnp.where(first, terms[:, 0], terms[:, 1])
        sent_ref[:, :, at] = jnp.where(first, terms[:, 1], terms[:, 0])
    wait_all(leaving)


def row_attention(place, info, tie, tokens, weights, rows, half):
    f32, bf16 = jnp.float32, jnp.bfloat16
    zs, deep, width = tokens[0][1].shape
    part = (deep - 16) // 2
    count = rows * part
    small = pl.BlockSpec(memory_space=pltpu.SMEM)
    anywhere = pl.BlockSpec(memory_space=pl.ANY)
    inside = pl.BlockSpec(memory_space=pltpu.VMEM)
    shapes = [
        ((count, width), bf16),
        ((2 * count, width), bf16),
        ((2 * count, width), bf16),
        ((width, 3 * half), bf16),
        ((16, width), f32),
        ((2, rows, part, 3 * half), bf16),
        ((2, rows, part, 2 * half), bf16),
        ((2, rows, part, half), bf16),
    ]
    return pl.pallas_call(
        partial(row_fwd_kernel, [step for step, _ in tokens], plan_of(weights)),
        in_specs=[small] * 3 + [anywhere] * (len(tokens) + len(weights)),
        out_specs=[inside] * len(shapes),
        out_shape=[jax.ShapeDtypeStruct(shape, kind) for shape, kind in shapes],
        scratch_shapes=[
            pltpu.VMEM((2, rows, 2 * part, width), bf16),
            pltpu.VMEM((8, 16, width), bf16),
            pltpu.SemaphoreType.DMA((24,)),
            pltpu.SemaphoreType.DMA((16,)),
        ],
        compiler_params=pltpu.CompilerParams(vmem_limit_bytes=56 * 2**20),
        cost_estimate=lasting(13),
    )(place, info, tie, *[v for _, v in tokens], *[v for _, v, _ in weights])


def row_attention_back(info, tie, near, far, own, got, weights, near_tokens, far_tokens):
    blocks, rows, part, lanes = near.shape
    count, width = rows * part, weights.shape[0]
    half = lanes // 3
    f32, bf16 = jnp.float32, jnp.bfloat16
    small = pl.BlockSpec(memory_space=pltpu.SMEM)
    anywhere = pl.BlockSpec(memory_space=pl.ANY)
    inside = pl.BlockSpec(memory_space=pltpu.VMEM)
    shapes = [((count, width), kind) for kind in (f32, bf16) * 2]
    shapes = shapes + [((4, width // 8, lanes), bf16)] * 2
    return pl.pallas_call(
        row_bwd_kernel,
        in_specs=[small, small] + [inside] * 4 + [anywhere] * 3,
        out_specs=[anywhere] * 4 + [inside] * 2,
        out_shape=[jax.ShapeDtypeStruct(shape, kind) for shape, kind in shapes],
        scratch_shapes=[
            pltpu.VMEM((blocks, rows, part, half), bf16),
            pltpu.VMEM((blocks, rows, part, lanes), bf16),
            pltpu.VMEM((blocks, rows, part, 2 * half), bf16),
            pltpu.VMEM(weights.shape, bf16),
            pltpu.VMEM(near_tokens.shape, bf16),
            pltpu.VMEM(far_tokens.shape, bf16),
            *[pltpu.VMEM(shape, kind) for shape, kind in shapes[:4]],
            pltpu.SemaphoreType.DMA((7,)),
        ],
        cost_estimate=lasting(16),
        compiler_params=pltpu.CompilerParams(vmem_limit_bytes=56 * 2**20),
    )(info, tie, near, far, own, got, weights, near_tokens, far_tokens)


def normed(value, gain, shift):
    centred = value - jnp.mean(value, axis=-1, keepdims=True)
    scale = lax.rsqrt(jnp.mean(centred * centred, axis=-1, keepdims=True) + eps_norm)
    unit = centred * scale
    return unit * gain + shift, unit, scale


def normed_back(grad, unit, scale, gain):
    inner = grad * gain
    mean = jnp.mean(inner, axis=-1, keepdims=True)
    along = jnp.mean(inner * unit, axis=-1, keepdims=True)
    return scale * (inner - mean - unit * along)


def column_masks(info_ref, rows, part):
    tokens = rows * part
    key = lax.broadcasted_iota(jnp.int32, (tokens, tokens), 0)
    query = lax.broadcasted_iota(jnp.int32, (tokens, tokens), 1)
    same = key % part == query % part
    return jnp.logical_and(same, key // part < info_ref[4])


def stacked(value, sides):
    return jnp.concatenate([only(side, value) for side in sides], axis=0)


def column_probs(query, key, keep, sides):
    scores = contract(stacked(key, sides), query, LAST) * (1.0 / math.sqrt(DH))
    tokens = query.shape[0]
    probs = []
    for n in (0, 1):
        part = jnp.where(keep, scores[n * tokens : (n + 1) * tokens], masked_score)
        expo = jnp.exp(part - jnp.max(part, axis=0, keepdims=True))
        probs.append(expo / jnp.sum(expo, axis=0, keepdims=True))
    return probs


def col_fwd_kernel(plan, info_ref, place_ref, *refs):
    stacks, refs = refs[: len(plan)], refs[len(plan) :]
    x_ref, own_ref, other_ref, gain_ref, acts_ref, one_ref, qkv_ref = refs[:7]
    resid_ref, normed_three_ref, mixed_ref, three_ref, col_ref, seven_ref, sem = refs[7:]
    copies = placing(plan, col_attn_at, place_ref, stacks, [three_ref, col_ref, seven_ref], sem)
    for copy in copies:
        copy.start()
    bf16 = jnp.bfloat16
    rows, cols, lanes = qkv_ref.shape
    width = lanes // 3
    part = 16
    own, other = own_ref[...], other_ref[...]
    flip = info_ref[2] == 0
    mixed_one = jnp.concatenate(
        [jnp.where(flip, own, other), jnp.where(flip, other, own)], axis=1
    )
    acts_ref[:, :width] = mixed_one
    for copy in copies:
        copy.wait()
    stream = (x_ref[...].astype(jnp.float32) + contract(mixed_one, three_ref[...], PLAIN)).astype(bf16)
    one_ref[...] = stream
    normed_two = normed(stream.astype(jnp.float32), gain_ref[2:3], gain_ref[3:4])[0].astype(bf16)
    acts_ref[:, width : 2 * width] = normed_two
    for n in range(3):
        at = slice(n * width, (n + 1) * width)
        found = contract(normed_two, col_ref[:, at], PLAIN).astype(bf16)
        qkv_ref[:, :, at] = found.reshape(rows, cols, width)
    keep = column_masks(info_ref, rows, part)
    sides = head_lanes(TILE)

    def attend(b, carry):
        at = pl.ds(pl.multiple_of(b * part, part), part)
        def tile(n, t):
            lane = n * width + t * TILE
            return qkv_ref[:, at, lane : lane + TILE].reshape(rows * part, TILE)
        tiles = range(width // TILE)
        probs = [column_probs(tile(0, t), tile(1, t), keep, sides) for t in tiles]
        for t in tiles:
            low = jnp.concatenate(probs[t], axis=0).astype(bf16)
            mixed = contract(low, stacked(tile(2, t), sides), FIRST).astype(bf16)
            mixed_ref[:, at, t * TILE : (t + 1) * TILE] = mixed.reshape(rows, part, TILE)
        return carry

    lax.fori_loop(0, cols // part, attend, 0)
    mixed = mixed_ref[...].reshape(rows * cols, width)
    acts_ref[:, 2 * width :] = mixed
    resid = one_ref[...].astype(jnp.float32) + contract(mixed, seven_ref[...], PLAIN)
    resid_ref[...] = resid
    normed_three_ref[...] = normed(resid, gain_ref[4:5], gain_ref[5:6])[0].astype(bf16)


def col_bwd_kernel(plan, info_ref, place_ref, *refs):
    stacks, refs = refs[: len(plan)], refs[len(plan) :]
    up_ref, da_ref, out_ref, got_ref, resid_ref, one_ref, qkv_ref, gain_ref = refs[:8]
    result_ref, stream_ref, own_ref, other_ref, mine_ref, theirs_ref, norms_ref = refs[8:15]
    dqkv_ref, do_ref, three_ref, col_ref, seven_ref, sem = refs[15:]
    copies = placing(plan, col_attn_at, place_ref, stacks, [three_ref, col_ref, seven_ref], sem)
    for copy in copies:
        copy.start()
    bf16 = jnp.bfloat16
    f32 = jnp.float32
    rows, cols, lanes = qkv_ref.shape
    width = lanes // 3
    part = 16
    result_ref[...] = (resid_ref[...] + out_ref[...] + got_ref[0].astype(f32)).astype(bf16)
    da = da_ref[...] + got_ref[1].astype(f32)
    gain = gain_ref[4:5]
    _, unit, scale = normed(resid_ref[...], gain, 0.0)
    grad_three = up_ref[...].astype(f32) + normed_back(da, unit, scale, gain)
    norms_ref[2:3] = jnp.sum(da * unit, axis=0, keepdims=True)
    norms_ref[3:4] = jnp.sum(da, axis=0, keepdims=True)
    branch = grad_three.astype(bf16)
    half = width // 2
    flip = info_ref[2] == 0

    def put_halves(first, value):
        at = slice(first, first + half)
        mine_ref[:, at] = jnp.where(flip, value[:, :half], value[:, half:])
        theirs_ref[:, at] = jnp.where(flip, value[:, half:], value[:, :half])

    put_halves(4 * half, branch)
    for copy in copies:
        copy.wait()
    do_ref[...] = contract(branch, seven_ref[...], LAST).astype(bf16).reshape(rows, cols, width)
    keep = column_masks(info_ref, rows, part)
    sides = head_lanes(TILE)
    ratio = 1.0 / math.sqrt(DH)

    def attend(b, carry):
        at = pl.ds(pl.multiple_of(b * part, part), part)
        tokens = rows * part

        def tile(n, t):
            lane = n * width + t * TILE
            return qkv_ref[:, at, lane : lane + TILE].reshape(tokens, TILE)

        def out_tile(t):
            return do_ref[:, at, t * TILE : (t + 1) * TILE].reshape(tokens, TILE)

        def put(n, t, value):
            lane = n * width + t * TILE
            dqkv_ref[:, at, lane : lane + TILE] = value.astype(bf16).reshape(rows, part, TILE)

        for t in range(width // TILE):
            query, key, out = tile(0, t), tile(1, t), out_tile(t)
            keys = stacked(key, sides)
            probs = column_probs(query, key, keep, sides)
            grads = contract(stacked(tile(2, t), sides), out, LAST)
            deltas = []
            for n, p in enumerate(probs):
                g = grads[n * tokens : (n + 1) * tokens]
                deltas.append((p * (g - jnp.sum(p * g, axis=0, keepdims=True))).astype(bf16))
            put(0, t, contract(jnp.concatenate(deltas, axis=0), keys, FIRST) * ratio)
            wide = jnp.concatenate(deltas, axis=1)
            put(1, t, contract(wide, stacked(query, sides), PLAIN) * ratio)
            wide = jnp.concatenate([p.astype(bf16) for p in probs], axis=1)
            put(2, t, contract(wide, stacked(out, sides), PLAIN))
        return carry

    lax.fori_loop(0, cols // part, attend, 0)
    dqkv = dqkv_ref[...].reshape(rows * cols, lanes)
    for n in range(3):
        put_halves((n + 1) * half, dqkv[:, n * width : (n + 1) * width])
    grad_normed = contract(dqkv, col_ref[...], LAST)
    gain = gain_ref[2:3]
    _, unit, scale = normed(one_ref[...].astype(f32), gain, 0.0)
    norms_ref[0:1] = jnp.sum(grad_normed * unit, axis=0, keepdims=True)
    norms_ref[1:2] = jnp.sum(grad_normed, axis=0, keepdims=True)
    stream = (grad_three + normed_back(grad_normed, unit, scale, gain)).astype(bf16)
    stream_ref[...] = stream
    put_halves(0, stream)
    mixed = contract(stream, three_ref[...], LAST).astype(bf16)
    own_ref[...] = jnp.where(flip, mixed[:, :half], mixed[:, half:])
    other_ref[...] = jnp.where(flip, mixed[:, half:], mixed[:, :half])


def tokens_back_kernel(
    info_ref, near_ref, near_got_ref, far_got_ref, x_ref, stream_ref, gain_ref, norms_ref,
    blocks_ref,
):
    f32 = jnp.float32
    grad = near_ref[...] + near_got_ref[...].astype(f32) + far_got_ref[...].astype(f32)
    gain = gain_ref[0:1]
    _, unit, scale = normed(x_ref[...].astype(f32), gain, 0.0)
    found = stream_ref[...].astype(f32) + normed_back(grad, unit, scale, gain)
    rows, deep, width = blocks_ref.shape
    part = deep - 16
    blocks_ref[:, :part] = found.astype(jnp.bfloat16).reshape(rows, part, width)
    sums = [
        jnp.sum(grad * unit, axis=0, keepdims=True),
        jnp.sum(grad, axis=0, keepdims=True),
        norms_ref[...],
        jnp.zeros((2, width), f32),
    ]
    sums = jnp.concatenate(sums, axis=0)
    depth = width // 8
    lane = lax.broadcasted_iota(jnp.int32, (width, TILE), 0)
    place = lax.broadcasted_iota(jnp.int32, (width, TILE), 1)
    for shard in range(8):
        chosen = jnp.logical_and(lane == shard * depth + place, place < depth)
        found = lax.dot_general(
            sums,
            chosen.astype(f32),
            (PLAIN, ((), ())),
            precision=lax.Precision.HIGHEST,
            preferred_element_type=f32,
        )
        found = jnp.concatenate([found, jnp.zeros((8, TILE), f32)], axis=0)
        blocks_ref[shard, part:, :TILE] = found.astype(jnp.bfloat16)
        blocks_ref[shard, part:, TILE:] = jnp.zeros((16, width - TILE), jnp.bfloat16)


def attn_terms_kernel(place_ref, acts_ref, got_ref, mine_ref, theirs_ref, sent_ref, kept_ref):
    width = acts_ref.shape[1] // 3
    half = width // 2
    depth = sent_ref.shape[1]
    turned = [
        jnp.concatenate([ref[:, n * width : (n + 1) * width].T for ref in (acts_ref, got_ref)], axis=1)
        for n in range(3)
    ]
    first = place_ref[3] == 0
    for n, m in enumerate((0, 1, 1, 1, 2)):
        at = slice(n * half, (n + 1) * half)
        grads = jnp.concatenate([mine_ref[:, at], theirs_ref[:, at]], axis=0)
        terms = contract(turned[m], grads, PLAIN).astype(jnp.bfloat16)
        terms = terms.reshape(sent_ref.shape[0], 2, depth, half)
        kept_ref[:, :, at] = jnp.where(first, terms[:, 0], terms[:, 1])
        sent_ref[:, :, at] = jnp.where(first, terms[:, 1], terms[:, 0])


def column_call(kernel, info, place, pieces, args, outs, scratch, time):
    width = args[-1].shape[1]
    bf16 = jnp.bfloat16
    small = pl.BlockSpec(memory_space=pltpu.SMEM)
    inside = pl.BlockSpec(memory_space=pltpu.VMEM)
    anywhere = pl.BlockSpec(memory_space=pl.ANY)
    return pl.pallas_call(
        partial(kernel, plan_of(pieces)),
        in_specs=[small] * 2 + [anywhere] * len(pieces) + [inside] * len(args),
        out_specs=[inside] * len(outs),
        out_shape=[jax.ShapeDtypeStruct(shape, kind) for shape, kind in outs],
        scratch_shapes=[
            *scratch,
            pltpu.VMEM((width, width), bf16),
            pltpu.VMEM((width, 3 * width), bf16),
            pltpu.VMEM((width, width), bf16),
            pltpu.SemaphoreType.DMA((160,)),
        ],
        cost_estimate=lasting(time),
        compiler_params=pltpu.CompilerParams(vmem_limit_bytes=56 * 2**20),
    )(info, place, *[value for _, value, _ in pieces], *args)


def last_sums_kernel(place_ref, own_ref, *refs):
    f32 = jnp.float32
    got, (before_ref, sum_ref, squares_ref) = refs[:3], refs[3:]
    total = own_ref[...].astype(f32)
    for ref in got:
        total = total + ref[...].astype(f32)
    low = total.astype(jnp.bfloat16)
    sum_ref[...] = low
    low = low.astype(f32)
    squares = jnp.sum(low * low, axis=1, keepdims=True)
    squares = jnp.sum(squares, axis=0, keepdims=True) + before_ref[0:1, 0:1]
    squares_ref[...] = jnp.broadcast_to(squares[None], squares_ref.shape)


def clip_factor(squares_ref):
    total = jnp.sum(squares_ref[:, 0:1, 0:1], axis=0)
    return clip_bound / jnp.maximum(jnp.sqrt(total), clip_bound)


def adam_kernel(
    place_ref, squares_ref, row_ref, row_other_ref, col_ref, col_other_ref, w_ref, first_ref, second_ref, *outs
):
    count, _, width = w_ref.shape
    half = width // 2
    low = place_ref[2] == 0
    early = pl.program_id(0) == 0
    factor = clip_factor(squares_ref)
    for n in range(count):
        at = slice((n + 1) * half, (n + 2) * half)
        own, other = col_ref[:, at], col_other_ref[:, at]
        if n < 3:
            at = slice(n * half, (n + 1) * half)
            sooner, sooner_other = row_ref[:, at], row_other_ref[:, at]
        else:
            sooner, sooner_other = col_ref[:, :half], col_other_ref[:, :half]
        own, other = jnp.where(early, sooner, own), jnp.where(early, sooner_other, other)
        grad = jnp.concatenate([jnp.where(low, own, other), jnp.where(low, other, own)], axis=1)
        grad = grad.astype(jnp.float32) * factor
        first, second, weight = adam_update(w_ref[n], first_ref[n], second_ref[n], grad, matrix_rate)
        for ref, value in zip(outs, (first, second, weight, weight.astype(jnp.bfloat16))):
            ref[n] = value


def attn_adam(place, squares, grads, weight, first, second):
    small = pl.BlockSpec(memory_space=pltpu.SMEM)
    inside = pl.BlockSpec(memory_space=pltpu.VMEM)
    block = pl.BlockSpec((4, *weight.shape[1:]), lambda m: (m, 0, 0))
    kinds = [jnp.float32] * 3 + [jnp.bfloat16]
    return pl.pallas_call(
        adam_kernel,
        grid=(weight.shape[0] // 4,),
        in_specs=[small] + [inside] * 5 + [block] * 3,
        out_specs=[block] * 4,
        out_shape=[jax.ShapeDtypeStruct(weight.shape, kind) for kind in kinds],
        compiler_params=pltpu.CompilerParams(vmem_limit_bytes=40 * 2**20),
    )(place, squares, *grads, weight, first, second)


def ffn_adam_kernel(place_ref, squares_ref, *refs):
    pieces, refs = refs[:4], refs[4:]
    low, even = place_ref[2] == 0, place_ref[3] == 0
    factor = clip_factor(squares_ref)
    depth = pieces[0].shape[0]
    part = depth // 2
    half = pl.program_id(0)

    def by_matrix(first, second):
        return jnp.where(even, first, second), jnp.where(even, second, first)

    def put(grad, ins, outs):
        values = adam_update(*[ref[...] for ref in ins], grad * factor, matrix_rate)
        for ref, value in zip(outs, (*values, values[2].astype(jnp.bfloat16))):
            ref[...] = value

    rows = pl.ds(pl.multiple_of(half * part, 16), part)
    owns = by_matrix(pieces[0][rows], pieces[1][rows])
    others = by_matrix(pieces[2][rows], pieces[3][rows])
    for n, (own, other) in enumerate(zip(owns, others)):
        grad = jnp.concatenate([jnp.where(low, own, other), jnp.where(low, other, own)], axis=1)
        put(grad.astype(jnp.float32), refs[3 * n : 3 * n + 3], refs[6 + 4 * n : 10 + 4 * n])


def ffn_adam(place, squares, pieces, ins, outs):
    small = pl.BlockSpec(memory_space=pltpu.SMEM)
    inside = pl.BlockSpec(memory_space=pltpu.VMEM)
    depth, hidden = ins[0].shape
    block = pl.BlockSpec((depth // 2, hidden), lambda n: (n, 0))
    kinds = [jnp.float32] * 3 + [jnp.bfloat16]
    return pl.pallas_call(
        ffn_adam_kernel,
        grid=(2,),
        in_specs=[small] + [inside] * 5 + [block] * 6,
        out_specs=[block] * 8,
        out_shape=[jax.ShapeDtypeStruct((depth, hidden), kind) for kind in kinds * 2],
        compiler_params=pltpu.CompilerParams(vmem_limit_bytes=58 * 2**20),
    )(place, squares, *pieces, *ins, *[value.T for value in outs])


def whole_call(kernel, info, args, outs, time):
    inside = pl.BlockSpec(memory_space=pltpu.VMEM)
    return pl.pallas_call(
        kernel,
        in_specs=[pl.BlockSpec(memory_space=pltpu.SMEM)] + [inside] * len(args),
        out_specs=[inside] * len(outs),
        out_shape=[jax.ShapeDtypeStruct(shape, kind) for shape, kind in outs],
        cost_estimate=lasting(time),
        compiler_params=pltpu.CompilerParams(vmem_limit_bytes=56 * 2**20),
    )(info, *args)


def gelu_pair(u):
    ratio = math.sqrt(2.0 / math.pi)
    square = u * u
    tanh = jnp.tanh(ratio * u * (1.0 + 0.044715 * square))
    rise = 0.5 * (1.0 + tanh)
    slope = (0.5 * ratio) * (1.0 - tanh * tanh) * (1.0 + (3.0 * 0.044715) * square)
    return u * rise, rise + u * slope


def ffn_kernel(plan, place_ref, a_ref, a_got_ref, up_ref, up_got_ref, *refs):
    bf16 = jnp.bfloat16
    stacks, refs = refs[: len(plan)], refs[len(plan) :]
    out_ref, da_ref, others_ref = refs[:3]
    y_sent_ref, y_kept_ref, x_sent_ref, x_kept_ref = refs[3:7]
    w_ref, turned_ref, out_sum, da_sum, sem = refs[7:]
    count, width = a_ref.shape
    chunk = w_ref.shape[1] // 2
    copies = placing(plan, ffn_at, place_ref, stacks, [w_ref], sem, steps=False)
    for copy in copies:
        copy.start()
    for n, ref in enumerate((a_ref, a_got_ref, up_ref, up_got_ref)):
        turned_ref[n // 2, :, (n % 2) * count : (n % 2 + 1) * count] = ref[...].T
    for copy in copies:
        copy.wait()
    for step in (0, 1):
        lane = slice(step * chunk, (step + 1) * chunk)
        w_in = w_ref[:width, lane]
        w_out = w_ref[width:, lane]
        activs, grads = [], []
        for n, (tokens, ups) in enumerate(((a_ref, up_ref), (a_got_ref, up_got_ref))):
            at = slice(n * count, (n + 1) * count)
            activ, slope = gelu_pair(contract(tokens[...], w_in, PLAIN))
            activ = activ.astype(bf16)
            grad = (contract(ups[...], w_out, PLAIN) * slope).astype(bf16)
            out, da = contract(activ, w_out, LAST), contract(grad, w_in, LAST)
            if step == 0:
                out_sum[at] = out
                da_sum[at] = da
            elif n == 0:
                out_ref[...] = out_sum[at] + out
                da_ref[...] = da_sum[at] + da
            else:
                others_ref[0] = (out_sum[at] + out).astype(bf16)
                others_ref[1] = (da_sum[at] + da).astype(bf16)
            activs.append(activ)
            grads.append(grad)
        in_terms = contract(turned_ref[0], jnp.concatenate(grads, axis=0), PLAIN).astype(bf16)
        out_terms = contract(turned_ref[1], jnp.concatenate(activs, axis=0), PLAIN).astype(bf16)
        if step == 0:
            first = place_ref[3] == 0
            y_kept_ref[...] = jnp.where(first, in_terms, out_terms)
            y_sent_ref[...] = jnp.where(first, out_terms, in_terms)
        else:
            first = place_ref[1] == 0
            zs, _, depth, _ = x_sent_ref.shape
            for n, terms in enumerate((in_terms, out_terms)):
                terms = terms.reshape(zs, 2, depth, chunk)
                x_kept_ref[:, n] = jnp.where(first, terms[:, 0], terms[:, 1])
                x_sent_ref[:, n] = jnp.where(first, terms[:, 1], terms[:, 0])


def feed_forward(place, normed_own, normed_got, up_own, up_got, pieces):
    count, width = normed_own.shape
    half = pieces[0][1].shape[-1]
    anywhere = pl.BlockSpec(memory_space=pl.ANY)
    inside = pl.BlockSpec(memory_space=pltpu.VMEM)
    f32, bf16 = jnp.float32, jnp.bfloat16
    shapes = [((count, width), f32)] * 2 + [((2, count, width), bf16)]
    shapes = shapes + [((width, half // 2), bf16)] * 2 + [((4, 2, width // 8, half // 2), bf16)] * 2
    return pl.pallas_call(
        partial(ffn_kernel, plan_of(pieces)),
        in_specs=[pl.BlockSpec(memory_space=pltpu.SMEM)] + [inside] * 4 + [anywhere] * len(pieces),
        out_specs=[inside] * 7,
        out_shape=[jax.ShapeDtypeStruct(shape, kind) for shape, kind in shapes],
        scratch_shapes=[
            pltpu.VMEM((2 * width, half), bf16),
            pltpu.VMEM((2, width, 2 * count), bf16),
            pltpu.VMEM((2 * count, width), f32),
            pltpu.VMEM((2 * count, width), f32),
            pltpu.SemaphoreType.DMA((16,)),
        ],
        cost_estimate=lasting(22),
        compiler_params=pltpu.CompilerParams(vmem_limit_bytes=56 * 2**20),
    )(place, normed_own, normed_got, up_own, up_got, *[value for _, value, _ in pieces])


def added(a, b):
    return (a.astype(jnp.float32) + b.astype(jnp.float32)).astype(jnp.bfloat16)


def gather_turned(column, z):
    return [
        lax.ppermute(pick(column, lax.bitwise_xor(z, i), 0), "z", [(k, k ^ i) for k in range(4)])
        for i in (1, 2, 3)
    ]


def z_summed(column, z):
    parts = [pick(column, z, 0)] + gather_turned(column, z)
    return sum(part.astype(jnp.float32) for part in parts).astype(jnp.bfloat16)


def paired_body(
    tokens,
    cotangent,
    col_count,
    row_count,
    attn_weight,
    in_weight,
    out_weight,
    norm_param,
    attn_first,
    attn_second,
    in_first,
    in_second,
    out_first,
    out_second,
    norm_first,
    norm_second,
):
    f32 = jnp.float32
    bf16 = jnp.bfloat16
    z, x, y, c = (lax.axis_index(name) for name in ("z", "x", "y", "c"))
    width = tokens.shape[-1]
    hidden = in_weight.shape[1]
    depth = in_weight.shape[0]
    half = width // 2
    hidden_half = hidden // 2

    counts = jnp.stack([col_count, row_count])
    other_counts = swap(counts, "c")
    mine = jnp.where(z // 2 == c, counts, other_counts)
    mine = pick(mine, z % 2, 1)
    cols_live, rows_live = mine[0], mine[1]
    place = jnp.stack([z, x, c, y]).astype(jnp.int32)
    info = jnp.concatenate([place[:3], mine, place[3:]])
    tie = (lax.rsqrt(rows_live.astype(f32)) * (1.0 / math.sqrt(DH))).reshape(1)

    attn_low = attn_weight.astype(bf16)
    halves = attn_low.reshape(8, depth, 2, half)
    row_half = jnp.moveaxis(pick(halves[:3], c, 2), 0, 1).reshape(2, depth // 2, 3 * half)
    row_quarter = pick(row_half, y, 0)
    col_quarter = pick(pick(halves[3:], c, 2).reshape(5, 2, depth // 2, half), y, 1)
    row_z = gather_z(row_quarter)
    ffn_low = [in_weight.astype(bf16), out_weight.astype(bf16).T]
    ffn_low = [
        jnp.where(c == 0, low[:, :hidden_half], low[:, hidden_half:]) for low in ffn_low
    ]
    ffn_quarter = jnp.where(y == 0, *ffn_low)

    lanes = jnp.arange(width, dtype=jnp.int32) // depth
    norm_low = jnp.tile(norm_param.astype(bf16), (1, width // depth))
    norm_rows = jnp.where(lanes[None] == z * 2 + x, norm_low, jnp.zeros_like(norm_low))
    norm_rows = jnp.pad(norm_rows, ((0, 10), (0, 0)))
    part = tokens.shape[2] // 4
    tokens_here = merge_cores(tokens, c).reshape(4, 2 * part, width)
    parts = [
        jnp.concatenate([pick(tokens_here, lax.bitwise_xor(z, i), 0), norm_rows]) for i in range(4)
    ]
    parts = [parts[0]] + [
        lax.ppermute(parts[i], "z", [(k, k ^ i) for k in range(4)]) for i in (1, 2, 3)
    ]
    row_pieces = spread(jnp.stack(row_z))
    row_x, row_y, *parts, col_quarter = together(
        row_pieces[1][1], row_pieces[2][1], *parts, col_quarter
    )
    tokens_z = jnp.stack(parts)
    up = merge_cores(cotangent, c).reshape(4, 2, part, width)
    up = joined(pick(up, x, 1)[:, None], swap(pick(up, 1 - x, 1), "x")[:, None], x, 1)
    col_z = gather_z(col_quarter)
    tokens_x, row_last, ffn_quarter, up, *col_z = together(
        swap(tokens_z, "x"), swap(row_x, "y"), ffn_quarter, up, *col_z
    )
    steps = [(0, 0, 0), (1, 0, 0), (0, 1, 0), (1, 1, 0)]
    row_stacks = [row_pieces[0][1], row_x, row_y, row_last]
    row_pieces = [(step, value, 0) for step, value in zip(steps, row_stacks)]
    col_z = jnp.stack(col_z)
    ffn_z = lax.all_to_all(
        jnp.broadcast_to(ffn_quarter, (4, *ffn_quarter.shape)), "z", 0, 0, tiled=True
    )
    col_x, col_y = swap(col_z, "x"), swap(col_z, "y")
    col_across = across(col_x, col_y)
    col_x, col_y, ffn_z, up = together(col_x, col_y, ffn_z, up)
    tokens_far, *col_across = together(swap(tokens_x, "c"), *col_across)
    ffn_x, ffn_y = swap(ffn_z, "x"), swap(ffn_z, "y")
    up = lax.all_to_all(up, "z", 0, 0, tiled=True)

    rows = 8
    count = rows * part
    stream_zero, near_normed, far_normed, w_row, norm_gain, near, far, mixed_heads = row_attention(
        place,
        info,
        tie,
        [((0, 0), tokens_z), ((1, 0), tokens_x), ((0, 1), swap(tokens_z, "c")), ((1, 1), tokens_far)],
        row_pieces,
        rows,
        half,
    )
    mixed_heads = mixed_heads.reshape(2, count, half)
    col_stacks = [col_z, col_x, col_y]
    mixed_heads, ffn_x, ffn_y, *col_others = together(
        mixed_heads, ffn_x, ffn_y, *[swap(value, "c") for value in col_stacks]
    )
    up = up.reshape(rows, part, width)
    col_pieces = [(step, v, 0) for step, v in zip(steps, col_stacks)] + across_pieces(*col_across)
    col_others = [(step, v, 0) for step, v in zip(steps, col_others)]
    col_others = col_others + across_pieces(*[swap(v, "c") for v in col_across])
    col_pieces = col_pieces + [((j, m, 1), v, first) for (j, m, _), v, first in col_others]
    ffn_pieces = [(step, v, 0) for step, v in zip(steps, [ffn_z, ffn_x, ffn_y])]

    whole_shape, wide_shape = ((count, width), bf16), ((rows, part, 3 * width), bf16)
    acts, stream_one, qkv_two, resid_three, normed_three = column_call(
        col_fwd_kernel,
        info,
        place,
        col_pieces,
        [stream_zero, mixed_heads[0], swap(mixed_heads[1], "c"), norm_gain],
        [((count, 3 * width), bf16), whole_shape, wide_shape, ((count, width), f32), whole_shape],
        [pltpu.VMEM((rows, part, width), bf16)],
        14,
    )
    normed_three, *ffn_across = together(normed_three, *across(ffn_x, ffn_y))
    ffn_pieces = ffn_pieces + across_pieces(*ffn_across)

    column = x * (2 * part) + c * part + jnp.arange(part, dtype=jnp.int32)
    live = jnp.logical_and(
        (jnp.arange(rows, dtype=jnp.int32) < rows_live)[:, None], (column < cols_live)[None, :]
    )
    up = jnp.where(live[..., None], up, jnp.zeros_like(up)).reshape(count, width)
    out_own, da_own, other_parts, *ffn_terms = feed_forward(
        place, normed_three, swap(normed_three, "c"), up, swap(up, "c"), ffn_pieces
    )
    other_parts = swap(other_parts, "c")
    y_sent, y_kept, x_sent, x_kept = ffn_terms
    y_got, x_got = swap(y_sent, "y"), swap(x_sent, "x")

    acts_got = swap(acts, "c")
    result, grad_stream, grad_own, grad_other, attn_mine, attn_theirs, col_norms = column_call(
        col_bwd_kernel,
        info,
        place,
        col_pieces,
        [up, da_own, out_own, other_parts, resid_three, stream_one, qkv_two, norm_gain],
        [whole_shape] * 2
        + [((count, half), bf16)] * 2
        + [((count, 5 * half), bf16)] * 2
        + [((4, width), f32)],
        [pltpu.VMEM((rows, part, 3 * width), bf16), pltpu.VMEM((rows, part, width), bf16)],
        23,
    )

    result, x_got, y_got = together(result, x_got, y_got)
    block_out = to_blocks(result.reshape(rows, part, width))
    ffn_to_x, ffn_x, ffn_to_y, ffn_y = next_sums(place, y_kept, y_got, x_kept, x_got)
    near_part, near_theirs, far_part, far_theirs, row_sent, row_kept = row_attention_back(
        info, tie, near, far, grad_own, swap(grad_other, "c"), w_row, near_normed, far_normed
    )
    (
        row_sent, far_theirs, near_theirs, attn_theirs, block_out, ffn_x_got, ffn_y_got
    ) = together(
        row_sent, far_theirs, near_theirs, attn_theirs, block_out,
        swap(ffn_to_x, "x"), swap(ffn_to_y, "y"),
    )
    row_got = swap(row_sent, "x")
    far_sum = added(far_part, swap(far_theirs, "c"))
    far_sum, attn_mine = together(far_sum, attn_mine)
    far_got = swap(far_sum, "x")
    near_got = swap(near_theirs, "c")
    attn_sent, attn_kept = whole_call(
        attn_terms_kernel,
        place,
        [acts, acts_got, attn_mine, swap(attn_theirs, "c")],
        [((8, depth // 2, 5 * half), bf16)] * 2,
        9,
    )
    ffn_column = jnp.concatenate([added(ffn_x, ffn_x_got), added(ffn_y, ffn_y_got)], axis=2)
    ffn_own = lax.all_to_all(ffn_column, "z", 0, 0, tiled=True)
    attn_sent, attn_kept, ffn_own, row_got = together(attn_sent, attn_kept, ffn_own, row_got)
    attn_got = swap(attn_sent, "y")
    ffn_own = jnp.sum(ffn_own.astype(f32), axis=0).astype(bf16)
    ffn_own, row_got, block_out = together(ffn_own, row_got, block_out)
    row_own = z_summed(added(row_kept, row_got), z)
    attn_pair_terms = added(attn_kept, attn_got).reshape(4, 2, depth // 2, 5 * half)
    attn_column = pick(attn_pair_terms, x, 1)
    attn_x_got = swap(pick(attn_pair_terms, 1 - x, 1), "x")
    blocks = whole_call(
        tokens_back_kernel,
        info,
        [near_part, near_got, far_got, stream_zero, grad_stream, norm_gain, col_norms],
        [((rows, part + 16, width), bf16)],
        5,
    )[0]
    blocks, row_own = together(blocks, row_own)
    blocks = to_blocks(blocks)
    grad_tokens = to_rows(blocks[:, :part], c).astype(f32)
    norm_grad = jnp.sum(blocks[:, part : part + 8, :TILE].astype(f32), axis=0)
    block_out = to_rows(block_out, c)
    attn_column = added(attn_column, attn_x_got)
    norm_parts = [norm_grad] + [
        lax.ppermute(norm_grad, ("y", "c"), [(k, k ^ i) for k in range(4)]) for i in (1, 2, 3)
    ]
    norm_grad = (norm_parts[0] + norm_parts[1]) + (norm_parts[2] + norm_parts[3])
    norm_grad = norm_grad[:6, :depth]
    row_grad = added(row_own, swap(row_own, "y"))
    before = jnp.sum(jnp.square(ffn_own.astype(f32)))
    before = before + 0.5 * jnp.sum(jnp.square(row_grad.astype(f32)))
    before = before + 0.25 * jnp.sum(norm_grad * norm_grad)
    attn_own, squares = whole_call(
        last_sums_kernel,
        place,
        [
            pick(attn_column, z, 0),
            *gather_turned(attn_column, z),
            jnp.broadcast_to(before, (8, TILE)),
        ],
        [((depth // 2, 5 * half), bf16), ((32, 8, TILE), f32)],
        2,
    )
    attn_own, block_out = together(attn_own, block_out)
    squares = lax.all_to_all(squares, ("z", "x", "y", "c"), 0, 0, tiled=True)
    attn_grad_b = joined(attn_own, swap(attn_own, "y"), y, 0)
    ffn_grads = [ffn_own, swap(ffn_own, "y")]

    row_other = swap(row_grad, "c")
    attn_other = swap(attn_grad_b, "c")
    ffn_others = [swap(piece, "c") for piece in ffn_grads]

    grad_norm = jnp.sqrt(jnp.sum(squares[:, 0, 0]))
    factor = clip_bound / jnp.maximum(grad_norm, clip_bound)
    attn_first_new, attn_second_new, attn_weight_new, attn_copy = attn_adam(
        place,
        squares,
        (row_grad, row_other, attn_grad_b, attn_other),
        attn_weight,
        attn_first,
        attn_second,
    )
    in_first_new, in_second_new, in_weight_new, in_copy, *turned = ffn_adam(
        place,
        squares,
        [*ffn_grads, *ffn_others],
        (in_weight, in_first, in_second),
        (out_weight, out_first, out_second),
    )
    out_first_new, out_second_new, out_weight_new, out_copy = [value.T for value in turned]
    norm_first_new, norm_second_new, norm_new = adam_update(
        norm_param, norm_first, norm_second, norm_grad * factor, norm_rate
    )
    return (
        block_out,
        grad_tokens,
        grad_norm,
        attn_first_new,
        attn_second_new,
        attn_weight_new,
        attn_copy,
        in_first_new,
        in_second_new,
        in_weight_new,
        in_copy,
        out_first_new,
        out_second_new,
        out_weight_new,
        out_copy,
        norm_first_new,
        norm_second_new,
        norm_new,
    )


def paired_layout(mesh):
    return dict(mesh.shape) == {"seq": 8, "grp": 4}


def mapped(run, mesh, seq, grp):
    placed = (
        P(grp, seq, None, None),
        P(grp, seq, None, None),
        P(grp),
        P(grp),
        P(None, seq, None),
        P(seq, None),
        P(None, seq),
        P(None, seq),
        P(None, seq, None),
        P(None, seq, None),
        P(seq, None),
        P(seq, None),
        P(None, seq),
        P(None, seq),
        P(None, seq),
        P(None, seq),
    )
    return jax.shard_map(
        run,
        mesh=mesh,
        in_specs=placed,
        out_specs=(
            P(grp, seq, None, None),
            P(grp, seq, None, None),
            P(),
            P(None, seq, None),
            P(None, seq, None),
            P(None, seq, None),
            P(None, seq, None),
            P(seq, None),
            P(seq, None),
            P(seq, None),
            P(seq, None),
            P(None, seq),
            P(None, seq),
            P(None, seq),
            P(None, seq),
            P(None, seq),
            P(None, seq),
            P(None, seq),
        ),
        check_vma=False,
    )


def solution(mesh):
    if not paired_layout(mesh):
        return mapped(general_body, mesh, "seq", "grp")
    fine = Mesh(mesh.devices.reshape(4, 2, 2, 2), ("z", "x", "y", "c"))
    return mapped(paired_body, fine, ("z", "x"), ("y", "c"))
```
